32 devices in a mesh: seq: 8 (over z, y), batch: 4 (over x, core).
Axes of the slice: x: 2, y: 2, z: 4, core: 2. Of those that a mesh axis runs over, the one named last changes fastest.
Arguments:
- tokens: bfloat16 [8, 2048, 512], P('batch', 'seq'), may hold values from -6 to 6
- norm_gain: bfloat16 [2, 512], P(None, 'seq'), may hold values from 0.099609375 to 1.8984375
- w_forget: bfloat16 [2, 512, 1024], P(None, 'seq', 'batch'), may hold values from -0.25 to 0.25
- w_input: bfloat16 [2, 512, 1024], P(None, 'seq', 'batch'), may hold values from -0.25 to 0.25
- w_cand: bfloat16 [2, 512, 1024], P(None, 'seq', 'batch'), may hold values from -0.25 to 0.25
- forget_bias: bfloat16 [2, 1024], P(None, 'seq'), may hold values from 1 to 4
- input_bias: bfloat16 [2, 1024], P(None, 'seq'), may hold values from -10 to -4
- w_out: bfloat16 [2, 1024, 512], P(None, 'seq', 'batch'), may hold values from -0.1875 to 0.1875
- mlp_gain: bfloat16 [2, 512], P(None, 'seq'), may hold values from 0.099609375 to 1.8984375
- w_up: bfloat16 [2, 512, 2048], P(None, 'seq', 'batch'), may hold values from -0.25 to 0.25
- w_down: bfloat16 [2, 2048, 512], P(None, 'seq', 'batch'), may hold values from -0.125 to 0.125
- cotangent: bfloat16 [8, 2048, 512], P('batch', 'seq'), may hold values from -6 to 6
Outputs:
- output: bfloat16 [8, 2048, 512], P('batch', 'seq')
- grad_tokens: bfloat16 [8, 2048, 512], P('batch', 'seq')
- grad_norm_gain: float32 [2, 512], P(None, 'seq')
- grad_w_forget: float32 [2, 512, 1024], P(None, 'seq', 'batch')
- grad_w_input: float32 [2, 512, 1024], P(None, 'seq', 'batch')
- grad_w_cand: float32 [2, 512, 1024], P(None, 'seq', 'batch')
- grad_forget_bias: float32 [2, 1024], P(None, 'seq')
- grad_input_bias: float32 [2, 1024], P(None, 'seq')
- grad_w_out: float32 [2, 1024, 512], P(None, 'seq', 'batch')
- grad_mlp_gain: float32 [2, 512], P(None, 'seq')
- grad_w_up: float32 [2, 512, 2048], P(None, 'seq', 'batch')
- grad_w_down: float32 [2, 2048, 512], P(None, 'seq', 'batch')
The draws below stay inside these ranges and needn't reach their ends.
All inputs are finite; a program needn't handle non-finite values.
Results may differ from the reference program's by a relative error of at most 0.011.
Values may be sent and summed in bfloat16 or wider, within the bound.
No kernel may reach another device: no remote copies, remote signals or barrier semaphores. Data moves between devices by JAX's collectives and lax.ppermute only.
A program may use at most 192 MiB of HBM per device.

```python
import math
import jax
import jax.numpy as jnp
from jax import lax

D = 512
H = 1024
FF = 2048
LAYERS = 2
LENGTH = 2048
SEQS = 8


def steps_of(key, extent, cuts, low, high):
    gain = 1.0
    for dim, shards_of in cuts:
        steps = jax.random.uniform(jax.random.fold_in(jax.random.fold_in(key, 6), dim), (shards_of,), jnp.float32, low / len(cuts), high / len(cuts))
        gain = gain * jnp.repeat(jnp.exp(steps), extent[dim] // shards_of).reshape((-1,) + (1,) * (len(extent) - 1 - dim))
    return gain


def normal_values(key, shape, width, most, shards=(), held_as=jnp.bfloat16):
    factor_of = steps_of(key, shape, shards, -0.22, 0.18) if shards else 1.0
    entries = jax.random.normal(key, shape, jnp.float32) * width * factor_of
    return jnp.minimum(jnp.maximum(entries, -most), most).astype(held_as)


def setup_inputs(seed: int = 0) -> dict:
    streams_of = jax.random.split(jax.random.key(seed), 13)
    return {
        "tokens": normal_values(streams_of[0], (SEQS, LENGTH, D), 1.0, 6.0, ((0, 4), (1, 8))),
        "norm_gain": jnp.clip(1.0 + 0.18 * jax.random.normal(streams_of[1], (LAYERS, D), jnp.float32), 0.099609375, 1.8984375).astype(jnp.bfloat16),
        "w_forget": normal_values(streams_of[2], (LAYERS, D, H), D ** -0.5, 0.25, ((1, 8), (2, 4))),
        "w_input": normal_values(streams_of[3], (LAYERS, D, H), D ** -0.5, 0.25, ((1, 8), (2, 4))),
        "w_cand": normal_values(streams_of[4], (LAYERS, D, H), D ** -0.5, 0.25, ((1, 8), (2, 4))),
        "forget_bias": jnp.clip(1.0 + 3.0 * jax.random.uniform(streams_of[5], (LAYERS, H), jnp.float32) ** steps_of(streams_of[5], (LAYERS, H), ((1, 8),), -0.2, 0.2), 1.0, 4.0).astype(jnp.bfloat16),
        "input_bias": jnp.clip(-10.0 + 6.0 * jax.random.uniform(streams_of[6], (LAYERS, H), jnp.float32) ** steps_of(streams_of[6], (LAYERS, H), ((1, 8),), -0.2, 0.2), -10.0, -4.0).astype(jnp.bfloat16),
        "w_out": normal_values(streams_of[7], (LAYERS, H, D), H ** -0.5, 0.1875, ((1, 8), (2, 4))),
        "mlp_gain": jnp.clip(1.0 + 0.18 * jax.random.normal(streams_of[8], (LAYERS, D), jnp.float32), 0.099609375, 1.8984375).astype(jnp.bfloat16),
        "w_up": normal_values(streams_of[9], (LAYERS, D, FF), D ** -0.5, 0.25, ((1, 8), (2, 4))),
        "w_down": normal_values(streams_of[10], (LAYERS, FF, D), FF ** -0.5, 0.125, ((1, 8), (2, 4))),
        "cotangent": normal_values(streams_of[11], (SEQS, LENGTH, D), 1.0, 6.0, ((0, 4), (1, 8))),
    }


@jax.custom_vjp
def low(v):
    return lax.optimization_barrier(v.astype(jnp.bfloat16)).astype(jnp.float32)

@jax.custom_vjp
def low_back(v):
    return v

def low_keep(v):
    return (low(v), None)

def low_pass(kept, grad):
    return (grad,)

def back_keep(v):
    return (v, None)

def back_low(kept, grad):
    return (low(grad),)
low.defvjp(low_keep, low_pass)
low_back.defvjp(back_keep, back_low)
epsilon = 1e-05

def rms_norm(values, gain_vec):
    return values * lax.rsqrt(lax.optimization_barrier(jnp.mean(values * values, axis=-1, keepdims=True)) + epsilon) * gain_vec

def product(left, weight):
    return jnp.einsum('std,dh->sth', left, weight, precision=lax.Precision.HIGHEST)

def link(earlier, latter):
    return (earlier[0] * latter[0], latter[0] * earlier[1] + latter[1])

def gate_pair(z_forget, z_input, z_cand):
    differ = jax.nn.softplus(-z_forget) - jax.nn.softplus(-z_input)
    return (jax.nn.sigmoid(-differ), jax.nn.sigmoid(differ) * jax.nn.softplus(z_cand))

def gelu_exact(values):
    return jax.nn.gelu(values, approximate=False)

def block_forward(stream, weights):
    gain_one, forget_w, input_w, cand_w, forget_b, input_b, out_w, gain_two, up_w, down_w = weights
    normed = low(rms_norm(stream, gain_one))
    z_forget = low_back(product(normed, forget_w) + forget_b)
    z_input = low_back(product(normed, input_w) + input_b)
    z_cand = low_back(product(normed, cand_w))
    decay, inflow = gate_pair(z_forget, z_input, z_cand)
    hidden = lax.associative_scan(link, (decay, inflow), axis=1)[1]
    middle = stream + low_back(product(low(hidden), out_w))
    normed_two = low(rms_norm(middle, gain_two))
    pre_act = low_back(product(normed_two, up_w))
    return middle + low_back(product(low(gelu_exact(pre_act)), down_w))

def forward(params, stream):
    for layer_at in range(LAYERS):
        stream = block_forward(stream, tuple((member[layer_at] for member in params)))
    return stream

def reference(tokens, norm_gain, w_forget, w_input, w_cand, forget_bias, input_bias, w_out, mlp_gain, w_up, w_down, cotangent):
    params = tuple((member.astype(jnp.float32) for member in (norm_gain, w_forget, w_input, w_cand, forget_bias, input_bias, w_out, mlp_gain, w_up, w_down)))
    group = math.gcd(SEQS, max(1, 4096 // LENGTH))
    inputs = tokens.astype(jnp.float32).reshape(SEQS // group, group, LENGTH, D)
    cotans = cotangent.astype(jnp.float32).reshape(SEQS // group, group, LENGTH, D)

    def step(totals, pair):
        stream, cot = pair
        result, back = jax.vjp(forward, params, stream)
        grad_params, grad_stream = back(cot)
        totals = tuple((acc + new for acc, new in zip(totals, grad_params)))
        return (totals, (result.astype(jnp.bfloat16), grad_stream.astype(jnp.bfloat16)))
    start = tuple((jnp.zeros(member.shape, jnp.float32) for member in params))
    totals, (results, grads) = lax.scan(step, start, (inputs, cotans))
    return (results.reshape(SEQS, LENGTH, D), grads.reshape(SEQS, LENGTH, D), totals[0], totals[1], totals[2], totals[3], totals[4], totals[5], totals[6], totals[7], totals[8], totals[9])
```

```python
import functools

import jax
import jax.numpy as jnp
from jax import lax
from jax.experimental import pallas as pl
from jax.experimental.pallas import tpu as pltpu
from jax.sharding import PartitionSpec as P

LAYERS = 2
EPS = 1e-05
NS, NB, LANE = 8, 4, 128
CHUNKS = 8
VMEM = 56 * 1024 * 1024
F32, BF16 = jnp.float32, jnp.bfloat16


def dot(left, right):
    return lax.dot_general(left, right, (((1,), (0,)), ((), ())), preferred_element_type=F32)


def dot_nt(left, right):
    return lax.dot_general(left, right, (((1,), (1,)), ((), ())), preferred_element_type=F32)


def dot_tn(left, right):
    return lax.dot_general(left, right, (((0,), (0,)), ((), ())), preferred_element_type=F32)


def columns_of(ref, start, rows, slabs):
    parts = [
        ref[:, 0, start + j * rows : start + (j + 1) * rows, :].reshape(NS * rows, LANE)
        for j in range(slabs)
    ]
    return jnp.concatenate(parts, axis=1)


def rows_of(ref):
    parts = [ref[:, j].reshape(-1, LANE) for j in range(NB)]
    return jnp.concatenate(parts, axis=1)


def rms_scale(values):
    return lax.rsqrt(jnp.mean(values * values, axis=-1, keepdims=True) + EPS)


def rms_back(values, gain, grad):
    scale = rms_scale(values)
    unit = values * scale
    inner = grad * gain
    back = scale * (inner - unit * jnp.mean(inner * unit, axis=-1, keepdims=True))
    return back, jnp.sum(grad * unit, axis=0, keepdims=True)


def gate_kernel(
    seqs, steps, x_ref, gain_ref, bias_ref, w_ref,
    normed_ref, decay_ref, inflow_ref, cand_ref, ff_ref, fi_ref, fc_ref, cp_ref, ch_ref, fin_ref,
    zf, zi, zc,
):
    rows = w_ref.shape[2] // 6
    width = 2 * LANE

    @pl.when(pl.program_id(0) == 0)
    def _():
        x = x_ref[...].astype(F32)
        normed_ref[...] = (x * rms_scale(x) * gain_ref[...]).astype(BF16)

    normed = normed_ref[...]
    zf[...] = dot(normed, columns_of(w_ref, 0, rows, 2)) + bias_ref[0:1, :]
    zi[...] = dot(normed, columns_of(w_ref, 2 * rows, rows, 2)) + bias_ref[1:2, :]
    zc[...] = dot(normed, columns_of(w_ref, 4 * rows, rows, 2))

    block = 4 * CHUNKS

    def turn(at, carry):
        carry = list(carry)
        for seq in range(seqs):
            span = pl.ds(pl.multiple_of(seq * steps * CHUNKS + at * block, block), block)
            f, i, c = zf[span, :], zi[span, :], zc[span, :]
            low = jnp.minimum(jnp.minimum(f, i), 0.0)
            e0, ef, ei = jnp.exp(low), jnp.exp(low - f), jnp.exp(low - i)
            a, b = e0 + ef, e0 + ei
            inv = 1.0 / (a + b)
            decay, other = b * inv, a * inv
            ec = jnp.exp(-jnp.abs(c))
            cand = jnp.maximum(c, 0.0) + jnp.log1p(ec)
            slope = jnp.where(c >= 0.0, 1.0, ec) / (1.0 + ec)
            inflow = other * cand
            decay_ref[span, :] = decay
            inflow_ref[span, :] = inflow
            cand_ref[span, :] = cand
            ff_ref[span, :] = (ef * inv * decay).astype(BF16)
            fi_ref[span, :] = (ei * inv * other).astype(BF16)
            fc_ref[span, :] = (other * slope).astype(BF16)
            prod, state = carry[2 * seq], carry[2 * seq + 1]
            for k in range(4):
                d = decay[k * CHUNKS : (k + 1) * CHUNKS]
                prod = prod * d
                state = state * d + inflow[k * CHUNKS : (k + 1) * CHUNKS]
            carry[2 * seq], carry[2 * seq + 1] = prod, state
        return tuple(carry)

    one, zero = jnp.ones((CHUNKS, width), F32), jnp.zeros((CHUNKS, width), F32)
    carry = lax.fori_loop(0, steps // 4, turn, (one, zero) * seqs)
    for seq in range(seqs):
        prod, state = carry[2 * seq], carry[2 * seq + 1]
        cp_ref[seq], ch_ref[seq] = prod, state
        whole, last = prod[0:1], state[0:1]
        for c in range(1, CHUNKS):
            whole, last = whole * prod[c : c + 1], last * prod[c : c + 1] + state[c : c + 1]
        fin_ref[seq : seq + 1, :] = whole
        fin_ref[seqs + seq : seqs + seq + 1, :] = last


def mix_kernel(
    seqs, steps, x_ref, gain_ref, decay_ref, inflow_ref, cp_ref, ch_ref, ent_ref, wo_ref, wu_ref, wd_ref,
    hidden_ref, hb_ref, e_ref, mid_ref, n2_ref, act_ref, slope_ref, out_ref,
    acc, pre,
):
    at_step = pl.program_id(0)
    block = 4 * CHUNKS

    @pl.when(at_step == 0)
    def _():
        acc[...] = x_ref[...].astype(F32)

    @pl.when(at_step < NB)
    def _():
        for seq in range(seqs):
            state = ent_ref[seq : seq + 1, :]
            for c in range(CHUNKS):
                e_ref[seq, c : c + 1, :] = state
                state = state * cp_ref[seq, c : c + 1, :] + ch_ref[seq, c : c + 1, :]

        def turn(at, carry):
            carry = list(carry)
            for seq in range(seqs):
                span = pl.ds(pl.multiple_of(seq * steps * CHUNKS + at * block, block), block)
                d, u = decay_ref[span, :], inflow_ref[span, :]
                state, found = carry[seq], []
                for k in range(4):
                    state = state * d[k * CHUNKS : (k + 1) * CHUNKS] + u[k * CHUNKS : (k + 1) * CHUNKS]
                    found.append(state)
                carry[seq] = state
                hidden = jnp.concatenate(found, axis=0)
                hidden_ref[span, :] = hidden
                hb_ref[span, :] = hidden.astype(BF16)
            return tuple(carry)

        lax.fori_loop(0, steps // 4, turn, tuple(e_ref[seq] for seq in range(seqs)))
        acc[...] += dot(hb_ref[...], rows_of(wo_ref))

    @pl.when(at_step == NB - 1)
    def _():
        middle = acc[...]
        mid_ref[...] = middle
        n2_ref[...] = (middle * rms_scale(middle) * gain_ref[...]).astype(BF16)

    @pl.when(at_step >= NB)
    def _():
        pre[...] = dot(n2_ref[...], columns_of(wu_ref, 0, wu_ref.shape[2] // 4, 4))

        def turn(at, _):
            span = pl.ds(pl.multiple_of(at * 16, 16), 16)
            v = pre[span, :]
            phi = 0.5 + 0.5 * lax.erf(v * 0.7071067811865476)
            act_ref[span, :] = (v * phi).astype(BF16)
            slope_ref[span, :] = (phi + v * (0.3989422804014327 * jnp.exp(v * v * -0.5))).astype(BF16)
            return 0

        lax.fori_loop(0, pre.shape[0] // 16, turn, 0)
        acc[...] += dot(act_ref[...], rows_of(wd_ref))

    @pl.when(at_step == 2 * NB - 1)
    def _():
        out_ref[...] = acc[...].astype(out_ref.dtype)


def mlp_back_kernel(
    seqs, steps, g_ref, gain_ref, mid_ref, slope_ref, decay_ref, wo_ref, wu_ref, wd_ref,
    gr_ref, gpre_ref, gmid_ref, go_ref, ggain_ref, gh_ref, cp_ref, ca_ref, fin_ref,
    acc,
):
    at_step = pl.program_id(0)
    block = 4 * CHUNKS
    width = decay_ref.shape[1]

    @pl.when(at_step == 0)
    def _():
        gr_ref[...] = g_ref[...].astype(BF16)
        acc[...] = jnp.zeros_like(acc)

    @pl.when(at_step < NB)
    def _():
        gact = dot_nt(gr_ref[...], rows_of(wd_ref))
        gpre_ref[...] = (gact * slope_ref[...].astype(F32)).astype(BF16)
        acc[...] += dot_nt(gpre_ref[...], columns_of(wu_ref, 0, wu_ref.shape[2] // 4, 4))

    @pl.when(at_step == NB - 1)
    def _():
        back, ggain = rms_back(mid_ref[...], gain_ref[...], acc[...])
        ggain_ref[...] = ggain
        gmid = g_ref[...].astype(F32) + back
        gmid_ref[...] = gmid
        go_ref[...] = gmid.astype(BF16)

    @pl.when(at_step >= NB)
    def _():
        gh_ref[...] = dot_nt(go_ref[...], rows_of(wo_ref))

        def turn(turn_at, carry):
            at = steps // 4 - 1 - turn_at
            carry = list(carry)
            for seq in range(seqs):
                span = pl.ds(pl.multiple_of(seq * steps * CHUNKS + at * block, block), block)
                d, g = decay_ref[span, :], gh_ref[span, :]
                prod, state = carry[2 * seq], carry[2 * seq + 1]
                for k in reversed(range(4)):
                    dk = d[k * CHUNKS : (k + 1) * CHUNKS]
                    prod = prod * dk
                    state = dk * (g[k * CHUNKS : (k + 1) * CHUNKS] + state)
                carry[2 * seq], carry[2 * seq + 1] = prod, state
            return tuple(carry)

        one, zero = jnp.ones((CHUNKS, width), F32), jnp.zeros((CHUNKS, width), F32)
        carry = lax.fori_loop(0, steps // 4, turn, (one, zero) * seqs)
        for seq in range(seqs):
            prod, state = carry[2 * seq], carry[2 * seq + 1]
            cp_ref[seq], ca_ref[seq] = prod, state
            whole, last = prod[CHUNKS - 1 :], state[CHUNKS - 1 :]
            for c in reversed(range(CHUNKS - 1)):
                whole, last = whole * prod[c : c + 1], last * prod[c : c + 1] + state[c : c + 1]
            fin_ref[seq : seq + 1, :] = whole
            fin_ref[seqs + seq : seqs + seq + 1, :] = last


def gate_back_kernel(
    seqs, steps, x_ref, gain_ref, gmid_ref, gh_ref, decay_ref, hidden_ref, e_ref, cand_ref, ff_ref, fi_ref, fc_ref,
    cp_ref, ca_ref, ent_ref, w_ref,
    dzf_ref, dzi_ref, dzc_ref, gbias_ref, gstream_ref, ggain_ref,
    acc, start,
):
    at_step = pl.program_id(0)
    block = 4 * CHUNKS
    width = decay_ref.shape[1]
    rows = w_ref.shape[2] // 6

    @pl.when(at_step == 0)
    def _():
        acc[...] = jnp.zeros_like(acc)

    for seq in range(seqs):
        state = ent_ref[seq : seq + 1, :]
        for c in reversed(range(CHUNKS)):
            start[seq, c : c + 1, :] = state
            state = state * cp_ref[seq, c : c + 1, :] + ca_ref[seq, c : c + 1, :]

    def turn(turn_at, carry):
        at = steps // 4 - 1 - turn_at
        carry = list(carry)
        sum_f, sum_i = carry[seqs], carry[seqs + 1]
        for seq in range(seqs):
            base = seq * steps * CHUNKS + at * block
            span = pl.ds(pl.multiple_of(base, block), block)
            before = hidden_ref[pl.ds(pl.multiple_of(jnp.maximum(base - CHUNKS, 0), CHUNKS), CHUNKS), :]
            before = jnp.where(at == 0, e_ref[seq], before)
            d, g = decay_ref[span, :], gh_ref[span, :]
            previous = jnp.concatenate([before, hidden_ref[span, :][: block - CHUNKS]], axis=0)
            state, found = carry[seq], []
            for k in reversed(range(4)):
                now = g[k * CHUNKS : (k + 1) * CHUNKS] + state
                found.append(now)
                state = d[k * CHUNKS : (k + 1) * CHUNKS] * now
            carry[seq] = state
            gstate = jnp.concatenate(found[::-1], axis=0)
            both = gstate * (cand_ref[span, :] - previous)
            dzf = (-ff_ref[span, :].astype(F32) * both).astype(BF16)
            dzi = (fi_ref[span, :].astype(F32) * both).astype(BF16)
            dzf_ref[span, :] = dzf
            dzi_ref[span, :] = dzi
            dzc_ref[span, :] = (fc_ref[span, :].astype(F32) * gstate).astype(BF16)
            wide_f, wide_i = dzf.astype(F32), dzi.astype(F32)
            for k in range(4):
                sum_f = sum_f + wide_f[k * CHUNKS : (k + 1) * CHUNKS]
                sum_i = sum_i + wide_i[k * CHUNKS : (k + 1) * CHUNKS]
        carry[seqs], carry[seqs + 1] = sum_f, sum_i
        return tuple(carry)

    zero = jnp.zeros((CHUNKS, width), F32)
    carry = lax.fori_loop(0, steps // 4, turn, tuple(start[seq] for seq in range(seqs)) + (zero, zero))
    gbias_ref[0:1, :] = jnp.sum(carry[seqs], axis=0, keepdims=True)
    gbias_ref[1:2, :] = jnp.sum(carry[seqs + 1], axis=0, keepdims=True)
    acc[...] += (
        dot_nt(dzf_ref[...], columns_of(w_ref, 0, rows, 2))
        + dot_nt(dzi_ref[...], columns_of(w_ref, 2 * rows, rows, 2))
        + dot_nt(dzc_ref[...], columns_of(w_ref, 4 * rows, rows, 2))
    )

    @pl.when(at_step == NB - 1)
    def _():
        back, ggain = rms_back(x_ref[...].astype(F32), gain_ref[...], acc[...])
        ggain_ref[...] = ggain
        gstream_ref[...] = (gmid_ref[...] + back).astype(gstream_ref.dtype)


def put_columns(ref, start, rows, slabs, value):
    for j in range(slabs):
        part = value[:, j * LANE : (j + 1) * LANE].astype(BF16)
        ref[:, 0, start + j * rows : start + (j + 1) * rows, :] = part.reshape(NS, rows, LANE)


def put_rows(ref, value):
    for j in range(NB):
        part = value[:, j * LANE : (j + 1) * LANE].astype(BF16)
        ref[:, j] = part.reshape(ref.shape[0], -1, LANE)


def mlp_weight_kernel(act_ref, gr_ref, n2_ref, gpre_ref, hb_ref, go_ref, gu_ref, gd_ref, go_out_ref):
    put_columns(gu_ref, 0, gu_ref.shape[2] // 4, 4, dot_tn(n2_ref[...], gpre_ref[...]))
    put_rows(gd_ref, dot_tn(act_ref[...], gr_ref[...]))
    put_rows(go_out_ref, dot_tn(hb_ref[...], go_ref[...]))


def gate_weight_kernel(normed_ref, dzf_ref, dzi_ref, dzc_ref, g_ref):
    rows = g_ref.shape[2] // 6
    normed = normed_ref[...]
    put_columns(g_ref, 0, rows, 2, dot_tn(normed, dzf_ref[...]))
    put_columns(g_ref, 2 * rows, rows, 2, dot_tn(normed, dzi_ref[...]))
    put_columns(g_ref, 4 * rows, rows, 2, dot_tn(normed, dzc_ref[...]))


def shape(dims, dtype=F32):
    return jax.ShapeDtypeStruct(dims, dtype)


def call(kernel, grid, ins, outs, scratch, flops, name):
    moved = sum(a.size * a.dtype.itemsize for a, _, _ in ins)
    moved += sum(s.size * s.dtype.itemsize for s, _, _ in outs)
    return pl.pallas_call(
        kernel,
        grid=(grid,),
        in_specs=[pl.BlockSpec(block, index) for _, block, index in ins],
        out_specs=[pl.BlockSpec(block, index) for _, block, index in outs],
        out_shape=[s for s, _, _ in outs],
        scratch_shapes=scratch,
        compiler_params=pltpu.CompilerParams(vmem_limit_bytes=VMEM),
        cost_estimate=pl.CostEstimate(flops=flops, bytes_accessed=moved, transcendentals=0),
        name=name,
    )(*[a for a, _, _ in ins])


def whole(array):
    dims = array.shape
    return (array, dims, lambda i: (0,) * len(dims))


def whole_out(dims, dtype=F32):
    return (shape(dims, dtype), dims, lambda i: (0,) * len(dims))


def first(i):
    return jnp.minimum(i, NB - 1)


def second(i):
    return jnp.maximum(i - NB, 0)


class Sizes:
    def __init__(self, seqs, length, d, h, ff):
        self.seqs, self.steps, self.n = seqs, length // CHUNKS, seqs * length
        self.d, self.h, self.ff = d, h, ff
        self.hb, self.fb = h // NB, ff // NB


def gate_forward(sz, x, gain, bias, wa):
    n, d, h, w, s = sz.n, sz.d, sz.h, sz.hb, sz.seqs
    col = lambda i: (0, i)
    return call(
        functools.partial(gate_kernel, s, sz.steps), NB,
        [whole(x), whole(gain), (bias, (2, w), col), (wa, (NS, 1) + wa.shape[2:], lambda i: (0, i, 0, 0))],
        [whole_out((n, d), BF16)]
        + [(shape((n, h)), (n, w), col)] * 3
        + [(shape((n, h), BF16), (n, w), col)] * 3
        + [(shape((s, CHUNKS, h)), (s, CHUNKS, w), lambda i: (0, 0, i))] * 2
        + [(shape((2 * s, h)), (2 * s, w), col)],
        [pltpu.VMEM((n, w), F32)] * 3, 6 * n * d * h, "gates",
    )


def weights_b(wb):
    r = wb.shape[2]
    tall, short = 2 * r // 5, r // 5
    return (tall, short)


def mix_forward(sz, x, gain, decay, inflow, cp, ch, ent, wb, last):
    n, d, h, ff, w, f, s = sz.n, sz.d, sz.h, sz.ff, sz.hb, sz.fb, sz.seqs
    tall, short = weights_b(wb)
    col = lambda i: (0, first(i))
    late = lambda i: (0, second(i))
    deep = lambda i: (0, 0, first(i))
    return call(
        functools.partial(mix_kernel, s, sz.steps), 2 * NB,
        [
            whole(x), whole(gain), (decay, (n, w), col), (inflow, (n, w), col),
            (cp, (s, CHUNKS, w), deep), (ch, (s, CHUNKS, w), deep), (ent, (s, w), col),
            (wb, (NS // NB, NB, short, LANE), lambda i: (first(i), 0, 4, 0)),
            (wb, (NS, 1, tall, LANE), lambda i: (0, second(i), 0, 0)),
            (wb, (NS // NB, NB, tall, LANE), lambda i: (second(i), 0, 1, 0)),
        ],
        [
            (shape((n, h)), (n, w), col), (shape((n, h), BF16), (n, w), col),
            (shape((s, CHUNKS, h)), (s, CHUNKS, w), deep),
            whole_out((n, d)), whole_out((n, d), BF16),
            (shape((n, ff), BF16), (n, f), late), (shape((n, ff), BF16), (n, f), late),
            whole_out((n, d), BF16 if last else F32),
        ],
        [pltpu.VMEM((n, d), F32), pltpu.VMEM((n, f), F32)], 2 * n * d * (h + 2 * ff), "mix",
    )


def mlp_backward(sz, g, gain, mid, slope, decay, wb):
    n, d, h, ff, w, f, s = sz.n, sz.d, sz.h, sz.ff, sz.hb, sz.fb, sz.seqs
    tall, short = weights_b(wb)
    col = lambda i: (0, second(i))
    early = lambda i: (0, first(i))
    deep = lambda i: (0, 0, second(i))
    return call(
        functools.partial(mlp_back_kernel, s, sz.steps), 2 * NB,
        [
            whole(g), whole(gain), whole(mid), (slope, (n, f), early), (decay, (n, w), col),
            (wb, (NS // NB, NB, short, LANE), lambda i: (second(i), 0, 4, 0)),
            (wb, (NS, 1, tall, LANE), lambda i: (0, first(i), 0, 0)),
            (wb, (NS // NB, NB, tall, LANE), lambda i: (first(i), 0, 1, 0)),
        ],
        [
            whole_out((n, d), BF16), (shape((n, ff), BF16), (n, f), early), whole_out((n, d)), whole_out((n, d), BF16),
            whole_out((1, d)), (shape((n, h)), (n, w), col),
            (shape((s, CHUNKS, h)), (s, CHUNKS, w), deep), (shape((s, CHUNKS, h)), (s, CHUNKS, w), deep),
            (shape((2 * s, h)), (2 * s, w), col),
        ],
        [pltpu.VMEM((n, d), F32)], 2 * n * d * (h + 2 * ff), "mlp_back",
    )


def gate_backward(sz, x, gain, gmid, gh, decay, hidden, e, cand, ff_, fi_, fc_, cp, ca, ent, wa, last):
    n, d, h, w, s = sz.n, sz.d, sz.h, sz.hb, sz.seqs
    col = lambda i: (0, i)
    deep = lambda i: (0, 0, i)
    wide = lambda a: (a, (n, w), col)
    return call(
        functools.partial(gate_back_kernel, s, sz.steps), NB,
        [
            whole(x), whole(gain), whole(gmid), wide(gh), wide(decay), wide(hidden), (e, (s, CHUNKS, w), deep),
            wide(cand), wide(ff_), wide(fi_), wide(fc_), (cp, (s, CHUNKS, w), deep), (ca, (s, CHUNKS, w), deep),
            (ent, (s, w), col), (wa, (NS, 1) + wa.shape[2:], lambda i: (0, i, 0, 0)),
        ],
        [(shape((n, h), BF16), (n, w), col)] * 3
        + [(shape((2, h)), (2, w), col), whole_out((n, d), BF16 if last else F32), whole_out((1, d))],
        [pltpu.VMEM((n, d), F32), pltpu.VMEM((s, CHUNKS, w), F32)], 6 * n * d * h, "gate_back",
    )


def mlp_weights(sz, act, gr, n2, gpre, hb, go):
    n, d, h, ff, w, f = sz.n, sz.d, sz.h, sz.ff, sz.hb, sz.fb
    col = lambda i: (0, i)
    return call(
        mlp_weight_kernel, NB,
        [(act, (n, f), col), whole(gr), whole(n2), (gpre, (n, f), col), (hb, (n, w), col), whole(go)],
        [
            (shape((NS, NB, d * ff // (32 * LANE), LANE), BF16), (NS, 1, d * ff // (32 * LANE), LANE), lambda i: (0, i, 0, 0)),
            (shape((NS, NB, ff // NS, LANE), BF16), (NS // NB, NB, ff // NS, LANE), lambda i: (i, 0, 0, 0)),
            (shape((NS, NB, h // NS, LANE), BF16), (NS // NB, NB, h // NS, LANE), lambda i: (i, 0, 0, 0)),
        ],
        [], 2 * n * d * (h + 2 * ff), "mlp_weights",
    )


def gate_weights(sz, normed, dzf, dzi, dzc):
    n, d, h, w = sz.n, sz.d, sz.h, sz.hb
    col = lambda i: (0, i)
    rows = 3 * d * h // (32 * LANE)
    return call(
        gate_weight_kernel, NB,
        [whole(normed), (dzf, (n, w), col), (dzi, (n, w), col), (dzc, (n, w), col)],
        [(shape((NS, NB, rows, LANE), BF16), (NS, 1, rows, LANE), lambda i: (0, i, 0, 0))],
        [], 6 * n * d * h, "gate_weights",
    )[0]


def enter(fin, seqs, backward):
    count, mine = lax.axis_size("seq"), lax.axis_index("seq")
    prod, state = fin[:seqs], fin[seqs:]
    pre_p, pre_s = jnp.ones_like(prod), jnp.zeros_like(state)
    bit = 1
    while bit < count:
        other = lax.ppermute(jnp.concatenate([prod, state]), "seq", [(i, i ^ bit) for i in range(count)])
        o_p, o_s = other[:seqs], other[seqs:]
        upper = ((mine // bit) % 2 == 1) ^ backward
        pre_p, pre_s = jnp.where(upper, o_p * pre_p, pre_p), jnp.where(upper, pre_p * o_s + pre_s, pre_s)
        state = jnp.where(upper, prod * o_s + state, o_p * state + o_s)
        prod = prod * o_p
        bit *= 2
    return pre_s


def slabs(matrix, seq_count, batch_count):
    rows, cols = matrix.shape[0] // NS, matrix.shape[1] // NB
    cut = matrix.reshape(NS, rows, NB, cols // LANE, LANE).transpose(0, 2, 3, 1, 4)
    return cut.reshape(NS, NB, rows * cols // LANE, LANE)


def unslab(blocks, rows, cols):
    r, c = rows // NS, cols // NB
    cut = blocks.reshape(NS, NB, c // LANE, r, LANE).transpose(0, 3, 1, 2, 4)
    return cut.reshape(rows, cols)


def own_slab(shard):
    rows, cols = shard.shape
    return shard.reshape(rows, cols // LANE, LANE).transpose(1, 0, 2).reshape(-1, LANE)


def body(
    tokens, norm_gain, w_forget, w_input, w_cand, forget_bias, input_bias, w_out, mlp_gain, w_up, w_down, cotangent
):
    seqs, length, d = tokens.shape
    seq_count, batch_count = lax.axis_size("seq"), lax.axis_size("batch")
    h, ff = w_forget.shape[2] * batch_count, w_up.shape[2] * batch_count
    sz = Sizes(seqs, length, d, h, ff)
    both = ("seq", "batch")
    standard = (seq_count, batch_count) == (NS, NB)

    widest = max(v.shape[1] for v in (norm_gain, forget_bias, input_bias, mlp_gain))
    vec = jnp.concatenate(
        [
            jnp.pad(v[l : l + 1], ((0, 0), (0, widest - v.shape[1])))
            for l in range(LAYERS)
            for v in (norm_gain, forget_bias, input_bias, mlp_gain)
        ]
    )
    if standard:
        parts = []
        for l in range(LAYERS):
            parts += [own_slab(m[l]) for m in (w_forget, w_input, w_cand, w_up, w_down, w_out)]
        pack = jnp.concatenate(parts + [jnp.pad(vec, ((0, 8), (0, LANE - widest)))])
        got = lax.all_gather(pack, both, axis=0, tiled=False).reshape(NS, NB, -1, LANE)
        gate_rows, mlp_rows = 3 * d * h // (32 * LANE), (h + 2 * ff) * d // (32 * LANE)
        layer_rows = gate_rows + mlp_rows
        was = [got[:, :, l * layer_rows : l * layer_rows + gate_rows] for l in range(LAYERS)]
        wbs = [got[:, :, l * layer_rows + gate_rows : (l + 1) * layer_rows] for l in range(LAYERS)]
        vecs = got[:, 0, LAYERS * layer_rows : LAYERS * layer_rows + 4 * LAYERS, :widest]
        vecs = vecs.transpose(1, 0, 2)
    else:
        was, wbs = [], []

        def full(m):
            m = lax.all_gather(m, "batch", axis=1, tiled=True)
            return lax.all_gather(m, "seq", axis=0, tiled=True)

        for l in range(LAYERS):
            cut = [slabs(full(m[l]), NS, NB) for m in (w_forget, w_input, w_cand, w_up, w_down, w_out)]
            was.append(jnp.concatenate(cut[:3], axis=2))
            wbs.append(jnp.concatenate(cut[3:], axis=2))
        vecs = lax.all_gather(vec, "seq", axis=1, tiled=False)

    def vector(l, which, size):
        return vecs[4 * l + which][:, : size // seq_count].reshape(1, size).astype(F32)

    def to_rows(v):
        return v.reshape(seqs, CHUNKS, sz.steps, d).transpose(0, 2, 1, 3).reshape(sz.n, d)

    def from_rows(v):
        return v.reshape(seqs, sz.steps, CHUNKS, d).transpose(0, 2, 1, 3).reshape(seqs, length, d)

    stream, grad = to_rows(tokens), to_rows(cotangent)
    kept = []
    for l in range(LAYERS):
        gain_one, gain_two = vector(l, 0, d), vector(l, 3, d)
        bias = jnp.concatenate([vector(l, 1, h), vector(l, 2, h)])
        normed, decay, inflow, cand, f_f, f_i, f_c, cp, ch, fin = gate_forward(sz, stream, gain_one, bias, was[l])
        ent = enter(fin, seqs, False)
        hidden, hb, e, mid, n2, act, slope, result = mix_forward(
            sz, stream, gain_two, decay, inflow, cp, ch, ent, wbs[l], l == LAYERS - 1
        )
        kept.append((stream, gain_one, gain_two, normed, decay, cand, f_f, f_i, f_c, hidden, hb, e, mid, n2, act, slope))
        stream = result
    output = from_rows(stream)

    grads = [None] * LAYERS
    for l in reversed(range(LAYERS)):
        x, gain_one, gain_two, normed, decay, cand, f_f, f_i, f_c, hidden, hb, e, mid, n2, act, slope = kept[l]
        gr, gpre, gmid, go, ggain_two, gh, cp, ca, fin = mlp_backward(sz, grad, gain_two, mid, slope, decay, wbs[l])
        ent = enter(fin, seqs, True)
        gu, gd, gwo = mlp_weights(sz, act, gr, n2, gpre, hb, go)
        dzf, dzi, dzc, gbias, grad, ggain_one = gate_backward(
            sz, x, gain_one, gmid, gh, decay, hidden, e, cand, f_f, f_i, f_c, cp, ca, ent, was[l], l == 0
        )
        gg = gate_weights(sz, normed, dzf, dzi, dzc)
        grads[l] = (gg, gu, gd, gwo, ggain_one, gbias, ggain_two)
    grad_tokens = from_rows(grad)

    third = d * h // (32 * LANE)
    shard_shapes = (w_forget, w_input, w_cand, w_up, w_down, w_out)
    if standard:
        sent = [g for l in range(LAYERS) for g in grads[l][:4]]
        sent = jnp.concatenate([g.reshape(NS * NB, -1, LANE) for g in sent], axis=1)
        mine = lax.psum_scatter(sent, both, scatter_dimension=0, tiled=False)
        at, found = 0, []
        for l in range(LAYERS):
            layer = []
            for m in shard_shapes:
                r, c = m.shape[1:]
                part = mine[at : at + r * c // LANE].reshape(c // LANE, r, LANE)
                layer.append(part.transpose(1, 0, 2).reshape(r, c).astype(F32))
                at += r * c // LANE
            found.append(layer)
    else:
        found = []
        for l in range(LAYERS):
            gg, gu, gd, gwo = grads[l][:4]
            blocks = [gg[:, :, :third], gg[:, :, third : 2 * third], gg[:, :, 2 * third :], gu, gd, gwo]
            layer = []
            for m, g in zip(shard_shapes, blocks):
                v = unslab(g, m.shape[1] * seq_count, m.shape[2] * batch_count)
                v = lax.psum_scatter(v, "seq", scatter_dimension=0, tiled=True)
                layer.append(lax.psum_scatter(v, "batch", scatter_dimension=1, tiled=True).astype(F32))
            found.append(layer)
    found = [jnp.stack([found[l][m] for l in range(LAYERS)]) for m in range(6)]

    small = jnp.concatenate(
        [v.reshape(seq_count, -1) for l in range(LAYERS) for v in (grads[l][4], grads[l][5][0], grads[l][5][1], grads[l][6])],
        axis=1,
    )
    small = lax.psum(lax.psum_scatter(small, "seq", scatter_dimension=0, tiled=True), "batch")
    sizes = (d // seq_count, h // seq_count, h // seq_count, d // seq_count)
    vector_grads, at = [], 0
    for l in range(LAYERS):
        layer = []
        for size in sizes:
            layer.append(small[0, at : at + size])
            at += size
        vector_grads.append(layer)
    g_norm, g_fb, g_ib, g_mlp = [jnp.stack([vector_grads[l][m] for l in range(LAYERS)]) for m in range(4)]
    g_f, g_i, g_c, g_up, g_down, g_out = found
    return output, grad_tokens, g_norm, g_f, g_i, g_c, g_fb, g_ib, g_out, g_mlp, g_up, g_down


def solution(mesh):
    split, vector, matrix = P("batch", "seq", None), P(None, "seq"), P(None, "seq", "batch")
    order = (vector, matrix, matrix, matrix, vector, vector, matrix, vector, matrix, matrix)
    return jax.shard_map(
        body,
        mesh=mesh,
        in_specs=(split,) + order + (split,),
        out_specs=(split, split) + order,
        check_vma=False,
    )
```

```python
import functools

import jax
import jax.numpy as jnp
from jax import lax
from jax.experimental import pallas as pl
from jax.experimental.pallas import tpu as pltpu
from jax.sharding import PartitionSpec as P

LAYERS = 2
EPS = 1e-05
NS, NB, LANE = 8, 4, 128
CHUNKS = 8
VMEM = 56 * 1024 * 1024
F32, BF16 = jnp.float32, jnp.bfloat16


def dot(left, right):
    return lax.dot_general(left, right, (((1,), (0,)), ((), ())), preferred_element_type=F32)


def dot_nt(left, right):
    return lax.dot_general(left, right, (((1,), (1,)), ((), ())), preferred_element_type=F32)


def dot_tn(left, right):
    return lax.dot_general(left, right, (((0,), (0,)), ((), ())), preferred_element_type=F32)


def columns_of(ref, slabs=2):
    rows = ref.shape[2] // slabs
    parts = [ref[:, 0, j * rows : (j + 1) * rows, :].reshape(NS * rows, LANE) for j in range(slabs)]
    return jnp.concatenate(parts, axis=1)


def rows_of(ref):
    parts = [ref[:, j].reshape(-1, LANE) for j in range(NB)]
    return jnp.concatenate(parts, axis=1)


def rms_scale(values):
    return lax.rsqrt(jnp.mean(values * values, axis=-1, keepdims=True) + EPS)


def rms_back(values, gain, grad):
    scale = rms_scale(values)
    unit = values * scale
    inner = grad * gain
    back = scale * (inner - unit * jnp.mean(inner * unit, axis=-1, keepdims=True))
    return back, jnp.sum(grad * unit, axis=0, keepdims=True)


def gate_kernel(
    seqs, steps, x_ref, gain_ref, bias_ref, wf_ref, wi_ref, wc_ref,
    normed_ref, decay_ref, inflow_ref, cand_ref, ff_ref, fi_ref, fc_ref, cp_ref, ch_ref, fin_ref,
    zf, zi, zc,
):
    width = 2 * LANE

    @pl.when(pl.program_id(0) == 0)
    def _():
        x = x_ref[...].astype(F32)
        normed_ref[...] = (x * rms_scale(x) * gain_ref[0:1, :]).astype(BF16)

    normed = normed_ref[...]
    zf[...] = dot(normed, columns_of(wf_ref)) + bias_ref[0:1, :]
    zi[...] = dot(normed, columns_of(wi_ref)) + bias_ref[1:2, :]
    zc[...] = dot(normed, columns_of(wc_ref))

    block = 4 * CHUNKS

    def turn(at, carry):
        carry = list(carry)
        for seq in range(seqs):
            span = pl.ds(pl.multiple_of(seq * steps * CHUNKS + at * block, block), block)
            f, i, c = zf[span, :], zi[span, :], zc[span, :]
            low = jnp.minimum(jnp.minimum(f, i), 0.0)
            e0, ef, ei = jnp.exp(low), jnp.exp(low - f), jnp.exp(low - i)
            a, b = e0 + ef, e0 + ei
            inv = 1.0 / (a + b)
            decay, other = b * inv, a * inv
            ec = jnp.exp(-jnp.abs(c))
            cand = jnp.maximum(c, 0.0) + jnp.log1p(ec)
            slope = jnp.where(c >= 0.0, 1.0, ec) / (1.0 + ec)
            inflow = other * cand
            decay_ref[span, :] = decay
            inflow_ref[span, :] = inflow
            cand_ref[span, :] = cand
            ff_ref[span, :] = (ef * inv * decay).astype(BF16)
            fi_ref[span, :] = (ei * inv * other).astype(BF16)
            fc_ref[span, :] = (other * slope).astype(BF16)
            prod, state = carry[2 * seq], carry[2 * seq + 1]
            for k in range(4):
                d = decay[k * CHUNKS : (k + 1) * CHUNKS]
                prod = prod * d
                state = state * d + inflow[k * CHUNKS : (k + 1) * CHUNKS]
            carry[2 * seq], carry[2 * seq + 1] = prod, state
        return tuple(carry)

    one, zero = jnp.ones((CHUNKS, width), F32), jnp.zeros((CHUNKS, width), F32)
    carry = lax.fori_loop(0, steps // 4, turn, (one, zero) * seqs)
    for seq in range(seqs):
        prod, state = carry[2 * seq], carry[2 * seq + 1]
        cp_ref[seq], ch_ref[seq] = prod, state
        whole, last = prod[0:1], state[0:1]
        for c in range(1, CHUNKS):
            whole, last = whole * prod[c : c + 1], last * prod[c : c + 1] + state[c : c + 1]
        fin_ref[seq : seq + 1, :] = whole
        fin_ref[seqs + seq : seqs + seq + 1, :] = last


def mix_kernel(
    seqs, steps, x_ref, gain_ref, decay_ref, inflow_ref, cp_ref, ch_ref, ent_ref, wo_ref, wu_ref, wd_ref,
    hidden_ref, hb_ref, e_ref, mid_ref, n2_ref, act_ref, slope_ref, out_ref,
    acc, pre,
):
    at_step = pl.program_id(0)
    block = 4 * CHUNKS

    @pl.when(at_step == 0)
    def _():
        acc[...] = x_ref[...].astype(F32)

    @pl.when(at_step < NB)
    def _():
        for seq in range(seqs):
            state = ent_ref[seq : seq + 1, :]
            for c in range(CHUNKS):
                e_ref[seq, c : c + 1, :] = state
                state = state * cp_ref[seq, c : c + 1, :] + ch_ref[seq, c : c + 1, :]

        def turn(at, carry):
            carry = list(carry)
            for seq in range(seqs):
                span = pl.ds(pl.multiple_of(seq * steps * CHUNKS + at * block, block), block)
                d, u = decay_ref[span, :], inflow_ref[span, :]
                state, found = carry[seq], []
                for k in range(4):
                    state = state * d[k * CHUNKS : (k + 1) * CHUNKS] + u[k * CHUNKS : (k + 1) * CHUNKS]
                    found.append(state)
                carry[seq] = state
                hidden = jnp.concatenate(found, axis=0)
                hidden_ref[span, :] = hidden
                hb_ref[span, :] = hidden.astype(BF16)
            return tuple(carry)

        lax.fori_loop(0, steps // 4, turn, tuple(e_ref[seq] for seq in range(seqs)))
        acc[...] += dot(hb_ref[...], rows_of(wo_ref))

    @pl.when(at_step == NB - 1)
    def _():
        middle = acc[...]
        mid_ref[...] = middle
        n2_ref[...] = (middle * rms_scale(middle) * gain_ref[1:2, :]).astype(BF16)

    @pl.when(at_step >= NB)
    def _():
        pre[...] = dot(n2_ref[...], columns_of(wu_ref, 4))

        def turn(at, _):
            span = pl.ds(pl.multiple_of(at * 16, 16), 16)
            v = pre[span, :]
            phi = 0.5 + 0.5 * lax.erf(v * 0.7071067811865476)
            act_ref[span, :] = (v * phi).astype(BF16)
            slope_ref[span, :] = (phi + v * (0.3989422804014327 * jnp.exp(v * v * -0.5))).astype(BF16)
            return 0

        lax.fori_loop(0, pre.shape[0] // 16, turn, 0)
        acc[...] += dot(act_ref[...], rows_of(wd_ref))

    @pl.when(at_step == 2 * NB - 1)
    def _():
        out_ref[...] = acc[...].astype(out_ref.dtype)


def mlp_back_kernel(
    seqs, steps, g_ref, gain_ref, mid_ref, slope_ref, decay_ref, wo_ref, wu_ref, wd_ref,
    gr_ref, gpre_ref, gmid_ref, go_ref, ggain_ref, gh_ref, cp_ref, ca_ref, fin_ref,
    acc,
):
    at_step = pl.program_id(0)
    block = 4 * CHUNKS
    width = decay_ref.shape[1]

    @pl.when(at_step == 0)
    def _():
        gr_ref[...] = g_ref[...].astype(BF16)
        acc[...] = jnp.zeros_like(acc)

    @pl.when(at_step < NB)
    def _():
        gact = dot_nt(gr_ref[...], rows_of(wd_ref))
        gpre_ref[...] = (gact * slope_ref[...].astype(F32)).astype(BF16)
        acc[...] += dot_nt(gpre_ref[...], columns_of(wu_ref, 4))

    @pl.when(at_step == NB - 1)
    def _():
        back, ggain = rms_back(mid_ref[...], gain_ref[1:2, :], acc[...])
        ggain_ref[...] = ggain
        gmid = g_ref[...].astype(F32) + back
        gmid_ref[...] = gmid
        go_ref[...] = gmid.astype(BF16)

    @pl.when(at_step >= NB)
    def _():
        gh_ref[...] = dot_nt(go_ref[...], rows_of(wo_ref))

        def turn(turn_at, carry):
            at = steps // 4 - 1 - turn_at
            carry = list(carry)
            for seq in range(seqs):
                span = pl.ds(pl.multiple_of(seq * steps * CHUNKS + at * block, block), block)
                d, g = decay_ref[span, :], gh_ref[span, :]
                prod, state = carry[2 * seq], carry[2 * seq + 1]
                for k in reversed(range(4)):
                    dk = d[k * CHUNKS : (k + 1) * CHUNKS]
                    prod = prod * dk
                    state = dk * (g[k * CHUNKS : (k + 1) * CHUNKS] + state)
                carry[2 * seq], carry[2 * seq + 1] = prod, state
            return tuple(carry)

        one, zero = jnp.ones((CHUNKS, width), F32), jnp.zeros((CHUNKS, width), F32)
        carry = lax.fori_loop(0, steps // 4, turn, (one, zero) * seqs)
        for seq in range(seqs):
            prod, state = carry[2 * seq], carry[2 * seq + 1]
            cp_ref[seq], ca_ref[seq] = prod, state
            whole, last = prod[CHUNKS - 1 :], state[CHUNKS - 1 :]
            for c in reversed(range(CHUNKS - 1)):
                whole, last = whole * prod[c : c + 1], last * prod[c : c + 1] + state[c : c + 1]
            fin_ref[seq : seq + 1, :] = whole
            fin_ref[seqs + seq : seqs + seq + 1, :] = last


def gate_back_kernel(
    seqs, steps, x_ref, gain_ref, gmid_ref, gh_ref, decay_ref, hidden_ref, e_ref, cand_ref, ff_ref, fi_ref, fc_ref,
    cp_ref, ca_ref, ent_ref, wf_ref, wi_ref, wc_ref,
    dzf_ref, dzi_ref, dzc_ref, gbias_ref, gstream_ref, ggain_ref,
    acc, start,
):
    at_step = pl.program_id(0)
    block = 4 * CHUNKS
    width = decay_ref.shape[1]

    @pl.when(at_step == 0)
    def _():
        acc[...] = jnp.zeros_like(acc)

    for seq in range(seqs):
        state = ent_ref[seq : seq + 1, :]
        for c in reversed(range(CHUNKS)):
            start[seq, c : c + 1, :] = state
            state = state * cp_ref[seq, c : c + 1, :] + ca_ref[seq, c : c + 1, :]

    def turn(turn_at, carry):
        at = steps // 4 - 1 - turn_at
        carry = list(carry)
        sum_f, sum_i = carry[seqs], carry[seqs + 1]
        for seq in range(seqs):
            base = seq * steps * CHUNKS + at * block
            span = pl.ds(pl.multiple_of(base, block), block)
            before = hidden_ref[pl.ds(pl.multiple_of(jnp.maximum(base - CHUNKS, 0), CHUNKS), CHUNKS), :]
            before = jnp.where(at == 0, e_ref[seq], before)
            d, g = decay_ref[span, :], gh_ref[span, :]
            previous = jnp.concatenate([before, hidden_ref[span, :][: block - CHUNKS]], axis=0)
            state, found = carry[seq], []
            for k in reversed(range(4)):
                now = g[k * CHUNKS : (k + 1) * CHUNKS] + state
                found.append(now)
                state = d[k * CHUNKS : (k + 1) * CHUNKS] * now
            carry[seq] = state
            gstate = jnp.concatenate(found[::-1], axis=0)
            both = gstate * (cand_ref[span, :] - previous)
            dzf = (-ff_ref[span, :].astype(F32) * both).astype(BF16)
            dzi = (fi_ref[span, :].astype(F32) * both).astype(BF16)
            dzf_ref[span, :] = dzf
            dzi_ref[span, :] = dzi
            dzc_ref[span, :] = (fc_ref[span, :].astype(F32) * gstate).astype(BF16)
            wide_f, wide_i = dzf.astype(F32), dzi.astype(F32)
            for k in range(4):
                sum_f = sum_f + wide_f[k * CHUNKS : (k + 1) * CHUNKS]
                sum_i = sum_i + wide_i[k * CHUNKS : (k + 1) * CHUNKS]
        carry[seqs], carry[seqs + 1] = sum_f, sum_i
        return tuple(carry)

    zero = jnp.zeros((CHUNKS, width), F32)
    carry = lax.fori_loop(0, steps // 4, turn, tuple(start[seq] for seq in range(seqs)) + (zero, zero))
    gbias_ref[0:1, :] = jnp.sum(carry[seqs], axis=0, keepdims=True)
    gbias_ref[1:2, :] = jnp.sum(carry[seqs + 1], axis=0, keepdims=True)
    acc[...] += (
        dot_nt(dzf_ref[...], columns_of(wf_ref))
        + dot_nt(dzi_ref[...], columns_of(wi_ref))
        + dot_nt(dzc_ref[...], columns_of(wc_ref))
    )

    @pl.when(at_step == NB - 1)
    def _():
        back, ggain = rms_back(x_ref[...].astype(F32), gain_ref[0:1, :], acc[...])
        ggain_ref[...] = ggain
        gstream_ref[...] = (gmid_ref[...] + back).astype(gstream_ref.dtype)


def send_or_keep(mine, keep_ref, send_ref, put):
    @pl.when(mine)
    def _():
        put(keep_ref)

    @pl.when(jnp.logical_not(mine))
    def _():
        put(send_ref)


def put_columns(pos_ref, keep_ref, send_ref, start, value):
    at = pl.program_id(0)
    x, core = at // 2, at % 2
    rows = value.shape[0] // NS

    def put(ref):
        for j in range(value.shape[1] // LANE):
            part = value[:, j * LANE : (j + 1) * LANE].astype(BF16).reshape(NS, rows, LANE)
            ref[:, x, start + j * rows : start + (j + 1) * rows, :] = part

    send_or_keep(core == pos_ref[0], keep_ref, send_ref, put)


def put_rows(pos_ref, keep_ref, send_ref, value):
    count = NS // NB
    for j in range(NB):
        part = value[:, j * LANE : (j + 1) * LANE].astype(BF16).reshape(count, -1, LANE)

        def put(ref):
            ref[pl.ds(pl.program_id(0) * count, count), j // 2] = part

        send_or_keep(pos_ref[0] == j % 2, keep_ref, send_ref, put)


def up_weight_kernel(pos_ref, n2_ref, gpre_ref, keep_ref, send_ref):
    put_columns(pos_ref, keep_ref, send_ref, 0, dot_tn(n2_ref[...], gpre_ref[...]))


def row_weight_kernel(pos_ref, left_ref, right_ref, keep_ref, send_ref):
    put_rows(pos_ref, keep_ref, send_ref, dot_tn(left_ref[...], right_ref[...]))


def gate_weight_kernel(vectors, pos_ref, normed_ref, dzf_ref, dzi_ref, dzc_ref, *refs):
    keep_ref, send_ref = refs[-3:-1] if vectors else refs[-2:]
    normed = normed_ref[...]
    rows = normed.shape[1] // NS * dzf_ref.shape[1] // LANE
    for m, dz in enumerate((dzf_ref, dzi_ref, dzc_ref)):
        put_columns(pos_ref, keep_ref, send_ref, m * rows, dot_tn(normed, dz[...]))
    if vectors:
        scratch = refs[-1]

        @pl.when(pl.program_id(0) == 0)
        def _():
            scratch[...] = jnp.zeros_like(scratch)
            row = 0
            for ref in refs[:-3]:
                wide = ref.shape[1] // NS
                for r in range(ref.shape[0]):
                    for s in range(NS):
                        scratch[s, row : row + 1, :wide] = ref[r : r + 1, s * wide : (s + 1) * wide]
                    row += 1
            found = scratch[...].astype(BF16)
            for x in range(2):
                keep_ref[:, x, 3 * rows :, :] = found
                send_ref[:, x, 3 * rows :, :] = found


def add(*parts):
    total = parts[0].astype(F32)
    for part in parts[1:]:
        total = total + part.astype(F32)
    return total


def pair_sum_kernel(rows, cut, pos_ref, *refs):
    count = len(rows)
    keeps, gots = refs[:count], refs[count : 2 * count]
    send_a, keep_a, send_b, keep_b = refs[2 * count :]
    x, y = pos_ref[1], pos_ref[2]
    at = 0
    for keep, got, r in zip(keeps, gots, rows):
        mid = min(max(cut - at, 0), r)
        if mid:
            for v in range(2):
                for out, ix in ((send_a, 1 - x), (keep_a, x)):
                    out[0, v, at : at + mid] = add(keep[0, v, ix, :mid], got[0, v, ix, :mid]).astype(BF16)
        if mid < r:
            low = at + mid - cut
            for v in range(2):
                for out, iy in ((send_b, 1 - y), (keep_b, y)):
                    out[0, v, low : low + r - mid] = add(keep[0, iy, v, mid:], got[0, iy, v, mid:]).astype(BF16)
        at += r


def plane_sum_kernel(pos_ref, keep_a, got_a, keep_b, got_b, send2_a, keep2_a, send2_b, keep2_b):
    x, y = pos_ref[1], pos_ref[2]
    for keep, got, send2, keep2, mine in ((keep_a, got_a, send2_a, keep2_a, y), (keep_b, got_b, send2_b, keep2_b, x)):
        send2[0] = add(keep[0, 1 - mine], got[0, 1 - mine]).astype(BF16)
        keep2[0] = add(keep[0, mine], got[0, mine]).astype(BF16)


def line_sum_kernel(pos_ref, keep_a, got_a, keep_b, got_b, *outs):
    cut = keep_a.shape[1]
    for k, out in enumerate(outs):
        z = pos_ref[3] ^ k
        out[:cut] = add(keep_a[z], got_a[z]).astype(BF16)
        out[cut:] = add(keep_b[z], got_b[z]).astype(BF16)


def line_total_kernel(*refs):
    refs[-1][...] = add(*[ref[...] for ref in refs[:-1]])


def finish_kernel(layout, *refs):
    at = 0
    ins = sum(parts for parts, _ in layout)
    outs = refs[ins:]
    for parts, pieces in layout:
        got = refs[at : at + parts]
        at += parts
        row = 0
        for out, layer, vectors in pieces:
            ref = outs[out]
            if vectors:
                ref[layer : layer + 1, :] = add(*[g[...] for g in got])[row : row + 1, : ref.shape[1]]
                row += 1
                continue
            r = ref.shape[1]
            for j in range(ref.shape[2] // LANE):
                ref[layer, :, j * LANE : (j + 1) * LANE] = add(*[g[row : row + r] for g in got])
                row += r


def pack_kernel(groups, *refs):
    ins = refs[: len(refs) - len(groups) - 1]
    outs, scratch = refs[len(ins) : -1], refs[-1]
    for out, group in zip(outs, groups):
        row = 0
        vec = 0
        for which, layer, vector in group:
            ref = ins[which]
            if vector:
                if vec == 0:
                    scratch[...] = jnp.zeros_like(scratch)
                scratch[vec : vec + 1, : ref.shape[1]] = ref[...].astype(F32)[layer : layer + 1]
                vec += 1
                continue
            r = ref.shape[1]
            for j in range(ref.shape[2] // LANE):
                out[row : row + r, :] = ref[layer, :, j * LANE : (j + 1) * LANE]
                row += r
        if vec:
            out[row:, :] = scratch[...].astype(BF16)


def line_gather_kernel(pos_ref, *refs):
    out = refs[-1]
    for k, part in enumerate(refs[:-1]):
        out[pos_ref[3] ^ k] = part[...]


def plane_gather_kernel(pos_ref, *refs):
    at, half, out = pl.program_id(0), pl.num_programs(0) // 2, refs[-1]
    core, x, y = pos_ref[0], pos_ref[1], pos_ref[2]
    count = len(refs) // 2
    for c in range(2):
        own, from_x, from_y, low = refs[count * c : count * c + 4]
        out[0, y, x, core ^ c] = own[0]
        out[0, y, x ^ 1, core ^ c] = from_x[0]
        out[0, y ^ 1, x, core ^ c] = from_y[0]

        if count == 4:
            out[0, y ^ 1, x ^ 1, core ^ c] = low[0]
            continue
        high = refs[count * c + 4]

        @pl.when(at < half)
        def _():
            out[0, y ^ 1, x ^ 1, core ^ c] = low[0]

        @pl.when(at >= half)
        def _():
            out[0, y ^ 1, x ^ 1, core ^ c] = high[0]


def vector_kernel(gained, w_ref, *refs):
    outs, scratch = refs[:-1], refs[-1]
    scratch[...] = w_ref[:, 0].astype(F32)
    for l in range(LAYERS):
        for which in range(4):
            out, row = ((outs[2 * l], which // 3) if which in (0, 3) else (outs[2 * l + 1], which - 1))
            wide = out.shape[1] // NS
            for s in range(NS):
                out[row : row + 1, s * wide : (s + 1) * wide] = scratch[s, 4 * l + which : 4 * l + which + 1, :wide]


def shape(dims, dtype=F32):
    return jax.ShapeDtypeStruct(dims, dtype)


def call(kernel, grid, ins, outs, scratch, us, name):
    moved = sum(a.size * a.dtype.itemsize for a, _, _ in ins)
    moved += sum(s.size * s.dtype.itemsize for s, _, _ in outs)

    def spec(a, block, index):
        if a.dtype == jnp.int32:
            return pl.BlockSpec(memory_space=pltpu.SMEM)
        return pl.BlockSpec(block, index)

    found = pl.pallas_call(
        kernel,
        grid=(grid,),
        in_specs=[spec(*one) for one in ins],
        out_specs=[spec(*one) for one in outs],
        out_shape=[s for s, _, _ in outs],
        scratch_shapes=scratch,
        compiler_params=pltpu.CompilerParams(vmem_limit_bytes=VMEM),
        cost_estimate=pl.CostEstimate(flops=int(us * 1.1e9) + 1, bytes_accessed=1024, transcendentals=0),
        name=name,
    )(*[a for a, _, _ in ins])
    return found if len(found) > 1 else found[0]


def whole(array):
    dims = array.shape
    return (array, dims, lambda i: (0,) * len(dims))


def whole_out(dims, dtype=F32):
    return (shape(dims, dtype), dims, lambda i: (0,) * len(dims))


def first(i):
    return jnp.minimum(i, NB - 1)


def second(i):
    return jnp.maximum(i - NB, 0)


class Sizes:
    def __init__(self, seqs, length, d, h, ff):
        self.seqs, self.steps, self.n = seqs, length // CHUNKS, seqs * length
        self.d, self.h, self.ff = d, h, ff
        self.hb, self.fb = h // NB, ff // NB


def column_weight(view, at):
    array, rows, place = view
    return (array, (NS, 1, rows, LANE), lambda i: (0, at(i), place, 0))


def row_weight(view, at):
    array, rows, place = view
    return (array, (NS // NB, NB, rows, LANE), lambda i: (at(i), 0, place, 0))


def same(i):
    return i


def gate_forward(sz, x, gain, bias, w):
    n, d, h, wide, s = sz.n, sz.d, sz.h, sz.hb, sz.seqs
    col = lambda i: (0, i)
    return call(
        functools.partial(gate_kernel, s, sz.steps), NB,
        [whole(x), whole(gain), (bias, (2, wide), col)] + [column_weight(w[m], same) for m in "fic"],
        [whole_out((n, d), BF16)]
        + [(shape((n, h)), (n, wide), col)] * 3
        + [(shape((n, h), BF16), (n, wide), col)] * 3
        + [(shape((s, CHUNKS, h)), (s, CHUNKS, wide), lambda i: (0, 0, i))] * 2
        + [(shape((2 * s, h)), (2 * s, wide), col)],
        [pltpu.VMEM((n, wide), F32)] * 3, 9, "gates",
    )


def mix_forward(sz, x, gain, decay, inflow, cp, ch, ent, wt, last):
    n, d, h, ff, w, f, s = sz.n, sz.d, sz.h, sz.ff, sz.hb, sz.fb, sz.seqs
    col = lambda i: (0, first(i))
    late = lambda i: (0, second(i))
    deep = lambda i: (0, 0, first(i))
    return call(
        functools.partial(mix_kernel, s, sz.steps), 2 * NB,
        [
            whole(x), whole(gain), (decay, (n, w), col), (inflow, (n, w), col),
            (cp, (s, CHUNKS, w), deep), (ch, (s, CHUNKS, w), deep), (ent, (s, w), col),
            row_weight(wt["o"], first), column_weight(wt["u"], second), row_weight(wt["d"], second),
        ],
        [
            (shape((n, h)), (n, w), col), (shape((n, h), BF16), (n, w), col),
            (shape((s, CHUNKS, h)), (s, CHUNKS, w), deep),
            whole_out((n, d)), whole_out((n, d), BF16),
            (shape((n, ff), BF16), (n, f), late), (shape((n, ff), BF16), (n, f), late),
            whole_out((n, d), BF16 if last else F32),
        ],
        [pltpu.VMEM((n, d), F32), pltpu.VMEM((n, f), F32)], 14, "mix",
    )


def mlp_backward(sz, g, gain, mid, slope, decay, wt):
    n, d, h, ff, w, f, s = sz.n, sz.d, sz.h, sz.ff, sz.hb, sz.fb, sz.seqs
    col = lambda i: (0, second(i))
    early = lambda i: (0, first(i))
    deep = lambda i: (0, 0, second(i))
    return call(
        functools.partial(mlp_back_kernel, s, sz.steps), 2 * NB,
        [
            whole(g), whole(gain), whole(mid), (slope, (n, f), early), (decay, (n, w), col),
            row_weight(wt["o"], second), column_weight(wt["u"], first), row_weight(wt["d"], first),
        ],
        [
            whole_out((n, d), BF16), (shape((n, ff), BF16), (n, f), early), whole_out((n, d)), whole_out((n, d), BF16),
            whole_out((1, d)), (shape((n, h)), (n, w), col),
            (shape((s, CHUNKS, h)), (s, CHUNKS, w), deep), (shape((s, CHUNKS, h)), (s, CHUNKS, w), deep),
            (shape((2 * s, h)), (2 * s, w), col),
        ],
        [pltpu.VMEM((n, d), F32)], 12, "mlp_back",
    )


def gate_backward(sz, x, gain, gmid, gh, decay, hidden, e, cand, ff_, fi_, fc_, cp, ca, ent, wt, last):
    n, d, h, w, s = sz.n, sz.d, sz.h, sz.hb, sz.seqs
    col = lambda i: (0, i)
    deep = lambda i: (0, 0, i)
    wide = lambda a: (a, (n, w), col)
    return call(
        functools.partial(gate_back_kernel, s, sz.steps), NB,
        [
            whole(x), whole(gain), whole(gmid), wide(gh), wide(decay), wide(hidden), (e, (s, CHUNKS, w), deep),
            wide(cand), wide(ff_), wide(fi_), wide(fc_), (cp, (s, CHUNKS, w), deep), (ca, (s, CHUNKS, w), deep),
            (ent, (s, w), col),
        ] + [column_weight(wt[m], same) for m in "fic"],
        [(shape((n, h), BF16), (n, w), col)] * 3
        + [(shape((2, h)), (2, w), col), whole_out((n, d), BF16 if last else F32), whole_out((1, d))],
        [pltpu.VMEM((n, d), F32), pltpu.VMEM((s, CHUNKS, w), F32)], 10, "gate_back",
    )


def up_weights(sz, pos, n2, gpre):
    n, d, ff, f = sz.n, sz.d, sz.ff, sz.fb
    dims = (NS, 2, d * ff // (32 * LANE), LANE)
    return call(
        up_weight_kernel, NB, [whole(pos), whole(n2), (gpre, (n, f), lambda i: (0, i))],
        [whole_out(dims, BF16)] * 2, [], 5, "up_weights",
    )


def row_weights(sz, pos, left, right, name):
    n, k, d = sz.n, left.shape[1], sz.d
    dims = (NS, 2, k // NS, LANE)
    return call(
        row_weight_kernel, NB, [whole(pos), (left, (n, k // NB), lambda i: (0, i)), whole(right)],
        [whole_out(dims, BF16)] * 2, [], 5, name,
    )


def gate_weights(sz, pos, normed, dzf, dzi, dzc, vectors):
    n, d, h, w = sz.n, sz.d, sz.h, sz.hb
    col = lambda i: (0, i)
    rows = 3 * d * h // (32 * LANE) + (16 if vectors else 0)
    return call(
        functools.partial(gate_weight_kernel, bool(vectors)), NB,
        [whole(pos), whole(normed), (dzf, (n, w), col), (dzi, (n, w), col), (dzc, (n, w), col)]
        + [whole(v) for v in vectors],
        [whole_out((NS, 2, rows, LANE), BF16)] * 2,
        [pltpu.VMEM((NS, 16, LANE), F32)] if vectors else [], 0, "gate_weights",
    )


def swap(array, axes, bits):
    count = lax.axis_size(axes)
    return lax.ppermute(array, axes, [(i, i ^ bits) for i in range(count)])


BOTH = ("seq", "batch")


def after(array, *others):
    return lax.optimization_barrier((array,) + others)[0]


def sum_cut(rows):
    total = sum(rows)
    if len(rows) == 1:
        return total // 2 // 16 * 16
    return rows[0] if rows[0] * 5 >= total * 2 else rows[0] + rows[1]


def by_line(a):
    return (a, (1,) + a.shape[1:], lambda i: (i,) + (0,) * (len(a.shape) - 1))


def by_line_out(*dims):
    return (shape(dims, BF16), (1,) + dims[1:], lambda i: (i,) + (0,) * (len(dims) - 1))


def core_exchange(pairs):
    return [(keep, swap(send, "batch", 1)) for keep, send in pairs]


def pair_sum(pos, pairs):
    rows = tuple(keep.shape[2] for keep, _ in pairs)
    cut, total = sum_cut(rows), sum(rows)
    view = lambda a: by_line(a.reshape((4, 2, 2) + a.shape[2:]))
    two = [by_line_out(4, 2, cut, LANE)] * 2 + [by_line_out(4, 2, total - cut, LANE)] * 2
    return call(
        functools.partial(pair_sum_kernel, rows, cut), 4,
        [whole(pos)] + [view(keep) for keep, _ in pairs] + [view(got) for _, got in pairs], two, [], 0, "pair_sum",
    )


def plane_exchange(parts, first, second):
    send_a, keep_a, send_b, keep_b = parts
    return keep_a, swap(send_a, *first), keep_b, swap(send_b, *second)


X_AXIS, Y_AXIS = ("batch", 2), ("seq", 1)


def plane_sum(pos, parts):
    cut, rest = parts[0].shape[2], parts[2].shape[2]
    one = [by_line_out(4, cut, LANE)] * 2 + [by_line_out(4, rest, LANE)] * 2
    return call(plane_sum_kernel, 4, [whole(pos)] + [by_line(a) for a in parts], one, [], 0, "plane_sum")


def line_sum(pos, parts):
    total = parts[0].shape[1] + parts[2].shape[1]
    return call(
        line_sum_kernel, 1, [whole(pos)] + [whole(a) for a in parts], [whole_out((total, LANE), BF16)] * 4, [], 0, "line_sum",
    )


def line_exchange(parts):
    return [parts[0]] + [swap(part, "seq", 2 * (k + 1)) for k, part in enumerate(parts[1:])]


def reduce_rest(pos, parts):
    parts = plane_sum(pos, plane_exchange(parts, X_AXIS, Y_AXIS))
    return line_exchange(line_sum(pos, plane_exchange(parts, Y_AXIS, X_AXIS)))


def gather(pos, owns, direct):
    lines = []
    for own in owns:
        if lines:
            own = after(own, *lines[:2])
        parts = [own] + [swap(own, "seq", 2 * k) for k in range(1, 4)]
        lines.append(
            call(
                line_gather_kernel, 1, [whole(pos)] + [whole(p) for p in parts],
                [whole_out((4,) + own.shape, BF16)], [], 2, "line_gather",
            )
        )
    found, last = [], ()
    for at, line in enumerate(lines):
        rows = line.shape[1]
        sent = after(line, *last) if last else line
        from_x, from_y = swap(sent, *X_AXIS), swap(sent, *Y_AXIS)
        if at in direct:
            diagonal = swap(sent, BOTH, 6)
            last = (from_x, from_y, diagonal)
            parts = [line, from_x, from_y, diagonal]
        else:
            low, high = swap(from_x[:2], *Y_AXIS), swap(from_y[2:], *X_AXIS)
            last = (from_x, from_y) if at == 0 else (low, high)
            parts = [line, from_x, from_y, low, high]
        parts += [swap(p, "batch", 1) for p in parts]
        maps = [lambda i: (i, 0, 0)] * 3
        maps += maps[:1] if at in direct else [lambda i: (jnp.minimum(i, 1), 0, 0), lambda i: (jnp.maximum(i - 2, 0), 0, 0)]
        place = lambda i: (i, 0, 0, 0, 0, 0)
        got = call(
            plane_gather_kernel, 4, [whole(pos)] + [(p, (1, rows, LANE), m) for p, m in zip(parts, maps * 2)],
            [(shape((4, 2, 2, 2, rows, LANE), BF16), (1, 2, 2, 2, rows, LANE), place)], [], 5, "plane_gather",
        )
        found.append(got.reshape(NS, NB, rows, LANE))
    return found, lines


def enter(fin, seqs, backward, fill=()):
    count, mine = lax.axis_size("seq"), lax.axis_index("seq")
    prod, state = fin[:seqs], fin[seqs:]
    pre_p, pre_s = jnp.ones_like(prod), jnp.zeros_like(state)
    bit, message, done = 1, fin, []
    for step in range(int(count).bit_length() - 1):
        other = lax.ppermute(message, "seq", [(i, i ^ bit) for i in range(count)])
        if step < len(fill):
            done.append(fill[step](message))
        o_p, o_s = other[:seqs], other[seqs:]
        upper = ((mine // bit) % 2 == 1) ^ backward
        pre_p, pre_s = jnp.where(upper, o_p * pre_p, pre_p), jnp.where(upper, pre_p * o_s + pre_s, pre_s)
        state = jnp.where(upper, prod * o_s + state, o_p * state + o_s)
        prod = prod * o_p
        message = jnp.concatenate([prod, state])
        if step < len(fill):
            message = after(message, *done[-1])
        bit *= 2
    return pre_s, done


def slabs(matrix, seq_count, batch_count):
    rows, cols = matrix.shape[0] // NS, matrix.shape[1] // NB
    cut = matrix.reshape(NS, rows, NB, cols // LANE, LANE).transpose(0, 2, 3, 1, 4)
    return cut.reshape(NS, NB, rows * cols // LANE, LANE)


def unslab(blocks, rows, cols):
    r, c = rows // NS, cols // NB
    cut = blocks.reshape(NS, NB, c // LANE, r, LANE).transpose(0, 3, 1, 2, 4)
    return cut.reshape(rows, cols)


def body(
    tokens, norm_gain, w_forget, w_input, w_cand, forget_bias, input_bias, w_out, mlp_gain, w_up, w_down, cotangent
):
    seqs, length, d = tokens.shape
    seq_count, batch_count = lax.axis_size("seq"), lax.axis_size("batch")
    h, ff = w_forget.shape[2] * batch_count, w_up.shape[2] * batch_count
    sz = Sizes(seqs, length, d, h, ff)
    standard = (seq_count, batch_count) == (NS, NB)
    matrices = {"u": w_up, "d": w_down, "o": w_out, "f": w_forget, "i": w_input, "c": w_cand}
    vectors = (norm_gain, forget_bias, input_bias, mlp_gain)
    slab_rows = {"u": d * ff // (32 * LANE), "d": ff // NS, "o": h // NS}
    slab_rows.update({m: d * h // (32 * LANE) for m in "fic"})
    order = {name: k for k, name in enumerate(matrices)}

    if standard:
        s_at, b_at = lax.axis_index("seq"), lax.axis_index("batch")
        pos = jnp.stack([b_at % 2, b_at // 2, s_at % 2, s_at // 2]).astype(jnp.int32)
        groups = []
        for l in range(LAYERS):
            vecs = [(6 + k, at, True) for at in range(LAYERS) for k in range(4)] if l == 0 else []
            groups += [[(order[m], l, False) for m in "fic"] + vecs, [(order[m], l, False) for m in "udo"]]
        rows = [sum(slab_rows["udofic"[which]] for which, _, vec in g if not vec) for g in groups]
        rows[0] += 16
        packs = call(
            functools.partial(pack_kernel, groups), 1, [whole(m) for m in matrices.values()] + [whole(v) for v in vectors],
            [whole_out((r, LANE), BF16) for r in rows], [pltpu.VMEM((16, LANE), F32)], 2, "pack",
        )
        got, lines = gather(pos, packs, (2,))
        places = {"f": 0, "i": 1, "c": 2, "u": 0, "d": 1, "o": 4}
        weights = [{m: (got[2 * l + (m in "udo")], slab_rows[m], places[m]) for m in "udofic"} for l in range(LAYERS)]
        vecs = call(
            functools.partial(vector_kernel, None), 1,
            [(got[0], (NS, 1, 16, LANE), lambda i: (0, 0, 3 * slab_rows["f"] // 16, 0))],
            [whole_out((2, size)) for l in range(LAYERS) for size in (d, h)],
            [pltpu.VMEM((NS, 16, LANE), F32)], 1, "vectors",
        )
        gains, biases = vecs[0::2], vecs[1::2]
    else:
        pos = jnp.zeros((4,), jnp.int32)

        def full(m):
            m = lax.all_gather(m, "batch", axis=1, tiled=True)
            return lax.all_gather(m, "seq", axis=0, tiled=True)

        weights = [
            {m: (slabs(full(matrices[m][l]), NS, NB), slab_rows[m], 0) for m in "udofic"} for l in range(LAYERS)
        ]
        whole_vectors = [lax.all_gather(v, "seq", axis=1, tiled=True).astype(F32) for v in vectors]
        gains = [jnp.stack([whole_vectors[0][l], whole_vectors[3][l]]) for l in range(LAYERS)]
        biases = [jnp.stack([whole_vectors[1][l], whole_vectors[2][l]]) for l in range(LAYERS)]

    def to_rows(v):
        return v.reshape(seqs, CHUNKS, sz.steps, d).transpose(0, 2, 1, 3).reshape(sz.n, d)

    def from_rows(v):
        return v.reshape(seqs, sz.steps, CHUNKS, d).transpose(0, 2, 1, 3).reshape(seqs, length, d)

    stream, grad = to_rows(tokens), to_rows(cotangent)
    kept = []
    for l in range(LAYERS):
        normed, decay, inflow, cand, f_f, f_i, f_c, cp, ch, fin = gate_forward(sz, stream, gains[l], biases[l], weights[l])
        ent, _ = enter(fin, seqs, False)
        if standard and l + 1 < LAYERS:
            ent = after(ent, lines[2 * l + 3])
        hidden, hb, e, mid, n2, act, slope, result = mix_forward(
            sz, stream, gains[l], decay, inflow, cp, ch, ent, weights[l], l == LAYERS - 1
        )
        kept.append((stream, normed, decay, cand, f_f, f_i, f_c, hidden, hb, e, mid, n2, act, slope))
        stream = result
    output = from_rows(stream)

    vector_grads, sums, pending = [None] * LAYERS, [], []
    waiting, held = None, []
    for l in reversed(range(LAYERS)):
        x, normed, decay, cand, f_f, f_i, f_c, hidden, hb, e, mid, n2, act, slope = kept[l]
        gr, gpre, gmid, go, ggain_two, gh, cp, ca, fin = mlp_backward(sz, grad, gains[l], mid, slope, decay, weights[l])
        if waiting:
            names, parts = waiting
            parts = line_sum(pos, [after(parts[0], fin), *parts[1:]])
            gpre = after(gpre, parts[0])
            waiting = (names, line_exchange(parts))
        fill = [
            lambda m: up_weights(sz, pos, after(n2, m), gpre),
            lambda m: row_weights(sz, pos, after(act, m), gr, "down_weights"),
            lambda m: row_weights(sz, pos, after(hb, m), go, "out_weights"),
        ]
        ent, pairs = enter(fin, seqs, True, fill)
        if standard:
            names = [(l, m) for m in "udo"] + (held[0] if held else [])
            early = pair_sum(pos, core_exchange(pairs) + held[1:])
            gmid = after(gmid, early[0])
        dzf, dzi, dzc, gbias, grad, ggain_one = gate_backward(
            sz, x, gains[l], gmid, gh, decay, hidden, e, cand, f_f, f_i, f_c, cp, ca, ent, weights[l], l == 0
        )
        vector_grads[l] = (ggain_one, gbias, ggain_two)
        final = [v for each in vector_grads for v in each] if l == 0 and standard else []
        gate_pair = gate_weights(sz, pos, normed, dzf, dzi, dzc, final)
        if not standard:
            pending.append((l, pairs + [gate_pair]))
            continue
        parts = list(plane_exchange(early, X_AXIS, Y_AXIS))
        parts[0] = after(parts[0], gate_pair[0])
        parts = plane_sum(pos, parts)
        if l > 0:
            held = [[(l, m) for m in "fic"]] + core_exchange([gate_pair])
            grad = after(grad, parts[0])
            waiting = (names, plane_exchange(parts, Y_AXIS, X_AXIS))
        else:
            done = parts[0]
            if waiting:
                names_1, parts_1 = waiting
                parts_1[0] = after(parts_1[0], gate_pair[0])
                done = call(line_total_kernel, 1, [whole(p) for p in parts_1], [whole_out(parts_1[0].shape)], [], 0, "line_total")
                sums.append((names_1, [done]))
            late = pair_sum(pos, core_exchange([(gate_pair[0], after(gate_pair[1], parts[0], done))]))
            sums.append((names, line_exchange(line_sum(pos, plane_exchange(parts, Y_AXIS, X_AXIS)))))
            sums.append(([(l, m) for m in "fic"] + [(at, k) for at in range(LAYERS) for k in range(4)], reduce_rest(pos, late)))
    grad_tokens = from_rows(grad)

    if standard:
        layout, ins = [], []
        for names, parts in sums:
            pieces = [(order[m], l, False) if m in order else (6 + m, l, True) for l, m in names]
            layout.append((len(parts), pieces))
            ins += [whole(p) for p in parts]
        found = call(
            functools.partial(finish_kernel, layout), 1, ins,
            [whole_out(m.shape) for m in matrices.values()] + [whole_out(v.shape) for v in vectors], [], 3, "finish",
        )
        g_up, g_down, g_out, g_f, g_i, g_c, g_norm, g_fb, g_ib, g_mlp = found
    else:
        per_layer = {}
        for l, pairs in pending:
            blocks = [jnp.stack([keep, send], axis=2).reshape(NS, NB, -1, LANE) for keep, send in pairs]
            gates = jnp.split(blocks[3], 3, axis=2)
            for m, g in zip("udofic", blocks[:3] + gates):
                v = unslab(g, matrices[m].shape[1] * seq_count, matrices[m].shape[2] * batch_count)
                v = lax.psum_scatter(v, "seq", scatter_dimension=0, tiled=True)
                per_layer[m, l] = lax.psum_scatter(v, "batch", scatter_dimension=1, tiled=True).astype(F32)
        g_up, g_down, g_out, g_f, g_i, g_c = [
            jnp.stack([per_layer[m, l] for l in range(LAYERS)]) for m in matrices
        ]
        rows = [
            (ggain_one[0], gbias[0], gbias[1], ggain_two[0]) for ggain_one, gbias, ggain_two in vector_grads
        ]
        g_norm, g_fb, g_ib, g_mlp = [
            lax.psum(lax.psum_scatter(jnp.stack([r[k] for r in rows]), "seq", scatter_dimension=1, tiled=True), "batch")
            for k in range(4)
        ]
    return output, grad_tokens, g_norm, g_f, g_i, g_c, g_fb, g_ib, g_out, g_mlp, g_up, g_down


def solution(mesh):
    split, vector, matrix = P("batch", "seq", None), P(None, "seq"), P(None, "seq", "batch")
    order = (vector, matrix, matrix, matrix, vector, vector, matrix, vector, matrix, matrix)
    return jax.shard_map(
        body,
        mesh=mesh,
        in_specs=(split,) + order + (split,),
        out_specs=(split, split) + order,
        check_vma=False,
    )
```

```python
import functools

import jax
import jax.numpy as jnp
from jax import lax
from jax.experimental import pallas as pl
from jax.experimental.pallas import tpu as pltpu
from jax.sharding import PartitionSpec as P

LAYERS = 2
EPS = 1e-05
NS, NB, LANE = 8, 4, 128
CHUNKS = 8
VMEM = 20 * 1024 * 1024
F32, BF16 = jnp.float32, jnp.bfloat16


def dot(left, right):
    return lax.dot_general(left, right, (((1,), (0,)), ((), ())), preferred_element_type=F32)


def dot_nt(left, right):
    return lax.dot_general(left, right, (((1,), (1,)), ((), ())), preferred_element_type=F32)


def dot_tn(left, right):
    return lax.dot_general(left, right, (((0,), (0,)), ((), ())), preferred_element_type=F32)


def columns_of(ref, slabs=2):
    rows = ref.shape[2] // slabs
    parts = [ref[:, 0, j * rows : (j + 1) * rows, :].reshape(NS * rows, LANE) for j in range(slabs)]
    return jnp.concatenate(parts, axis=1)


def rows_of(ref):
    parts = [ref[:, j].reshape(-1, LANE) for j in range(NB)]
    return jnp.concatenate(parts, axis=1)


def rms_scale(values):
    return lax.rsqrt(jnp.mean(values * values, axis=-1, keepdims=True) + EPS)


def rms_back(values, gain, grad):
    scale = rms_scale(values)
    unit = values * scale
    inner = grad * gain
    back = scale * (inner - unit * jnp.mean(inner * unit, axis=-1, keepdims=True))
    return back, jnp.sum(grad * unit, axis=0, keepdims=True)


def gate_kernel(
    seqs, steps, x_ref, gain_ref, bias_ref, wf_ref, wi_ref, wc_ref,
    normed_ref, decay_ref, inflow_ref, cand_ref, ff_ref, fi_ref, fc_ref, cp_ref, ch_ref, fin_ref,
    zf, zi, zc,
):
    width = 2 * LANE

    @pl.when(pl.program_id(0) == 0)
    def _():
        x = x_ref[...].astype(F32)
        normed_ref[...] = (x * rms_scale(x) * gain_ref[0:1, :]).astype(BF16)

    normed = normed_ref[...]
    zf[...] = dot(normed, columns_of(wf_ref)) + bias_ref[0:1, :]
    zi[...] = dot(normed, columns_of(wi_ref)) + bias_ref[1:2, :]
    zc[...] = dot(normed, columns_of(wc_ref))

    block = 4 * CHUNKS

    def turn(at, carry):
        carry = list(carry)
        for seq in range(seqs):
            span = pl.ds(pl.multiple_of(seq * steps * CHUNKS + at * block, block), block)
            f, i, c = zf[span, :], zi[span, :], zc[span, :]
            low = jnp.minimum(jnp.minimum(f, i), 0.0)
            e0, ef, ei = jnp.exp(low), jnp.exp(low - f), jnp.exp(low - i)
            a, b = e0 + ef, e0 + ei
            inv = 1.0 / (a + b)
            decay, other = b * inv, a * inv
            ec = jnp.exp(-jnp.abs(c))
            cand = jnp.maximum(c, 0.0) + jnp.log1p(ec)
            slope = jnp.where(c >= 0.0, 1.0, ec) / (1.0 + ec)
            inflow = other * cand
            decay_ref[span, :] = decay
            inflow_ref[span, :] = inflow
            cand_ref[span, :] = cand
            ff_ref[span, :] = (ef * inv * decay).astype(BF16)
            fi_ref[span, :] = (ei * inv * other).astype(BF16)
            fc_ref[span, :] = (other * slope).astype(BF16)
            prod, state = carry[2 * seq], carry[2 * seq + 1]
            for k in range(4):
                d = decay[k * CHUNKS : (k + 1) * CHUNKS]
                prod = prod * d
                state = state * d + inflow[k * CHUNKS : (k + 1) * CHUNKS]
            carry[2 * seq], carry[2 * seq + 1] = prod, state
        return tuple(carry)

    one, zero = jnp.ones((CHUNKS, width), F32), jnp.zeros((CHUNKS, width), F32)
    carry = lax.fori_loop(0, steps // 4, turn, (one, zero) * seqs)
    for seq in range(seqs):
        prod, state = carry[2 * seq], carry[2 * seq + 1]
        cp_ref[seq], ch_ref[seq] = prod, state
        whole, last = prod[0:1], state[0:1]
        for c in range(1, CHUNKS):
            whole, last = whole * prod[c : c + 1], last * prod[c : c + 1] + state[c : c + 1]
        fin_ref[seq : seq + 1, :] = whole
        fin_ref[seqs + seq : seqs + seq + 1, :] = last


def mix_kernel(
    seqs, steps, x_ref, gain_ref, decay_ref, inflow_ref, cp_ref, ch_ref, ent_ref, wo_ref, wu_ref, wd_ref,
    hidden_ref, hb_ref, e_ref, mid_ref, n2_ref, act_ref, slope_ref, out_ref,
    acc, pre,
):
    at_step = pl.program_id(0)
    block = 4 * CHUNKS

    @pl.when(at_step == 0)
    def _():
        acc[...] = x_ref[...].astype(F32)

    @pl.when(at_step < NB)
    def _():
        for seq in range(seqs):
            state = ent_ref[seq : seq + 1, :]
            for c in range(CHUNKS):
                e_ref[seq, c : c + 1, :] = state
                state = state * cp_ref[seq, c : c + 1, :] + ch_ref[seq, c : c + 1, :]

        def turn(at, carry):
            carry = list(carry)
            for seq in range(seqs):
                span = pl.ds(pl.multiple_of(seq * steps * CHUNKS + at * block, block), block)
                d, u = decay_ref[span, :], inflow_ref[span, :]
                state, found = carry[seq], []
                for k in range(4):
                    state = state * d[k * CHUNKS : (k + 1) * CHUNKS] + u[k * CHUNKS : (k + 1) * CHUNKS]
                    found.append(state)
                carry[seq] = state
                hidden = jnp.concatenate(found, axis=0)
                hidden_ref[span, :] = hidden
                hb_ref[span, :] = hidden.astype(BF16)
            return tuple(carry)

        lax.fori_loop(0, steps // 4, turn, tuple(e_ref[seq] for seq in range(seqs)))
        acc[...] += dot(hb_ref[...], rows_of(wo_ref))

    @pl.when(at_step == NB - 1)
    def _():
        middle = acc[...]
        mid_ref[...] = middle
        n2_ref[...] = (middle * rms_scale(middle) * gain_ref[1:2, :]).astype(BF16)

    @pl.when(at_step >= NB)
    def _():
        pre[...] = dot(n2_ref[...], columns_of(wu_ref, 4))

        def turn(at, _):
            span = pl.ds(pl.multiple_of(at * 16, 16), 16)
            v = pre[span, :]
            phi = 0.5 + 0.5 * lax.erf(v * 0.7071067811865476)
            act_ref[span, :] = (v * phi).astype(BF16)
            slope_ref[span, :] = (phi + v * (0.3989422804014327 * jnp.exp(v * v * -0.5))).astype(BF16)
            return 0

        lax.fori_loop(0, pre.shape[0] // 16, turn, 0)
        acc[...] += dot(act_ref[...], rows_of(wd_ref))

    @pl.when(at_step == 2 * NB - 1)
    def _():
        out_ref[...] = acc[...].astype(out_ref.dtype)


def mlp_back_kernel(
    seqs, steps, g_ref, gain_ref, mid_ref, slope_ref, decay_ref, wo_ref, wu_ref, wd_ref,
    gr_ref, gpre_ref, gmid_ref, go_ref, ggain_ref, gh_ref, cp_ref, ca_ref, fin_ref,
    acc,
):
    at_step = pl.program_id(0)
    block = 4 * CHUNKS
    width = decay_ref.shape[1]

    @pl.when(at_step == 0)
    def _():
        gr_ref[...] = g_ref[...].astype(BF16)
        acc[...] = jnp.zeros_like(acc)

    @pl.when(at_step < NB)
    def _():
        gact = dot_nt(gr_ref[...], rows_of(wd_ref))
        gpre_ref[...] = (gact * slope_ref[...].astype(F32)).astype(BF16)
        acc[...] += dot_nt(gpre_ref[...], columns_of(wu_ref, 4))

    @pl.when(at_step == NB - 1)
    def _():
        back, ggain = rms_back(mid_ref[...], gain_ref[1:2, :], acc[...])
        ggain_ref[...] = ggain
        gmid = g_ref[...].astype(F32) + back
        gmid_ref[...] = gmid
        go_ref[...] = gmid.astype(BF16)

    @pl.when(at_step >= NB)
    def _():
        gh_ref[...] = dot_nt(go_ref[...], rows_of(wo_ref))

        def turn(turn_at, carry):
            at = steps // 4 - 1 - turn_at
            carry = list(carry)
            for seq in range(seqs):
                span = pl.ds(pl.multiple_of(seq * steps * CHUNKS + at * block, block), block)
                d, g = decay_ref[span, :], gh_ref[span, :]
                prod, state = carry[2 * seq], carry[2 * seq + 1]
                for k in reversed(range(4)):
                    dk = d[k * CHUNKS : (k + 1) * CHUNKS]
                    prod = prod * dk
                    state = dk * (g[k * CHUNKS : (k + 1) * CHUNKS] + state)
                carry[2 * seq], carry[2 * seq + 1] = prod, state
            return tuple(carry)

        one, zero = jnp.ones((CHUNKS, width), F32), jnp.zeros((CHUNKS, width), F32)
        carry = lax.fori_loop(0, steps // 4, turn, (one, zero) * seqs)
        for seq in range(seqs):
            prod, state = carry[2 * seq], carry[2 * seq + 1]
            cp_ref[seq], ca_ref[seq] = prod, state
            whole, last = prod[CHUNKS - 1 :], state[CHUNKS - 1 :]
            for c in reversed(range(CHUNKS - 1)):
                whole, last = whole * prod[c : c + 1], last * prod[c : c + 1] + state[c : c + 1]
            fin_ref[seq : seq + 1, :] = whole
            fin_ref[seqs + seq : seqs + seq + 1, :] = last


def gate_back_kernel(
    seqs, steps, x_ref, gain_ref, gmid_ref, gh_ref, decay_ref, hidden_ref, e_ref, cand_ref, ff_ref, fi_ref, fc_ref,
    cp_ref, ca_ref, ent_ref, wf_ref, wi_ref, wc_ref,
    dzf_ref, dzi_ref, dzc_ref, gbias_ref, gstream_ref, ggain_ref,
    acc, start,
):
    at_step = pl.program_id(0)
    block = 4 * CHUNKS
    width = decay_ref.shape[1]

    @pl.when(at_step == 0)
    def _():
        acc[...] = jnp.zeros_like(acc)

    for seq in range(seqs):
        state = ent_ref[seq : seq + 1, :]
        for c in reversed(range(CHUNKS)):
            start[seq, c : c + 1, :] = state
            state = state * cp_ref[seq, c : c + 1, :] + ca_ref[seq, c : c + 1, :]

    def turn(turn_at, carry):
        at = steps // 4 - 1 - turn_at
        carry = list(carry)
        sum_f, sum_i = carry[seqs], carry[seqs + 1]
        for seq in range(seqs):
            base = seq * steps * CHUNKS + at * block
            span = pl.ds(pl.multiple_of(base, block), block)
            before = hidden_ref[pl.ds(pl.multiple_of(jnp.maximum(base - CHUNKS, 0), CHUNKS), CHUNKS), :]
            before = jnp.where(at == 0, e_ref[seq], before)
            d, g = decay_ref[span, :], gh_ref[span, :]
            previous = jnp.concatenate([before, hidden_ref[span, :][: block - CHUNKS]], axis=0)
            state, found = carry[seq], []
            for k in reversed(range(4)):
                now = g[k * CHUNKS : (k + 1) * CHUNKS] + state
                found.append(now)
                state = d[k * CHUNKS : (k + 1) * CHUNKS] * now
            carry[seq] = state
            gstate = jnp.concatenate(found[::-1], axis=0)
            both = gstate * (cand_ref[span, :] - previous)
            dzf = (-ff_ref[span, :].astype(F32) * both).astype(BF16)
            dzi = (fi_ref[span, :].astype(F32) * both).astype(BF16)
            dzf_ref[span, :] = dzf
            dzi_ref[span, :] = dzi
            dzc_ref[span, :] = (fc_ref[span, :].astype(F32) * gstate).astype(BF16)
            wide_f, wide_i = dzf.astype(F32), dzi.astype(F32)
            for k in range(4):
                sum_f = sum_f + wide_f[k * CHUNKS : (k + 1) * CHUNKS]
                sum_i = sum_i + wide_i[k * CHUNKS : (k + 1) * CHUNKS]
        carry[seqs], carry[seqs + 1] = sum_f, sum_i
        return tuple(carry)

    zero = jnp.zeros((CHUNKS, width), F32)
    carry = lax.fori_loop(0, steps // 4, turn, tuple(start[seq] for seq in range(seqs)) + (zero, zero))
    gbias_ref[0:1, :] = jnp.sum(carry[seqs], axis=0, keepdims=True)
    gbias_ref[1:2, :] = jnp.sum(carry[seqs + 1], axis=0, keepdims=True)
    acc[...] += (
        dot_nt(dzf_ref[...], columns_of(wf_ref))
        + dot_nt(dzi_ref[...], columns_of(wi_ref))
        + dot_nt(dzc_ref[...], columns_of(wc_ref))
    )

    @pl.when(at_step == NB - 1)
    def _():
        back, ggain = rms_back(x_ref[...].astype(F32), gain_ref[0:1, :], acc[...])
        ggain_ref[...] = ggain
        gstream_ref[...] = (gmid_ref[...] + back).astype(gstream_ref.dtype)


def send_or_keep(mine, keep_ref, send_ref, put):
    @pl.when(mine)
    def _():
        put(keep_ref)

    @pl.when(jnp.logical_not(mine))
    def _():
        put(send_ref)


def put_columns(pos_ref, keep_ref, send_ref, start, value):
    at = pl.program_id(0)
    x, core = at // 2, at % 2
    rows = value.shape[0] // NS

    def put(ref):
        for j in range(value.shape[1] // LANE):
            part = value[:, j * LANE : (j + 1) * LANE].astype(BF16).reshape(NS, rows, LANE)
            ref[:, x, start + j * rows : start + (j + 1) * rows, :] = part

    send_or_keep(core == pos_ref[0], keep_ref, send_ref, put)


def put_rows(pos_ref, keep_ref, send_ref, value):
    count = NS // NB
    for j in range(NB):
        part = value[:, j * LANE : (j + 1) * LANE].astype(BF16).reshape(count, -1, LANE)

        def put(ref):
            ref[pl.ds(pl.program_id(0) * count, count), j // 2] = part

        send_or_keep(pos_ref[0] == j % 2, keep_ref, send_ref, put)


def up_weight_kernel(pos_ref, n2_ref, gpre_ref, keep_ref, send_ref):
    put_columns(pos_ref, keep_ref, send_ref, 0, dot_tn(n2_ref[...], gpre_ref[...]))


def row_weight_kernel(pos_ref, left_ref, right_ref, keep_ref, send_ref):
    put_rows(pos_ref, keep_ref, send_ref, dot_tn(left_ref[...], right_ref[...]))


def gate_weight_kernel(vectors, pos_ref, normed_ref, dzf_ref, dzi_ref, dzc_ref, *refs):
    keep_ref, send_ref = refs[-3:-1] if vectors else refs[-2:]
    normed = normed_ref[...]
    rows = normed.shape[1] // NS * dzf_ref.shape[1] // LANE
    for m, dz in enumerate((dzf_ref, dzi_ref, dzc_ref)):
        put_columns(pos_ref, keep_ref, send_ref, m * rows, dot_tn(normed, dz[...]))
    if vectors:
        scratch = refs[-1]

        @pl.when(pl.program_id(0) == 0)
        def _():
            scratch[...] = jnp.zeros_like(scratch)
            row = 0
            for ref in refs[:-3]:
                wide = ref.shape[1] // NS
                for r in range(ref.shape[0]):
                    for s in range(NS):
                        scratch[s, row : row + 1, :wide] = ref[r : r + 1, s * wide : (s + 1) * wide]
                    row += 1
            found = scratch[...].astype(BF16)
            for x in range(2):
                keep_ref[:, x, 3 * rows :, :] = found
                send_ref[:, x, 3 * rows :, :] = found


def add(*parts):
    total = parts[0].astype(F32)
    for part in parts[1:]:
        total = total + part.astype(F32)
    return total


def pair_sum_kernel(rows, cut, pos_ref, *refs):
    count = len(rows)
    keeps, gots = refs[:count], refs[count : 2 * count]
    send_a, keep_a, send_b, keep_b = refs[2 * count :]
    x, y = pos_ref[1], pos_ref[2]
    at = 0
    for keep, got, r in zip(keeps, gots, rows):
        mid = min(max(cut - at, 0), r)
        if mid:
            for v in range(2):
                for out, ix in ((send_a, 1 - x), (keep_a, x)):
                    out[0, v, at : at + mid] = add(keep[0, v, ix, :mid], got[0, v, ix, :mid]).astype(BF16)
        if mid < r:
            low = at + mid - cut
            for v in range(2):
                for out, iy in ((send_b, 1 - y), (keep_b, y)):
                    out[0, v, low : low + r - mid] = add(keep[0, iy, v, mid:], got[0, iy, v, mid:]).astype(BF16)
        at += r


def plane_sum_kernel(pos_ref, keep_a, got_a, keep_b, got_b, send2_a, keep2_a, send2_b, keep2_b):
    x, y = pos_ref[1], pos_ref[2]
    for keep, got, send2, keep2, mine in ((keep_a, got_a, send2_a, keep2_a, y), (keep_b, got_b, send2_b, keep2_b, x)):
        send2[0] = add(keep[0, 1 - mine], got[0, 1 - mine]).astype(BF16)
        keep2[0] = add(keep[0, mine], got[0, mine]).astype(BF16)


def line_sum_kernel(pos_ref, keep_a, got_a, keep_b, got_b, *outs):
    cut = keep_a.shape[1]
    for k, out in enumerate(outs):
        z = pos_ref[3] ^ k
        out[:cut] = add(keep_a[z], got_a[z]).astype(BF16)
        out[cut:] = add(keep_b[z], got_b[z]).astype(BF16)


def line_total_kernel(*refs):
    refs[-1][...] = add(*[ref[...] for ref in refs[:-1]])


def finish_kernel(layout, *refs):
    at = 0
    ins = sum(parts for parts, _ in layout)
    outs = refs[ins:]
    for parts, pieces in layout:
        got = refs[at : at + parts]
        at += parts
        row = 0
        for out, layer, vectors in pieces:
            ref = outs[out]
            if vectors:
                ref[layer : layer + 1, :] = add(*[g[...] for g in got])[row : row + 1, : ref.shape[1]]
                row += 1
                continue
            r = ref.shape[1]
            for j in range(ref.shape[2] // LANE):
                ref[layer, :, j * LANE : (j + 1) * LANE] = add(*[g[row : row + r] for g in got])
                row += r


def pack_kernel(groups, *refs):
    ins = refs[: len(refs) - len(groups) - 1]
    outs, scratch = refs[len(ins) : -1], refs[-1]
    for out, group in zip(outs, groups):
        row = 0
        vec = 0
        for which, layer, vector in group:
            ref = ins[which]
            if vector:
                if vec == 0:
                    scratch[...] = jnp.zeros_like(scratch)
                scratch[vec : vec + 1, : ref.shape[1]] = ref[...].astype(F32)[layer : layer + 1]
                vec += 1
                continue
            r = ref.shape[1]
            for j in range(ref.shape[2] // LANE):
                out[row : row + r, :] = ref[layer, :, j * LANE : (j + 1) * LANE]
                row += r
        if vec:
            out[row:, :] = scratch[...].astype(BF16)


def line_gather_kernel(pos_ref, *refs):
    row = 0
    for out in refs[4:]:
        rows = out.shape[1]
        for k, part in enumerate(refs[:4]):
            out[pos_ref[3] ^ k] = part[row : row + rows, :]
        row += rows


def plane_gather_kernel(pos_ref, *refs):
    at, half, out = pl.program_id(0), pl.num_programs(0) // 2, refs[-1]
    core, x, y = pos_ref[0], pos_ref[1], pos_ref[2]
    count = len(refs) // 2

    def put(step_y, step_x, c, part):
        out[0, y ^ step_y, x ^ step_x, core ^ c] = part[0]

    for c in range(2):
        own, from_x, from_y, *diagonal = refs[count * c : count * (c + 1)]
        put(0, 0, c, own)
        put(0, 1, c, from_x)
        put(1, 0, c, from_y)
        if len(diagonal) == 1:
            put(1, 1, c, diagonal[0])
            continue
        pl.when(at < half)(functools.partial(put, 1, 1, c, diagonal[0]))
        pl.when(at >= half)(functools.partial(put, 1, 1, c, diagonal[1]))


def vector_kernel(gained, w_ref, *refs):
    outs, scratch = refs[:-1], refs[-1]
    scratch[...] = w_ref[:, 0].astype(F32)
    for l in range(LAYERS):
        for which in range(4):
            out, row = ((outs[2 * l], which // 3) if which in (0, 3) else (outs[2 * l + 1], which - 1))
            wide = out.shape[1] // NS
            for s in range(NS):
                out[row : row + 1, s * wide : (s + 1) * wide] = scratch[s, 4 * l + which : 4 * l + which + 1, :wide]


def shape(dims, dtype=F32):
    return jax.ShapeDtypeStruct(dims, dtype)


def call(kernel, grid, ins, outs, scratch, us, name):
    def spec(a, block, index):
        if a.dtype == jnp.int32:
            return pl.BlockSpec(memory_space=pltpu.SMEM)
        return pl.BlockSpec(block, index)

    found = pl.pallas_call(
        kernel,
        grid=(grid,),
        in_specs=[spec(*one) for one in ins],
        out_specs=[pl.BlockSpec(block, index) for _, block, index, *_ in outs],
        out_shape=[pltpu.HBM(one[0].shape, one[0].dtype) if one[3:] else one[0] for one in outs],
        scratch_shapes=scratch,
        compiler_params=pltpu.CompilerParams(vmem_limit_bytes=VMEM),
        cost_estimate=pl.CostEstimate(flops=int(us * 1.1e9) + 1, bytes_accessed=1024, transcendentals=0),
        name=name,
    )(*[a for a, _, _ in ins])
    return found if len(found) > 1 else found[0]


def far(array):
    return pltpu.with_memory_space_constraint(array, pltpu.HBM)


def whole(array):
    dims = array.shape
    return (array, dims, lambda i: (0,) * len(dims))


def whole_out(dims, dtype=F32):
    return (shape(dims, dtype), dims, lambda i: (0,) * len(dims))


def first(i):
    return jnp.minimum(i, NB - 1)


def second(i):
    return jnp.maximum(i - NB, 0)


class Sizes:
    def __init__(self, seqs, length, d, h, ff):
        self.seqs, self.steps, self.n = seqs, length // CHUNKS, seqs * length
        self.d, self.h, self.ff = d, h, ff
        self.hb, self.fb = h // NB, ff // NB


def column_weight(view, at, late=False):
    array, rows, place = view
    return (far(array) if late else array, (NS, 1, rows, LANE), lambda i: (0, at(i), place, 0))


def row_weight(view, at):
    array, rows, place = view
    return (array, (NS // NB, NB, rows, LANE), lambda i: (at(i), 0, place, 0))


def same(i):
    return i


def gate_forward(sz, x, gain, bias, w, save):
    n, d, h, wide, s = sz.n, sz.d, sz.h, sz.hb, sz.seqs
    col = lambda i: (0, i)
    return call(
        functools.partial(gate_kernel, s, sz.steps), NB,
        [whole(x), whole(gain), (bias, (2, wide), col)] + [column_weight(w[m], same) for m in "fic"],
        [whole_out((n, d), BF16) + save]
        + [(shape((n, h)), (n, wide), col) + save, (shape((n, h)), (n, wide), col), (shape((n, h)), (n, wide), col) + save]
        + [(shape((n, h), BF16), (n, wide), col) + save] * 3
        + [(shape((s, CHUNKS, h)), (s, CHUNKS, wide), lambda i: (0, 0, i))] * 2
        + [(shape((2 * s, h)), (2 * s, wide), col)],
        [pltpu.VMEM((n, wide), F32)] * 3, 9, "gates",
    )


def mix_forward(sz, x, gain, decay, inflow, cp, ch, ent, wt, last, save):
    n, d, h, ff, w, f, s = sz.n, sz.d, sz.h, sz.ff, sz.hb, sz.fb, sz.seqs
    col = lambda i: (0, first(i))
    late = lambda i: (0, second(i))
    deep = lambda i: (0, 0, first(i))
    return call(
        functools.partial(mix_kernel, s, sz.steps), 2 * NB,
        [
            whole(x), whole(gain), (decay, (n, w), col), (inflow, (n, w), col),
            (cp, (s, CHUNKS, w), deep), (ch, (s, CHUNKS, w), deep), (ent, (s, w), col),
            row_weight(wt["o"], first), column_weight(wt["u"], second), row_weight(wt["d"], second),
        ],
        [
            (shape((n, h)), (n, w), col, True), (shape((n, h), BF16), (n, w), col) + save,
            (shape((s, CHUNKS, h)), (s, CHUNKS, w), deep) + save,
            whole_out((n, d)) + save, whole_out((n, d), BF16) + save,
            (shape((n, ff), BF16), (n, f), late) + save, (shape((n, ff), BF16), (n, f), late) + save,
            whole_out((n, d), BF16 if last else F32),
        ],
        [pltpu.VMEM((n, d), F32), pltpu.VMEM((n, f), F32)], 14, "mix",
    )


def mlp_backward(sz, g, gain, mid, slope, decay, wt):
    n, d, h, ff, w, f, s = sz.n, sz.d, sz.h, sz.ff, sz.hb, sz.fb, sz.seqs
    col = lambda i: (0, second(i))
    early = lambda i: (0, first(i))
    deep = lambda i: (0, 0, second(i))
    return call(
        functools.partial(mlp_back_kernel, s, sz.steps), 2 * NB,
        [
            whole(g), whole(gain), whole(mid), (slope, (n, f), early), (decay, (n, w), col),
            row_weight(wt["o"], second), column_weight(wt["u"], first), row_weight(wt["d"], first),
        ],
        [
            whole_out((n, d), BF16), (shape((n, ff), BF16), (n, f), early), whole_out((n, d)), whole_out((n, d), BF16),
            whole_out((1, d)), (shape((n, h)), (n, w), col),
            (shape((s, CHUNKS, h)), (s, CHUNKS, w), deep), (shape((s, CHUNKS, h)), (s, CHUNKS, w), deep),
            (shape((2 * s, h)), (2 * s, w), col),
        ],
        [pltpu.VMEM((n, d), F32)], 12, "mlp_back",
    )


def gate_backward(sz, x, gain, gmid, gh, decay, hidden, e, cand, ff_, fi_, fc_, cp, ca, ent, wt, last):
    n, d, h, w, s = sz.n, sz.d, sz.h, sz.hb, sz.seqs
    col = lambda i: (0, i)
    deep = lambda i: (0, 0, i)
    wide = lambda a: (a, (n, w), col)
    return call(
        functools.partial(gate_back_kernel, s, sz.steps), NB,
        [
            whole(x), whole(gain), whole(gmid), wide(gh), wide(decay), wide(hidden), (e, (s, CHUNKS, w), deep),
            wide(cand), wide(ff_), wide(fi_), wide(fc_), (cp, (s, CHUNKS, w), deep), (ca, (s, CHUNKS, w), deep),
            (ent, (s, w), col),
        ] + [column_weight(wt[m], same, True) for m in "fic"],
        [(shape((n, h), BF16), (n, w), col)] * 3
        + [(shape((2, h)), (2, w), col), whole_out((n, d), BF16 if last else F32), whole_out((1, d))],
        [pltpu.VMEM((n, d), F32), pltpu.VMEM((s, CHUNKS, w), F32)], 10, "gate_back",
    )


def up_weights(sz, pos, n2, gpre):
    n, d, ff, f = sz.n, sz.d, sz.ff, sz.fb
    dims = (NS, 2, d * ff // (32 * LANE), LANE)
    return call(
        up_weight_kernel, NB, [whole(pos), whole(n2), (gpre, (n, f), lambda i: (0, i))],
        [whole_out(dims, BF16)] * 2, [], 5, "up_weights",
    )


def row_weights(sz, pos, left, right, name):
    n, k, d = sz.n, left.shape[1], sz.d
    dims = (NS, 2, k // NS, LANE)
    return call(
        row_weight_kernel, NB, [whole(pos), (left, (n, k // NB), lambda i: (0, i)), whole(right)],
        [whole_out(dims, BF16)] * 2, [], 5, name,
    )


def gate_weights(sz, pos, normed, dzf, dzi, dzc, vectors):
    n, d, h, w = sz.n, sz.d, sz.h, sz.hb
    col = lambda i: (0, i)
    rows = 3 * d * h // (32 * LANE) + (16 if vectors else 0)
    return call(
        functools.partial(gate_weight_kernel, bool(vectors)), NB,
        [whole(pos), whole(normed), (dzf, (n, w), col), (dzi, (n, w), col), (dzc, (n, w), col)]
        + [whole(v) for v in vectors],
        [whole_out((NS, 2, rows, LANE), BF16)] * 2,
        [pltpu.VMEM((NS, 16, LANE), F32)] if vectors else [], 0, "gate_weights",
    )


def swap(array, axes, bits):
    count = lax.axis_size(axes)
    return lax.ppermute(array, axes, [(i, i ^ bits) for i in range(count)])


BOTH = ("seq", "batch")


def after(array, *others):
    return lax.optimization_barrier((array,) + others)[0]


def sum_cut(rows):
    total = sum(rows)
    if len(rows) == 1:
        return total // 2 // 16 * 16
    return rows[0] if rows[0] * 5 >= total * 2 else rows[0] + rows[1]


def by_line(a):
    return (a, (1,) + a.shape[1:], lambda i: (i,) + (0,) * (len(a.shape) - 1))


def by_line_out(*dims):
    return (shape(dims, BF16), (1,) + dims[1:], lambda i: (i,) + (0,) * (len(dims) - 1))


def core_exchange(pairs):
    return [(keep, swap(send, "batch", 1)) for keep, send in pairs]


def pair_sum(pos, pairs):
    rows = tuple(keep.shape[2] for keep, _ in pairs)
    cut, total = sum_cut(rows), sum(rows)
    view = lambda a: by_line(a.reshape((4, 2, 2) + a.shape[2:]))
    two = [by_line_out(4, 2, cut, LANE)] * 2 + [by_line_out(4, 2, total - cut, LANE)] * 2
    return call(
        functools.partial(pair_sum_kernel, rows, cut), 4,
        [whole(pos)] + [view(keep) for keep, _ in pairs] + [view(got) for _, got in pairs], two, [], 0, "pair_sum",
    )


def plane_exchange(parts, first, second):
    send_a, keep_a, send_b, keep_b = parts
    return keep_a, swap(send_a, *first), keep_b, swap(send_b, *second)


X_AXIS, Y_AXIS = ("batch", 2), ("seq", 1)


def plane_sum(pos, parts):
    cut, rest = parts[0].shape[2], parts[2].shape[2]
    one = [by_line_out(4, cut, LANE)] * 2 + [by_line_out(4, rest, LANE)] * 2
    return call(plane_sum_kernel, 4, [whole(pos)] + [by_line(a) for a in parts], one, [], 0, "plane_sum")


def line_sum(pos, parts):
    total = parts[0].shape[1] + parts[2].shape[1]
    return call(
        line_sum_kernel, 1, [whole(pos)] + [whole(a) for a in parts], [whole_out((total, LANE), BF16)] * 4, [], 0, "line_sum",
    )


def line_exchange(parts):
    return [parts[0]] + [swap(part, "seq", 2 * (k + 1)) for k, part in enumerate(parts[1:])]


def reduce_rest(pos, parts):
    parts = plane_sum(pos, plane_exchange(parts, X_AXIS, Y_AXIS))
    return line_exchange(line_sum(pos, plane_exchange(parts, Y_AXIS, X_AXIS)))


def line_parts(own):
    return [own] + [swap(own, "seq", 2 * k) for k in range(1, 4)]


def line_gather(pos, parts, rows):
    return call(
        line_gather_kernel, 1, [whole(pos)] + [whole(far(p)) for p in parts],
        [whole_out((4, r, LANE), BF16) for r in rows], [], 2, "line_gather",
    )


def plane_parts(line, direct):
    from_x, from_y = swap(line, *X_AXIS), swap(line, *Y_AXIS)
    if direct:
        return [from_x, from_y, swap(line, BOTH, 6)]
    return [from_x, from_y, swap(from_x[:2], *Y_AXIS), swap(from_y[2:], *X_AXIS)]


def plane_gather(pos, line, parts, behind=()):
    rows = line.shape[1]
    parts = [line, *parts]
    parts += [swap(after(p, *behind) if behind else p, "batch", 1) for p in parts]
    maps = [lambda i: (i, 0, 0)] * 3
    maps += maps[:1] if len(parts) == 8 else [lambda i: (jnp.minimum(i, 1), 0, 0), lambda i: (jnp.maximum(i - 2, 0), 0, 0)]
    got = call(
        plane_gather_kernel, 4, [whole(pos)] + [(far(p), (1, rows, LANE), m) for p, m in zip(parts, maps * 2)],
        [(shape((4, 2, 2, 2, rows, LANE), BF16), (1, 2, 2, 2, rows, LANE), lambda i: (i, 0, 0, 0, 0, 0))], [], 5, "plane_gather",
    )
    return got.reshape(NS, NB, rows, LANE)


def enter(fin, seqs, backward, fill=(), hold=None):
    count, mine = lax.axis_size("seq"), lax.axis_index("seq")
    prod, state = fin[:seqs], fin[seqs:]
    pre_p, pre_s = jnp.ones_like(prod), jnp.zeros_like(state)
    bit, message, done = 1, fin, []
    for step in range(int(count).bit_length() - 1):
        if hold and step in hold:
            message = after(message, *hold[step])
        other = lax.ppermute(message, "seq", [(i, i ^ bit) for i in range(count)])
        if step < len(fill):
            done.append(fill[step](message))
        o_p, o_s = other[:seqs], other[seqs:]
        upper = ((mine // bit) % 2 == 1) ^ backward
        pre_p, pre_s = jnp.where(upper, o_p * pre_p, pre_p), jnp.where(upper, pre_p * o_s + pre_s, pre_s)
        state = jnp.where(upper, prod * o_s + state, o_p * state + o_s)
        prod = prod * o_p
        message = jnp.concatenate([prod, state])
        if step < len(fill):
            message = after(message, *done[-1])
        bit *= 2
    return pre_s, done


def slabs(matrix, seq_count, batch_count):
    rows, cols = matrix.shape[0] // NS, matrix.shape[1] // NB
    cut = matrix.reshape(NS, rows, NB, cols // LANE, LANE).transpose(0, 2, 3, 1, 4)
    return cut.reshape(NS, NB, rows * cols // LANE, LANE)


def unslab(blocks, rows, cols):
    r, c = rows // NS, cols // NB
    cut = blocks.reshape(NS, NB, c // LANE, r, LANE).transpose(0, 3, 1, 2, 4)
    return cut.reshape(rows, cols)


def body(
    tokens, norm_gain, w_forget, w_input, w_cand, forget_bias, input_bias, w_out, mlp_gain, w_up, w_down, cotangent
):
    seqs, length, d = tokens.shape
    seq_count, batch_count = lax.axis_size("seq"), lax.axis_size("batch")
    h, ff = w_forget.shape[2] * batch_count, w_up.shape[2] * batch_count
    sz = Sizes(seqs, length, d, h, ff)
    standard = (seq_count, batch_count) == (NS, NB)
    matrices = {"u": w_up, "d": w_down, "o": w_out, "f": w_forget, "i": w_input, "c": w_cand}
    vectors = (norm_gain, forget_bias, input_bias, mlp_gain)
    slab_rows = {"u": d * ff // (32 * LANE), "d": ff // NS, "o": h // NS}
    slab_rows.update({m: d * h // (32 * LANE) for m in "fic"})
    order = {name: k for k, name in enumerate(matrices)}

    if standard:
        s_at, b_at = lax.axis_index("seq"), lax.axis_index("batch")
        pos = jnp.stack([b_at % 2, b_at // 2, s_at % 2, s_at // 2]).astype(jnp.int32)
        vecs = [(6 + k, at, True) for at in range(LAYERS) for k in range(4)]
        groups = [[(order[m], 0, False) for m in "fic"] + vecs, [(order[m], 0, False) for m in "udo"]]
        groups += [[(order[m], l, False) for m in "ficudo"] for l in range(1, LAYERS)]
        rows = [sum(slab_rows["udofic"[which]] for which, _, vec in g if not vec) for g in groups]
        rows[0] += 16
        packs = call(
            functools.partial(pack_kernel, groups), 1,
            [whole(far(m)) for m in matrices.values()] + [whole(far(v)) for v in vectors],
            [whole_out((r, LANE), BF16) for r in rows], [pltpu.VMEM((16, LANE), F32)], 2, "pack",
        )
        line_g0 = line_gather(pos, line_parts(packs[0]), rows[:1])
        parts_g0 = plane_parts(line_g0, False)
        line_r0 = line_gather(pos, line_parts(after(packs[1], line_g0)), rows[1:2])
        parts_r0 = plane_parts(after(line_r0, *parts_g0[:2]), False)
        lines = line_gather(pos, line_parts(after(packs[2], line_r0)), (rows[2] - rows[1], rows[1]))
        got = [plane_gather(pos, line_g0, parts_g0), plane_gather(pos, line_r0, parts_r0)]
        places = {"f": 0, "i": 1, "c": 2, "u": 0, "d": 1, "o": 4}
        view = lambda got: {m: (got[m in "udo"], slab_rows[m], places[m]) for m in "udofic"}
        weights = [view(got)]
        vecs = call(
            functools.partial(vector_kernel, None), 1,
            [(got[0], (NS, 1, 16, LANE), lambda i: (0, 0, 3 * slab_rows["f"] // 16, 0))],
            [whole_out((2, size)) for l in range(LAYERS) for size in (d, h)],
            [pltpu.VMEM((NS, 16, LANE), F32)], 1, "vectors",
        )
        gains, biases = vecs[0::2], vecs[1::2]
    else:
        pos = jnp.zeros((4,), jnp.int32)

        def full(m):
            m = lax.all_gather(m, "batch", axis=1, tiled=True)
            return lax.all_gather(m, "seq", axis=0, tiled=True)

        weights = [
            {m: (slabs(full(matrices[m][l]), NS, NB), slab_rows[m], 0) for m in "udofic"} for l in range(LAYERS)
        ]
        whole_vectors = [lax.all_gather(v, "seq", axis=1, tiled=True).astype(F32) for v in vectors]
        gains = [jnp.stack([whole_vectors[0][l], whole_vectors[3][l]]) for l in range(LAYERS)]
        biases = [jnp.stack([whole_vectors[1][l], whole_vectors[2][l]]) for l in range(LAYERS)]

    def to_rows(v):
        return v.reshape(seqs, CHUNKS, sz.steps, d).transpose(0, 2, 1, 3).reshape(sz.n, d)

    def from_rows(v):
        return v.reshape(seqs, sz.steps, CHUNKS, d).transpose(0, 2, 1, 3).reshape(seqs, length, d)

    stream, grad = to_rows(tokens), to_rows(cotangent)
    kept = []
    for l in range(LAYERS):
        save = (True,) if l + 1 < LAYERS else ()
        normed, decay, inflow, cand, f_f, f_i, f_c, cp, ch, fin = gate_forward(
            sz, stream, gains[l], biases[l], weights[l], (True,)
        )
        if standard and l + 1 < LAYERS:
            ent, _ = enter(fin, seqs, False, (), {1: lines[:1], 2: parts_r0[2:]})
        else:
            ent, _ = enter(fin, seqs, False, (), {1: parts_r1[:2]} if standard and l else None)
        hidden, hb, e, mid, n2, act, slope, result = mix_forward(
            sz, stream, gains[l], decay, inflow, cp, ch, ent, weights[l], l == LAYERS - 1, save
        )
        if standard and l + 1 < LAYERS:
            line_g1, line_r1 = lines
            parts_g1 = plane_parts(after(line_g1, *parts_r0[2:]), True)
            parts_r1 = plane_parts(after(line_r1, *parts_g1), False)
            got = [plane_gather(pos, line_g1, parts_g1, (result,)), plane_gather(pos, line_r1, parts_r1)]
            weights.append(view(got))
        kept.append((stream, normed, decay, cand, f_f, f_i, f_c, hidden, hb, e, mid, n2, act, slope))
        stream = result
    output = from_rows(stream)

    vector_grads, sums, pending = [None] * LAYERS, [], []
    waiting, held = None, []
    for l in reversed(range(LAYERS)):
        x, normed, decay, cand, f_f, f_i, f_c, hidden, hb, e, mid, n2, act, slope = kept[l]
        place = far if l + 1 < LAYERS else lambda a: a
        decay, cand, f_f, f_i, f_c, hidden = map(far, (decay, cand, f_f, f_i, f_c, hidden))
        mid, slope = place(mid), place(slope)
        gr, gpre, gmid, go, ggain_two, gh, cp, ca, fin = mlp_backward(sz, grad, gains[l], mid, slope, decay, weights[l])
        def up(message):
            return up_weights(sz, pos, place(after(n2, message)), gpre)

        def down(message):
            left = after(act, message)
            if waiting:
                names, parts = waiting
                parts = line_sum(pos, [after(parts[0], message), *parts[1:]])
                left = after(left, parts[0])
                waiting[1] = line_exchange(parts)
            return row_weights(sz, pos, place(left), gr, "down_weights")

        def out(message):
            return row_weights(sz, pos, place(after(hb, message)), go, "out_weights")

        ent, pairs = enter(fin, seqs, True, (up, down, out))
        if standard:
            names = [(l, m) for m in "udo"] + (held[0] if held else [])
            early = pair_sum(pos, core_exchange(pairs) + held[1:])
            gmid = after(gmid, early[0])
        dzf, dzi, dzc, gbias, grad, ggain_one = gate_backward(
            sz, x, gains[l], gmid, gh, decay, hidden, e, cand, f_f, f_i, f_c, cp, ca, ent, weights[l], l == 0
        )
        vector_grads[l] = (ggain_one, gbias, ggain_two)
        final = [v for each in vector_grads for v in each] if l == 0 and standard else []
        gate_pair = gate_weights(sz, pos, far(normed), dzf, dzi, dzc, final)
        if not standard:
            pending.append((l, pairs + [gate_pair]))
            continue
        parts = list(plane_exchange(early, X_AXIS, Y_AXIS))
        parts[0] = after(parts[0], gate_pair[0])
        parts = plane_sum(pos, parts)
        if l > 0:
            held = [[(l, m) for m in "fic"]] + core_exchange([gate_pair])
            grad = after(grad, parts[0])
            waiting = [names, plane_exchange(parts, Y_AXIS, X_AXIS)]
        else:
            done = parts[0]
            if waiting:
                names_1, parts_1 = waiting
                parts_1[0] = after(parts_1[0], gate_pair[0])
                done = call(line_total_kernel, 1, [whole(p) for p in parts_1], [whole_out(parts_1[0].shape)], [], 0, "line_total")
                sums.append((names_1, [done]))
            late = pair_sum(pos, core_exchange([(gate_pair[0], after(gate_pair[1], parts[0], done))]))
            sums.append((names, line_exchange(line_sum(pos, plane_exchange(parts, Y_AXIS, X_AXIS)))))
            sums.append(([(l, m) for m in "fic"] + [(at, k) for at in range(LAYERS) for k in range(4)], reduce_rest(pos, late)))
    grad_tokens = from_rows(grad)

    if standard:
        layout, ins = [], []
        for names, parts in sums:
            pieces = [(order[m], l, False) if m in order else (6 + m, l, True) for l, m in names]
            layout.append((len(parts), pieces))
            ins += [whole(p) for p in parts]
        found = call(
            functools.partial(finish_kernel, layout), 1, ins,
            [whole_out(m.shape) for m in matrices.values()] + [whole_out(v.shape) for v in vectors], [], 3, "finish",
        )
        g_up, g_down, g_out, g_f, g_i, g_c, g_norm, g_fb, g_ib, g_mlp = found
    else:
        per_layer = {}
        for l, pairs in pending:
            blocks = [jnp.stack([keep, send], axis=2).reshape(NS, NB, -1, LANE) for keep, send in pairs]
            gates = jnp.split(blocks[3], 3, axis=2)
            for m, g in zip("udofic", blocks[:3] + gates):
                v = unslab(g, matrices[m].shape[1] * seq_count, matrices[m].shape[2] * batch_count)
                v = lax.psum_scatter(v, "seq", scatter_dimension=0, tiled=True)
                per_layer[m, l] = lax.psum_scatter(v, "batch", scatter_dimension=1, tiled=True).astype(F32)
        g_up, g_down, g_out, g_f, g_i, g_c = [
            jnp.stack([per_layer[m, l] for l in range(LAYERS)]) for m in matrices
        ]
        rows = [
            (ggain_one[0], gbias[0], gbias[1], ggain_two[0]) for ggain_one, gbias, ggain_two in vector_grads
        ]
        g_norm, g_fb, g_ib, g_mlp = [
            lax.psum(lax.psum_scatter(jnp.stack([r[k] for r in rows]), "seq", scatter_dimension=1, tiled=True), "batch")
            for k in range(4)
        ]
    return output, grad_tokens, g_norm, g_f, g_i, g_c, g_fb, g_ib, g_out, g_mlp, g_up, g_down


def solution(mesh):
    split, vector, matrix = P("batch", "seq", None), P(None, "seq"), P(None, "seq", "batch")
    order = (vector, matrix, matrix, matrix, vector, vector, matrix, vector, matrix, matrix)
    return jax.shard_map(
        body,
        mesh=mesh,
        in_specs=(split,) + order + (split,),
        out_specs=(split, split) + order,
        check_vma=False,
    )
```

```python
import functools

import jax
import jax.numpy as jnp
from jax import lax
from jax.experimental import pallas as pl
from jax.experimental.pallas import tpu as pltpu
from jax.sharding import PartitionSpec as P

LAYERS = 2
EPS = 1e-05
NS, NB, LANE = 8, 4, 128
CHUNKS = 8
STEPS = 2
GATE_STEPS = 4
TURN, WIDE = 2, 256
VMEM = 28 * 1024 * 1024
F32, BF16 = jnp.float32, jnp.bfloat16


def dot(left, right):
    return lax.dot_general(left, right, (((1,), (0,)), ((), ())), preferred_element_type=F32)


def dot_nt(left, right):
    return lax.dot_general(left, right, (((1,), (1,)), ((), ())), preferred_element_type=F32)


def dot_tn(left, right):
    return lax.dot_general(left, right, (((0,), (0,)), ((), ())), preferred_element_type=F32)


def columns_of(ref, slabs=2):
    rows = ref.shape[2] // slabs
    parts = [
        ref[:, b, j * rows : (j + 1) * rows, :].reshape(NS * rows, LANE) for b in range(ref.shape[1]) for j in range(slabs)
    ]
    return jnp.concatenate(parts, axis=1)


def rows_of(ref):
    parts = [ref[:, j].reshape(-1, LANE) for j in range(NB)]
    return jnp.concatenate(parts, axis=1)


def rms_scale(values):
    return lax.rsqrt(jnp.mean(values * values, axis=-1, keepdims=True) + EPS)


def rms_back(values, gain, grad):
    scale = rms_scale(values)
    unit = values * scale
    inner = grad * gain
    back = scale * (inner - unit * jnp.mean(inner * unit, axis=-1, keepdims=True))
    return back, jnp.sum(grad * unit, axis=0, keepdims=True)


def gate_kernel(
    seqs, steps, x_ref, gain_ref, bias_ref, wf_ref, wi_ref, wc_ref,
    normed_ref, decay_ref, inflow_ref, cand_ref, ff_ref, fi_ref, fc_ref, cp_ref, ch_ref, fin_ref,
    z,
):
    width = decay_ref.shape[1]

    @pl.when(pl.program_id(0) == 0)
    def _():
        x = x_ref[...].astype(F32)
        normed_ref[...] = (x * rms_scale(x) * gain_ref[0:1, :]).astype(BF16)

    weights = jnp.concatenate([columns_of(ref) for ref in (wf_ref, wi_ref, wc_ref)], axis=1)
    block = TURN * CHUNKS
    places = [(seq, left) for seq in range(seqs) for left in range(0, width, WIDE)]

    def turn(of, at, carry):
        carry = list(carry)
        for k, (seq, left) in enumerate(places):
            if seq != of:
                continue
            span = slice(seq * steps * CHUNKS + at * block, seq * steps * CHUNKS + (at + 1) * block)
            cols = slice(left, left + WIDE)
            f = z[span, cols] + bias_ref[0:1, cols]
            i = z[span, width + left : width + left + WIDE] + bias_ref[1:2, cols]
            c = z[span, 2 * width + left : 2 * width + left + WIDE]
            low = jnp.minimum(jnp.minimum(f, i), 0.0)
            e0, ef, ei = jnp.exp(low), jnp.exp(low - f), jnp.exp(low - i)
            a, b = e0 + ef, e0 + ei
            inv = 1.0 / (a + b)
            decay, other = b * inv, a * inv
            ec = jnp.exp(-jnp.abs(c))
            cand = jnp.maximum(c, 0.0) + jnp.log1p(ec)
            slope = jnp.where(c >= 0.0, 1.0, ec) / (1.0 + ec)
            inflow = other * cand
            decay_ref[span, cols] = decay
            inflow_ref[span, cols] = inflow
            cand_ref[span, cols] = cand
            ff_ref[span, cols] = (ef * inv * decay).astype(BF16)
            fi_ref[span, cols] = (ei * inv * other).astype(BF16)
            fc_ref[span, cols] = (other * slope).astype(BF16)
            prod, state = carry[2 * k], carry[2 * k + 1]
            for t in range(TURN):
                d = decay[t * CHUNKS : (t + 1) * CHUNKS]
                prod = prod * d
                state = state * d + inflow[t * CHUNKS : (t + 1) * CHUNKS]
            carry[2 * k], carry[2 * k + 1] = prod, state
        return tuple(carry)

    one, zero = jnp.ones((CHUNKS, WIDE), F32), jnp.zeros((CHUNKS, WIDE), F32)
    carry = (one, zero) * len(places)
    for seq in range(seqs):
        rows = slice(seq * steps * CHUNKS, (seq + 1) * steps * CHUNKS)
        z[rows, :] = dot(normed_ref[rows, :], weights)
        for at in range(steps // TURN):
            carry = turn(seq, at, carry)
    for k, (seq, left) in enumerate(places):
        prod, state = carry[2 * k], carry[2 * k + 1]
        cols = slice(left, left + WIDE)
        cp_ref[seq, :, cols], ch_ref[seq, :, cols] = prod, state
        whole, last = prod[0:1], state[0:1]
        for c in range(1, CHUNKS):
            whole, last = whole * prod[c : c + 1], last * prod[c : c + 1] + state[c : c + 1]
        fin_ref[seq : seq + 1, cols] = whole
        fin_ref[seqs + seq : seqs + seq + 1, cols] = last


def mix_kernel(
    seqs, steps, x_ref, gain_ref, decay_ref, inflow_ref, cp_ref, ch_ref, ent_ref, wo_ref, wu_ref, wd_ref,
    hidden_ref, hb_ref, e_ref, mid_ref, n2_ref, act_ref, slope_ref, out_ref,
    acc,
):
    at_step = pl.program_id(0)
    block = TURN * CHUNKS
    width = decay_ref.shape[1]
    places = [(seq, left) for seq in range(seqs) for left in range(0, width, WIDE)]

    @pl.when(at_step == 0)
    def _():
        acc[...] = x_ref[...].astype(F32)

    @pl.when(at_step < STEPS)
    def _():
        for seq in range(seqs):
            state = ent_ref[seq : seq + 1, :]
            for c in range(CHUNKS):
                e_ref[seq, c : c + 1, :] = state
                state = state * cp_ref[seq, c : c + 1, :] + ch_ref[seq, c : c + 1, :]

        def turn(at, carry):
            carry = list(carry)
            for k, (seq, left) in enumerate(places):
                span = pl.ds(pl.multiple_of(seq * steps * CHUNKS + at * block, block), block)
                cols = slice(left, left + WIDE)
                d, u = decay_ref[span, cols], inflow_ref[span, cols]
                state, found = carry[k], []
                for t in range(TURN):
                    state = state * d[t * CHUNKS : (t + 1) * CHUNKS] + u[t * CHUNKS : (t + 1) * CHUNKS]
                    found.append(state)
                carry[k] = state
                hidden = jnp.concatenate(found, axis=0)
                hidden_ref[span, cols] = hidden
                hb_ref[span, cols] = hidden.astype(BF16)
            return tuple(carry)

        lax.fori_loop(0, steps // TURN, turn, tuple(e_ref[seq, :, left : left + WIDE] for seq, left in places))
        acc[...] += dot(hb_ref[...], rows_of(wo_ref))

    @pl.when(at_step == STEPS - 1)
    def _():
        middle = acc[...]
        mid_ref[...] = middle
        n2_ref[...] = (middle * rms_scale(middle) * gain_ref[1:2, :]).astype(BF16)

    @pl.when(at_step >= STEPS)
    def _():
        w_up, w_down = columns_of(wu_ref, 4), rows_of(wd_ref)
        size = acc.shape[0] // 2
        for k in range(2):
            span = slice(k * size, (k + 1) * size)
            v = dot(n2_ref[span, :], w_up)
            phi = 0.5 + 0.5 * lax.erf(v * 0.7071067811865476)
            act = (v * phi).astype(BF16)
            act_ref[span, :] = act
            slope_ref[span, :] = (phi + v * (0.3989422804014327 * jnp.exp(v * v * -0.5))).astype(BF16)
            acc[span, :] += dot(act, w_down)

    @pl.when(at_step == 2 * STEPS - 1)
    def _():
        out_ref[...] = acc[...].astype(out_ref.dtype)


def mlp_back_kernel(
    seqs, steps, g_ref, gain_ref, mid_ref, slope_ref, decay_ref, wo_ref, wu_ref, wd_ref,
    gr_ref, gpre_ref, gmid_ref, go_ref, ggain_ref, gh_ref, cp_ref, ca_ref, fin_ref,
    acc,
):
    at_step = pl.program_id(0)
    block = TURN * CHUNKS
    width = decay_ref.shape[1]
    places = [(seq, left) for seq in range(seqs) for left in range(0, width, WIDE)]

    @pl.when(at_step == 0)
    def _():
        gr_ref[...] = g_ref[...].astype(BF16)
        acc[...] = jnp.zeros_like(acc)

    @pl.when(at_step < STEPS)
    def _():
        gact = dot_nt(gr_ref[...], rows_of(wd_ref))
        gpre_ref[...] = (gact * slope_ref[...].astype(F32)).astype(BF16)
        acc[...] += dot_nt(gpre_ref[...], columns_of(wu_ref, 4))

    @pl.when(at_step == STEPS - 1)
    def _():
        back, ggain = rms_back(mid_ref[...], gain_ref[1:2, :], acc[...])
        ggain_ref[...] = ggain
        gmid = g_ref[...].astype(F32) + back
        gmid_ref[...] = gmid
        go_ref[...] = gmid.astype(BF16)

    @pl.when(at_step >= STEPS)
    def _():
        gh_ref[...] = dot_nt(go_ref[...], rows_of(wo_ref))

        def turn(turn_at, carry):
            at = steps // TURN - 1 - turn_at
            carry = list(carry)
            for k, (seq, left) in enumerate(places):
                span = pl.ds(pl.multiple_of(seq * steps * CHUNKS + at * block, block), block)
                cols = slice(left, left + WIDE)
                d, g = decay_ref[span, cols], gh_ref[span, cols]
                prod, state = carry[2 * k], carry[2 * k + 1]
                for t in reversed(range(TURN)):
                    dk = d[t * CHUNKS : (t + 1) * CHUNKS]
                    prod = prod * dk
                    state = dk * (g[t * CHUNKS : (t + 1) * CHUNKS] + state)
                carry[2 * k], carry[2 * k + 1] = prod, state
            return tuple(carry)

        one, zero = jnp.ones((CHUNKS, WIDE), F32), jnp.zeros((CHUNKS, WIDE), F32)
        carry = lax.fori_loop(0, steps // TURN, turn, (one, zero) * len(places))
        for k, (seq, left) in enumerate(places):
            prod, state = carry[2 * k], carry[2 * k + 1]
            cols = slice(left, left + WIDE)
            cp_ref[seq, :, cols], ca_ref[seq, :, cols] = prod, state
            whole, last = prod[CHUNKS - 1 :], state[CHUNKS - 1 :]
            for c in reversed(range(CHUNKS - 1)):
                whole, last = whole * prod[c : c + 1], last * prod[c : c + 1] + state[c : c + 1]
            fin_ref[seq : seq + 1, cols] = whole
            fin_ref[seqs + seq : seqs + seq + 1, cols] = last


def gate_back_kernel(
    seqs, steps, others, pos_ref, x_ref, gain_ref, gmid_ref, gh_ref, decay_ref, hidden_ref, e_ref, cand_ref,
    ff_ref, fi_ref, fc_ref, cp_ref, ca_ref, ent_ref, normed_ref, wf_ref, wi_ref, wc_ref, *refs,
):
    given = refs[: len(others)]
    keep_ref, send_ref, gbias_ref, gstream_ref, ggain_ref, acc, start, dz, rest = refs[len(others) :]
    at_step = pl.program_id(0)
    block = TURN * CHUNKS
    width = decay_ref.shape[1]
    places = [(seq, left) for seq in range(seqs) for left in range(0, width, WIDE)]

    @pl.when(at_step == 0)
    def _():
        acc[...] = jnp.zeros_like(acc)

    for seq in range(seqs):
        state = ent_ref[seq : seq + 1, :]
        for c in reversed(range(CHUNKS)):
            start[seq, c : c + 1, :] = state
            state = state * cp_ref[seq, c : c + 1, :] + ca_ref[seq, c : c + 1, :]

    def turn(of, at, carry):
        carry = list(carry)
        for k, (seq, left) in enumerate(places):
            if seq != of:
                continue
            cols = slice(left, left + WIDE)
            state, sum_f, sum_i = carry[3 * k : 3 * k + 3]
            base = seq * steps * CHUNKS + at * block
            span = slice(base, base + block)
            before = hidden_ref[base - CHUNKS : base, cols] if at else e_ref[seq, :, cols]
            d, g = decay_ref[span, cols], gh_ref[span, cols]
            previous = jnp.concatenate([before, hidden_ref[span, cols][: block - CHUNKS]], axis=0)
            found = []
            for t in reversed(range(TURN)):
                now = g[t * CHUNKS : (t + 1) * CHUNKS] + state
                found.append(now)
                state = d[t * CHUNKS : (t + 1) * CHUNKS] * now
            gstate = jnp.concatenate(found[::-1], axis=0)
            both = gstate * (cand_ref[span, cols] - previous)
            dzf = (-ff_ref[span, cols].astype(F32) * both).astype(BF16)
            dzi = (fi_ref[span, cols].astype(F32) * both).astype(BF16)
            dz[span, left : left + WIDE] = dzf
            dz[span, width + left : width + left + WIDE] = dzi
            dz[span, 2 * width + left : 2 * width + left + WIDE] = (fc_ref[span, cols].astype(F32) * gstate).astype(BF16)
            wide_f, wide_i = dzf.astype(F32), dzi.astype(F32)
            for t in range(TURN):
                sum_f = sum_f + wide_f[t * CHUNKS : (t + 1) * CHUNKS]
                sum_i = sum_i + wide_i[t * CHUNKS : (t + 1) * CHUNKS]
            carry[3 * k : 3 * k + 3] = state, sum_f, sum_i
        return tuple(carry)

    zero = jnp.zeros((CHUNKS, WIDE), F32)
    first_carry = [v for seq, left in places for v in (start[seq, :, left : left + WIDE], zero, zero)]
    carry = tuple(first_carry)
    weights = jnp.concatenate([columns_of(ref) for ref in (wf_ref, wi_ref, wc_ref)], axis=1)
    grad = None
    for seq in range(seqs):
        rows = slice(seq * steps * CHUNKS, (seq + 1) * steps * CHUNKS)
        for at in reversed(range(steps // TURN)):
            carry = turn(seq, at, carry)
        acc[rows, :] += dot_nt(dz[rows, :], weights)
        part = dot_tn(normed_ref[rows, :], dz[rows, :])
        grad = part if grad is None else grad + part
    for row in range(2):
        for left in range(0, width, WIDE):
            total = sum(carry[3 * k + 1 + row] for k, place in enumerate(places) if place[1] == left)
            gbias_ref[row : row + 1, left : left + WIDE] = jnp.sum(total, axis=0, keepdims=True)
    rows = wf_ref.shape[2]
    for m in range(3):
        put_columns(pos_ref, keep_ref, send_ref, m * rows, grad[:, m * width : (m + 1) * width])

    @pl.when(at_step == STEPS - 1)
    def _():
        back, ggain = rms_back(x_ref[...].astype(F32), gain_ref[0:1, :], acc[...])
        ggain_ref[...] = ggain
        gstream_ref[...] = (gmid_ref[...] + back).astype(gstream_ref.dtype)

    if others:

        def rows_to(ref, first_row):
            wide = ref.shape[1] // NS
            for r in range(ref.shape[0]):
                for s in range(NS):
                    rest[s, first_row + r : first_row + r + 1, :wide] = ref[r : r + 1, s * wide : (s + 1) * wide]

        @pl.when(at_step == 0)
        def _():
            rest[...] = jnp.zeros_like(rest)
            for ref, first_row in zip(given, others):
                rows_to(ref, first_row)

        wide = width * STEPS // NS
        for row in range(2):
            for s in range(width // wide):
                rest[at_step * (width // wide) + s, 1 + row : 2 + row, :wide] = gbias_ref[row : row + 1, s * wide : (s + 1) * wide]

        @pl.when(at_step == STEPS - 1)
        def _():
            rows_to(ggain_ref, 0)
            found = rest[...].astype(BF16)
            for x in range(2):
                keep_ref[:, x, 3 * rows :, :] = found
                send_ref[:, x, 3 * rows :, :] = found


def send_or_keep(mine, keep_ref, send_ref, put):
    @pl.when(mine)
    def _():
        put(keep_ref)

    @pl.when(jnp.logical_not(mine))
    def _():
        put(send_ref)


def put_columns(pos_ref, keep_ref, send_ref, start, value):
    rows, width = value.shape[0] // NS, value.shape[1] // 2
    x = pl.program_id(0)
    for core in range(2):
        parts = [
            value[:, left : left + LANE].astype(BF16).reshape(NS, rows, LANE)
            for left in range(core * width, (core + 1) * width, LANE)
        ]

        def put(ref):
            for j, part in enumerate(parts):
                ref[:, x, start + j * rows : start + (j + 1) * rows, :] = part

        send_or_keep(pos_ref[0] == core, keep_ref, send_ref, put)


def put_rows(pos_ref, keep_ref, send_ref, value):
    count = NS // STEPS
    for j in range(NB):
        part = value[:, j * LANE : (j + 1) * LANE].astype(BF16).reshape(count, -1, LANE)

        def put(ref):
            ref[pl.ds(pl.program_id(0) * count, count), j // 2] = part

        send_or_keep(pos_ref[0] == j % 2, keep_ref, send_ref, put)


def up_weight_kernel(pos_ref, n2_ref, gpre_ref, keep_ref, send_ref):
    put_columns(pos_ref, keep_ref, send_ref, 0, dot_tn(n2_ref[...], gpre_ref[...]))


def row_weight_kernel(pos_ref, left_ref, right_ref, keep_ref, send_ref):
    put_rows(pos_ref, keep_ref, send_ref, dot_tn(left_ref[...], right_ref[...]))


def add(*parts):
    total = parts[0].astype(F32)
    for part in parts[1:]:
        total = total + part.astype(F32)
    return total


def pair_sum_kernel(rows, pos_ref, *refs):
    count = len(rows)
    send, stay = refs[2 * count :]
    core, x, y, step = pos_ref[0], pos_ref[1], pos_ref[2], pos_ref[4]
    at = 0
    for keep, got, r in zip(refs[:count], refs[count : 2 * count], rows):
        for v in range(2):
            for out, first in ((send, 1 - step), (stay, step)):
                iy, ix = jnp.where(core == 0, v, first), jnp.where(core == 0, first, v)
                out[0, v, at : at + r] = add(keep[0, iy, ix], got[0, iy, ix]).astype(BF16)
        at += r


def plane_sum_kernel(pos_ref, keep, got, send, stay):
    second = pos_ref[5]
    send[0] = add(keep[0, 1 - second], got[0, 1 - second]).astype(BF16)
    stay[0] = add(keep[0, second], got[0, second]).astype(BF16)


def line_sum_kernel(pos_ref, keep, got, send, stay):
    core, first = pos_ref[0], pos_ref[6]
    for v in range(2):
        for out, f in ((send, 1 - first), (stay, first)):
            z = jnp.where(core == 0, f + 2 * v, 2 * f + v)
            out[v] = add(keep[z], got[z]).astype(BF16)


def last_sum_kernel(pos_ref, keep, got, send, stay):
    second = pos_ref[7]
    send[...] = add(keep[1 - second], got[1 - second]).astype(BF16)
    stay[...] = add(keep[second], got[second]).astype(BF16)


def total_kernel(keep, got, out):
    out[...] = add(keep[...], got[...])


def finish_kernel(layout, *refs):
    at = 0
    ins = sum(parts for parts, _ in layout)
    outs = refs[ins:]
    for parts, pieces in layout:
        got = refs[at : at + parts]
        at += parts
        row = 0
        for out, layer, vectors in pieces:
            ref = outs[out]
            if vectors:
                ref[layer : layer + 1, :] = add(*[g[...] for g in got])[row : row + 1, : ref.shape[1]]
                row += 1
                continue
            r = ref.shape[1]
            for j in range(ref.shape[2] // LANE):
                ref[layer, :, j * LANE : (j + 1) * LANE] = add(*[g[row : row + r] for g in got])
                row += r


def pack_kernel(groups, *refs):
    ins = refs[: len(refs) - len(groups) - 1]
    outs, scratch = refs[len(ins) : -1], refs[-1]
    for out, group in zip(outs, groups):
        row = 0
        vec = 0
        for which, layer, vector in group:
            ref = ins[which]
            if vector:
                if vec == 0:
                    scratch[...] = jnp.zeros_like(scratch)
                scratch[vec : vec + 1, : ref.shape[1]] = ref[...].astype(F32)[layer : layer + 1]
                vec += 1
                continue
            r = ref.shape[1]
            for j in range(ref.shape[2] // LANE):
                out[row : row + r, :] = ref[layer, :, j * LANE : (j + 1) * LANE]
                row += r
        if vec:
            out[row:, :] = scratch[...].astype(BF16)


def line_gather_kernel(pos_ref, *refs):
    row = 0
    for out in refs[4:]:
        rows = out.shape[1]
        for k, part in enumerate(refs[:4]):
            out[pos_ref[3] ^ k] = part[row : row + rows, :]
        row += rows


def plane_gather_kernel(pos_ref, *refs):
    out = refs[-1]
    at, half = pl.program_id(0), pl.num_programs(0) // 2
    core, x, y = pos_ref[0], pos_ref[1], pos_ref[2]
    count = len(refs) // 2
    for c in range(2):
        own, first, second, *diagonal = refs[count * c : count * (c + 1)]
        other = core ^ c
        turn = other if count == 4 else 0
        out[0, y, x, other] = own[0]
        out[0, y ^ turn, x ^ (1 - turn), other] = first[0]
        out[0, y ^ (1 - turn), x ^ turn, other] = second[0]
        if count == 4:
            out[0, y ^ 1, x ^ 1, other] = diagonal[0][0]
            continue

        @pl.when(at < half)
        def _():
            out[0, y ^ 1, x ^ 1, other] = diagonal[0][0]

        @pl.when(at >= half)
        def _():
            out[0, y ^ 1, x ^ 1, other] = diagonal[1][0]


def vector_kernel(gained, w_ref, *refs):
    outs, scratch = refs[:-1], refs[-1]
    scratch[...] = w_ref[:, 0].astype(F32)
    for l in range(LAYERS):
        for which in range(4):
            out, row = ((outs[2 * l], which // 3) if which in (0, 3) else (outs[2 * l + 1], which - 1))
            wide = out.shape[1] // NS
            for s in range(NS):
                out[row : row + 1, s * wide : (s + 1) * wide] = scratch[s, 4 * l + which : 4 * l + which + 1, :wide]


def shape(dims, dtype=F32):
    return jax.ShapeDtypeStruct(dims, dtype)


def call(kernel, grid, ins, outs, scratch, us, name):
    def spec(a, block, index):
        if a.dtype == jnp.int32:
            return pl.BlockSpec(memory_space=pltpu.SMEM)
        return pl.BlockSpec(block, index)

    found = pl.pallas_call(
        kernel,
        grid=(grid,),
        in_specs=[spec(*one) for one in ins],
        out_specs=[pl.BlockSpec(block, index) for _, block, index, *_ in outs],
        out_shape=[pltpu.HBM(one[0].shape, one[0].dtype) if one[3:] else one[0] for one in outs],
        scratch_shapes=scratch,
        compiler_params=pltpu.CompilerParams(vmem_limit_bytes=VMEM),
        cost_estimate=pl.CostEstimate(flops=int(us * 1.1e9) + 1, bytes_accessed=1024, transcendentals=0),
        name=name,
    )(*[a for a, _, _ in ins])
    return found if len(found) > 1 else found[0]


def far(array):
    return pltpu.with_memory_space_constraint(array, pltpu.HBM)


def whole(array):
    dims = array.shape
    return (array, dims, lambda i: (0,) * len(dims))


def whole_out(dims, dtype=F32):
    return (shape(dims, dtype), dims, lambda i: (0,) * len(dims))


def first(i):
    return jnp.minimum(i, STEPS - 1)


def second(i):
    return jnp.maximum(i - STEPS, 0)


class Sizes:
    def __init__(self, seqs, length, d, h, ff):
        self.seqs, self.steps, self.n = seqs, length // CHUNKS, seqs * length
        self.d, self.h, self.ff = d, h, ff
        self.hb, self.fb = h // STEPS, ff // STEPS


def column_weight(view, at, late=False, steps=STEPS):
    array, rows, place = view
    return (far(array) if late else array, (NS, NB // steps, rows, LANE), lambda i: (0, at(i), place, 0))


def row_weight(view, at):
    array, rows, place = view
    return (array, (NS // STEPS, NB, rows, LANE), lambda i: (at(i), 0, place, 0))


def same(i):
    return i


def gate_forward(sz, x, gain, bias, w, save):
    n, d, h, wide, s = sz.n, sz.d, sz.h, sz.h // GATE_STEPS, sz.seqs
    col = lambda i: (0, i)
    return call(
        functools.partial(gate_kernel, s, sz.steps), GATE_STEPS,
        [whole(x), whole(gain), (bias, (2, wide), col)] + [column_weight(w[m], same, False, GATE_STEPS) for m in "fic"],
        [whole_out((n, d), BF16) + save]
        + [(shape((n, h)), (n, wide), col) + save, (shape((n, h)), (n, wide), col), (shape((n, h)), (n, wide), col) + save]
        + [(shape((n, h), BF16), (n, wide), col) + save] * 3
        + [(shape((s, CHUNKS, h)), (s, CHUNKS, wide), lambda i: (0, 0, i))] * 2
        + [(shape((2 * s, h)), (2 * s, wide), col)],
        [pltpu.VMEM((n, 3 * wide), F32)], 9, "gates",
    )


def mix_forward(sz, x, gain, decay, inflow, cp, ch, ent, wt, last, save):
    n, d, h, ff, w, f, s = sz.n, sz.d, sz.h, sz.ff, sz.hb, sz.fb, sz.seqs
    col = lambda i: (0, first(i))
    late = lambda i: (0, second(i))
    deep = lambda i: (0, 0, first(i))
    return call(
        functools.partial(mix_kernel, s, sz.steps), 2 * STEPS,
        [
            whole(x), whole(gain), (decay, (n, w), col), (inflow, (n, w), col),
            (cp, (s, CHUNKS, w), deep), (ch, (s, CHUNKS, w), deep), (ent, (s, w), col),
            row_weight(wt["o"], first), column_weight(wt["u"], second), row_weight(wt["d"], second),
        ],
        [
            (shape((n, h)), (n, w), col, True), (shape((n, h), BF16), (n, w), col) + save,
            (shape((s, CHUNKS, h)), (s, CHUNKS, w), deep) + save,
            whole_out((n, d)) + save, whole_out((n, d), BF16) + save,
            (shape((n, ff), BF16), (n, f), late) + save, (shape((n, ff), BF16), (n, f), late) + save,
            whole_out((n, d), BF16 if last else F32),
        ],
        [pltpu.VMEM((n, d), F32)], 14, "mix",
    )


def mlp_backward(sz, g, gain, mid, slope, decay, wt):
    n, d, h, ff, w, f, s = sz.n, sz.d, sz.h, sz.ff, sz.hb, sz.fb, sz.seqs
    col = lambda i: (0, second(i))
    early = lambda i: (0, first(i))
    deep = lambda i: (0, 0, second(i))
    return call(
        functools.partial(mlp_back_kernel, s, sz.steps), 2 * STEPS,
        [
            whole(g), whole(gain), whole(mid), (slope, (n, f), early), (decay, (n, w), col),
            row_weight(wt["o"], second), column_weight(wt["u"], first), row_weight(wt["d"], first),
        ],
        [
            whole_out((n, d), BF16), (shape((n, ff), BF16), (n, f), early), whole_out((n, d)), whole_out((n, d), BF16),
            whole_out((1, d)), (shape((n, h)), (n, w), col),
            (shape((s, CHUNKS, h)), (s, CHUNKS, w), deep), (shape((s, CHUNKS, h)), (s, CHUNKS, w), deep),
            (shape((2 * s, h)), (2 * s, w), col),
        ],
        [pltpu.VMEM((n, d), F32)], 12, "mlp_back",
    )


def gate_backward(sz, pos, x, gain, gmid, gh, decay, hidden, e, cand, ff_, fi_, fc_, cp, ca, ent, normed, wt, last, vectors):
    n, d, h, w, s = sz.n, sz.d, sz.h, sz.hb, sz.seqs
    col = lambda i: (0, i)
    deep = lambda i: (0, 0, i)
    wide = lambda a: (a, (n, w), col)
    rows = 3 * d * h // (32 * LANE) + (16 if vectors else 0)
    return call(
        functools.partial(gate_back_kernel, s, sz.steps, tuple(row for _, row in vectors)), STEPS,
        [
            whole(pos), whole(x), whole(gain), whole(gmid), wide(gh), wide(decay), wide(hidden), (e, (s, CHUNKS, w), deep),
            wide(cand), wide(ff_), wide(fi_), wide(fc_), (cp, (s, CHUNKS, w), deep), (ca, (s, CHUNKS, w), deep),
            (ent, (s, w), col), whole(normed),
        ] + [column_weight(wt[m], same, True) for m in "fic"] + [whole(v) for v, _ in vectors],
        [whole_out((NS, 2, rows, LANE), BF16)] * 2
        + [(shape((2, h)), (2, w), col), whole_out((n, d), BF16 if last else F32), whole_out((1, d))],
        [
            pltpu.VMEM((n, d), F32), pltpu.VMEM((s, CHUNKS, w), F32), pltpu.VMEM((n, 3 * w), BF16),
            pltpu.VMEM((NS, 16, LANE), F32),
        ], 16, "gate_back",
    )


def up_weights(sz, pos, n2, gpre):
    n, d, ff, f = sz.n, sz.d, sz.ff, sz.fb
    dims = (NS, 2, d * ff // (32 * LANE), LANE)
    return call(
        up_weight_kernel, STEPS, [whole(pos), whole(n2), (gpre, (n, f), lambda i: (0, i))],
        [whole_out(dims, BF16)] * 2, [], 5, "up_weights",
    )


def row_weights(sz, pos, left, right, name):
    n, k, d = sz.n, left.shape[1], sz.d
    dims = (NS, 2, k // NS, LANE)
    return call(
        row_weight_kernel, STEPS, [whole(pos), (left, (n, k // STEPS), lambda i: (0, i)), whole(right)],
        [whole_out(dims, BF16)] * 2, [], 5, name,
    )


def swap(array, axes, bits):
    count = lax.axis_size(axes)
    return lax.ppermute(array, axes, [(i, i ^ bits) for i in range(count)])


BOTH = ("seq", "batch")


def after(array, *others):
    return lax.optimization_barrier((array,) + others)[0]


def by_line(a):
    return (a, (1,) + a.shape[1:], lambda i: (i,) + (0,) * (len(a.shape) - 1))


def by_line_out(*dims):
    return (shape(dims, BF16), (1,) + dims[1:], lambda i: (i,) + (0,) * (len(dims) - 1))


def core_exchange(pairs):
    return [(keep, swap(send, "batch", 1)) for keep, send in pairs]


FIRST, SECOND, FIRST_Z, SECOND_Z = (2, 4), (4, 2), (8, 16), (16, 8)


def cross(array, bits):
    count = lax.axis_size(BOTH)
    return lax.ppermute(array, BOTH, [(i, i ^ bits[i % 2]) for i in range(count)])


def pair_sum(pos, pairs):
    rows = tuple(keep.shape[2] for keep, _ in pairs)
    view = lambda a: by_line(a.reshape((4, 2, 2) + a.shape[2:]))
    return call(
        functools.partial(pair_sum_kernel, rows), 4,
        [whole(pos)] + [view(keep) for keep, _ in pairs] + [view(got) for _, got in pairs],
        [by_line_out(4, 2, sum(rows), LANE)] * 2, [], 0, "pair_sum",
    )


def onward(parts, bits):
    return [parts[1], cross(parts[0], bits)]


def plane_sum(pos, parts):
    rows = parts[0].shape[2]
    return call(
        plane_sum_kernel, 4, [whole(pos)] + [by_line(a) for a in parts], [by_line_out(4, rows, LANE)] * 2, [], 0, "plane_sum",
    )


def line_sum(pos, parts):
    rows = parts[0].shape[1]
    return call(
        line_sum_kernel, 1, [whole(pos)] + [whole(a) for a in parts], [whole_out((2, rows, LANE), BF16)] * 2, [], 0, "line_sum",
    )


def last_sum(pos, parts):
    rows = parts[0].shape[1]
    return call(
        last_sum_kernel, 1, [whole(pos)] + [whole(a) for a in parts], [whole_out((rows, LANE), BF16)] * 2, [], 0, "last_sum",
    )


SUMS = ((plane_sum, SECOND), (line_sum, FIRST_Z), (last_sum, SECOND_Z))


class Reduction:
    def __init__(self, pos, names, pairs):
        self.pos, self.names, self.stage = pos, names, 0
        self.parts = pair_sum(pos, pairs)
        self.seen = self.parts[0]
        self.parts = onward(self.parts, FIRST)

    def step(self, *others):
        work, bits = SUMS[self.stage]
        if others:
            self.parts[0] = after(self.parts[0], *others)
        parts = work(self.pos, self.parts)
        self.stage, self.seen, self.parts = self.stage + 1, parts[0], onward(parts, bits)
        return self.seen

    def total(self, *others):
        keep, got = self.parts
        keep = after(keep, *others)
        total = call(total_kernel, 1, [whole(keep), whole(got)], [whole_out(keep.shape)], [], 0, "total")
        self.parts = [total]
        return total


def line_parts(own):
    return [own] + [swap(own, "seq", 2 * k) for k in range(1, 4)]


def line_gather(pos, parts, rows):
    return call(
        line_gather_kernel, 1, [whole(pos)] + [whole(far(p)) for p in parts],
        [whole_out((4, r, LANE), BF16) for r in rows], [], 2, "line_gather",
    )


X_AXIS, Y_AXIS = ("batch", 2), ("seq", 1)


def plane_gather(pos, line, parts, behind=()):
    rows = line.shape[1]
    parts = [line, *parts]
    parts += [swap(after(p, *behind) if behind else p, "batch", 1) for p in parts]
    each, low, high = (lambda i: (i, 0, 0)), (lambda i: (jnp.minimum(i, 1), 0, 0)), (lambda i: (jnp.maximum(i - 2, 0), 0, 0))
    maps = [each] * 4 if len(parts) == 8 else [each, each, each, low, high]
    got = call(
        plane_gather_kernel, 4, [whole(pos)] + [(far(p), (1, rows, LANE), m) for p, m in zip(parts, maps * 2)],
        [(shape((4, 2, 2, 2, rows, LANE), BF16), (1, 2, 2, 2, rows, LANE), lambda i: (i, 0, 0, 0, 0, 0))], [], 5, "plane_gather",
    )
    return got.reshape(NS, NB, rows, LANE)


def enter(fin, seqs, backward, fill=(), hold=None):
    count, mine = lax.axis_size("seq"), lax.axis_index("seq")
    prod, state = fin[:seqs], fin[seqs:]
    pre_p, pre_s = jnp.ones_like(prod), jnp.zeros_like(state)
    bit, message, done = 1, fin, []
    for step in range(int(count).bit_length() - 1):
        if hold and step in hold:
            message = after(message, *hold[step])
        other = lax.ppermute(message, "seq", [(i, i ^ bit) for i in range(count)])
        if step < len(fill):
            done.append(fill[step](message))
        o_p, o_s = other[:seqs], other[seqs:]
        upper = ((mine // bit) % 2 == 1) ^ backward
        pre_p, pre_s = jnp.where(upper, o_p * pre_p, pre_p), jnp.where(upper, pre_p * o_s + pre_s, pre_s)
        state = jnp.where(upper, prod * o_s + state, o_p * state + o_s)
        prod = prod * o_p
        message = jnp.concatenate([prod, state])
        if step < len(fill):
            message = after(message, *done[-1])
        bit *= 2
    return pre_s, done


def slabs(matrix, seq_count, batch_count):
    rows, cols = matrix.shape[0] // NS, matrix.shape[1] // NB
    cut = matrix.reshape(NS, rows, NB, cols // LANE, LANE).transpose(0, 2, 3, 1, 4)
    return cut.reshape(NS, NB, rows * cols // LANE, LANE)


def unslab(blocks, rows, cols):
    r, c = rows // NS, cols // NB
    cut = blocks.reshape(NS, NB, c // LANE, r, LANE).transpose(0, 3, 1, 2, 4)
    return cut.reshape(rows, cols)


def body(
    tokens, norm_gain, w_forget, w_input, w_cand, forget_bias, input_bias, w_out, mlp_gain, w_up, w_down, cotangent
):
    seqs, length, d = tokens.shape
    seq_count, batch_count = lax.axis_size("seq"), lax.axis_size("batch")
    h, ff = w_forget.shape[2] * batch_count, w_up.shape[2] * batch_count
    sz = Sizes(seqs, length, d, h, ff)
    standard = (seq_count, batch_count) == (NS, NB)
    matrices = {"u": w_up, "d": w_down, "o": w_out, "f": w_forget, "i": w_input, "c": w_cand}
    vectors = (norm_gain, forget_bias, input_bias, mlp_gain)
    slab_rows = {"u": d * ff // (32 * LANE), "d": ff // NS, "o": h // NS}
    slab_rows.update({m: d * h // (32 * LANE) for m in "fic"})
    order = {name: k for k, name in enumerate(matrices)}

    if standard:
        s_at, b_at = lax.axis_index("seq"), lax.axis_index("batch")
        core, x, y, z = b_at % 2, b_at // 2, s_at % 2, s_at // 2
        turned = [jnp.where(core == 0, a, b) for a, b in ((x, y), (y, x), (z % 2, z // 2), (z // 2, z % 2))]
        pos = jnp.stack([core, x, y, z, *turned]).astype(jnp.int32)
        vecs = [(6 + k, at, True) for at in range(LAYERS) for k in range(4)]
        groups = []
        for l in range(LAYERS):
            groups += [[(order[m], l, False) for m in "fic"] + vecs * (l == 0), [(order[m], l, False) for m in "udo"]]
        gate_rows, rest_rows = sum(slab_rows[m] for m in "fic"), sum(slab_rows[m] for m in "udo")
        rows = [gate_rows + 16, rest_rows] + [gate_rows, rest_rows] * (LAYERS - 1)
        packs = call(
            functools.partial(pack_kernel, groups), 1,
            [whole(far(m)) for m in matrices.values()] + [whole(far(v)) for v in vectors],
            [whole_out((r, LANE), BF16) for r in rows], [pltpu.VMEM((16, LANE), F32)], 2, "pack",
        )
        line_g0 = line_gather(pos, line_parts(packs[0]), rows[:1])
        parts_g0 = [swap(line_g0, *X_AXIS), swap(line_g0, *Y_AXIS)]
        parts_g0 += [swap(parts_g0[0][:2], *Y_AXIS), swap(parts_g0[1][2:], *X_AXIS)]
        line_r0 = line_gather(pos, line_parts(after(packs[1], line_g0)), rows[1:2])
        sent_r0 = after(line_r0, *parts_g0[:2])
        parts_r0 = [cross(sent_r0, FIRST), cross(sent_r0, SECOND)]
        line_g1 = line_gather(pos, line_parts(after(packs[2], line_r0)), rows[2:3])
        got = [plane_gather(pos, line_g0, parts_g0), None]
        places = {"f": 0, "i": 1, "c": 2, "u": 0, "d": 1, "o": 4}
        view = lambda got: {m: (got[m in "udo"], slab_rows[m], places[m]) for m in "udofic"}
        weights, lines_at, parts_at = [view(got)], [line_r0], [parts_r0]
        vecs = call(
            functools.partial(vector_kernel, None), 1,
            [(got[0], (NS, 1, 16, LANE), lambda i: (0, 0, 3 * slab_rows["f"] // 16, 0))],
            [whole_out((2, size)) for l in range(LAYERS) for size in (d, h)],
            [pltpu.VMEM((NS, 16, LANE), F32)], 1, "vectors",
        )
        gains, biases = vecs[0::2], vecs[1::2]
    else:
        pos = jnp.zeros((8,), jnp.int32)

        def full(m):
            m = lax.all_gather(m, "batch", axis=1, tiled=True)
            return lax.all_gather(m, "seq", axis=0, tiled=True)

        weights = [
            {m: (slabs(full(matrices[m][l]), NS, NB), slab_rows[m], 0) for m in "udofic"} for l in range(LAYERS)
        ]
        whole_vectors = [lax.all_gather(v, "seq", axis=1, tiled=True).astype(F32) for v in vectors]
        gains = [jnp.stack([whole_vectors[0][l], whole_vectors[3][l]]) for l in range(LAYERS)]
        biases = [jnp.stack([whole_vectors[1][l], whole_vectors[2][l]]) for l in range(LAYERS)]

    def to_rows(v):
        return v.reshape(seqs, CHUNKS, sz.steps, d).transpose(0, 2, 1, 3).reshape(sz.n, d)

    def from_rows(v):
        return v.reshape(seqs, sz.steps, CHUNKS, d).transpose(0, 2, 1, 3).reshape(seqs, length, d)

    stream, grad = to_rows(tokens), to_rows(cotangent)
    kept = []
    for l in range(LAYERS):
        save = (True,) if l + 1 < LAYERS else ()
        normed, decay, inflow, cand, f_f, f_i, f_c, cp, ch, fin = gate_forward(
            sz, stream, gains[l], biases[l], weights[l], (True,)
        )
        if standard:
            near, beside = parts_at[l]
            diagonal = cross(after(near, fin), SECOND)
            hold = {1: [line_g1] if l + 1 < LAYERS else [near], 2: [diagonal]}
            ent, _ = enter(fin, seqs, False, (), hold)
            rest = plane_gather(pos, lines_at[l], [near, beside, diagonal])
            weights[l] = view([weights[l]["f"][0], rest])
        else:
            ent, _ = enter(fin, seqs, False)
        hidden, hb, e, mid, n2, act, slope, result = mix_forward(
            sz, stream, gains[l], decay, inflow, cp, ch, ent, weights[l], l == LAYERS - 1, save
        )
        if standard and l + 1 < LAYERS:
            own, *others = line_parts(after(packs[2 * l + 3], ent))
            line_r = line_gather(pos, [after(own, result), *others], rows[2 * l + 3 : 2 * l + 4])
            sent_g = after(line_g1, diagonal)
            parts_g = [cross(sent_g, FIRST), cross(sent_g, SECOND), swap(sent_g, BOTH, 6)]
            sent_r = after(line_r, *parts_g)
            weights.append(view([plane_gather(pos, line_g1, parts_g, (result,)), None]))
            lines_at.append(line_r)
            parts_at.append([cross(sent_r, FIRST), cross(sent_r, SECOND)])
        kept.append((stream, normed, decay, cand, f_f, f_i, f_c, hidden, hb, e, mid, n2, act, slope))
        stream = result
    output = from_rows(stream)

    vector_grads, sums, pending = [None] * LAYERS, [], []
    above = None
    for l in reversed(range(LAYERS)):
        x, normed, decay, cand, f_f, f_i, f_c, hidden, hb, e, mid, n2, act, slope = kept[l]
        place = far if l + 1 < LAYERS else lambda a: a
        decay, cand, f_f, f_i, f_c, hidden = map(far, (decay, cand, f_f, f_i, f_c, hidden))
        mid, slope = place(mid), place(slope)
        gr, gpre, gmid, go, ggain_two, gh, cp, ca, fin = mlp_backward(sz, grad, gains[l], mid, slope, decay, weights[l])

        def up(message):
            if above:
                message = above[0].step(message)
            return up_weights(sz, pos, place(after(n2, message)), gpre)

        def down(message):
            if above:
                message = above[1].step(message)
            return row_weights(sz, pos, place(after(act, message)), gr, "down_weights")

        def out(message):
            if above:
                message = above[0].step(message)
            return row_weights(sz, pos, place(after(hb, message)), go, "out_weights")

        ent, pairs = enter(fin, seqs, True, (up, down, out))
        if standard:
            mlp = Reduction(pos, [(l, m) for m in "udo"], core_exchange(pairs))
            gmid = after(gmid, mlp.seen)
        final = []
        if l == 0 and standard:
            final = [(ggain_two, 3)]
            for at in range(1, LAYERS):
                final += [(v, 4 * at + row) for v, row in zip(vector_grads[at], (0, 1, 3))]
        *gate_pair, gbias, grad, ggain_one = gate_backward(
            sz, pos, x, gains[l], gmid, gh, decay, hidden, e, cand, f_f, f_i, f_c, cp, ca, ent, far(normed), weights[l],
            l == 0, final,
        )
        vector_grads[l] = (ggain_one, gbias, ggain_two)
        if not standard:
            pending.append((l, pairs + [gate_pair]))
            continue
        if above:
            above[1].step(gate_pair[0])
            above[0].step(above[1].seen)
            mlp.step(above[0].seen)
            gate_pair[1] = after(gate_pair[1], mlp.seen)
        names = [(l, m) for m in "fic"]
        if l == 0:
            names += [(at, k) for at in range(LAYERS) for k in range(4)]
        gates = Reduction(pos, names, core_exchange([gate_pair]))
        if l > 0:
            grad, above = after(grad, gates.seen), [mlp, gates]
            continue
        gates.step(above[1].step(gates.seen))
        gates.step(above[0].total(gates.seen))
        mlp.step()
        gates.step(above[1].total(gates.seen))
        mlp.step()
        sums = [(one.names, one.parts) for one in (*above, mlp, gates)]
    grad_tokens = from_rows(grad)

    if standard:
        layout, ins = [], []
        for names, parts in sums:
            pieces = [(order[m], l, False) if m in order else (6 + m, l, True) for l, m in names]
            layout.append((len(parts), pieces))
            ins += [whole(p) for p in parts]
        found = call(
            functools.partial(finish_kernel, layout), 1, ins,
            [whole_out(m.shape) for m in matrices.values()] + [whole_out(v.shape) for v in vectors], [], 3, "finish",
        )
        g_up, g_down, g_out, g_f, g_i, g_c, g_norm, g_fb, g_ib, g_mlp = found
    else:
        per_layer = {}
        for l, pairs in pending:
            blocks = [jnp.stack([keep, send], axis=2).reshape(NS, NB, -1, LANE) for keep, send in pairs]
            gates = jnp.split(blocks[3], 3, axis=2)
            for m, g in zip("udofic", blocks[:3] + gates):
                v = unslab(g, matrices[m].shape[1] * seq_count, matrices[m].shape[2] * batch_count)
                v = lax.psum_scatter(v, "seq", scatter_dimension=0, tiled=True)
                per_layer[m, l] = lax.psum_scatter(v, "batch", scatter_dimension=1, tiled=True).astype(F32)
        g_up, g_down, g_out, g_f, g_i, g_c = [
            jnp.stack([per_layer[m, l] for l in range(LAYERS)]) for m in matrices
        ]
        rows = [
            (ggain_one[0], gbias[0], gbias[1], ggain_two[0]) for ggain_one, gbias, ggain_two in vector_grads
        ]
        g_norm, g_fb, g_ib, g_mlp = [
            lax.psum(lax.psum_scatter(jnp.stack([r[k] for r in rows]), "seq", scatter_dimension=1, tiled=True), "batch")
            for k in range(4)
        ]
    return output, grad_tokens, g_norm, g_f, g_i, g_c, g_fb, g_ib, g_out, g_mlp, g_up, g_down


def solution(mesh):
    split, vector, matrix = P("batch", "seq", None), P(None, "seq"), P(None, "seq", "batch")
    order = (vector, matrix, matrix, matrix, vector, vector, matrix, vector, matrix, matrix)
    return jax.shard_map(
        body,
        mesh=mesh,
        in_specs=(split,) + order + (split,),
        out_specs=(split, split) + order,
        check_vma=False,
    )
```

```python
import functools

import jax
import jax.numpy as jnp
from jax import lax
from jax.experimental import pallas as pl
from jax.experimental.pallas import tpu as pltpu
from jax.sharding import PartitionSpec as P

LAYERS = 2
EPS = 1e-05
NS, NB, LANE = 8, 4, 128
CHUNKS = 8
STEPS = 2
GATE_STEPS = 4
TURN, WIDE = 2, 256
VMEM = 28 * 1024 * 1024
F32, BF16 = jnp.float32, jnp.bfloat16


def dot(left, right):
    return lax.dot_general(left, right, (((1,), (0,)), ((), ())), preferred_element_type=F32)


def dot_nt(left, right):
    return lax.dot_general(left, right, (((1,), (1,)), ((), ())), preferred_element_type=F32)


def dot_tn(left, right):
    return lax.dot_general(left, right, (((0,), (0,)), ((), ())), preferred_element_type=F32)


def columns_of(ref, slabs=2):
    rows = ref.shape[2] // slabs
    parts = [
        ref[:, b, j * rows : (j + 1) * rows, :].reshape(NS * rows, LANE) for b in range(ref.shape[1]) for j in range(slabs)
    ]
    return jnp.concatenate(parts, axis=1)


def rows_of(ref):
    parts = [ref[:, j].reshape(-1, LANE) for j in range(NB)]
    return jnp.concatenate(parts, axis=1)


def rms_scale(values):
    return lax.rsqrt(jnp.mean(values * values, axis=-1, keepdims=True) + EPS)


def rms_back(values, gain, grad):
    scale = rms_scale(values)
    unit = values * scale
    inner = grad * gain
    back = scale * (inner - unit * jnp.mean(inner * unit, axis=-1, keepdims=True))
    return back, jnp.sum(grad * unit, axis=0, keepdims=True)


def gate_kernel(
    seqs, steps, x_ref, gain_ref, bias_ref, wf_ref, wi_ref, wc_ref,
    normed_ref, decay_ref, inflow_ref, cand_ref, ff_ref, fi_ref, fc_ref, cp_ref, ch_ref, fin_ref,
    z,
):
    width = decay_ref.shape[1]

    @pl.when(pl.program_id(0) == 0)
    def _():
        x = x_ref[...].astype(F32)
        normed_ref[...] = (x * rms_scale(x) * gain_ref[0:1, :]).astype(BF16)

    weights = jnp.concatenate([columns_of(ref) for ref in (wf_ref, wi_ref, wc_ref)], axis=1)
    block = TURN * CHUNKS
    places = [(seq, left) for seq in range(seqs) for left in range(0, width, WIDE)]

    def turn(of, at, carry):
        carry = list(carry)
        for k, (seq, left) in enumerate(places):
            if seq != of:
                continue
            span = slice(seq * steps * CHUNKS + at * block, seq * steps * CHUNKS + (at + 1) * block)
            cols = slice(left, left + WIDE)
            f = z[span, cols] + bias_ref[0:1, cols]
            i = z[span, width + left : width + left + WIDE] + bias_ref[1:2, cols]
            c = z[span, 2 * width + left : 2 * width + left + WIDE]
            low = jnp.minimum(jnp.minimum(f, i), 0.0)
            e0, ef, ei = jnp.exp(low), jnp.exp(low - f), jnp.exp(low - i)
            a, b = e0 + ef, e0 + ei
            inv = 1.0 / (a + b)
            decay, other = b * inv, a * inv
            ec = jnp.exp(-jnp.abs(c))
            cand = jnp.maximum(c, 0.0) + jnp.log1p(ec)
            slope = jnp.where(c >= 0.0, 1.0, ec) / (1.0 + ec)
            inflow = other * cand
            decay_ref[span, cols] = decay
            inflow_ref[span, cols] = inflow
            cand_ref[span, cols] = cand
            ff_ref[span, cols] = (ef * inv * decay).astype(BF16)
            fi_ref[span, cols] = (ei * inv * other).astype(BF16)
            fc_ref[span, cols] = (other * slope).astype(BF16)
            prod, state = carry[2 * k], carry[2 * k + 1]
            for t in range(TURN):
                d = decay[t * CHUNKS : (t + 1) * CHUNKS]
                prod = prod * d
                state = state * d + inflow[t * CHUNKS : (t + 1) * CHUNKS]
            carry[2 * k], carry[2 * k + 1] = prod, state
        return tuple(carry)

    one, zero = jnp.ones((CHUNKS, WIDE), F32), jnp.zeros((CHUNKS, WIDE), F32)
    carry = (one, zero) * len(places)
    for seq in range(seqs):
        rows = slice(seq * steps * CHUNKS, (seq + 1) * steps * CHUNKS)
        z[rows, :] = dot(normed_ref[rows, :], weights)
        for at in range(steps // TURN):
            carry = turn(seq, at, carry)
    for k, (seq, left) in enumerate(places):
        prod, state = carry[2 * k], carry[2 * k + 1]
        cols = slice(left, left + WIDE)
        cp_ref[seq, :, cols], ch_ref[seq, :, cols] = prod, state
        whole, last = prod[0:1], state[0:1]
        for c in range(1, CHUNKS):
            whole, last = whole * prod[c : c + 1], last * prod[c : c + 1] + state[c : c + 1]
        fin_ref[seq : seq + 1, cols] = whole
        fin_ref[seqs + seq : seqs + seq + 1, cols] = last


def mix_kernel(
    seqs, steps, x_ref, gain_ref, decay_ref, inflow_ref, cp_ref, ch_ref, ent_ref, wo_ref, wu_ref, wd_ref,
    hidden_ref, hb_ref, e_ref, mid_ref, n2_ref, act_ref, slope_ref, out_ref,
    acc,
):
    at_step = pl.program_id(0)
    block = TURN * CHUNKS
    width = decay_ref.shape[1]
    places = [(seq, left) for seq in range(seqs) for left in range(0, width, WIDE)]

    @pl.when(at_step == 0)
    def _():
        acc[...] = x_ref[...].astype(F32)

    @pl.when(at_step < STEPS)
    def _():
        for seq in range(seqs):
            state = ent_ref[seq : seq + 1, :]
            for c in range(CHUNKS):
                e_ref[seq, c : c + 1, :] = state
                state = state * cp_ref[seq, c : c + 1, :] + ch_ref[seq, c : c + 1, :]

        def turn(at, carry):
            carry = list(carry)
            for k, (seq, left) in enumerate(places):
                span = pl.ds(pl.multiple_of(seq * steps * CHUNKS + at * block, block), block)
                cols = slice(left, left + WIDE)
                d, u = decay_ref[span, cols], inflow_ref[span, cols]
                state, found = carry[k], []
                for t in range(TURN):
                    state = state * d[t * CHUNKS : (t + 1) * CHUNKS] + u[t * CHUNKS : (t + 1) * CHUNKS]
                    found.append(state)
                carry[k] = state
                hidden = jnp.concatenate(found, axis=0)
                hidden_ref[span, cols] = hidden
                hb_ref[span, cols] = hidden.astype(BF16)
            return tuple(carry)

        lax.fori_loop(0, steps // TURN, turn, tuple(e_ref[seq, :, left : left + WIDE] for seq, left in places))
        acc[...] += dot(hb_ref[...], rows_of(wo_ref))

    @pl.when(at_step == STEPS - 1)
    def _():
        middle = acc[...]
        mid_ref[...] = middle
        n2_ref[...] = (middle * rms_scale(middle) * gain_ref[1:2, :]).astype(BF16)

    @pl.when(at_step >= STEPS)
    def _():
        w_up, w_down = columns_of(wu_ref, 4), rows_of(wd_ref)
        size = acc.shape[0] // 2
        for k in range(2):
            span = slice(k * size, (k + 1) * size)
            v = dot(n2_ref[span, :], w_up)
            phi = 0.5 + 0.5 * lax.erf(v * 0.7071067811865476)
            act = (v * phi).astype(BF16)
            act_ref[span, :] = act
            slope_ref[span, :] = (phi + v * (0.3989422804014327 * jnp.exp(v * v * -0.5))).astype(BF16)
            acc[span, :] += dot(act, w_down)

    @pl.when(at_step == 2 * STEPS - 1)
    def _():
        out_ref[...] = acc[...].astype(out_ref.dtype)


def mlp_back_kernel(
    seqs, steps, g_ref, gain_ref, mid_ref, slope_ref, decay_ref, wo_ref, wu_ref, wd_ref,
    gr_ref, gpre_ref, gmid_ref, go_ref, ggain_ref, gh_ref, cp_ref, ca_ref, fin_ref,
    acc,
):
    at_step = pl.program_id(0)
    block = TURN * CHUNKS
    width = decay_ref.shape[1]
    places = [(seq, left) for seq in range(seqs) for left in range(0, width, WIDE)]

    @pl.when(at_step == 0)
    def _():
        gr_ref[...] = g_ref[...].astype(BF16)
        acc[...] = jnp.zeros_like(acc)

    @pl.when(at_step < STEPS)
    def _():
        gact = dot_nt(gr_ref[...], rows_of(wd_ref))
        gpre_ref[...] = (gact * slope_ref[...].astype(F32)).astype(BF16)
        acc[...] += dot_nt(gpre_ref[...], columns_of(wu_ref, 4))

    @pl.when(at_step == STEPS - 1)
    def _():
        back, ggain = rms_back(mid_ref[...], gain_ref[1:2, :], acc[...])
        ggain_ref[...] = ggain
        gmid = g_ref[...].astype(F32) + back
        gmid_ref[...] = gmid
        go_ref[...] = gmid.astype(BF16)

    @pl.when(at_step >= STEPS)
    def _():
        gh_ref[...] = dot_nt(go_ref[...], rows_of(wo_ref))

        def turn(turn_at, carry):
            at = steps // TURN - 1 - turn_at
            carry = list(carry)
            for k, (seq, left) in enumerate(places):
                span = pl.ds(pl.multiple_of(seq * steps * CHUNKS + at * block, block), block)
                cols = slice(left, left + WIDE)
                d, g = decay_ref[span, cols], gh_ref[span, cols]
                prod, state = carry[2 * k], carry[2 * k + 1]
                for t in reversed(range(TURN)):
                    dk = d[t * CHUNKS : (t + 1) * CHUNKS]
                    prod = prod * dk
                    state = dk * (g[t * CHUNKS : (t + 1) * CHUNKS] + state)
                carry[2 * k], carry[2 * k + 1] = prod, state
            return tuple(carry)

        one, zero = jnp.ones((CHUNKS, WIDE), F32), jnp.zeros((CHUNKS, WIDE), F32)
        carry = lax.fori_loop(0, steps // TURN, turn, (one, zero) * len(places))
        for k, (seq, left) in enumerate(places):
            prod, state = carry[2 * k], carry[2 * k + 1]
            cols = slice(left, left + WIDE)
            cp_ref[seq, :, cols], ca_ref[seq, :, cols] = prod, state
            whole, last = prod[CHUNKS - 1 :], state[CHUNKS - 1 :]
            for c in reversed(range(CHUNKS - 1)):
                whole, last = whole * prod[c : c + 1], last * prod[c : c + 1] + state[c : c + 1]
            fin_ref[seq : seq + 1, cols] = whole
            fin_ref[seqs + seq : seqs + seq + 1, cols] = last


def gate_back_kernel(
    seqs, steps, others, pos_ref, x_ref, gain_ref, gmid_ref, gh_ref, decay_ref, hidden_ref, e_ref, cand_ref,
    ff_ref, fi_ref, fc_ref, cp_ref, ca_ref, ent_ref, normed_ref, wf_ref, wi_ref, wc_ref, *refs,
):
    given = refs[: len(others)]
    keep_ref, send_ref, gbias_ref, gstream_ref, ggain_ref, acc, start, dz, rest = refs[len(others) :]
    at_step = pl.program_id(0)
    block = TURN * CHUNKS
    width = decay_ref.shape[1]
    places = [(seq, left) for seq in range(seqs) for left in range(0, width, WIDE)]

    @pl.when(at_step == 0)
    def _():
        acc[...] = jnp.zeros_like(acc)

    for seq in range(seqs):
        state = ent_ref[seq : seq + 1, :]
        for c in reversed(range(CHUNKS)):
            start[seq, c : c + 1, :] = state
            state = state * cp_ref[seq, c : c + 1, :] + ca_ref[seq, c : c + 1, :]

    def turn(of, at, carry):
        carry = list(carry)
        for k, (seq, left) in enumerate(places):
            if seq != of:
                continue
            cols = slice(left, left + WIDE)
            state, sum_f, sum_i = carry[3 * k : 3 * k + 3]
            base = seq * steps * CHUNKS + at * block
            span = slice(base, base + block)
            before = hidden_ref[base - CHUNKS : base, cols] if at else e_ref[seq, :, cols]
            d, g = decay_ref[span, cols], gh_ref[span, cols]
            previous = jnp.concatenate([before, hidden_ref[span, cols][: block - CHUNKS]], axis=0)
            found = []
            for t in reversed(range(TURN)):
                now = g[t * CHUNKS : (t + 1) * CHUNKS] + state
                found.append(now)
                state = d[t * CHUNKS : (t + 1) * CHUNKS] * now
            gstate = jnp.concatenate(found[::-1], axis=0)
            both = gstate * (cand_ref[span, cols] - previous)
            dzf = (-ff_ref[span, cols].astype(F32) * both).astype(BF16)
            dzi = (fi_ref[span, cols].astype(F32) * both).astype(BF16)
            dz[span, left : left + WIDE] = dzf
            dz[span, width + left : width + left + WIDE] = dzi
            dz[span, 2 * width + left : 2 * width + left + WIDE] = (fc_ref[span, cols].astype(F32) * gstate).astype(BF16)
            wide_f, wide_i = dzf.astype(F32), dzi.astype(F32)
            for t in range(TURN):
                sum_f = sum_f + wide_f[t * CHUNKS : (t + 1) * CHUNKS]
                sum_i = sum_i + wide_i[t * CHUNKS : (t + 1) * CHUNKS]
            carry[3 * k : 3 * k + 3] = state, sum_f, sum_i
        return tuple(carry)

    zero = jnp.zeros((CHUNKS, WIDE), F32)
    first_carry = [v for seq, left in places for v in (start[seq, :, left : left + WIDE], zero, zero)]
    carry = tuple(first_carry)
    weights = jnp.concatenate([columns_of(ref) for ref in (wf_ref, wi_ref, wc_ref)], axis=1)
    grad = None
    for seq in range(seqs):
        rows = slice(seq * steps * CHUNKS, (seq + 1) * steps * CHUNKS)
        for at in reversed(range(steps // TURN)):
            carry = turn(seq, at, carry)
        acc[rows, :] += dot_nt(dz[rows, :], weights)
        part = dot_tn(normed_ref[rows, :], dz[rows, :])
        grad = part if grad is None else grad + part
    for row in range(2):
        for left in range(0, width, WIDE):
            total = sum(carry[3 * k + 1 + row] for k, place in enumerate(places) if place[1] == left)
            gbias_ref[row : row + 1, left : left + WIDE] = jnp.sum(total, axis=0, keepdims=True)
    rows = wf_ref.shape[2]
    for m in range(3):
        put_columns(pos_ref, keep_ref, send_ref, m * rows, grad[:, m * width : (m + 1) * width])

    @pl.when(at_step == STEPS - 1)
    def _():
        back, ggain = rms_back(x_ref[...].astype(F32), gain_ref[0:1, :], acc[...])
        ggain_ref[...] = ggain
        gstream_ref[...] = (gmid_ref[...] + back).astype(gstream_ref.dtype)

    if others:

        def rows_to(ref, first_row):
            wide = ref.shape[1] // NS
            for r in range(ref.shape[0]):
                for s in range(NS):
                    rest[s, first_row + r : first_row + r + 1, :wide] = ref[r : r + 1, s * wide : (s + 1) * wide]

        @pl.when(at_step == 0)
        def _():
            rest[...] = jnp.zeros_like(rest)
            for ref, first_row in zip(given, others):
                rows_to(ref, first_row)

        wide = width * STEPS // NS
        for row in range(2):
            for s in range(width // wide):
                rest[at_step * (width // wide) + s, 1 + row : 2 + row, :wide] = gbias_ref[row : row + 1, s * wide : (s + 1) * wide]

        @pl.when(at_step == STEPS - 1)
        def _():
            rows_to(ggain_ref, 0)
            found = rest[...].astype(BF16)
            for x in range(2):
                keep_ref[:, x, 3 * rows :, :] = found
                send_ref[:, x, 3 * rows :, :] = found


def send_or_keep(mine, keep_ref, send_ref, put):
    @pl.when(mine)
    def _():
        put(keep_ref)

    @pl.when(jnp.logical_not(mine))
    def _():
        put(send_ref)


def put_columns(pos_ref, keep_ref, send_ref, start, value):
    rows, width = value.shape[0] // NS, value.shape[1] // 2
    x = pl.program_id(0)
    for core in range(2):
        parts = [
            value[:, left : left + LANE].astype(BF16).reshape(NS, rows, LANE)
            for left in range(core * width, (core + 1) * width, LANE)
        ]

        def put(ref):
            for j, part in enumerate(parts):
                ref[:, x, start + j * rows : start + (j + 1) * rows, :] = part

        send_or_keep(pos_ref[0] == core, keep_ref, send_ref, put)


def put_rows(pos_ref, keep_ref, send_ref, value):
    count = NS // STEPS
    for j in range(NB):
        part = value[:, j * LANE : (j + 1) * LANE].astype(BF16).reshape(count, -1, LANE)

        def put(ref):
            ref[pl.ds(pl.program_id(0) * count, count), j // 2] = part

        send_or_keep(pos_ref[0] == j % 2, keep_ref, send_ref, put)


def up_weight_kernel(pos_ref, n2_ref, gpre_ref, keep_ref, send_ref):
    put_columns(pos_ref, keep_ref, send_ref, 0, dot_tn(n2_ref[...], gpre_ref[...]))


def row_weight_kernel(pos_ref, left_ref, right_ref, keep_ref, send_ref):
    put_rows(pos_ref, keep_ref, send_ref, dot_tn(left_ref[...], right_ref[...]))


def add(*parts):
    total = parts[0].astype(F32)
    for part in parts[1:]:
        total = total + part.astype(F32)
    return total


def pair_sum_kernel(rows, pos_ref, *refs):
    count = len(rows)
    send, stay = refs[2 * count :]
    core, x, y, step = pos_ref[0], pos_ref[1], pos_ref[2], pos_ref[4]
    at = 0
    for keep, got, r in zip(refs[:count], refs[count : 2 * count], rows):
        for v in range(2):
            for out, first in ((send, 1 - step), (stay, step)):
                iy, ix = jnp.where(core == 0, v, first), jnp.where(core == 0, first, v)
                out[0, v, at : at + r] = add(keep[0, iy, ix], got[0, iy, ix]).astype(BF16)
        at += r


def plane_sum_kernel(pos_ref, *refs):
    second = pos_ref[5]
    *pairs, send, stay = refs
    at = 0
    for keep, got in zip(pairs[::2], pairs[1::2]):
        rows = slice(at, at + keep.shape[2])
        send[0, rows, :] = add(keep[0, 1 - second], got[0, 1 - second]).astype(BF16)
        stay[0, rows, :] = add(keep[0, second], got[0, second]).astype(BF16)
        at += keep.shape[2]


def line_sum_kernel(pos_ref, *refs):
    core, first = pos_ref[0], pos_ref[6]
    *pairs, send, stay = refs
    at = 0
    for keep, got in zip(pairs[::2], pairs[1::2]):
        rows = slice(at, at + keep.shape[1])
        for v in range(2):
            for out, f in ((send, 1 - first), (stay, first)):
                z = jnp.where(core == 0, f + 2 * v, 2 * f + v)
                out[v, rows, :] = add(keep[z], got[z]).astype(BF16)
        at += keep.shape[1]


def last_sum_kernel(pos_ref, keep, got, send, stay):
    second = pos_ref[7]
    send[...] = add(keep[1 - second], got[1 - second]).astype(BF16)
    stay[...] = add(keep[second], got[second]).astype(BF16)


def total_kernel(keep, got, out):
    out[...] = add(keep[...], got[...])


def finish_kernel(layout, *refs):
    at = 0
    ins = sum(parts for parts, _ in layout)
    outs = refs[ins:]
    for parts, pieces in layout:
        got = refs[at : at + parts]
        at += parts
        row = 0
        for out, layer, vectors in pieces:
            ref = outs[out]
            if vectors:
                ref[layer : layer + 1, :] = add(*[g[...] for g in got])[row : row + 1, : ref.shape[1]]
                row += 1
                continue
            r = ref.shape[1]
            for j in range(ref.shape[2] // LANE):
                ref[layer, :, j * LANE : (j + 1) * LANE] = add(*[g[row : row + r] for g in got])
                row += r


def pack_kernel(groups, *refs):
    ins = refs[: len(refs) - len(groups) - 1]
    outs, scratch = refs[len(ins) : -1], refs[-1]
    for out, group in zip(outs, groups):
        row = 0
        vec = 0
        for which, layer, vector in group:
            ref = ins[which]
            if vector:
                if vec == 0:
                    scratch[...] = jnp.zeros_like(scratch)
                scratch[vec : vec + 1, : ref.shape[1]] = ref[...].astype(F32)[layer : layer + 1]
                vec += 1
                continue
            r = ref.shape[1]
            for j in range(ref.shape[2] // LANE):
                out[row : row + r, :] = ref[layer, :, j * LANE : (j + 1) * LANE]
                row += r
        if vec:
            out[row:, :] = scratch[...].astype(BF16)


def line_gather_kernel(pos_ref, *refs):
    row = 0
    for out in refs[4:]:
        rows = out.shape[1]
        for k, part in enumerate(refs[:4]):
            out[pos_ref[3] ^ k] = part[row : row + rows, :]
        row += rows


def plane_gather_kernel(pos_ref, *refs):
    out = refs[-1]
    at, half = pl.program_id(0), pl.num_programs(0) // 2
    core, x, y = pos_ref[0], pos_ref[1], pos_ref[2]
    count = len(refs) // 2
    for c in range(2):
        own, first, second, *diagonal = refs[count * c : count * (c + 1)]
        other = core ^ c
        turn = other if count == 4 else 0
        out[0, y, x, other] = own[0]
        out[0, y ^ turn, x ^ (1 - turn), other] = first[0]
        out[0, y ^ (1 - turn), x ^ turn, other] = second[0]
        if count == 4:
            out[0, y ^ 1, x ^ 1, other] = diagonal[0][0]
            continue

        @pl.when(at < half)
        def _():
            out[0, y ^ 1, x ^ 1, other] = diagonal[0][0]

        @pl.when(at >= half)
        def _():
            out[0, y ^ 1, x ^ 1, other] = diagonal[1][0]


def vector_kernel(gained, w_ref, *refs):
    outs, scratch = refs[:-1], refs[-1]
    scratch[...] = w_ref[:, 0].astype(F32)
    for l in range(LAYERS):
        for which in range(4):
            out, row = ((outs[2 * l], which // 3) if which in (0, 3) else (outs[2 * l + 1], which - 1))
            wide = out.shape[1] // NS
            for s in range(NS):
                out[row : row + 1, s * wide : (s + 1) * wide] = scratch[s, 4 * l + which : 4 * l + which + 1, :wide]


def shape(dims, dtype=F32):
    return jax.ShapeDtypeStruct(dims, dtype)


def call(kernel, grid, ins, outs, scratch, us, name):
    def spec(a, block, index):
        if a.dtype == jnp.int32:
            return pl.BlockSpec(memory_space=pltpu.SMEM)
        return pl.BlockSpec(block, index)

    found = pl.pallas_call(
        kernel,
        grid=(grid,),
        in_specs=[spec(*one) for one in ins],
        out_specs=[pl.BlockSpec(block, index) for _, block, index, *_ in outs],
        out_shape=[pltpu.HBM(one[0].shape, one[0].dtype) if one[3:] else one[0] for one in outs],
        scratch_shapes=scratch,
        compiler_params=pltpu.CompilerParams(vmem_limit_bytes=VMEM),
        cost_estimate=pl.CostEstimate(flops=int(us * 1.1e9) + 1, bytes_accessed=1024, transcendentals=0),
        name=name,
    )(*[a for a, _, _ in ins])
    return found if len(found) > 1 else found[0]


def far(array):
    return pltpu.with_memory_space_constraint(array, pltpu.HBM)


def whole(array):
    dims = array.shape
    return (array, dims, lambda i: (0,) * len(dims))


def whole_out(dims, dtype=F32):
    return (shape(dims, dtype), dims, lambda i: (0,) * len(dims))


def first(i):
    return jnp.minimum(i, STEPS - 1)


def second(i):
    return jnp.maximum(i - STEPS, 0)


class Sizes:
    def __init__(self, seqs, length, d, h, ff):
        self.seqs, self.steps, self.n = seqs, length // CHUNKS, seqs * length
        self.d, self.h, self.ff = d, h, ff
        self.hb, self.fb = h // STEPS, ff // STEPS


def column_weight(view, at, late=False, steps=STEPS):
    array, rows, place = view
    return (far(array) if late else array, (NS, NB // steps, rows, LANE), lambda i: (0, at(i), place, 0))


def row_weight(view, at):
    array, rows, place = view
    return (array, (NS // STEPS, NB, rows, LANE), lambda i: (at(i), 0, place, 0))


def same(i):
    return i


def gate_forward(sz, x, gain, bias, w, save):
    n, d, h, wide, s = sz.n, sz.d, sz.h, sz.h // GATE_STEPS, sz.seqs
    col = lambda i: (0, i)
    return call(
        functools.partial(gate_kernel, s, sz.steps), GATE_STEPS,
        [whole(x), whole(gain), (bias, (2, wide), col)] + [column_weight(w[m], same, False, GATE_STEPS) for m in "fic"],
        [whole_out((n, d), BF16) + save]
        + [(shape((n, h)), (n, wide), col) + save, (shape((n, h)), (n, wide), col), (shape((n, h)), (n, wide), col) + save]
        + [(shape((n, h), BF16), (n, wide), col) + save] * 3
        + [(shape((s, CHUNKS, h)), (s, CHUNKS, wide), lambda i: (0, 0, i))] * 2
        + [(shape((2 * s, h)), (2 * s, wide), col)],
        [pltpu.VMEM((n, 3 * wide), F32)], 9, "gates",
    )


def mix_forward(sz, x, gain, decay, inflow, cp, ch, ent, wt, last, save):
    n, d, h, ff, w, f, s = sz.n, sz.d, sz.h, sz.ff, sz.hb, sz.fb, sz.seqs
    col = lambda i: (0, first(i))
    late = lambda i: (0, second(i))
    deep = lambda i: (0, 0, first(i))
    return call(
        functools.partial(mix_kernel, s, sz.steps), 2 * STEPS,
        [
            whole(x), whole(gain), (decay, (n, w), col), (inflow, (n, w), col),
            (cp, (s, CHUNKS, w), deep), (ch, (s, CHUNKS, w), deep), (ent, (s, w), col),
            row_weight(wt["o"], first), column_weight(wt["u"], second), row_weight(wt["d"], second),
        ],
        [
            (shape((n, h)), (n, w), col, True), (shape((n, h), BF16), (n, w), col) + save,
            (shape((s, CHUNKS, h)), (s, CHUNKS, w), deep) + save,
            whole_out((n, d)) + save, whole_out((n, d), BF16) + save,
            (shape((n, ff), BF16), (n, f), late) + save, (shape((n, ff), BF16), (n, f), late) + save,
            whole_out((n, d), BF16 if last else F32),
        ],
        [pltpu.VMEM((n, d), F32)], 14, "mix",
    )


def mlp_backward(sz, g, gain, mid, slope, decay, wt):
    n, d, h, ff, w, f, s = sz.n, sz.d, sz.h, sz.ff, sz.hb, sz.fb, sz.seqs
    col = lambda i: (0, second(i))
    early = lambda i: (0, first(i))
    deep = lambda i: (0, 0, second(i))
    return call(
        functools.partial(mlp_back_kernel, s, sz.steps), 2 * STEPS,
        [
            whole(g), whole(gain), whole(mid), (slope, (n, f), early), (decay, (n, w), col),
            row_weight(wt["o"], second), column_weight(wt["u"], first), row_weight(wt["d"], first),
        ],
        [
            whole_out((n, d), BF16), (shape((n, ff), BF16), (n, f), early), whole_out((n, d)), whole_out((n, d), BF16),
            whole_out((1, d)), (shape((n, h)), (n, w), col),
            (shape((s, CHUNKS, h)), (s, CHUNKS, w), deep), (shape((s, CHUNKS, h)), (s, CHUNKS, w), deep),
            (shape((2 * s, h)), (2 * s, w), col),
        ],
        [pltpu.VMEM((n, d), F32)], 12, "mlp_back",
    )


def gate_backward(sz, pos, x, gain, gmid, gh, decay, hidden, e, cand, ff_, fi_, fc_, cp, ca, ent, normed, wt, last, vectors):
    n, d, h, w, s = sz.n, sz.d, sz.h, sz.hb, sz.seqs
    col = lambda i: (0, i)
    deep = lambda i: (0, 0, i)
    wide = lambda a: (a, (n, w), col)
    rows = 3 * d * h // (32 * LANE) + (16 if vectors else 0)
    return call(
        functools.partial(gate_back_kernel, s, sz.steps, tuple(row for _, row in vectors)), STEPS,
        [
            whole(pos), whole(x), whole(gain), whole(gmid), wide(gh), wide(decay), wide(hidden), (e, (s, CHUNKS, w), deep),
            wide(cand), wide(ff_), wide(fi_), wide(fc_), (cp, (s, CHUNKS, w), deep), (ca, (s, CHUNKS, w), deep),
            (ent, (s, w), col), whole(normed),
        ] + [column_weight(wt[m], same, True) for m in "fic"] + [whole(v) for v, _ in vectors],
        [whole_out((NS, 2, rows, LANE), BF16)] * 2
        + [(shape((2, h)), (2, w), col), whole_out((n, d), BF16 if last else F32), whole_out((1, d))],
        [
            pltpu.VMEM((n, d), F32), pltpu.VMEM((s, CHUNKS, w), F32), pltpu.VMEM((n, 3 * w), BF16),
            pltpu.VMEM((NS, 16, LANE), F32),
        ], 16, "gate_back",
    )


def up_weights(sz, pos, n2, gpre):
    n, d, ff, f = sz.n, sz.d, sz.ff, sz.fb
    dims = (NS, 2, d * ff // (32 * LANE), LANE)
    return call(
        up_weight_kernel, STEPS, [whole(pos), whole(n2), (gpre, (n, f), lambda i: (0, i))],
        [whole_out(dims, BF16)] * 2, [], 5, "up_weights",
    )


def row_weights(sz, pos, left, right, name):
    n, k, d = sz.n, left.shape[1], sz.d
    dims = (NS, 2, k // NS, LANE)
    return call(
        row_weight_kernel, STEPS, [whole(pos), (left, (n, k // STEPS), lambda i: (0, i)), whole(right)],
        [whole_out(dims, BF16)] * 2, [], 5, name,
    )


def swap(array, axes, bits):
    count = lax.axis_size(axes)
    return lax.ppermute(array, axes, [(i, i ^ bits) for i in range(count)])


BOTH = ("seq", "batch")


def after(array, *others):
    return lax.optimization_barrier((array,) + others)[0]


def by_line(a):
    return (a, (1,) + a.shape[1:], lambda i: (i,) + (0,) * (len(a.shape) - 1))


def by_line_out(*dims):
    return (shape(dims, BF16), (1,) + dims[1:], lambda i: (i,) + (0,) * (len(dims) - 1))


def core_exchange(pairs):
    return [(keep, swap(send, "batch", 1)) for keep, send in pairs]


FIRST, SECOND, FIRST_Z, SECOND_Z = (2, 4), (4, 2), (8, 16), (16, 8)


def cross(array, bits):
    count = lax.axis_size(BOTH)
    return lax.ppermute(array, BOTH, [(i, i ^ bits[i % 2]) for i in range(count)])


def pair_sum(pos, pairs):
    rows, lines = tuple(keep.shape[2] for keep, _ in pairs), pairs[0][0].shape[0] // 2
    view = lambda a: by_line(a.reshape((lines, 2, 2) + a.shape[2:]))
    return call(
        functools.partial(pair_sum_kernel, rows), lines,
        [whole(pos)] + [view(keep) for keep, _ in pairs] + [view(got) for _, got in pairs],
        [by_line_out(lines, 2, sum(rows), LANE)] * 2, [], 0, "pair_sum",
    )


def onward(parts, bits):
    return [parts[1], cross(parts[0], bits)]


def plane_sum(pos, parts):
    rows, lines = sum(part.shape[2] for part in parts[::2]), parts[0].shape[0]
    return call(
        plane_sum_kernel, lines, [whole(pos)] + [by_line(a) for a in parts], [by_line_out(lines, rows, LANE)] * 2, [], 0,
        "plane_sum",
    )


def line_sum(pos, parts):
    rows = sum(part.shape[1] for part in parts[::2])
    return call(
        line_sum_kernel, 1, [whole(pos)] + [whole(a) for a in parts], [whole_out((2, rows, LANE), BF16)] * 2, [], 0, "line_sum",
    )


def last_sum(pos, parts):
    rows = parts[0].shape[1]
    return call(
        last_sum_kernel, 1, [whole(pos)] + [whole(a) for a in parts], [whole_out((rows, LANE), BF16)] * 2, [], 0, "last_sum",
    )


SUMS = ((plane_sum, SECOND), (line_sum, FIRST_Z), (last_sum, SECOND_Z))


class Reduction:
    def __init__(self, pos, names, pairs):
        self.pos, self.names, self.stage = pos, names, 0
        self.parts = pair_sum(pos, pairs)
        self.seen = self.parts[0]
        self.parts = onward(self.parts, FIRST)

    def join(self, other):
        self.names, self.parts = self.names + other.names, self.parts + other.parts

    def step(self, *others):
        work, bits = SUMS[self.stage]
        if others:
            self.parts[0] = after(self.parts[0], *others)
        parts = work(self.pos, self.parts)
        self.stage, self.seen, self.parts = self.stage + 1, parts[0], onward(parts, bits)
        return self.seen

    def one_more(self, others, work, bits):
        if others:
            self.parts[0] = after(self.parts[0], *others)
        parts = work(self.pos, self.parts)
        self.seen, self.parts = parts[0], onward(parts, bits)
        return self.seen

    def total(self, *others):
        keep, got = self.parts
        keep = after(keep, *others)
        total = call(total_kernel, 1, [whole(keep), whole(got)], [whole_out(keep.shape)], [], 0, "total")
        self.parts = [total]
        return total


class UprightReduction(Reduction):
    def __init__(self, pos, names, pair):
        self.pos, self.names, self.stage = pos, names, 0
        self.rows = pair[0].shape[2]
        self.parts = [part.reshape(4, 4 * self.rows, LANE) for part in pair]
        self.one_more((), line_sum, FIRST_Z)

    def step(self, *others):
        self.stage += 1
        if self.stage == 1:
            return self.one_more(others, last_sum, SECOND_Z)
        if self.stage == 2:
            pairs = lambda pos, parts: pair_sum(pos, [tuple(part.reshape(2, 2, self.rows, LANE) for part in parts)])
            return self.one_more(others, pairs, FIRST)
        self.one_more(others, plane_sum, SECOND)
        self.parts = [part[0] for part in self.parts]
        return self.seen


def line_parts(own):
    return [own] + [swap(own, "seq", 2 * k) for k in range(1, 4)]


def line_gather(pos, parts, rows):
    return call(
        line_gather_kernel, 1, [whole(pos)] + [whole(far(p)) for p in parts],
        [whole_out((4, r, LANE), BF16) for r in rows], [], 2, "line_gather",
    )


X_AXIS, Y_AXIS = ("batch", 2), ("seq", 1)


def plane_gather(pos, line, parts, behind=()):
    rows = line.shape[1]
    parts = [line, *parts]
    parts += [swap(after(p, *behind) if behind else p, "batch", 1) for p in parts]
    each, low, high = (lambda i: (i, 0, 0)), (lambda i: (jnp.minimum(i, 1), 0, 0)), (lambda i: (jnp.maximum(i - 2, 0), 0, 0))
    maps = [each] * 4 if len(parts) == 8 else [each, each, each, low, high]
    got = call(
        plane_gather_kernel, 4, [whole(pos)] + [(far(p), (1, rows, LANE), m) for p, m in zip(parts, maps * 2)],
        [(shape((4, 2, 2, 2, rows, LANE), BF16), (1, 2, 2, 2, rows, LANE), lambda i: (i, 0, 0, 0, 0, 0))], [], 5, "plane_gather",
    )
    return got.reshape(NS, NB, rows, LANE)


def enter(fin, seqs, backward, fill=(), hold=None):
    count, mine = lax.axis_size("seq"), lax.axis_index("seq")
    prod, state = fin[:seqs], fin[seqs:]
    pre_p, pre_s = jnp.ones_like(prod), jnp.zeros_like(state)
    bit, message, done = 1, fin, []
    for step in range(int(count).bit_length() - 1):
        if hold and step in hold:
            message = after(message, *hold[step])
        other = lax.ppermute(message, "seq", [(i, i ^ bit) for i in range(count)])
        if step < len(fill):
            done.append(fill[step](message))
        o_p, o_s = other[:seqs], other[seqs:]
        upper = ((mine // bit) % 2 == 1) ^ backward
        pre_p, pre_s = jnp.where(upper, o_p * pre_p, pre_p), jnp.where(upper, pre_p * o_s + pre_s, pre_s)
        state = jnp.where(upper, prod * o_s + state, o_p * state + o_s)
        prod = prod * o_p
        message = jnp.concatenate([prod, state])
        if step < len(fill):
            message = after(message, *done[-1])
        bit *= 2
    return pre_s, done


def slabs(matrix, seq_count, batch_count):
    rows, cols = matrix.shape[0] // NS, matrix.shape[1] // NB
    cut = matrix.reshape(NS, rows, NB, cols // LANE, LANE).transpose(0, 2, 3, 1, 4)
    return cut.reshape(NS, NB, rows * cols // LANE, LANE)


def unslab(blocks, rows, cols):
    r, c = rows // NS, cols // NB
    cut = blocks.reshape(NS, NB, c // LANE, r, LANE).transpose(0, 3, 1, 2, 4)
    return cut.reshape(rows, cols)


def body(
    tokens, norm_gain, w_forget, w_input, w_cand, forget_bias, input_bias, w_out, mlp_gain, w_up, w_down, cotangent
):
    seqs, length, d = tokens.shape
    seq_count, batch_count = lax.axis_size("seq"), lax.axis_size("batch")
    h, ff = w_forget.shape[2] * batch_count, w_up.shape[2] * batch_count
    sz = Sizes(seqs, length, d, h, ff)
    standard = (seq_count, batch_count) == (NS, NB)
    matrices = {"u": w_up, "d": w_down, "o": w_out, "f": w_forget, "i": w_input, "c": w_cand}
    vectors = (norm_gain, forget_bias, input_bias, mlp_gain)
    slab_rows = {"u": d * ff // (32 * LANE), "d": ff // NS, "o": h // NS}
    slab_rows.update({m: d * h // (32 * LANE) for m in "fic"})
    order = {name: k for k, name in enumerate(matrices)}

    if standard:
        s_at, b_at = lax.axis_index("seq"), lax.axis_index("batch")
        core, x, y, z = b_at % 2, b_at // 2, s_at % 2, s_at // 2
        turned = [jnp.where(core == 0, a, b) for a, b in ((x, y), (y, x), (z % 2, z // 2), (z // 2, z % 2))]
        pos = jnp.stack([core, x, y, z, *turned]).astype(jnp.int32)
        vecs = [(6 + k, at, True) for at in range(LAYERS) for k in range(4)]
        groups = []
        for l in range(LAYERS):
            groups += [[(order[m], l, False) for m in "fic"] + vecs * (l == 0), [(order[m], l, False) for m in "udo"]]
        gate_rows, rest_rows = sum(slab_rows[m] for m in "fic"), sum(slab_rows[m] for m in "udo")
        rows = [gate_rows + 16, rest_rows] + [gate_rows, rest_rows] * (LAYERS - 1)
        packs = call(
            functools.partial(pack_kernel, groups), 1,
            [whole(far(m)) for m in matrices.values()] + [whole(far(v)) for v in vectors],
            [whole_out((r, LANE), BF16) for r in rows], [pltpu.VMEM((16, LANE), F32)], 2, "pack",
        )
        line_g0 = line_gather(pos, line_parts(packs[0]), rows[:1])
        parts_g0 = [swap(line_g0, *X_AXIS), swap(line_g0, *Y_AXIS)]
        parts_g0 += [swap(parts_g0[0][:2], *Y_AXIS), swap(parts_g0[1][2:], *X_AXIS)]
        line_r0 = line_gather(pos, line_parts(after(packs[1], line_g0)), rows[1:2])
        sent_r0 = after(line_r0, *parts_g0[:2])
        parts_r0 = [cross(sent_r0, FIRST), cross(sent_r0, SECOND)]
        line_g1 = line_gather(pos, line_parts(after(packs[2], line_r0)), rows[2:3])
        got = [plane_gather(pos, line_g0, parts_g0), None]
        places = {"f": 0, "i": 1, "c": 2, "u": 0, "d": 1, "o": 4}
        view = lambda got: {m: (got[m in "udo"], slab_rows[m], places[m]) for m in "udofic"}
        weights, lines_at, parts_at = [view(got)], [line_r0], [parts_r0]
        vecs = call(
            functools.partial(vector_kernel, None), 1,
            [(got[0], (NS, 1, 16, LANE), lambda i: (0, 0, 3 * slab_rows["f"] // 16, 0))],
            [whole_out((2, size)) for l in range(LAYERS) for size in (d, h)],
            [pltpu.VMEM((NS, 16, LANE), F32)], 1, "vectors",
        )
        gains, biases = vecs[0::2], vecs[1::2]
    else:
        pos = jnp.zeros((8,), jnp.int32)

        def full(m):
            m = lax.all_gather(m, "batch", axis=1, tiled=True)
            return lax.all_gather(m, "seq", axis=0, tiled=True)

        weights = [
            {m: (slabs(full(matrices[m][l]), NS, NB), slab_rows[m], 0) for m in "udofic"} for l in range(LAYERS)
        ]
        whole_vectors = [lax.all_gather(v, "seq", axis=1, tiled=True).astype(F32) for v in vectors]
        gains = [jnp.stack([whole_vectors[0][l], whole_vectors[3][l]]) for l in range(LAYERS)]
        biases = [jnp.stack([whole_vectors[1][l], whole_vectors[2][l]]) for l in range(LAYERS)]

    def to_rows(v):
        return v.reshape(seqs, CHUNKS, sz.steps, d).transpose(0, 2, 1, 3).reshape(sz.n, d)

    def from_rows(v):
        return v.reshape(seqs, sz.steps, CHUNKS, d).transpose(0, 2, 1, 3).reshape(seqs, length, d)

    stream, grad = to_rows(tokens), to_rows(cotangent)
    kept = []
    for l in range(LAYERS):
        save = (True,) if l + 1 < LAYERS else ()
        normed, decay, inflow, cand, f_f, f_i, f_c, cp, ch, fin = gate_forward(
            sz, stream, gains[l], biases[l], weights[l], (True,)
        )
        if standard:
            near, beside = parts_at[l]
            diagonal = cross(after(near, fin), SECOND)
            hold = {1: [line_g1] if l + 1 < LAYERS else [near], 2: [diagonal]}
            ent, _ = enter(fin, seqs, False, (), hold)
            rest = plane_gather(pos, lines_at[l], [near, beside, diagonal])
            weights[l] = view([weights[l]["f"][0], rest])
        else:
            ent, _ = enter(fin, seqs, False)
        hidden, hb, e, mid, n2, act, slope, result = mix_forward(
            sz, stream, gains[l], decay, inflow, cp, ch, ent, weights[l], l == LAYERS - 1, save
        )
        if standard and l + 1 < LAYERS:
            own, *others = line_parts(after(packs[2 * l + 3], ent))
            line_r = line_gather(pos, [after(own, result), *others], rows[2 * l + 3 : 2 * l + 4])
            sent_g = after(line_g1, diagonal)
            parts_g = [cross(sent_g, FIRST), cross(sent_g, SECOND), swap(sent_g, BOTH, 6)]
            sent_r = after(line_r, *parts_g)
            weights.append(view([plane_gather(pos, line_g1, parts_g, (result,)), None]))
            lines_at.append(line_r)
            parts_at.append([cross(sent_r, FIRST), cross(sent_r, SECOND)])
        kept.append((stream, normed, decay, cand, f_f, f_i, f_c, hidden, hb, e, mid, n2, act, slope))
        stream = result
    output = from_rows(stream)

    vector_grads, sums, pending = [None] * LAYERS, [], []
    above = None
    for l in reversed(range(LAYERS)):
        x, normed, decay, cand, f_f, f_i, f_c, hidden, hb, e, mid, n2, act, slope = kept[l]
        place = far if l + 1 < LAYERS else lambda a: a
        decay, cand, f_f, f_i, f_c, hidden = map(far, (decay, cand, f_f, f_i, f_c, hidden))
        mid, slope = place(mid), place(slope)
        gr, gpre, gmid, go, ggain_two, gh, cp, ca, fin = mlp_backward(sz, grad, gains[l], mid, slope, decay, weights[l])

        def up(message):
            if above:
                message = above_up.step(message)
            return up_weights(sz, pos, place(after(n2, message)), gpre)

        def down(message):
            if above:
                message = above.step(message)
            return row_weights(sz, pos, place(after(act, message)), gr, "down_weights")

        def out(message):
            if above:
                message = above_up.step(message)
            return row_weights(sz, pos, place(after(hb, message)), go, "out_weights")

        ent, pairs = enter(fin, seqs, True, (up, down, out))
        if standard:
            if above:
                pairs[2] = (after(pairs[2][0], above.step(pairs[2][0])), pairs[2][1])
            exchanged = core_exchange(pairs)
            if not above:
                upright = UprightReduction(pos, [(l, "u")], exchanged[0])
                gmid = after(gmid, upright.seen)
            mlp = Reduction(pos, [(l, "d"), (l, "o")], exchanged[1:])
            gmid = after(gmid, mlp.seen)
        final = []
        if l == 0 and standard:
            final = [(ggain_two, 3)]
            for at in range(1, LAYERS):
                final += [(v, 4 * at + row) for v, row in zip(vector_grads[at], (0, 1, 3))]
        *gate_pair, gbias, grad, ggain_one = gate_backward(
            sz, pos, x, gains[l], gmid, gh, decay, hidden, e, cand, f_f, f_i, f_c, cp, ca, ent, far(normed), weights[l],
            l == 0, final,
        )
        vector_grads[l] = (ggain_one, gbias, ggain_two)
        if not standard:
            pending.append((l, pairs + [gate_pair]))
            continue
        if above:
            mlp.step(above_up.step(above.step(gate_pair[0])))
            upright = UprightReduction(pos, [(l, "u")], (after(exchanged[0][0], mlp.seen), exchanged[0][1]))
            gate_pair[1] = after(gate_pair[1], upright.seen)
        names = [(l, m) for m in "fic"]
        if l == 0:
            names += [(at, k) for at in range(LAYERS) for k in range(4)]
        gates = Reduction(pos, names, core_exchange([gate_pair]))
        if l > 0:
            grad, above, above_up = after(grad, gates.seen), mlp, upright
            above.join(gates)
            continue
        gates.step()
        upright.step(above.total(gates.seen))
        mlp.join(gates)
        mlp.step(upright.step(above_up.total(upright.seen)))
        mlp.step(upright.step(mlp.seen))
        sums = [(one.names, one.parts) for one in (above, above_up, mlp, upright)]
    grad_tokens = from_rows(grad)

    if standard:
        layout, ins = [], []
        for names, parts in sums:
            pieces = [(order[m], l, False) if m in order else (6 + m, l, True) for l, m in names]
            layout.append((len(parts), pieces))
            ins += [whole(p) for p in parts]
        found = call(
            functools.partial(finish_kernel, layout), 1, ins,
            [whole_out(m.shape) for m in matrices.values()] + [whole_out(v.shape) for v in vectors], [], 3, "finish",
        )
        g_up, g_down, g_out, g_f, g_i, g_c, g_norm, g_fb, g_ib, g_mlp = found
    else:
        per_layer = {}
        for l, pairs in pending:
            blocks = [jnp.stack([keep, send], axis=2).reshape(NS, NB, -1, LANE) for keep, send in pairs]
            gates = jnp.split(blocks[3], 3, axis=2)
            for m, g in zip("udofic", blocks[:3] + gates):
                v = unslab(g, matrices[m].shape[1] * seq_count, matrices[m].shape[2] * batch_count)
                v = lax.psum_scatter(v, "seq", scatter_dimension=0, tiled=True)
                per_layer[m, l] = lax.psum_scatter(v, "batch", scatter_dimension=1, tiled=True).astype(F32)
        g_up, g_down, g_out, g_f, g_i, g_c = [
            jnp.stack([per_layer[m, l] for l in range(LAYERS)]) for m in matrices
        ]
        rows = [
            (ggain_one[0], gbias[0], gbias[1], ggain_two[0]) for ggain_one, gbias, ggain_two in vector_grads
        ]
        g_norm, g_fb, g_ib, g_mlp = [
            lax.psum(lax.psum_scatter(jnp.stack([r[k] for r in rows]), "seq", scatter_dimension=1, tiled=True), "batch")
            for k in range(4)
        ]
    return output, grad_tokens, g_norm, g_f, g_i, g_c, g_fb, g_ib, g_out, g_mlp, g_up, g_down


def solution(mesh):
    split, vector, matrix = P("batch", "seq", None), P(None, "seq"), P(None, "seq", "batch")
    order = (vector, matrix, matrix, matrix, vector, vector, matrix, vector, matrix, matrix)
    return jax.shard_map(
        body,
        mesh=mesh,
        in_specs=(split,) + order + (split,),
        out_specs=(split, split) + order,
        check_vma=False,
    )
```

```python
import functools

import jax
import jax.numpy as jnp
from jax import lax
from jax.experimental import pallas as pl
from jax.experimental.pallas import tpu as pltpu
from jax.sharding import PartitionSpec as P

LAYERS = 2
EPS = 1e-05
NS, NB, LANE = 8, 4, 128
CHUNKS = 8
STEPS = 2
GATE_STEPS = 4
TURN, WIDE = 2, 256
VMEM = 28 * 1024 * 1024
F32, BF16 = jnp.float32, jnp.bfloat16


def dot(left, right):
    return lax.dot_general(left, right, (((1,), (0,)), ((), ())), preferred_element_type=F32)


def dot_nt(left, right):
    return lax.dot_general(left, right, (((1,), (1,)), ((), ())), preferred_element_type=F32)


def dot_tn(left, right):
    return lax.dot_general(left, right, (((0,), (0,)), ((), ())), preferred_element_type=F32)


def columns_of(ref, slabs=2):
    rows = ref.shape[2] // slabs
    parts = [
        ref[:, b, j * rows : (j + 1) * rows, :].reshape(NS * rows, LANE) for b in range(ref.shape[1]) for j in range(slabs)
    ]
    return jnp.concatenate(parts, axis=1)


def rows_of(ref):
    parts = [ref[:, j].reshape(-1, LANE) for j in range(NB)]
    return jnp.concatenate(parts, axis=1)


def rms_scale(values):
    return lax.rsqrt(jnp.mean(values * values, axis=-1, keepdims=True) + EPS)


def rms_back(values, gain, grad):
    scale = rms_scale(values)
    unit = values * scale
    inner = grad * gain
    back = scale * (inner - unit * jnp.mean(inner * unit, axis=-1, keepdims=True))
    return back, jnp.sum(grad * unit, axis=0, keepdims=True)


def gate_kernel(
    seqs, steps, x_ref, gain_ref, bias_ref, wf_ref, wi_ref, wc_ref,
    normed_ref, decay_ref, inflow_ref, cand_ref, ff_ref, fi_ref, fc_ref, cp_ref, ch_ref, fin_ref,
    z,
):
    width = decay_ref.shape[1]

    @pl.when(pl.program_id(0) == 0)
    def _():
        x = x_ref[...].astype(F32)
        normed_ref[...] = (x * rms_scale(x) * gain_ref[0:1, :]).astype(BF16)

    weights = jnp.concatenate([columns_of(ref) for ref in (wf_ref, wi_ref, wc_ref)], axis=1)
    block = TURN * CHUNKS
    places = [(seq, left) for seq in range(seqs) for left in range(0, width, WIDE)]

    def turn(of, at, carry):
        carry = list(carry)
        for k, (seq, left) in enumerate(places):
            if seq != of:
                continue
            span = slice(seq * steps * CHUNKS + at * block, seq * steps * CHUNKS + (at + 1) * block)
            cols = slice(left, left + WIDE)
            f = z[span, cols] + bias_ref[0:1, cols]
            i = z[span, width + left : width + left + WIDE] + bias_ref[1:2, cols]
            c = z[span, 2 * width + left : 2 * width + left + WIDE]
            low = jnp.minimum(jnp.minimum(f, i), 0.0)
            e0, ef, ei = jnp.exp(low), jnp.exp(low - f), jnp.exp(low - i)
            a, b = e0 + ef, e0 + ei
            inv = 1.0 / (a + b)
            decay, other = b * inv, a * inv
            ec = jnp.exp(-jnp.abs(c))
            cand = jnp.maximum(c, 0.0) + jnp.log1p(ec)
            slope = jnp.where(c >= 0.0, 1.0, ec) / (1.0 + ec)
            inflow = other * cand
            decay_ref[span, cols] = decay
            inflow_ref[span, cols] = inflow
            cand_ref[span, cols] = cand
            ff_ref[span, cols] = (ef * inv * decay).astype(BF16)
            fi_ref[span, cols] = (ei * inv * other).astype(BF16)
            fc_ref[span, cols] = (other * slope).astype(BF16)
            prod, state = carry[2 * k], carry[2 * k + 1]
            for t in range(TURN):
                d = decay[t * CHUNKS : (t + 1) * CHUNKS]
                prod = prod * d
                state = state * d + inflow[t * CHUNKS : (t + 1) * CHUNKS]
            carry[2 * k], carry[2 * k + 1] = prod, state
        return tuple(carry)

    one, zero = jnp.ones((CHUNKS, WIDE), F32), jnp.zeros((CHUNKS, WIDE), F32)
    carry = (one, zero) * len(places)
    for seq in range(seqs):
        rows = slice(seq * steps * CHUNKS, (seq + 1) * steps * CHUNKS)
        z[rows, :] = dot(normed_ref[rows, :], weights)
        for at in range(steps // TURN):
            carry = turn(seq, at, carry)
    for k, (seq, left) in enumerate(places):
        prod, state = carry[2 * k], carry[2 * k + 1]
        cols = slice(left, left + WIDE)
        cp_ref[seq, :, cols], ch_ref[seq, :, cols] = prod, state
        whole, last = prod[0:1], state[0:1]
        for c in range(1, CHUNKS):
            whole, last = whole * prod[c : c + 1], last * prod[c : c + 1] + state[c : c + 1]
        fin_ref[seq : seq + 1, cols] = whole
        fin_ref[seqs + seq : seqs + seq + 1, cols] = last


def mix_kernel(
    seqs, steps, x_ref, gain_ref, decay_ref, inflow_ref, cp_ref, ch_ref, ent_ref, wo_ref, wu_ref, wd_ref,
    hidden_ref, hb_ref, e_ref, mid_ref, n2_ref, act_ref, slope_ref, out_ref,
    acc,
):
    at_step = pl.program_id(0)
    block = TURN * CHUNKS
    width = decay_ref.shape[1]
    places = [(seq, left) for seq in range(seqs) for left in range(0, width, WIDE)]

    @pl.when(at_step == 0)
    def _():
        acc[...] = x_ref[...].astype(F32)

    @pl.when(at_step < STEPS)
    def _():
        for seq in range(seqs):
            state = ent_ref[seq : seq + 1, :]
            for c in range(CHUNKS):
                e_ref[seq, c : c + 1, :] = state
                state = state * cp_ref[seq, c : c + 1, :] + ch_ref[seq, c : c + 1, :]

        def turn(at, carry):
            carry = list(carry)
            for k, (seq, left) in enumerate(places):
                span = pl.ds(pl.multiple_of(seq * steps * CHUNKS + at * block, block), block)
                cols = slice(left, left + WIDE)
                d, u = decay_ref[span, cols], inflow_ref[span, cols]
                state, found = carry[k], []
                for t in range(TURN):
                    state = state * d[t * CHUNKS : (t + 1) * CHUNKS] + u[t * CHUNKS : (t + 1) * CHUNKS]
                    found.append(state)
                carry[k] = state
                hidden = jnp.concatenate(found, axis=0)
                hidden_ref[span, cols] = hidden
                hb_ref[span, cols] = hidden.astype(BF16)
            return tuple(carry)

        lax.fori_loop(0, steps // TURN, turn, tuple(e_ref[seq, :, left : left + WIDE] for seq, left in places))
        acc[...] += dot(hb_ref[...], rows_of(wo_ref))

    @pl.when(at_step == STEPS - 1)
    def _():
        middle = acc[...]
        mid_ref[...] = middle
        n2_ref[...] = (middle * rms_scale(middle) * gain_ref[1:2, :]).astype(BF16)

    @pl.when(at_step >= STEPS)
    def _():
        w_up, w_down = columns_of(wu_ref, 4), rows_of(wd_ref)
        size = acc.shape[0] // 2
        for k in range(2):
            span = slice(k * size, (k + 1) * size)
            v = dot(n2_ref[span, :], w_up)
            phi = 0.5 + 0.5 * lax.erf(v * 0.7071067811865476)
            act = (v * phi).astype(BF16)
            act_ref[span, :] = act
            slope_ref[span, :] = (phi + v * (0.3989422804014327 * jnp.exp(v * v * -0.5))).astype(BF16)
            acc[span, :] += dot(act, w_down)

    @pl.when(at_step == 2 * STEPS - 1)
    def _():
        out_ref[...] = acc[...].astype(out_ref.dtype)


def mlp_back_kernel(
    seqs, steps, g_ref, gain_ref, mid_ref, slope_ref, decay_ref, wo_ref, wu_ref, wd_ref,
    gr_ref, gpre_ref, gmid_ref, go_ref, ggain_ref, gh_ref, cp_ref, ca_ref, fin_ref,
    acc,
):
    at_step = pl.program_id(0)
    block = TURN * CHUNKS
    width = decay_ref.shape[1]
    places = [(seq, left) for seq in range(seqs) for left in range(0, width, WIDE)]

    @pl.when(at_step == 0)
    def _():
        gr_ref[...] = g_ref[...].astype(BF16)
        acc[...] = jnp.zeros_like(acc)

    @pl.when(at_step < STEPS)
    def _():
        gact = dot_nt(gr_ref[...], rows_of(wd_ref))
        gpre_ref[...] = (gact * slope_ref[...].astype(F32)).astype(BF16)
        acc[...] += dot_nt(gpre_ref[...], columns_of(wu_ref, 4))

    @pl.when(at_step == STEPS - 1)
    def _():
        back, ggain = rms_back(mid_ref[...], gain_ref[1:2, :], acc[...])
        ggain_ref[...] = ggain
        gmid = g_ref[...].astype(F32) + back
        gmid_ref[...] = gmid
        go_ref[...] = gmid.astype(BF16)

    @pl.when(at_step >= STEPS)
    def _():
        gh_ref[...] = dot_nt(go_ref[...], rows_of(wo_ref))

        def turn(turn_at, carry):
            at = steps // TURN - 1 - turn_at
            carry = list(carry)
            for k, (seq, left) in enumerate(places):
                span = pl.ds(pl.multiple_of(seq * steps * CHUNKS + at * block, block), block)
                cols = slice(left, left + WIDE)
                d, g = decay_ref[span, cols], gh_ref[span, cols]
                prod, state = carry[2 * k], carry[2 * k + 1]
                for t in reversed(range(TURN)):
                    dk = d[t * CHUNKS : (t + 1) * CHUNKS]
                    prod = prod * dk
                    state = dk * (g[t * CHUNKS : (t + 1) * CHUNKS] + state)
                carry[2 * k], carry[2 * k + 1] = prod, state
            return tuple(carry)

        one, zero = jnp.ones((CHUNKS, WIDE), F32), jnp.zeros((CHUNKS, WIDE), F32)
        carry = lax.fori_loop(0, steps // TURN, turn, (one, zero) * len(places))
        for k, (seq, left) in enumerate(places):
            prod, state = carry[2 * k], carry[2 * k + 1]
            cols = slice(left, left + WIDE)
            cp_ref[seq, :, cols], ca_ref[seq, :, cols] = prod, state
            whole, last = prod[CHUNKS - 1 :], state[CHUNKS - 1 :]
            for c in reversed(range(CHUNKS - 1)):
                whole, last = whole * prod[c : c + 1], last * prod[c : c + 1] + state[c : c + 1]
            fin_ref[seq : seq + 1, cols] = whole
            fin_ref[seqs + seq : seqs + seq + 1, cols] = last


def gate_back_kernel(
    seqs, steps, others, pos_ref, x_ref, gain_ref, gmid_ref, gh_ref, decay_ref, hidden_ref, e_ref, cand_ref,
    ff_ref, fi_ref, fc_ref, cp_ref, ca_ref, ent_ref, normed_ref, wf_ref, wi_ref, wc_ref, *refs,
):
    given = refs[: len(others)]
    keep_ref, send_ref, gbias_ref, gstream_ref, ggain_ref, acc, start, dz, rest = refs[len(others) :]
    at_step = pl.program_id(0)
    block = TURN * CHUNKS
    width = decay_ref.shape[1]
    places = [(seq, left) for seq in range(seqs) for left in range(0, width, WIDE)]

    @pl.when(at_step == 0)
    def _():
        acc[...] = jnp.zeros_like(acc)

    for seq in range(seqs):
        state = ent_ref[seq : seq + 1, :]
        for c in reversed(range(CHUNKS)):
            start[seq, c : c + 1, :] = state
            state = state * cp_ref[seq, c : c + 1, :] + ca_ref[seq, c : c + 1, :]

    def turn(of, at, carry):
        carry = list(carry)
        for k, (seq, left) in enumerate(places):
            if seq != of:
                continue
            cols = slice(left, left + WIDE)
            state, sum_f, sum_i = carry[3 * k : 3 * k + 3]
            base = seq * steps * CHUNKS + at * block
            span = slice(base, base + block)
            before = hidden_ref[base - CHUNKS : base, cols] if at else e_ref[seq, :, cols]
            d, g = decay_ref[span, cols], gh_ref[span, cols]
            previous = jnp.concatenate([before, hidden_ref[span, cols][: block - CHUNKS]], axis=0)
            found = []
            for t in reversed(range(TURN)):
                now = g[t * CHUNKS : (t + 1) * CHUNKS] + state
                found.append(now)
                state = d[t * CHUNKS : (t + 1) * CHUNKS] * now
            gstate = jnp.concatenate(found[::-1], axis=0)
            both = gstate * (cand_ref[span, cols] - previous)
            dzf = (-ff_ref[span, cols].astype(F32) * both).astype(BF16)
            dzi = (fi_ref[span, cols].astype(F32) * both).astype(BF16)
            dz[span, left : left + WIDE] = dzf
            dz[span, width + left : width + left + WIDE] = dzi
            dz[span, 2 * width + left : 2 * width + left + WIDE] = (fc_ref[span, cols].astype(F32) * gstate).astype(BF16)
            wide_f, wide_i = dzf.astype(F32), dzi.astype(F32)
            for t in range(TURN):
                sum_f = sum_f + wide_f[t * CHUNKS : (t + 1) * CHUNKS]
                sum_i = sum_i + wide_i[t * CHUNKS : (t + 1) * CHUNKS]
            carry[3 * k : 3 * k + 3] = state, sum_f, sum_i
        return tuple(carry)

    zero = jnp.zeros((CHUNKS, WIDE), F32)
    first_carry = [v for seq, left in places for v in (start[seq, :, left : left + WIDE], zero, zero)]
    carry = tuple(first_carry)
    weights = jnp.concatenate([columns_of(ref) for ref in (wf_ref, wi_ref, wc_ref)], axis=1)
    grad = None
    for seq in range(seqs):
        rows = slice(seq * steps * CHUNKS, (seq + 1) * steps * CHUNKS)
        for at in reversed(range(steps // TURN)):
            carry = turn(seq, at, carry)
        acc[rows, :] += dot_nt(dz[rows, :], weights)
        part = dot_tn(normed_ref[rows, :], dz[rows, :])
        grad = part if grad is None else grad + part
    for row in range(2):
        for left in range(0, width, WIDE):
            total = sum(carry[3 * k + 1 + row] for k, place in enumerate(places) if place[1] == left)
            gbias_ref[row : row + 1, left : left + WIDE] = jnp.sum(total, axis=0, keepdims=True)
    rows = wf_ref.shape[2]
    for m in range(3):
        put_columns(pos_ref, keep_ref, send_ref, m * rows, grad[:, m * width : (m + 1) * width])

    @pl.when(at_step == STEPS - 1)
    def _():
        back, ggain = rms_back(x_ref[...].astype(F32), gain_ref[0:1, :], acc[...])
        ggain_ref[...] = ggain
        gstream_ref[...] = (gmid_ref[...] + back).astype(gstream_ref.dtype)

    if others:

        def rows_to(ref, first_row):
            wide = ref.shape[1] // NS
            for r in range(ref.shape[0]):
                for s in range(NS):
                    rest[s, first_row + r : first_row + r + 1, :wide] = ref[r : r + 1, s * wide : (s + 1) * wide]

        @pl.when(at_step == 0)
        def _():
            rest[...] = jnp.zeros_like(rest)
            for ref, first_row in zip(given, others):
                rows_to(ref, first_row)

        wide = width * STEPS // NS
        for row in range(2):
            for s in range(width // wide):
                rest[at_step * (width // wide) + s, 1 + row : 2 + row, :wide] = gbias_ref[row : row + 1, s * wide : (s + 1) * wide]

        @pl.when(at_step == STEPS - 1)
        def _():
            rows_to(ggain_ref, 0)
            found = rest[...].astype(BF16)
            for x in range(2):
                keep_ref[:, x, 3 * rows :, :] = found
                send_ref[:, x, 3 * rows :, :] = found


def send_or_keep(mine, keep_ref, send_ref, put):
    @pl.when(mine)
    def _():
        put(keep_ref)

    @pl.when(jnp.logical_not(mine))
    def _():
        put(send_ref)


def put_columns(pos_ref, keep_ref, send_ref, start, value):
    rows, width = value.shape[0] // NS, value.shape[1] // 2
    x = pl.program_id(0)
    for core in range(2):
        parts = [
            value[:, left : left + LANE].astype(BF16).reshape(NS, rows, LANE)
            for left in range(core * width, (core + 1) * width, LANE)
        ]

        def put(ref):
            for j, part in enumerate(parts):
                ref[:, x, start + j * rows : start + (j + 1) * rows, :] = part

        send_or_keep(pos_ref[0] == core, keep_ref, send_ref, put)


def put_rows(pos_ref, keep_ref, send_ref, value):
    count = NS // STEPS
    for j in range(NB):
        part = value[:, j * LANE : (j + 1) * LANE].astype(BF16).reshape(count, -1, LANE)

        def put(ref):
            ref[pl.ds(pl.program_id(0) * count, count), j // 2] = part

        send_or_keep(pos_ref[0] == j % 2, keep_ref, send_ref, put)


def up_weight_kernel(pos_ref, n2_ref, gpre_ref, keep_ref, send_ref):
    put_columns(pos_ref, keep_ref, send_ref, 0, dot_tn(n2_ref[...], gpre_ref[...]))


def row_weight_kernel(pos_ref, left_ref, right_ref, keep_ref, send_ref):
    put_rows(pos_ref, keep_ref, send_ref, dot_tn(left_ref[...], right_ref[...]))


def add(*parts):
    total = parts[0].astype(F32)
    for part in parts[1:]:
        total = total + part.astype(F32)
    return total


def pair_sum_kernel(rows, pos_ref, *refs):
    count = len(rows)
    send, stay = refs[2 * count :]
    core, x, y, step = pos_ref[0], pos_ref[1], pos_ref[2], pos_ref[4]
    at = 0
    for keep, got, r in zip(refs[:count], refs[count : 2 * count], rows):
        for v in range(2):
            for out, first in ((send, 1 - step), (stay, step)):
                iy, ix = jnp.where(core == 0, v, first), jnp.where(core == 0, first, v)
                out[0, v, at : at + r] = add(keep[0, iy, ix], got[0, iy, ix]).astype(BF16)
        at += r


def plane_sum_kernel(pos_ref, *refs):
    second = pos_ref[5]
    *pairs, send, stay = refs
    at = 0
    for keep, got in zip(pairs[::2], pairs[1::2]):
        rows = slice(at, at + keep.shape[2])
        send[0, rows, :] = add(keep[0, 1 - second], got[0, 1 - second]).astype(BF16)
        stay[0, rows, :] = add(keep[0, second], got[0, second]).astype(BF16)
        at += keep.shape[2]


def line_sum_kernel(pos_ref, *refs):
    core, first = pos_ref[0], pos_ref[6]
    *pairs, send, stay = refs
    at = 0
    for keep, got in zip(pairs[::2], pairs[1::2]):
        rows = slice(at, at + keep.shape[1])
        for v in range(2):
            for out, f in ((send, 1 - first), (stay, first)):
                z = jnp.where(core == 0, f + 2 * v, 2 * f + v)
                out[v, rows, :] = add(keep[z], got[z]).astype(BF16)
        at += keep.shape[1]


def last_sum_kernel(pos_ref, keep, got, send, stay):
    second = pos_ref[7]
    send[...] = add(keep[1 - second], got[1 - second]).astype(BF16)
    stay[...] = add(keep[second], got[second]).astype(BF16)


def total_kernel(keep, got, out):
    out[...] = add(keep[...], got[...])


def finish_kernel(layout, *refs):
    at = 0
    ins = sum(parts for parts, _ in layout)
    outs = refs[ins:]
    for parts, pieces in layout:
        got = refs[at : at + parts]
        at += parts
        row = 0
        for out, layer, vectors in pieces:
            ref = outs[out]
            if vectors:
                ref[layer : layer + 1, :] = add(*[g[...] for g in got])[row : row + 1, : ref.shape[1]]
                row += 1
                continue
            r = ref.shape[1]
            for j in range(ref.shape[2] // LANE):
                ref[layer, :, j * LANE : (j + 1) * LANE] = add(*[g[row : row + r] for g in got])
                row += r


def pack_kernel(groups, *refs):
    ins = refs[: len(refs) - len(groups) - 1]
    outs, scratch = refs[len(ins) : -1], refs[-1]
    for out, group in zip(outs, groups):
        row = 0
        vec = 0
        for which, layer, vector in group:
            ref = ins[which]
            if vector:
                if vec == 0:
                    scratch[...] = jnp.zeros_like(scratch)
                scratch[vec : vec + 1, : ref.shape[1]] = ref[...].astype(F32)[layer : layer + 1]
                vec += 1
                continue
            r = ref.shape[1]
            for j in range(ref.shape[2] // LANE):
                out[row : row + r, :] = ref[layer, :, j * LANE : (j + 1) * LANE]
                row += r
        if vec:
            out[row:, :] = scratch[...].astype(BF16)


def line_gather_kernel(pos_ref, *refs):
    row = 0
    for out in refs[4:]:
        rows = out.shape[1]
        for k, part in enumerate(refs[:4]):
            out[pos_ref[3] ^ k] = part[row : row + rows, :]
        row += rows


def plane_gather_kernel(pos_ref, *refs):
    out = refs[-1]
    at, half = pl.program_id(0), pl.num_programs(0) // 2
    core, x, y = pos_ref[0], pos_ref[1], pos_ref[2]
    count = len(refs) // 2
    for c in range(2):
        own, first, second, *diagonal = refs[count * c : count * (c + 1)]
        other = core ^ c
        turn = other if count == 4 else 0
        out[0, y, x, other] = own[0]
        out[0, y ^ turn, x ^ (1 - turn), other] = first[0]
        out[0, y ^ (1 - turn), x ^ turn, other] = second[0]
        if count == 4:
            out[0, y ^ 1, x ^ 1, other] = diagonal[0][0]
            continue

        @pl.when(at < half)
        def _():
            out[0, y ^ 1, x ^ 1, other] = diagonal[0][0]

        @pl.when(at >= half)
        def _():
            out[0, y ^ 1, x ^ 1, other] = diagonal[1][0]


def vector_kernel(gained, w_ref, *refs):
    outs, scratch = refs[:-1], refs[-1]
    scratch[...] = w_ref[:, 0].astype(F32)
    for l in range(LAYERS):
        for which in range(4):
            out, row = ((outs[2 * l], which // 3) if which in (0, 3) else (outs[2 * l + 1], which - 1))
            wide = out.shape[1] // NS
            for s in range(NS):
                out[row : row + 1, s * wide : (s + 1) * wide] = scratch[s, 4 * l + which : 4 * l + which + 1, :wide]


def shape(dims, dtype=F32):
    return jax.ShapeDtypeStruct(dims, dtype)


def call(kernel, grid, ins, outs, scratch, us, name):
    def spec(a, block, index):
        if a.dtype == jnp.int32:
            return pl.BlockSpec(memory_space=pltpu.SMEM)
        return pl.BlockSpec(block, index)

    found = pl.pallas_call(
        kernel,
        grid=(grid,),
        in_specs=[spec(*one) for one in ins],
        out_specs=[pl.BlockSpec(block, index) for _, block, index, *_ in outs],
        out_shape=[pltpu.HBM(one[0].shape, one[0].dtype) if one[3:] else one[0] for one in outs],
        scratch_shapes=scratch,
        compiler_params=pltpu.CompilerParams(vmem_limit_bytes=VMEM),
        cost_estimate=pl.CostEstimate(flops=int(us * 1.1e9) + 1, bytes_accessed=1024, transcendentals=0),
        name=name,
    )(*[a for a, _, _ in ins])
    return found if len(found) > 1 else found[0]


def far(array):
    return pltpu.with_memory_space_constraint(array, pltpu.HBM)


def whole(array):
    dims = array.shape
    return (array, dims, lambda i: (0,) * len(dims))


def whole_out(dims, dtype=F32):
    return (shape(dims, dtype), dims, lambda i: (0,) * len(dims))


def first(i):
    return jnp.minimum(i, STEPS - 1)


def second(i):
    return jnp.maximum(i - STEPS, 0)


class Sizes:
    def __init__(self, seqs, length, d, h, ff):
        self.seqs, self.steps, self.n = seqs, length // CHUNKS, seqs * length
        self.d, self.h, self.ff = d, h, ff
        self.hb, self.fb = h // STEPS, ff // STEPS


def column_weight(view, at, late=False, steps=STEPS):
    array, rows, place = view
    return (far(array) if late else array, (NS, NB // steps, rows, LANE), lambda i: (0, at(i), place, 0))


def row_weight(view, at):
    array, rows, place = view
    return (array, (NS // STEPS, NB, rows, LANE), lambda i: (at(i), 0, place, 0))


def same(i):
    return i


def gate_forward(sz, x, gain, bias, w, save):
    n, d, h, wide, s = sz.n, sz.d, sz.h, sz.h // GATE_STEPS, sz.seqs
    col = lambda i: (0, i)
    return call(
        functools.partial(gate_kernel, s, sz.steps), GATE_STEPS,
        [whole(x), whole(gain), (bias, (2, wide), col)] + [column_weight(w[m], same, False, GATE_STEPS) for m in "fic"],
        [whole_out((n, d), BF16) + save]
        + [(shape((n, h)), (n, wide), col) + save, (shape((n, h)), (n, wide), col), (shape((n, h)), (n, wide), col) + save]
        + [(shape((n, h), BF16), (n, wide), col) + save] * 3
        + [(shape((s, CHUNKS, h)), (s, CHUNKS, wide), lambda i: (0, 0, i))] * 2
        + [(shape((2 * s, h)), (2 * s, wide), col)],
        [pltpu.VMEM((n, 3 * wide), F32)], 9, "gates",
    )


def mix_forward(sz, x, gain, decay, inflow, cp, ch, ent, wt, last, save):
    n, d, h, ff, w, f, s = sz.n, sz.d, sz.h, sz.ff, sz.hb, sz.fb, sz.seqs
    col = lambda i: (0, first(i))
    late = lambda i: (0, second(i))
    deep = lambda i: (0, 0, first(i))
    return call(
        functools.partial(mix_kernel, s, sz.steps), 2 * STEPS,
        [
            whole(x), whole(gain), (decay, (n, w), col), (inflow, (n, w), col),
            (cp, (s, CHUNKS, w), deep), (ch, (s, CHUNKS, w), deep), (ent, (s, w), col),
            row_weight(wt["o"], first), column_weight(wt["u"], second), row_weight(wt["d"], second),
        ],
        [
            (shape((n, h)), (n, w), col, True), (shape((n, h), BF16), (n, w), col) + save,
            (shape((s, CHUNKS, h)), (s, CHUNKS, w), deep) + save,
            whole_out((n, d)) + save, whole_out((n, d), BF16) + save,
            (shape((n, ff), BF16), (n, f), late) + save, (shape((n, ff), BF16), (n, f), late) + save,
            whole_out((n, d), BF16 if last else F32),
        ],
        [pltpu.VMEM((n, d), F32)], 14, "mix",
    )


def mlp_backward(sz, g, gain, mid, slope, decay, wt):
    n, d, h, ff, w, f, s = sz.n, sz.d, sz.h, sz.ff, sz.hb, sz.fb, sz.seqs
    col = lambda i: (0, second(i))
    early = lambda i: (0, first(i))
    deep = lambda i: (0, 0, second(i))
    return call(
        functools.partial(mlp_back_kernel, s, sz.steps), 2 * STEPS,
        [
            whole(g), whole(gain), whole(mid), (slope, (n, f), early), (decay, (n, w), col),
            row_weight(wt["o"], second), column_weight(wt["u"], first), row_weight(wt["d"], first),
        ],
        [
            whole_out((n, d), BF16), (shape((n, ff), BF16), (n, f), early), whole_out((n, d)), whole_out((n, d), BF16),
            whole_out((1, d)), (shape((n, h)), (n, w), col),
            (shape((s, CHUNKS, h)), (s, CHUNKS, w), deep), (shape((s, CHUNKS, h)), (s, CHUNKS, w), deep),
            (shape((2 * s, h)), (2 * s, w), col),
        ],
        [pltpu.VMEM((n, d), F32)], 12, "mlp_back",
    )


def gate_backward(sz, pos, x, gain, gmid, gh, decay, hidden, e, cand, ff_, fi_, fc_, cp, ca, ent, normed, wt, last, vectors):
    n, d, h, w, s = sz.n, sz.d, sz.h, sz.hb, sz.seqs
    col = lambda i: (0, i)
    deep = lambda i: (0, 0, i)
    wide = lambda a: (a, (n, w), col)
    rows = 3 * d * h // (32 * LANE) + (16 if vectors else 0)
    return call(
        functools.partial(gate_back_kernel, s, sz.steps, tuple(row for _, row in vectors)), STEPS,
        [
            whole(pos), whole(x), whole(gain), whole(gmid), wide(gh), wide(decay), wide(hidden), (e, (s, CHUNKS, w), deep),
            wide(cand), wide(ff_), wide(fi_), wide(fc_), (cp, (s, CHUNKS, w), deep), (ca, (s, CHUNKS, w), deep),
            (ent, (s, w), col), whole(normed),
        ] + [column_weight(wt[m], same, True) for m in "fic"] + [whole(v) for v, _ in vectors],
        [whole_out((NS, 2, rows, LANE), BF16)] * 2
        + [(shape((2, h)), (2, w), col), whole_out((n, d), BF16 if last else F32), whole_out((1, d))],
        [
            pltpu.VMEM((n, d), F32), pltpu.VMEM((s, CHUNKS, w), F32), pltpu.VMEM((n, 3 * w), BF16),
            pltpu.VMEM((NS, 16, LANE), F32),
        ], 16, "gate_back",
    )


def up_weights(sz, pos, n2, gpre):
    n, d, ff, f = sz.n, sz.d, sz.ff, sz.fb
    dims = (NS, 2, d * ff // (32 * LANE), LANE)
    return call(
        up_weight_kernel, STEPS, [whole(pos), whole(n2), (gpre, (n, f), lambda i: (0, i))],
        [whole_out(dims, BF16)] * 2, [], 5, "up_weights",
    )


def row_weights(sz, pos, left, right, name):
    n, k, d = sz.n, left.shape[1], sz.d
    dims = (NS, 2, k // NS, LANE)
    return call(
        row_weight_kernel, STEPS, [whole(pos), (left, (n, k // STEPS), lambda i: (0, i)), whole(right)],
        [whole_out(dims, BF16)] * 2, [], 5, name,
    )


def swap(array, axes, bits):
    count = lax.axis_size(axes)
    return lax.ppermute(array, axes, [(i, i ^ bits) for i in range(count)])


BOTH = ("seq", "batch")


def after(array, *others):
    return lax.optimization_barrier((array,) + others)[0]


def by_line(a):
    return (a, (1,) + a.shape[1:], lambda i: (i,) + (0,) * (len(a.shape) - 1))


def by_line_out(*dims):
    return (shape(dims, BF16), (1,) + dims[1:], lambda i: (i,) + (0,) * (len(dims) - 1))


def core_exchange(pairs):
    return [(keep, swap(send, "batch", 1)) for keep, send in pairs]


FIRST, SECOND, FIRST_Z, SECOND_Z = (2, 4), (4, 2), (8, 16), (16, 8)


def cross(array, bits):
    count = lax.axis_size(BOTH)
    return lax.ppermute(array, BOTH, [(i, i ^ bits[i % 2]) for i in range(count)])


def pair_sum(pos, pairs):
    rows, lines = tuple(keep.shape[2] for keep, _ in pairs), pairs[0][0].shape[0] // 2
    view = lambda a: by_line(a.reshape((lines, 2, 2) + a.shape[2:]))
    return call(
        functools.partial(pair_sum_kernel, rows), lines,
        [whole(pos)] + [view(keep) for keep, _ in pairs] + [view(got) for _, got in pairs],
        [by_line_out(lines, 2, sum(rows), LANE)] * 2, [], 0, "pair_sum",
    )


def onward(parts, bits):
    return [parts[1], cross(parts[0], bits)]


def plane_sum(pos, parts):
    rows, lines = sum(part.shape[2] for part in parts[::2]), parts[0].shape[0]
    return call(
        plane_sum_kernel, lines, [whole(pos)] + [by_line(a) for a in parts], [by_line_out(lines, rows, LANE)] * 2, [], 0,
        "plane_sum",
    )


def line_sum(pos, parts):
    rows = sum(part.shape[1] for part in parts[::2])
    return call(
        line_sum_kernel, 1, [whole(pos)] + [whole(a) for a in parts], [whole_out((2, rows, LANE), BF16)] * 2, [], 0, "line_sum",
    )


def last_sum(pos, parts):
    rows = parts[0].shape[1]
    return call(
        last_sum_kernel, 1, [whole(pos)] + [whole(a) for a in parts], [whole_out((rows, LANE), BF16)] * 2, [], 0, "last_sum",
    )


SUMS = ((plane_sum, SECOND), (line_sum, FIRST_Z), (last_sum, SECOND_Z))


class Reduction:
    def __init__(self, pos, names, pairs):
        self.pos, self.names, self.stage = pos, names, 0
        self.parts = pair_sum(pos, pairs)
        self.seen = self.parts[0]
        self.parts = onward(self.parts, FIRST)

    def join(self, other):
        self.names, self.parts = self.names + other.names, self.parts + other.parts

    def step(self, *others):
        work, bits = SUMS[self.stage]
        if others:
            self.parts[0] = after(self.parts[0], *others)
        parts = work(self.pos, self.parts)
        self.stage, self.seen, self.parts = self.stage + 1, parts[0], onward(parts, bits)
        return self.seen

    def one_more(self, others, work, bits):
        if others:
            self.parts[0] = after(self.parts[0], *others)
        parts = work(self.pos, self.parts)
        self.seen, self.parts = parts[0], onward(parts, bits)
        return self.seen

    def total(self, *others):
        keep, got = self.parts
        keep = after(keep, *others)
        total = call(total_kernel, 1, [whole(keep), whole(got)], [whole_out(keep.shape)], [], 0, "total")
        self.parts = [total]
        return total


class UprightReduction(Reduction):
    def __init__(self, pos, names, pair):
        self.pos, self.names, self.stage = pos, names, 0
        self.rows = pair[0].shape[2]
        self.parts = [part.reshape(4, 4 * self.rows, LANE) for part in pair]
        self.one_more((), line_sum, FIRST_Z)

    def step(self, *others):
        self.stage += 1
        if self.stage == 1:
            return self.one_more(others, last_sum, SECOND_Z)
        if self.stage == 2:
            pairs = lambda pos, parts: pair_sum(pos, [tuple(part.reshape(2, 2, self.rows, LANE) for part in parts)])
            return self.one_more(others, pairs, FIRST)
        self.one_more(others, plane_sum, SECOND)
        self.parts = [part[0] for part in self.parts]
        return self.seen


def line_parts(own):
    return [own] + [swap(own, "seq", 2 * k) for k in range(1, 4)]


def line_gather(pos, parts, rows):
    return call(
        line_gather_kernel, 1, [whole(pos)] + [whole(far(p)) for p in parts],
        [whole_out((4, r, LANE), BF16) for r in rows], [], 2, "line_gather",
    )


X_AXIS, Y_AXIS = ("batch", 2), ("seq", 1)


def plane_gather(pos, line, parts, behind=()):
    rows = line.shape[1]
    parts = [line, *parts]
    parts += [swap(after(p, *behind) if behind else p, "batch", 1) for p in parts]
    each, low, high = (lambda i: (i, 0, 0)), (lambda i: (jnp.minimum(i, 1), 0, 0)), (lambda i: (jnp.maximum(i - 2, 0), 0, 0))
    maps = [each] * 4 if len(parts) == 8 else [each, each, each, low, high]
    got = call(
        plane_gather_kernel, 4, [whole(pos)] + [(far(p), (1, rows, LANE), m) for p, m in zip(parts, maps * 2)],
        [(shape((4, 2, 2, 2, rows, LANE), BF16), (1, 2, 2, 2, rows, LANE), lambda i: (i, 0, 0, 0, 0, 0))], [], 5, "plane_gather",
    )
    return got.reshape(NS, NB, rows, LANE)


def enter(fin, seqs, backward, fill=(), hold=None):
    count, mine = lax.axis_size("seq"), lax.axis_index("seq")
    prod, state = fin[:seqs], fin[seqs:]
    pre_p, pre_s = jnp.ones_like(prod), jnp.zeros_like(state)
    bit, message, done, other = 1, fin, [], fin
    for step in range(int(count).bit_length() - 1):
        before = hold(step, other) if hold else ()
        if before:
            message = after(message, *before)
        other = lax.ppermute(message, "seq", [(i, i ^ bit) for i in range(count)])
        if step < len(fill):
            done.append(fill[step](message))
        o_p, o_s = other[:seqs], other[seqs:]
        upper = ((mine // bit) % 2 == 1) ^ backward
        pre_p, pre_s = jnp.where(upper, o_p * pre_p, pre_p), jnp.where(upper, pre_p * o_s + pre_s, pre_s)
        state = jnp.where(upper, prod * o_s + state, o_p * state + o_s)
        prod = prod * o_p
        message = jnp.concatenate([prod, state])
        if step < len(fill):
            message = after(message, *done[-1])
        bit *= 2
    return pre_s, done


def slabs(matrix, seq_count, batch_count):
    rows, cols = matrix.shape[0] // NS, matrix.shape[1] // NB
    cut = matrix.reshape(NS, rows, NB, cols // LANE, LANE).transpose(0, 2, 3, 1, 4)
    return cut.reshape(NS, NB, rows * cols // LANE, LANE)


def unslab(blocks, rows, cols):
    r, c = rows // NS, cols // NB
    cut = blocks.reshape(NS, NB, c // LANE, r, LANE).transpose(0, 3, 1, 2, 4)
    return cut.reshape(rows, cols)


def body(
    tokens, norm_gain, w_forget, w_input, w_cand, forget_bias, input_bias, w_out, mlp_gain, w_up, w_down, cotangent
):
    seqs, length, d = tokens.shape
    seq_count, batch_count = lax.axis_size("seq"), lax.axis_size("batch")
    h, ff = w_forget.shape[2] * batch_count, w_up.shape[2] * batch_count
    sz = Sizes(seqs, length, d, h, ff)
    standard = (seq_count, batch_count) == (NS, NB)
    matrices = {"u": w_up, "d": w_down, "o": w_out, "f": w_forget, "i": w_input, "c": w_cand}
    vectors = (norm_gain, forget_bias, input_bias, mlp_gain)
    slab_rows = {"u": d * ff // (32 * LANE), "d": ff // NS, "o": h // NS}
    slab_rows.update({m: d * h // (32 * LANE) for m in "fic"})
    order = {name: k for k, name in enumerate(matrices)}

    if standard:
        s_at, b_at = lax.axis_index("seq"), lax.axis_index("batch")
        core, x, y, z = b_at % 2, b_at // 2, s_at % 2, s_at // 2
        turned = [jnp.where(core == 0, a, b) for a, b in ((x, y), (y, x), (z % 2, z // 2), (z // 2, z % 2))]
        pos = jnp.stack([core, x, y, z, *turned]).astype(jnp.int32)
        vecs = [(6 + k, at, True) for at in range(LAYERS) for k in range(4)]
        groups = []
        for l in range(LAYERS):
            groups += [[(order[m], l, False) for m in "fic"] + vecs * (l == 0), [(order[m], l, False) for m in "udo"]]
        gate_rows, rest_rows = sum(slab_rows[m] for m in "fic"), sum(slab_rows[m] for m in "udo")
        rows = [gate_rows + 16, rest_rows] + [gate_rows, rest_rows] * (LAYERS - 1)
        packs = call(
            functools.partial(pack_kernel, groups), 1,
            [whole(far(m)) for m in matrices.values()] + [whole(far(v)) for v in vectors],
            [whole_out((r, LANE), BF16) for r in rows], [pltpu.VMEM((16, LANE), F32)], 2, "pack",
        )
        line_g0 = line_gather(pos, line_parts(packs[0]), rows[:1])
        parts_g0 = [swap(line_g0, *X_AXIS), swap(line_g0, *Y_AXIS)]
        parts_g0 += [swap(parts_g0[0][:2], *Y_AXIS), swap(parts_g0[1][2:], *X_AXIS)]
        line_r0 = line_gather(pos, line_parts(after(packs[1], line_g0)), rows[1:2])
        sent_r0 = after(line_r0, *parts_g0[:2])
        parts_r0 = [cross(sent_r0, FIRST), cross(sent_r0, SECOND)]
        parts_g1 = line_parts(after(packs[2], line_r0, *parts_g0[2:]))
        got = [plane_gather(pos, line_g0, parts_g0), None]
        places = {"f": 0, "i": 1, "c": 2, "u": 0, "d": 1, "o": 4}
        view = lambda got: {m: (got[m in "udo"], slab_rows[m], places[m]) for m in "udofic"}
        weights, lines_at, parts_at = [view(got)], [line_r0], [parts_r0]
        vecs = call(
            functools.partial(vector_kernel, None), 1,
            [(got[0], (NS, 1, 16, LANE), lambda i: (0, 0, 3 * slab_rows["f"] // 16, 0))],
            [whole_out((2, size)) for l in range(LAYERS) for size in (d, h)],
            [pltpu.VMEM((NS, 16, LANE), F32)], 1, "vectors",
        )
        gains, biases = vecs[0::2], vecs[1::2]
    else:
        pos = jnp.zeros((8,), jnp.int32)

        def full(m):
            m = lax.all_gather(m, "batch", axis=1, tiled=True)
            return lax.all_gather(m, "seq", axis=0, tiled=True)

        weights = [
            {m: (slabs(full(matrices[m][l]), NS, NB), slab_rows[m], 0) for m in "udofic"} for l in range(LAYERS)
        ]
        whole_vectors = [lax.all_gather(v, "seq", axis=1, tiled=True).astype(F32) for v in vectors]
        gains = [jnp.stack([whole_vectors[0][l], whole_vectors[3][l]]) for l in range(LAYERS)]
        biases = [jnp.stack([whole_vectors[1][l], whole_vectors[2][l]]) for l in range(LAYERS)]

    def to_rows(v):
        return v.reshape(seqs, CHUNKS, sz.steps, d).transpose(0, 2, 1, 3).reshape(sz.n, d)

    def from_rows(v):
        return v.reshape(seqs, sz.steps, CHUNKS, d).transpose(0, 2, 1, 3).reshape(seqs, length, d)

    stream, grad = to_rows(tokens), to_rows(cotangent)
    kept, diagonals = [], []
    for l in range(LAYERS):
        save = (True,) if l + 1 < LAYERS else ()
        normed, decay, inflow, cand, f_f, f_i, f_c, cp, ch, fin = gate_forward(
            sz, stream, gains[l], biases[l], weights[l], (True,)
        )
        if standard:
            near, beside = parts_at[l]
            if l + 1 < LAYERS:
                line_g1 = line_gather(pos, [after(parts_g1[0], fin), *parts_g1[1:]], rows[2:3])

            def hold(step, other):
                if step == 0:
                    return [line_g1] if l + 1 < LAYERS else []
                if step == 1:
                    diagonals.append(cross(after(near, other, beside), SECOND))
                return []

            ent, _ = enter(fin, seqs, False, (), hold)
            diagonal = diagonals[l] = after(diagonals[l], ent)
            rest = plane_gather(pos, lines_at[l], [near, beside, diagonal])
            weights[l] = view([weights[l]["f"][0], rest])
        else:
            ent, _ = enter(fin, seqs, False)
        hidden, hb, e, mid, n2, act, slope, result = mix_forward(
            sz, stream, gains[l], decay, inflow, cp, ch, ent, weights[l], l == LAYERS - 1, save
        )
        if standard and l + 1 < LAYERS:
            own, *others = line_parts(after(packs[2 * l + 3], ent))
            line_r = line_gather(pos, [after(own, result), *others], rows[2 * l + 3 : 2 * l + 4])
            sent_g = after(line_g1, diagonal)
            parts_g = [cross(sent_g, FIRST), cross(sent_g, SECOND)]
            parts_g.append(cross(after(parts_g[0], line_r), SECOND))
            sent_r = after(line_r, *parts_g[:2])
            weights.append(view([plane_gather(pos, line_g1, parts_g, (result,)), None]))
            lines_at.append(line_r)
            parts_at.append([cross(sent_r, FIRST), cross(sent_r, SECOND)])
        kept.append((stream, normed, decay, cand, f_f, f_i, f_c, hidden, hb, e, mid, n2, act, slope))
        stream = result
    output = from_rows(stream)

    vector_grads, sums, pending = [None] * LAYERS, [], []
    above = None
    for l in reversed(range(LAYERS)):
        x, normed, decay, cand, f_f, f_i, f_c, hidden, hb, e, mid, n2, act, slope = kept[l]
        place = far if l + 1 < LAYERS else lambda a: a
        decay, cand, f_f, f_i, f_c, hidden = map(far, (decay, cand, f_f, f_i, f_c, hidden))
        mid, slope = place(mid), place(slope)
        gr, gpre, gmid, go, ggain_two, gh, cp, ca, fin = mlp_backward(sz, grad, gains[l], mid, slope, decay, weights[l])

        def up(message):
            if above:
                message = above_up.step(message)
            return up_weights(sz, pos, place(after(n2, message)), gpre)

        def down(message):
            if above:
                message = above.step(message)
            return row_weights(sz, pos, place(after(act, message)), gr, "down_weights")

        def out(message):
            if above:
                message = above_up.step(message)
            return row_weights(sz, pos, place(after(hb, message)), go, "out_weights")

        ent, pairs = enter(fin, seqs, True, (up, down, out))
        if standard:
            if above:
                pairs[2] = (after(pairs[2][0], above.step(pairs[2][0])), pairs[2][1])
            exchanged = core_exchange(pairs)
            if not above:
                upright = UprightReduction(pos, [(l, "u")], exchanged[0])
                gmid = after(gmid, upright.seen)
            mlp = Reduction(pos, [(l, "d"), (l, "o")], exchanged[1:])
            gmid = after(gmid, mlp.seen)
        final = []
        if l == 0 and standard:
            final = [(ggain_two, 3)]
            for at in range(1, LAYERS):
                final += [(v, 4 * at + row) for v, row in zip(vector_grads[at], (0, 1, 3))]
        *gate_pair, gbias, grad, ggain_one = gate_backward(
            sz, pos, x, gains[l], gmid, gh, decay, hidden, e, cand, f_f, f_i, f_c, cp, ca, ent, far(normed), weights[l],
            l == 0, final,
        )
        vector_grads[l] = (ggain_one, gbias, ggain_two)
        if not standard:
            pending.append((l, pairs + [gate_pair]))
            continue
        if above:
            mlp.step(above_up.step(above.step(gate_pair[0])))
            upright = UprightReduction(pos, [(l, "u")], (after(exchanged[0][0], mlp.seen), exchanged[0][1]))
            gate_pair[1] = after(gate_pair[1], upright.seen)
        names = [(l, m) for m in "fic"]
        if l == 0:
            names += [(at, k) for at in range(LAYERS) for k in range(4)]
        gates = Reduction(pos, names, core_exchange([gate_pair]))
        if l > 0:
            grad, above, above_up = after(grad, gates.seen), mlp, upright
            above.join(gates)
            continue
        gates.step()
        upright.step(above.total(gates.seen))
        mlp.join(gates)
        mlp.step(upright.step(above_up.total(upright.seen)))
        mlp.step(upright.step(mlp.seen))
        sums = [(one.names, one.parts) for one in (above, above_up, mlp, upright)]
    grad_tokens = from_rows(grad)

    if standard:
        layout, ins = [], []
        for names, parts in sums:
            pieces = [(order[m], l, False) if m in order else (6 + m, l, True) for l, m in names]
            layout.append((len(parts), pieces))
            ins += [whole(p) for p in parts]
        found = call(
            functools.partial(finish_kernel, layout), 1, ins,
            [whole_out(m.shape) for m in matrices.values()] + [whole_out(v.shape) for v in vectors], [], 3, "finish",
        )
        g_up, g_down, g_out, g_f, g_i, g_c, g_norm, g_fb, g_ib, g_mlp = found
    else:
        per_layer = {}
        for l, pairs in pending:
            blocks = [jnp.stack([keep, send], axis=2).reshape(NS, NB, -1, LANE) for keep, send in pairs]
            gates = jnp.split(blocks[3], 3, axis=2)
            for m, g in zip("udofic", blocks[:3] + gates):
                v = unslab(g, matrices[m].shape[1] * seq_count, matrices[m].shape[2] * batch_count)
                v = lax.psum_scatter(v, "seq", scatter_dimension=0, tiled=True)
                per_layer[m, l] = lax.psum_scatter(v, "batch", scatter_dimension=1, tiled=True).astype(F32)
        g_up, g_down, g_out, g_f, g_i, g_c = [
            jnp.stack([per_layer[m, l] for l in range(LAYERS)]) for m in matrices
        ]
        rows = [
            (ggain_one[0], gbias[0], gbias[1], ggain_two[0]) for ggain_one, gbias, ggain_two in vector_grads
        ]
        g_norm, g_fb, g_ib, g_mlp = [
            lax.psum(lax.psum_scatter(jnp.stack([r[k] for r in rows]), "seq", scatter_dimension=1, tiled=True), "batch")
            for k in range(4)
        ]
    return output, grad_tokens, g_norm, g_f, g_i, g_c, g_fb, g_ib, g_out, g_mlp, g_up, g_down


def solution(mesh):
    split, vector, matrix = P("batch", "seq", None), P(None, "seq"), P(None, "seq", "batch")
    order = (vector, matrix, matrix, matrix, vector, vector, matrix, vector, matrix, matrix)
    return jax.shard_map(
        body,
        mesh=mesh,
        in_specs=(split,) + order + (split,),
        out_specs=(split, split) + order,
        check_vma=False,
    )
```

```python
import functools

import jax
import jax.numpy as jnp
from jax import lax
from jax.experimental import pallas as pl
from jax.experimental.pallas import tpu as pltpu
from jax.sharding import PartitionSpec as P

LAYERS = 2
EPS = 1e-05
NS, NB, LANE = 8, 4, 128
CHUNKS = 8
STEPS = 2
GATE_STEPS = 4
TURN, WIDE = 2, 256
VMEM = 28 * 1024 * 1024
F32, BF16 = jnp.float32, jnp.bfloat16


def dot(left, right):
    return lax.dot_general(left, right, (((1,), (0,)), ((), ())), preferred_element_type=F32)


def dot_nt(left, right):
    return lax.dot_general(left, right, (((1,), (1,)), ((), ())), preferred_element_type=F32)


def dot_tn(left, right):
    return lax.dot_general(left, right, (((0,), (0,)), ((), ())), preferred_element_type=F32)


def columns_of(ref, slabs=2):
    rows = ref.shape[2] // slabs
    parts = [
        ref[:, b, j * rows : (j + 1) * rows, :].reshape(NS * rows, LANE) for b in range(ref.shape[1]) for j in range(slabs)
    ]
    return jnp.concatenate(parts, axis=1)


def rows_of(ref):
    parts = [ref[:, j].reshape(-1, LANE) for j in range(NB)]
    return jnp.concatenate(parts, axis=1)


def rms_scale(values):
    return lax.rsqrt(jnp.mean(values * values, axis=-1, keepdims=True) + EPS)


def rms_back(values, gain, grad):
    scale = rms_scale(values)
    unit = values * scale
    inner = grad * gain
    back = scale * (inner - unit * jnp.mean(inner * unit, axis=-1, keepdims=True))
    return back, jnp.sum(grad * unit, axis=0, keepdims=True)


def gate_kernel(
    seqs, steps, x_ref, gain_ref, bias_ref, wf_ref, wi_ref, wc_ref,
    normed_ref, decay_ref, inflow_ref, cand_ref, ff_ref, fi_ref, fc_ref, cp_ref, ch_ref, fin_ref,
    z,
):
    width = decay_ref.shape[1]

    @pl.when(pl.program_id(0) == 0)
    def _():
        x = x_ref[...].astype(F32)
        normed_ref[...] = (x * rms_scale(x) * gain_ref[0:1, :]).astype(BF16)

    weights = jnp.concatenate([columns_of(ref) for ref in (wf_ref, wi_ref, wc_ref)], axis=1)
    block = TURN * CHUNKS
    places = [(seq, left) for seq in range(seqs) for left in range(0, width, WIDE)]

    def turn(of, at, carry):
        carry = list(carry)
        for k, (seq, left) in enumerate(places):
            if seq != of:
                continue
            span = slice(seq * steps * CHUNKS + at * block, seq * steps * CHUNKS + (at + 1) * block)
            cols = slice(left, left + WIDE)
            f = z[span, cols] + bias_ref[0:1, cols]
            i = z[span, width + left : width + left + WIDE] + bias_ref[1:2, cols]
            c = z[span, 2 * width + left : 2 * width + left + WIDE]
            low = jnp.minimum(jnp.minimum(f, i), 0.0)
            e0, ef, ei = jnp.exp(low), jnp.exp(low - f), jnp.exp(low - i)
            a, b = e0 + ef, e0 + ei
            inv = 1.0 / (a + b)
            decay, other = b * inv, a * inv
            ec = jnp.exp(-jnp.abs(c))
            cand = jnp.maximum(c, 0.0) + jnp.log1p(ec)
            slope = jnp.where(c >= 0.0, 1.0, ec) / (1.0 + ec)
            inflow = other * cand
            decay_ref[span, cols] = decay
            inflow_ref[span, cols] = inflow
            cand_ref[span, cols] = cand
            ff_ref[span, cols] = (ef * inv * decay).astype(BF16)
            fi_ref[span, cols] = (ei * inv * other).astype(BF16)
            fc_ref[span, cols] = (other * slope).astype(BF16)
            prod, state = carry[2 * k], carry[2 * k + 1]
            for t in range(TURN):
                d = decay[t * CHUNKS : (t + 1) * CHUNKS]
                prod = prod * d
                state = state * d + inflow[t * CHUNKS : (t + 1) * CHUNKS]
            carry[2 * k], carry[2 * k + 1] = prod, state
        return tuple(carry)

    one, zero = jnp.ones((CHUNKS, WIDE), F32), jnp.zeros((CHUNKS, WIDE), F32)
    carry = (one, zero) * len(places)
    for seq in range(seqs):
        rows = slice(seq * steps * CHUNKS, (seq + 1) * steps * CHUNKS)
        z[rows, :] = dot(normed_ref[rows, :], weights)
        for at in range(steps // TURN):
            carry = turn(seq, at, carry)
    for k, (seq, left) in enumerate(places):
        prod, state = carry[2 * k], carry[2 * k + 1]
        cols = slice(left, left + WIDE)
        cp_ref[seq, :, cols], ch_ref[seq, :, cols] = prod, state
        whole, last = prod[0:1], state[0:1]
        for c in range(1, CHUNKS):
            whole, last = whole * prod[c : c + 1], last * prod[c : c + 1] + state[c : c + 1]
        fin_ref[seq : seq + 1, cols] = whole
        fin_ref[seqs + seq : seqs + seq + 1, cols] = last


def mix_kernel(
    seqs, steps, x_ref, gain_ref, decay_ref, inflow_ref, cp_ref, ch_ref, ent_ref, wo_ref, wu_ref, wd_ref,
    hidden_ref, hb_ref, e_ref, mid_ref, n2_ref, act_ref, slope_ref, out_ref,
    acc,
):
    at_step = pl.program_id(0)
    block = TURN * CHUNKS
    width = decay_ref.shape[1]
    places = [(seq, left) for seq in range(seqs) for left in range(0, width, WIDE)]

    @pl.when(at_step == 0)
    def _():
        acc[...] = x_ref[...].astype(F32)

    @pl.when(at_step < STEPS)
    def _():
        for seq in range(seqs):
            state = ent_ref[seq : seq + 1, :]
            for c in range(CHUNKS):
                e_ref[seq, c : c + 1, :] = state
                state = state * cp_ref[seq, c : c + 1, :] + ch_ref[seq, c : c + 1, :]

        def turn(at, carry):
            carry = list(carry)
            for k, (seq, left) in enumerate(places):
                span = pl.ds(pl.multiple_of(seq * steps * CHUNKS + at * block, block), block)
                cols = slice(left, left + WIDE)
                d, u = decay_ref[span, cols], inflow_ref[span, cols]
                state, found = carry[k], []
                for t in range(TURN):
                    state = state * d[t * CHUNKS : (t + 1) * CHUNKS] + u[t * CHUNKS : (t + 1) * CHUNKS]
                    found.append(state)
                carry[k] = state
                hidden = jnp.concatenate(found, axis=0)
                hidden_ref[span, cols] = hidden
                hb_ref[span, cols] = hidden.astype(BF16)
            return tuple(carry)

        lax.fori_loop(0, steps // TURN, turn, tuple(e_ref[seq, :, left : left + WIDE] for seq, left in places))
        acc[...] += dot(hb_ref[...], rows_of(wo_ref))

    @pl.when(at_step == STEPS - 1)
    def _():
        middle = acc[...]
        mid_ref[...] = middle
        n2_ref[...] = (middle * rms_scale(middle) * gain_ref[1:2, :]).astype(BF16)

    @pl.when(at_step >= STEPS)
    def _():
        w_up, w_down = columns_of(wu_ref, 4), rows_of(wd_ref)
        size = acc.shape[0] // 2
        for k in range(2):
            span = slice(k * size, (k + 1) * size)
            v = dot(n2_ref[span, :], w_up)
            phi = 0.5 + 0.5 * lax.erf(v * 0.7071067811865476)
            act = (v * phi).astype(BF16)
            act_ref[span, :] = act
            slope_ref[span, :] = (phi + v * (0.3989422804014327 * jnp.exp(v * v * -0.5))).astype(BF16)
            acc[span, :] += dot(act, w_down)

    @pl.when(at_step == 2 * STEPS - 1)
    def _():
        out_ref[...] = acc[...].astype(out_ref.dtype)


def mlp_back_kernel(
    seqs, steps, g_ref, gain_ref, mid_ref, slope_ref, decay_ref, wo_ref, wu_ref, wd_ref,
    gr_ref, gpre_ref, gmid_ref, go_ref, ggain_ref, gh_ref, cp_ref, ca_ref, fin_ref,
    acc,
):
    at_step = pl.program_id(0)
    block = TURN * CHUNKS
    width = decay_ref.shape[1]
    places = [(seq, left) for seq in range(seqs) for left in range(0, width, WIDE)]

    @pl.when(at_step == 0)
    def _():
        gr_ref[...] = g_ref[...].astype(BF16)
        acc[...] = jnp.zeros_like(acc)

    @pl.when(at_step < STEPS)
    def _():
        gact = dot_nt(gr_ref[...], rows_of(wd_ref))
        gpre_ref[...] = (gact * slope_ref[...].astype(F32)).astype(BF16)
        acc[...] += dot_nt(gpre_ref[...], columns_of(wu_ref, 4))

    @pl.when(at_step == STEPS - 1)
    def _():
        back, ggain = rms_back(mid_ref[...], gain_ref[1:2, :], acc[...])
        ggain_ref[...] = ggain
        gmid = g_ref[...].astype(F32) + back
        gmid_ref[...] = gmid
        go_ref[...] = gmid.astype(BF16)

    @pl.when(at_step >= STEPS)
    def _():
        gh_ref[...] = dot_nt(go_ref[...], rows_of(wo_ref))

        def turn(turn_at, carry):
            at = steps // TURN - 1 - turn_at
            carry = list(carry)
            for k, (seq, left) in enumerate(places):
                span = pl.ds(pl.multiple_of(seq * steps * CHUNKS + at * block, block), block)
                cols = slice(left, left + WIDE)
                d, g = decay_ref[span, cols], gh_ref[span, cols]
                prod, state = carry[2 * k], carry[2 * k + 1]
                for t in reversed(range(TURN)):
                    dk = d[t * CHUNKS : (t + 1) * CHUNKS]
                    prod = prod * dk
                    state = dk * (g[t * CHUNKS : (t + 1) * CHUNKS] + state)
                carry[2 * k], carry[2 * k + 1] = prod, state
            return tuple(carry)

        one, zero = jnp.ones((CHUNKS, WIDE), F32), jnp.zeros((CHUNKS, WIDE), F32)
        carry = lax.fori_loop(0, steps // TURN, turn, (one, zero) * len(places))
        for k, (seq, left) in enumerate(places):
            prod, state = carry[2 * k], carry[2 * k + 1]
            cols = slice(left, left + WIDE)
            cp_ref[seq, :, cols], ca_ref[seq, :, cols] = prod, state
            whole, last = prod[CHUNKS - 1 :], state[CHUNKS - 1 :]
            for c in reversed(range(CHUNKS - 1)):
                whole, last = whole * prod[c : c + 1], last * prod[c : c + 1] + state[c : c + 1]
            fin_ref[seq : seq + 1, cols] = whole
            fin_ref[seqs + seq : seqs + seq + 1, cols] = last


def gate_back_kernel(
    seqs, steps, others, pos_ref, x_ref, gain_ref, gmid_ref, gh_ref, decay_ref, hidden_ref, e_ref, cand_ref,
    ff_ref, fi_ref, fc_ref, cp_ref, ca_ref, ent_ref, normed_ref, wf_ref, wi_ref, wc_ref, *refs,
):
    given = refs[: len(others)]
    keep_ref, send_ref, gbias_ref, gstream_ref, ggain_ref, acc, start, dz, rest = refs[len(others) :]
    at_step = pl.program_id(0)
    block = TURN * CHUNKS
    width = decay_ref.shape[1]
    places = [(seq, left) for seq in range(seqs) for left in range(0, width, WIDE)]

    @pl.when(at_step == 0)
    def _():
        acc[...] = jnp.zeros_like(acc)

    for seq in range(seqs):
        state = ent_ref[seq : seq + 1, :]
        for c in reversed(range(CHUNKS)):
            start[seq, c : c + 1, :] = state
            state = state * cp_ref[seq, c : c + 1, :] + ca_ref[seq, c : c + 1, :]

    def turn(of, at, carry):
        carry = list(carry)
        for k, (seq, left) in enumerate(places):
            if seq != of:
                continue
            cols = slice(left, left + WIDE)
            state, sum_f, sum_i = carry[3 * k : 3 * k + 3]
            base = seq * steps * CHUNKS + at * block
            span = slice(base, base + block)
            before = hidden_ref[base - CHUNKS : base, cols] if at else e_ref[seq, :, cols]
            d, g = decay_ref[span, cols], gh_ref[span, cols]
            previous = jnp.concatenate([before, hidden_ref[span, cols][: block - CHUNKS]], axis=0)
            found = []
            for t in reversed(range(TURN)):
                now = g[t * CHUNKS : (t + 1) * CHUNKS] + state
                found.append(now)
                state = d[t * CHUNKS : (t + 1) * CHUNKS] * now
            gstate = jnp.concatenate(found[::-1], axis=0)
            both = gstate * (cand_ref[span, cols] - previous)
            dzf = (-ff_ref[span, cols].astype(F32) * both).astype(BF16)
            dzi = (fi_ref[span, cols].astype(F32) * both).astype(BF16)
            dz[span, left : left + WIDE] = dzf
            dz[span, width + left : width + left + WIDE] = dzi
            dz[span, 2 * width + left : 2 * width + left + WIDE] = (fc_ref[span, cols].astype(F32) * gstate).astype(BF16)
            wide_f, wide_i = dzf.astype(F32), dzi.astype(F32)
            for t in range(TURN):
                sum_f = sum_f + wide_f[t * CHUNKS : (t + 1) * CHUNKS]
                sum_i = sum_i + wide_i[t * CHUNKS : (t + 1) * CHUNKS]
            carry[3 * k : 3 * k + 3] = state, sum_f, sum_i
        return tuple(carry)

    zero = jnp.zeros((CHUNKS, WIDE), F32)
    first_carry = [v for seq, left in places for v in (start[seq, :, left : left + WIDE], zero, zero)]
    carry = tuple(first_carry)
    weights = jnp.concatenate([columns_of(ref) for ref in (wf_ref, wi_ref, wc_ref)], axis=1)
    grad = None
    for seq in range(seqs):
        rows = slice(seq * steps * CHUNKS, (seq + 1) * steps * CHUNKS)
        for at in reversed(range(steps // TURN)):
            carry = turn(seq, at, carry)
        acc[rows, :] += dot_nt(dz[rows, :], weights)
        part = dot_tn(normed_ref[rows, :], dz[rows, :])
        grad = part if grad is None else grad + part
    for row in range(2):
        for left in range(0, width, WIDE):
            total = sum(carry[3 * k + 1 + row] for k, place in enumerate(places) if place[1] == left)
            gbias_ref[row : row + 1, left : left + WIDE] = jnp.sum(total, axis=0, keepdims=True)
    rows = wf_ref.shape[2]
    for m in range(3):
        put_columns(pos_ref, keep_ref, send_ref, m * rows, grad[:, m * width : (m + 1) * width])

    @pl.when(at_step == STEPS - 1)
    def _():
        back, ggain = rms_back(x_ref[...].astype(F32), gain_ref[0:1, :], acc[...])
        ggain_ref[...] = ggain
        gstream_ref[...] = (gmid_ref[...] + back).astype(gstream_ref.dtype)

    if others:

        def rows_to(ref, first_row):
            wide = ref.shape[1] // NS
            for r in range(ref.shape[0]):
                for s in range(NS):
                    rest[s, first_row + r : first_row + r + 1, :wide] = ref[r : r + 1, s * wide : (s + 1) * wide]

        @pl.when(at_step == 0)
        def _():
            rest[...] = jnp.zeros_like(rest)
            for ref, first_row in zip(given, others):
                rows_to(ref, first_row)

        wide = width * STEPS // NS
        for row in range(2):
            for s in range(width // wide):
                rest[at_step * (width // wide) + s, 1 + row : 2 + row, :wide] = gbias_ref[row : row + 1, s * wide : (s + 1) * wide]

        @pl.when(at_step == STEPS - 1)
        def _():
            rows_to(ggain_ref, 0)
            found = rest[...].astype(BF16)
            for x in range(2):
                keep_ref[:, x, 3 * rows :, :] = found
                send_ref[:, x, 3 * rows :, :] = found


def send_or_keep(mine, keep_ref, send_ref, put):
    @pl.when(mine)
    def _():
        put(keep_ref)

    @pl.when(jnp.logical_not(mine))
    def _():
        put(send_ref)


def put_columns(pos_ref, keep_ref, send_ref, start, value):
    rows, width = value.shape[0] // NS, value.shape[1] // 2
    x = pl.program_id(0)
    for core in range(2):
        parts = [
            value[:, left : left + LANE].astype(BF16).reshape(NS, rows, LANE)
            for left in range(core * width, (core + 1) * width, LANE)
        ]

        def put(ref):
            for j, part in enumerate(parts):
                ref[:, x, start + j * rows : start + (j + 1) * rows, :] = part

        send_or_keep(pos_ref[0] == core, keep_ref, send_ref, put)


def put_rows(pos_ref, keep_ref, send_ref, value):
    count = NS // STEPS
    for j in range(NB):
        part = value[:, j * LANE : (j + 1) * LANE].astype(BF16).reshape(count, -1, LANE)

        def put(ref):
            ref[pl.ds(pl.program_id(0) * count, count), j // 2] = part

        send_or_keep(pos_ref[0] == j % 2, keep_ref, send_ref, put)


def up_weight_kernel(pos_ref, n2_ref, gpre_ref, keep_ref, send_ref):
    put_columns(pos_ref, keep_ref, send_ref, 0, dot_tn(n2_ref[...], gpre_ref[...]))


def row_weight_kernel(pos_ref, left_ref, right_ref, keep_ref, send_ref):
    put_rows(pos_ref, keep_ref, send_ref, dot_tn(left_ref[...], right_ref[...]))


def add(*parts):
    total = parts[0].astype(F32)
    for part in parts[1:]:
        total = total + part.astype(F32)
    return total


def pair_sum_kernel(rows, pos_ref, *refs):
    count = len(rows)
    send, stay = refs[2 * count :]
    core, x, y, step = pos_ref[0], pos_ref[1], pos_ref[2], pos_ref[4]
    at = 0
    for keep, got, r in zip(refs[:count], refs[count : 2 * count], rows):
        for v in range(2):
            for out, first in ((send, 1 - step), (stay, step)):
                iy, ix = jnp.where(core == 0, v, first), jnp.where(core == 0, first, v)
                out[0, v, at : at + r] = add(keep[0, iy, ix], got[0, iy, ix]).astype(BF16)
        at += r


def plane_sum_kernel(pos_ref, *refs):
    second = pos_ref[5]
    *pairs, send, stay = refs
    at = 0
    for keep, got in zip(pairs[::2], pairs[1::2]):
        rows = slice(at, at + keep.shape[2])
        send[0, rows, :] = add(keep[0, 1 - second], got[0, 1 - second]).astype(BF16)
        stay[0, rows, :] = add(keep[0, second], got[0, second]).astype(BF16)
        at += keep.shape[2]


def line_sum_kernel(pos_ref, *refs):
    core, first = pos_ref[0], pos_ref[6]
    *pairs, send, stay = refs
    at = 0
    for keep, got in zip(pairs[::2], pairs[1::2]):
        rows = slice(at, at + keep.shape[1])
        for v in range(2):
            for out, f in ((send, 1 - first), (stay, first)):
                z = jnp.where(core == 0, f + 2 * v, 2 * f + v)
                out[v, rows, :] = add(keep[z], got[z]).astype(BF16)
        at += keep.shape[1]


def last_sum_kernel(pos_ref, keep, got, send, stay):
    second = pos_ref[7]
    send[...] = add(keep[1 - second], got[1 - second]).astype(BF16)
    stay[...] = add(keep[second], got[second]).astype(BF16)


def total_kernel(keep, got, out):
    out[...] = add(keep[...], got[...])


def finish_kernel(layout, *refs):
    at = 0
    ins = sum(parts for parts, _ in layout)
    outs = refs[ins:]
    for parts, pieces in layout:
        got = refs[at : at + parts]
        at += parts
        row = 0
        for out, layer, vectors in pieces:
            ref = outs[out]
            if vectors:
                ref[layer : layer + 1, :] = add(*[g[...] for g in got])[row : row + 1, : ref.shape[1]]
                row += 1
                continue
            r = ref.shape[1]
            for j in range(ref.shape[2] // LANE):
                ref[layer, :, j * LANE : (j + 1) * LANE] = add(*[g[row : row + r] for g in got])
                row += r


def pack_kernel(groups, *refs):
    ins = refs[: len(refs) - len(groups) - 1]
    outs, scratch = refs[len(ins) : -1], refs[-1]
    for out, group in zip(outs, groups):
        row = 0
        vec = 0
        for which, layer, vector in group:
            ref = ins[which]
            if vector:
                if vec == 0:
                    scratch[...] = jnp.zeros_like(scratch)
                scratch[vec : vec + 1, : ref.shape[1]] = ref[...].astype(F32)[layer : layer + 1]
                vec += 1
                continue
            r = ref.shape[1]
            for j in range(ref.shape[2] // LANE):
                out[row : row + r, :] = ref[layer, :, j * LANE : (j + 1) * LANE]
                row += r
        if vec:
            out[row:, :] = scratch[...].astype(BF16)


def line_gather_kernel(pos_ref, *refs):
    row = 0
    for out in refs[4:]:
        rows = out.shape[1]
        for k, part in enumerate(refs[:4]):
            out[pos_ref[3] ^ k] = part[row : row + rows, :]
        row += rows


def plane_gather_kernel(pos_ref, *refs):
    out = refs[-1]
    at, half = pl.program_id(0), pl.num_programs(0) // 2
    core, x, y = pos_ref[0], pos_ref[1], pos_ref[2]
    count = len(refs) // 2
    for c in range(2):
        own, first, second, *diagonal = refs[count * c : count * (c + 1)]
        other = core ^ c
        turn = other if count == 4 else 0
        out[0, y, x, other] = own[0]
        out[0, y ^ turn, x ^ (1 - turn), other] = first[0]
        out[0, y ^ (1 - turn), x ^ turn, other] = second[0]
        if count == 4:
            out[0, y ^ 1, x ^ 1, other] = diagonal[0][0]
            continue

        @pl.when(at < half)
        def _():
            out[0, y ^ 1, x ^ 1, other] = diagonal[0][0]

        @pl.when(at >= half)
        def _():
            out[0, y ^ 1, x ^ 1, other] = diagonal[1][0]


def vector_kernel(gained, w_ref, *refs):
    outs, scratch = refs[:-1], refs[-1]
    scratch[...] = w_ref[:, 0].astype(F32)
    for l in range(LAYERS):
        for which in range(4):
            out, row = ((outs[2 * l], which // 3) if which in (0, 3) else (outs[2 * l + 1], which - 1))
            wide = out.shape[1] // NS
            for s in range(NS):
                out[row : row + 1, s * wide : (s + 1) * wide] = scratch[s, 4 * l + which : 4 * l + which + 1, :wide]


def shape(dims, dtype=F32):
    return jax.ShapeDtypeStruct(dims, dtype)


def call(kernel, grid, ins, outs, scratch, us, name):
    def spec(a, block, index):
        if a.dtype == jnp.int32:
            return pl.BlockSpec(memory_space=pltpu.SMEM)
        return pl.BlockSpec(block, index)

    found = pl.pallas_call(
        kernel,
        grid=(grid,),
        in_specs=[spec(*one) for one in ins],
        out_specs=[pl.BlockSpec(block, index) for _, block, index, *_ in outs],
        out_shape=[pltpu.HBM(one[0].shape, one[0].dtype) if one[3:] else one[0] for one in outs],
        scratch_shapes=scratch,
        compiler_params=pltpu.CompilerParams(vmem_limit_bytes=VMEM),
        cost_estimate=pl.CostEstimate(flops=int(us * 1.1e9) + 1, bytes_accessed=1024, transcendentals=0),
        name=name,
    )(*[a for a, _, _ in ins])
    return found if len(found) > 1 else found[0]


def far(array):
    return pltpu.with_memory_space_constraint(array, pltpu.HBM)


def whole(array):
    dims = array.shape
    return (array, dims, lambda i: (0,) * len(dims))


def whole_out(dims, dtype=F32):
    return (shape(dims, dtype), dims, lambda i: (0,) * len(dims))


def first(i):
    return jnp.minimum(i, STEPS - 1)


def second(i):
    return jnp.maximum(i - STEPS, 0)


class Sizes:
    def __init__(self, seqs, length, d, h, ff):
        self.seqs, self.steps, self.n = seqs, length // CHUNKS, seqs * length
        self.d, self.h, self.ff = d, h, ff
        self.hb, self.fb = h // STEPS, ff // STEPS


def column_weight(view, at, late=False, steps=STEPS):
    array, rows, place = view
    return (far(array) if late else array, (NS, NB // steps, rows, LANE), lambda i: (0, at(i), place, 0))


def row_weight(view, at):
    array, rows, place = view
    return (array, (NS // STEPS, NB, rows, LANE), lambda i: (at(i), 0, place, 0))


def same(i):
    return i


def gate_forward(sz, x, gain, bias, w, save):
    n, d, h, wide, s = sz.n, sz.d, sz.h, sz.h // GATE_STEPS, sz.seqs
    col = lambda i: (0, i)
    return call(
        functools.partial(gate_kernel, s, sz.steps), GATE_STEPS,
        [whole(x), whole(gain), (bias, (2, wide), col)] + [column_weight(w[m], same, False, GATE_STEPS) for m in "fic"],
        [whole_out((n, d), BF16) + save]
        + [(shape((n, h)), (n, wide), col) + save, (shape((n, h)), (n, wide), col), (shape((n, h)), (n, wide), col) + save]
        + [(shape((n, h), BF16), (n, wide), col) + save] * 3
        + [(shape((s, CHUNKS, h)), (s, CHUNKS, wide), lambda i: (0, 0, i))] * 2
        + [(shape((2 * s, h)), (2 * s, wide), col)],
        [pltpu.VMEM((n, 3 * wide), F32)], 9, "gates",
    )


def mix_forward(sz, x, gain, decay, inflow, cp, ch, ent, wt, last, save):
    n, d, h, ff, w, f, s = sz.n, sz.d, sz.h, sz.ff, sz.hb, sz.fb, sz.seqs
    col = lambda i: (0, first(i))
    late = lambda i: (0, second(i))
    deep = lambda i: (0, 0, first(i))
    return call(
        functools.partial(mix_kernel, s, sz.steps), 2 * STEPS,
        [
            whole(x), whole(gain), (decay, (n, w), col), (inflow, (n, w), col),
            (cp, (s, CHUNKS, w), deep), (ch, (s, CHUNKS, w), deep), (ent, (s, w), col),
            row_weight(wt["o"], first), column_weight(wt["u"], second), row_weight(wt["d"], second),
        ],
        [
            (shape((n, h)), (n, w), col, True), (shape((n, h), BF16), (n, w), col) + save,
            (shape((s, CHUNKS, h)), (s, CHUNKS, w), deep) + save,
            whole_out((n, d)) + save, whole_out((n, d), BF16) + save,
            (shape((n, ff), BF16), (n, f), late) + save, (shape((n, ff), BF16), (n, f), late) + save,
            whole_out((n, d), BF16 if last else F32),
        ],
        [pltpu.VMEM((n, d), F32)], 14, "mix",
    )


def mlp_backward(sz, g, gain, mid, slope, decay, wt):
    n, d, h, ff, w, f, s = sz.n, sz.d, sz.h, sz.ff, sz.hb, sz.fb, sz.seqs
    col = lambda i: (0, second(i))
    early = lambda i: (0, first(i))
    deep = lambda i: (0, 0, second(i))
    return call(
        functools.partial(mlp_back_kernel, s, sz.steps), 2 * STEPS,
        [
            whole(g), whole(gain), whole(mid), (slope, (n, f), early), (decay, (n, w), col),
            row_weight(wt["o"], second), column_weight(wt["u"], first), row_weight(wt["d"], first),
        ],
        [
            whole_out((n, d), BF16), (shape((n, ff), BF16), (n, f), early), whole_out((n, d)), whole_out((n, d), BF16),
            whole_out((1, d)), (shape((n, h)), (n, w), col),
            (shape((s, CHUNKS, h)), (s, CHUNKS, w), deep), (shape((s, CHUNKS, h)), (s, CHUNKS, w), deep),
            (shape((2 * s, h)), (2 * s, w), col),
        ],
        [pltpu.VMEM((n, d), F32)], 12, "mlp_back",
    )


def gate_backward(sz, pos, x, gain, gmid, gh, decay, hidden, e, cand, ff_, fi_, fc_, cp, ca, ent, normed, wt, last, vectors):
    n, d, h, w, s = sz.n, sz.d, sz.h, sz.hb, sz.seqs
    col = lambda i: (0, i)
    deep = lambda i: (0, 0, i)
    wide = lambda a: (a, (n, w), col)
    rows = 3 * d * h // (32 * LANE) + (16 if vectors else 0)
    return call(
        functools.partial(gate_back_kernel, s, sz.steps, tuple(row for _, row in vectors)), STEPS,
        [
            whole(pos), whole(x), whole(gain), whole(gmid), wide(gh), wide(decay), wide(hidden), (e, (s, CHUNKS, w), deep),
            wide(cand), wide(ff_), wide(fi_), wide(fc_), (cp, (s, CHUNKS, w), deep), (ca, (s, CHUNKS, w), deep),
            (ent, (s, w), col), whole(normed),
        ] + [column_weight(wt[m], same, True) for m in "fic"] + [whole(v) for v, _ in vectors],
        [whole_out((NS, 2, rows, LANE), BF16)] * 2
        + [(shape((2, h)), (2, w), col), whole_out((n, d), BF16 if last else F32), whole_out((1, d))],
        [
            pltpu.VMEM((n, d), F32), pltpu.VMEM((s, CHUNKS, w), F32), pltpu.VMEM((n, 3 * w), BF16),
            pltpu.VMEM((NS, 16, LANE), F32),
        ], 16, "gate_back",
    )


def up_weights(sz, pos, n2, gpre):
    n, d, ff, f = sz.n, sz.d, sz.ff, sz.fb
    dims = (NS, 2, d * ff // (32 * LANE), LANE)
    return call(
        up_weight_kernel, STEPS, [whole(pos), whole(n2), (gpre, (n, f), lambda i: (0, i))],
        [whole_out(dims, BF16)] * 2, [], 5, "up_weights",
    )


def row_weights(sz, pos, left, right, name):
    n, k, d = sz.n, left.shape[1], sz.d
    dims = (NS, 2, k // NS, LANE)
    return call(
        row_weight_kernel, STEPS, [whole(pos), (left, (n, k // STEPS), lambda i: (0, i)), whole(right)],
        [whole_out(dims, BF16)] * 2, [], 5, name,
    )


def swap(array, axes, bits):
    count = lax.axis_size(axes)
    return lax.ppermute(array, axes, [(i, i ^ bits) for i in range(count)])


BOTH = ("seq", "batch")


def after(array, *others):
    return lax.optimization_barrier((array,) + others)[0]


def by_line(a):
    return (a, (1,) + a.shape[1:], lambda i: (i,) + (0,) * (len(a.shape) - 1))


def by_line_out(*dims):
    return (shape(dims, BF16), (1,) + dims[1:], lambda i: (i,) + (0,) * (len(dims) - 1))


def core_exchange(pairs):
    return [(keep, swap(send, "batch", 1)) for keep, send in pairs]


FIRST, SECOND, FIRST_Z, SECOND_Z = (2, 4), (4, 2), (8, 16), (16, 8)


def cross(array, bits):
    count = lax.axis_size(BOTH)
    return lax.ppermute(array, BOTH, [(i, i ^ bits[i % 2]) for i in range(count)])


def pair_sum(pos, pairs):
    rows, lines = tuple(keep.shape[2] for keep, _ in pairs), pairs[0][0].shape[0] // 2
    view = lambda a: by_line(a.reshape((lines, 2, 2) + a.shape[2:]))
    return call(
        functools.partial(pair_sum_kernel, rows), lines,
        [whole(pos)] + [view(keep) for keep, _ in pairs] + [view(got) for _, got in pairs],
        [by_line_out(lines, 2, sum(rows), LANE)] * 2, [], 3, "pair_sum",
    )


def onward(parts, bits):
    return [parts[1], cross(parts[0], bits)]


def plane_sum(pos, parts):
    rows, lines = sum(part.shape[2] for part in parts[::2]), parts[0].shape[0]
    return call(
        plane_sum_kernel, lines, [whole(pos)] + [by_line(a) for a in parts], [by_line_out(lines, rows, LANE)] * 2, [], 0,
        "plane_sum",
    )


def line_sum(pos, parts):
    rows = sum(part.shape[1] for part in parts[::2])
    return call(
        line_sum_kernel, 1, [whole(pos)] + [whole(a) for a in parts], [whole_out((2, rows, LANE), BF16)] * 2, [], 0, "line_sum",
    )


def last_sum(pos, parts):
    rows = parts[0].shape[1]
    return call(
        last_sum_kernel, 1, [whole(pos)] + [whole(a) for a in parts], [whole_out((rows, LANE), BF16)] * 2, [], 0, "last_sum",
    )


SUMS = ((plane_sum, SECOND), (line_sum, FIRST_Z), (last_sum, SECOND_Z))


class Reduction:
    def __init__(self, pos, names, pairs):
        self.pos, self.names, self.stage = pos, names, 0
        self.parts = pair_sum(pos, pairs)
        self.seen = self.parts[0]
        self.parts = onward(self.parts, FIRST)

    def join(self, other):
        self.names, self.parts = self.names + other.names, self.parts + other.parts

    def step(self, *others):
        work, bits = SUMS[self.stage]
        if others:
            self.parts[0] = after(self.parts[0], *others)
        parts = work(self.pos, self.parts)
        self.stage, self.seen, self.parts = self.stage + 1, parts[0], onward(parts, bits)
        return self.seen

    def one_more(self, others, work, bits):
        if others:
            self.parts[0] = after(self.parts[0], *others)
        parts = work(self.pos, self.parts)
        self.seen, self.parts = parts[0], onward(parts, bits)
        return self.seen

    def total(self, *others):
        keep, got = self.parts
        keep = after(keep, *others)
        total = call(total_kernel, 1, [whole(keep), whole(got)], [whole_out(keep.shape)], [], 0, "total")
        self.parts = [total]
        return total


class UprightReduction(Reduction):
    def __init__(self, pos, names, pair):
        self.pos, self.names, self.stage = pos, names, 0
        self.rows = pair[0].shape[2]
        self.parts = [part.reshape(4, 4 * self.rows, LANE) for part in pair]
        self.one_more((), line_sum, FIRST_Z)

    def step(self, *others):
        self.stage += 1
        if self.stage == 1:
            return self.one_more(others, last_sum, SECOND_Z)
        if self.stage == 2:
            pairs = lambda pos, parts: pair_sum(pos, [tuple(part.reshape(2, 2, self.rows, LANE) for part in parts)])
            return self.one_more(others, pairs, FIRST)
        self.one_more(others, plane_sum, SECOND)
        self.parts = [part[0] for part in self.parts]
        return self.seen


def line_parts(own):
    return [own] + [swap(own, "seq", 2 * k) for k in range(1, 4)]


def line_gather(pos, parts, rows):
    return call(
        line_gather_kernel, 1, [whole(pos)] + [whole(far(p)) for p in parts],
        [whole_out((4, r, LANE), BF16) for r in rows], [], 2, "line_gather",
    )


X_AXIS, Y_AXIS = ("batch", 2), ("seq", 1)


def plane_gather(pos, line, parts, behind=()):
    rows = line.shape[1]
    parts = [line, *parts]
    parts += [swap(after(p, *behind) if behind else p, "batch", 1) for p in parts]
    each, low, high = (lambda i: (i, 0, 0)), (lambda i: (jnp.minimum(i, 1), 0, 0)), (lambda i: (jnp.maximum(i - 2, 0), 0, 0))
    maps = [each] * 4 if len(parts) == 8 else [each, each, each, low, high]
    got = call(
        plane_gather_kernel, 4, [whole(pos)] + [(far(p), (1, rows, LANE), m) for p, m in zip(parts, maps * 2)],
        [(shape((4, 2, 2, 2, rows, LANE), BF16), (1, 2, 2, 2, rows, LANE), lambda i: (i, 0, 0, 0, 0, 0))], [], 5, "plane_gather",
    )
    return got.reshape(NS, NB, rows, LANE)


def enter(fin, seqs, backward, fill=(), hold=None):
    count, mine = lax.axis_size("seq"), lax.axis_index("seq")
    prod, state = fin[:seqs], fin[seqs:]
    pre_p, pre_s = jnp.ones_like(prod), jnp.zeros_like(state)
    bit, message, done, other = 1, fin, [], fin
    for step in range(int(count).bit_length() - 1):
        before = hold(step, other) if hold else ()
        if before:
            message = after(message, *before)
        other = lax.ppermute(message, "seq", [(i, i ^ bit) for i in range(count)])
        if step < len(fill):
            done.append(fill[step](message))
        if done and bit * 2 == count:
            other = after(other, *done[-1])
        o_p, o_s = other[:seqs], other[seqs:]
        upper = ((mine // bit) % 2 == 1) ^ backward
        pre_p, pre_s = jnp.where(upper, o_p * pre_p, pre_p), jnp.where(upper, pre_p * o_s + pre_s, pre_s)
        state = jnp.where(upper, prod * o_s + state, o_p * state + o_s)
        prod = prod * o_p
        message = jnp.concatenate([prod, state])
        if step < len(fill):
            message = after(message, *done[-1])
        bit *= 2
    return pre_s, done


def slabs(matrix, seq_count, batch_count):
    rows, cols = matrix.shape[0] // NS, matrix.shape[1] // NB
    cut = matrix.reshape(NS, rows, NB, cols // LANE, LANE).transpose(0, 2, 3, 1, 4)
    return cut.reshape(NS, NB, rows * cols // LANE, LANE)


def unslab(blocks, rows, cols):
    r, c = rows // NS, cols // NB
    cut = blocks.reshape(NS, NB, c // LANE, r, LANE).transpose(0, 3, 1, 2, 4)
    return cut.reshape(rows, cols)


def body(
    tokens, norm_gain, w_forget, w_input, w_cand, forget_bias, input_bias, w_out, mlp_gain, w_up, w_down, cotangent
):
    seqs, length, d = tokens.shape
    seq_count, batch_count = lax.axis_size("seq"), lax.axis_size("batch")
    h, ff = w_forget.shape[2] * batch_count, w_up.shape[2] * batch_count
    sz = Sizes(seqs, length, d, h, ff)
    standard = (seq_count, batch_count) == (NS, NB)
    matrices = {"u": w_up, "d": w_down, "o": w_out, "f": w_forget, "i": w_input, "c": w_cand}
    vectors = (norm_gain, forget_bias, input_bias, mlp_gain)
    slab_rows = {"u": d * ff // (32 * LANE), "d": ff // NS, "o": h // NS}
    slab_rows.update({m: d * h // (32 * LANE) for m in "fic"})
    order = {name: k for k, name in enumerate(matrices)}

    if standard:
        s_at, b_at = lax.axis_index("seq"), lax.axis_index("batch")
        core, x, y, z = b_at % 2, b_at // 2, s_at % 2, s_at // 2
        turned = [jnp.where(core == 0, a, b) for a, b in ((x, y), (y, x), (z % 2, z // 2), (z // 2, z % 2))]
        pos = jnp.stack([core, x, y, z, *turned]).astype(jnp.int32)
        vecs = [(6 + k, at, True) for at in range(LAYERS) for k in range(4)]
        groups = []
        for l in range(LAYERS):
            groups += [[(order[m], l, False) for m in "fic"] + vecs * (l == 0), [(order[m], l, False) for m in "udo"]]
        gate_rows, rest_rows = sum(slab_rows[m] for m in "fic"), sum(slab_rows[m] for m in "udo")
        rows = [gate_rows + 16, rest_rows] + [gate_rows, rest_rows] * (LAYERS - 1)
        packs = call(
            functools.partial(pack_kernel, groups), 1,
            [whole(far(m)) for m in matrices.values()] + [whole(far(v)) for v in vectors],
            [whole_out((r, LANE), BF16) for r in rows], [pltpu.VMEM((16, LANE), F32)], 2, "pack",
        )
        line_g0 = line_gather(pos, line_parts(packs[0]), rows[:1])
        parts_g0 = [swap(line_g0, *X_AXIS), swap(line_g0, *Y_AXIS)]
        parts_g0 += [swap(parts_g0[0][:2], *Y_AXIS), swap(parts_g0[1][2:], *X_AXIS)]
        line_r0 = line_gather(pos, line_parts(after(packs[1], line_g0)), rows[1:2])
        sent_r0 = after(line_r0, *parts_g0[:2])
        parts_r0 = [cross(sent_r0, FIRST), cross(sent_r0, SECOND)]
        parts_g1 = line_parts(after(packs[2], line_r0, *parts_g0[2:]))
        got = [plane_gather(pos, line_g0, parts_g0), None]
        places = {"f": 0, "i": 1, "c": 2, "u": 0, "d": 1, "o": 4}
        view = lambda got: {m: (got[m in "udo"], slab_rows[m], places[m]) for m in "udofic"}
        weights, lines_at, parts_at = [view(got)], [line_r0], [parts_r0]
        vecs = call(
            functools.partial(vector_kernel, None), 1,
            [(got[0], (NS, 1, 16, LANE), lambda i: (0, 0, 3 * slab_rows["f"] // 16, 0))],
            [whole_out((2, size)) for l in range(LAYERS) for size in (d, h)],
            [pltpu.VMEM((NS, 16, LANE), F32)], 1, "vectors",
        )
        gains, biases = vecs[0::2], vecs[1::2]
    else:
        pos = jnp.zeros((8,), jnp.int32)

        def full(m):
            m = lax.all_gather(m, "batch", axis=1, tiled=True)
            return lax.all_gather(m, "seq", axis=0, tiled=True)

        weights = [
            {m: (slabs(full(matrices[m][l]), NS, NB), slab_rows[m], 0) for m in "udofic"} for l in range(LAYERS)
        ]
        whole_vectors = [lax.all_gather(v, "seq", axis=1, tiled=True).astype(F32) for v in vectors]
        gains = [jnp.stack([whole_vectors[0][l], whole_vectors[3][l]]) for l in range(LAYERS)]
        biases = [jnp.stack([whole_vectors[1][l], whole_vectors[2][l]]) for l in range(LAYERS)]

    def to_rows(v):
        return v.reshape(seqs, CHUNKS, sz.steps, d).transpose(0, 2, 1, 3).reshape(sz.n, d)

    def from_rows(v):
        return v.reshape(seqs, sz.steps, CHUNKS, d).transpose(0, 2, 1, 3).reshape(seqs, length, d)

    stream, grad = to_rows(tokens), to_rows(cotangent)
    kept, diagonals = [], []
    for l in range(LAYERS):
        save = (True,) if l + 1 < LAYERS else ()
        normed, decay, inflow, cand, f_f, f_i, f_c, cp, ch, fin = gate_forward(
            sz, stream, gains[l], biases[l], weights[l], (True,)
        )
        if standard:
            near, beside = parts_at[l]
            if l + 1 < LAYERS:
                line_g1 = line_gather(pos, [after(parts_g1[0], fin), *parts_g1[1:]], rows[2:3])

            def hold(step, other):
                if step == 0:
                    return [line_g1] if l + 1 < LAYERS else []
                if step == 1:
                    diagonals.append(cross(after(near, other, beside), SECOND))
                return []

            ent, _ = enter(fin, seqs, False, (), hold)
            diagonal = diagonals[l] = after(diagonals[l], ent)
            rest = plane_gather(pos, lines_at[l], [near, beside, diagonal])
            weights[l] = view([weights[l]["f"][0], rest])
        else:
            ent, _ = enter(fin, seqs, False)
        hidden, hb, e, mid, n2, act, slope, result = mix_forward(
            sz, stream, gains[l], decay, inflow, cp, ch, ent, weights[l], l == LAYERS - 1, save
        )
        if standard and l + 1 < LAYERS:
            own, *others = line_parts(after(packs[2 * l + 3], ent))
            line_r = line_gather(pos, [after(own, result), *others], rows[2 * l + 3 : 2 * l + 4])
            sent_g = after(line_g1, diagonal)
            parts_g = [cross(sent_g, FIRST), cross(sent_g, SECOND)]
            parts_g.append(cross(after(parts_g[0], line_r), SECOND))
            sent_r = after(line_r, *parts_g[:2])
            weights.append(view([plane_gather(pos, line_g1, parts_g, (result,)), None]))
            lines_at.append(line_r)
            parts_at.append([cross(sent_r, FIRST), cross(sent_r, SECOND)])
        kept.append((stream, normed, decay, cand, f_f, f_i, f_c, hidden, hb, e, mid, n2, act, slope))
        stream = result
    output = from_rows(stream)

    vector_grads, sums, pending = [None] * LAYERS, [], []
    above = None
    for l in reversed(range(LAYERS)):
        x, normed, decay, cand, f_f, f_i, f_c, hidden, hb, e, mid, n2, act, slope = kept[l]
        place = far if l + 1 < LAYERS else lambda a: a
        decay, cand, f_f, f_i, f_c, hidden = map(far, (decay, cand, f_f, f_i, f_c, hidden))
        mid, slope = place(mid), place(slope)
        gr, gpre, gmid, go, ggain_two, gh, cp, ca, fin = mlp_backward(sz, grad, gains[l], mid, slope, decay, weights[l])

        def up(message):
            if above:
                message = above_up.step(message)
            return up_weights(sz, pos, place(after(n2, message)), gpre)

        def down(message):
            if above:
                message = above.step(message)
            return row_weights(sz, pos, place(after(act, message)), gr, "down_weights")

        def out(message):
            return row_weights(sz, pos, place(after(hb, message)), go, "out_weights")

        def both(message):
            return [*down(message), *out(message)]

        def begin(message):
            if above:
                message = above_up.step(message)
            exchanged = core_exchange([made[0], made[1][:2], made[1][2:]])
            upright = None
            if not above:
                upright = UprightReduction(pos, [(l, "u")], (after(exchanged[0][0], message), exchanged[0][1]))
                message = upright.seen
            (keep, got), *others = exchanged[1:]
            begun.extend([exchanged, upright, Reduction(pos, [(l, "d"), (l, "o")], [(after(keep, message), got), *others])])
            return [begun[2].seen]

        made, begun = [], []

        def keep_made(work):
            def run(message):
                made.append(work(message))
                return made[-1]

            return run

        if standard:
            ent, _ = enter(fin, seqs, True, (keep_made(up), keep_made(both), begin))
            exchanged, upright, mlp = begun
            gmid = after(gmid, mlp.seen)
        else:
            ent, pairs = enter(fin, seqs, True, (up, down, out))
        final = []
        if l == 0 and standard:
            final = [(ggain_two, 3)]
            for at in range(1, LAYERS):
                final += [(v, 4 * at + row) for v, row in zip(vector_grads[at], (0, 1, 3))]
        *gate_pair, gbias, grad, ggain_one = gate_backward(
            sz, pos, x, gains[l], gmid, gh, decay, hidden, e, cand, f_f, f_i, f_c, cp, ca, ent, far(normed), weights[l],
            l == 0, final,
        )
        vector_grads[l] = (ggain_one, gbias, ggain_two)
        if not standard:
            pending.append((l, pairs + [gate_pair]))
            continue
        names = [(l, m) for m in "fic"]
        if l == 0:
            names += [(at, k) for at in range(LAYERS) for k in range(4)]
        if above:
            gate_pair[1] = after(gate_pair[1], above.step(gate_pair[0]))
        ((keep, got),) = core_exchange([gate_pair])
        gates = Reduction(pos, names, [(keep, got)])
        if l == 0:
            upright = UprightReduction(pos, [(l, "u")], (after(exchanged[0][0], gates.seen), exchanged[0][1]))
        if l > 0:
            grad, above, above_up = after(grad, gates.seen), mlp, upright
            above.join(gates)
            continue
        mlp.step(above_up.step(above.step(upright.seen)))
        gates.step(mlp.seen)
        above_up.total(upright.step(above.total(gates.seen)))
        mlp.join(gates)
        mlp.step(above_up.parts[0])
        upright.step(mlp.seen)
        mlp.step(upright.step())
        sums = [(one.names, one.parts) for one in (above, above_up, mlp, upright)]
    grad_tokens = from_rows(grad)

    if standard:
        layout, ins = [], []
        for names, parts in sums:
            pieces = [(order[m], l, False) if m in order else (6 + m, l, True) for l, m in names]
            layout.append((len(parts), pieces))
            ins += [whole(p) for p in parts]
        found = call(
            functools.partial(finish_kernel, layout), 1, ins,
            [whole_out(m.shape) for m in matrices.values()] + [whole_out(v.shape) for v in vectors], [], 3, "finish",
        )
        g_up, g_down, g_out, g_f, g_i, g_c, g_norm, g_fb, g_ib, g_mlp = found
    else:
        per_layer = {}
        for l, pairs in pending:
            blocks = [jnp.stack([keep, send], axis=2).reshape(NS, NB, -1, LANE) for keep, send in pairs]
            gates = jnp.split(blocks[3], 3, axis=2)
            for m, g in zip("udofic", blocks[:3] + gates):
                v = unslab(g, matrices[m].shape[1] * seq_count, matrices[m].shape[2] * batch_count)
                v = lax.psum_scatter(v, "seq", scatter_dimension=0, tiled=True)
                per_layer[m, l] = lax.psum_scatter(v, "batch", scatter_dimension=1, tiled=True).astype(F32)
        g_up, g_down, g_out, g_f, g_i, g_c = [
            jnp.stack([per_layer[m, l] for l in range(LAYERS)]) for m in matrices
        ]
        rows = [
            (ggain_one[0], gbias[0], gbias[1], ggain_two[0]) for ggain_one, gbias, ggain_two in vector_grads
        ]
        g_norm, g_fb, g_ib, g_mlp = [
            lax.psum(lax.psum_scatter(jnp.stack([r[k] for r in rows]), "seq", scatter_dimension=1, tiled=True), "batch")
            for k in range(4)
        ]
    return output, grad_tokens, g_norm, g_f, g_i, g_c, g_fb, g_ib, g_out, g_mlp, g_up, g_down


def solution(mesh):
    split, vector, matrix = P("batch", "seq", None), P(None, "seq"), P(None, "seq", "batch")
    order = (vector, matrix, matrix, matrix, vector, vector, matrix, vector, matrix, matrix)
    return jax.shard_map(
        body,
        mesh=mesh,
        in_specs=(split,) + order + (split,),
        out_specs=(split, split) + order,
        check_vma=False,
    )
```

```python
import functools

import jax
import jax.numpy as jnp
from jax import lax
from jax.experimental import pallas as pl
from jax.experimental.pallas import tpu as pltpu
from jax.sharding import PartitionSpec as P

LAYERS = 2
EPS = 1e-05
NS, NB, LANE = 8, 4, 128
CHUNKS = 8
STEPS = 2
GATE_STEPS = 4
TURN, WIDE = 2, 256
VMEM = 28 * 1024 * 1024
F32, BF16 = jnp.float32, jnp.bfloat16


def dot(left, right):
    return lax.dot_general(left, right, (((1,), (0,)), ((), ())), preferred_element_type=F32)


def dot_nt(left, right):
    return lax.dot_general(left, right, (((1,), (1,)), ((), ())), preferred_element_type=F32)


def dot_tn(left, right):
    return lax.dot_general(left, right, (((0,), (0,)), ((), ())), preferred_element_type=F32)


def columns_of(ref, slabs=2):
    rows = ref.shape[2] // slabs
    parts = [
        ref[:, b, j * rows : (j + 1) * rows, :].reshape(NS * rows, LANE) for b in range(ref.shape[1]) for j in range(slabs)
    ]
    return jnp.concatenate(parts, axis=1)


def rows_of(ref):
    parts = [ref[:, j].reshape(-1, LANE) for j in range(NB)]
    return jnp.concatenate(parts, axis=1)


def rms_scale(values):
    return lax.rsqrt(jnp.mean(values * values, axis=-1, keepdims=True) + EPS)


def rms_back(values, gain, grad):
    scale = rms_scale(values)
    unit = values * scale
    inner = grad * gain
    back = scale * (inner - unit * jnp.mean(inner * unit, axis=-1, keepdims=True))
    return back, jnp.sum(grad * unit, axis=0, keepdims=True)


def gate_kernel(
    seqs, steps, x_ref, gain_ref, bias_ref, wf_ref, wi_ref, wc_ref,
    normed_ref, decay_ref, inflow_ref, cand_ref, ff_ref, fi_ref, fc_ref, cp_ref, ch_ref, fin_ref,
    z,
):
    width = decay_ref.shape[1]

    @pl.when(pl.program_id(0) == 0)
    def _():
        x = x_ref[...].astype(F32)
        normed_ref[...] = (x * rms_scale(x) * gain_ref[0:1, :]).astype(BF16)

    weights = jnp.concatenate([columns_of(ref) for ref in (wf_ref, wi_ref, wc_ref)], axis=1)
    block = TURN * CHUNKS
    places = [(seq, left) for seq in range(seqs) for left in range(0, width, WIDE)]

    def turn(of, at, carry):
        carry = list(carry)
        for k, (seq, left) in enumerate(places):
            if seq != of:
                continue
            span = slice(seq * steps * CHUNKS + at * block, seq * steps * CHUNKS + (at + 1) * block)
            cols = slice(left, left + WIDE)
            f = z[span, cols] + bias_ref[0:1, cols]
            i = z[span, width + left : width + left + WIDE] + bias_ref[1:2, cols]
            c = z[span, 2 * width + left : 2 * width + left + WIDE]
            low = jnp.minimum(jnp.minimum(f, i), 0.0)
            e0, ef, ei = jnp.exp(low), jnp.exp(low - f), jnp.exp(low - i)
            a, b = e0 + ef, e0 + ei
            inv = 1.0 / (a + b)
            decay, other = b * inv, a * inv
            ec = jnp.exp(-jnp.abs(c))
            cand = jnp.maximum(c, 0.0) + jnp.log1p(ec)
            slope = jnp.where(c >= 0.0, 1.0, ec) / (1.0 + ec)
            inflow = other * cand
            decay_ref[span, cols] = decay
            inflow_ref[span, cols] = inflow
            cand_ref[span, cols] = cand
            ff_ref[span, cols] = (ef * inv * decay).astype(BF16)
            fi_ref[span, cols] = (ei * inv * other).astype(BF16)
            fc_ref[span, cols] = (other * slope).astype(BF16)
            prod, state = carry[2 * k], carry[2 * k + 1]
            for t in range(TURN):
                d = decay[t * CHUNKS : (t + 1) * CHUNKS]
                prod = prod * d
                state = state * d + inflow[t * CHUNKS : (t + 1) * CHUNKS]
            carry[2 * k], carry[2 * k + 1] = prod, state
        return tuple(carry)

    one, zero = jnp.ones((CHUNKS, WIDE), F32), jnp.zeros((CHUNKS, WIDE), F32)
    carry = (one, zero) * len(places)
    for seq in range(seqs):
        rows = slice(seq * steps * CHUNKS, (seq + 1) * steps * CHUNKS)
        z[rows, :] = dot(normed_ref[rows, :], weights)
        for at in range(steps // TURN):
            carry = turn(seq, at, carry)
    for k, (seq, left) in enumerate(places):
        prod, state = carry[2 * k], carry[2 * k + 1]
        cols = slice(left, left + WIDE)
        cp_ref[seq, :, cols], ch_ref[seq, :, cols] = prod, state
        whole, last = prod[0:1], state[0:1]
        for c in range(1, CHUNKS):
            whole, last = whole * prod[c : c + 1], last * prod[c : c + 1] + state[c : c + 1]
        fin_ref[seq : seq + 1, cols] = whole
        fin_ref[seqs + seq : seqs + seq + 1, cols] = last


def mix_kernel(
    seqs, steps, x_ref, gain_ref, decay_ref, inflow_ref, cp_ref, ch_ref, ent_ref, wo_ref, wu_ref, wd_ref,
    hidden_ref, hb_ref, e_ref, mid_ref, n2_ref, act_ref, slope_ref, out_ref,
    acc,
):
    at_step = pl.program_id(0)
    block = TURN * CHUNKS
    width = decay_ref.shape[1]
    places = [(seq, left) for seq in range(seqs) for left in range(0, width, WIDE)]

    @pl.when(at_step == 0)
    def _():
        acc[...] = x_ref[...].astype(F32)

    @pl.when(at_step < STEPS)
    def _():
        for seq in range(seqs):
            state = ent_ref[seq : seq + 1, :]
            for c in range(CHUNKS):
                e_ref[seq, c : c + 1, :] = state
                state = state * cp_ref[seq, c : c + 1, :] + ch_ref[seq, c : c + 1, :]

        def turn(at, carry):
            carry = list(carry)
            for k, (seq, left) in enumerate(places):
                span = pl.ds(pl.multiple_of(seq * steps * CHUNKS + at * block, block), block)
                cols = slice(left, left + WIDE)
                d, u = decay_ref[span, cols], inflow_ref[span, cols]
                state, found = carry[k], []
                for t in range(TURN):
                    state = state * d[t * CHUNKS : (t + 1) * CHUNKS] + u[t * CHUNKS : (t + 1) * CHUNKS]
                    found.append(state)
                carry[k] = state
                hidden = jnp.concatenate(found, axis=0)
                hidden_ref[span, cols] = hidden
                hb_ref[span, cols] = hidden.astype(BF16)
            return tuple(carry)

        lax.fori_loop(0, steps // TURN, turn, tuple(e_ref[seq, :, left : left + WIDE] for seq, left in places))
        acc[...] += dot(hb_ref[...], rows_of(wo_ref))

    @pl.when(at_step == STEPS - 1)
    def _():
        middle = acc[...]
        mid_ref[...] = middle
        n2_ref[...] = (middle * rms_scale(middle) * gain_ref[1:2, :]).astype(BF16)

    @pl.when(at_step >= STEPS)
    def _():
        w_up, w_down = columns_of(wu_ref, 4), rows_of(wd_ref)
        size = acc.shape[0] // 2
        for k in range(2):
            span = slice(k * size, (k + 1) * size)
            v = dot(n2_ref[span, :], w_up)
            phi = 0.5 + 0.5 * lax.erf(v * 0.7071067811865476)
            act = (v * phi).astype(BF16)
            act_ref[span, :] = act
            slope_ref[span, :] = (phi + v * (0.3989422804014327 * jnp.exp(v * v * -0.5))).astype(BF16)
            acc[span, :] += dot(act, w_down)

    @pl.when(at_step == 2 * STEPS - 1)
    def _():
        out_ref[...] = acc[...].astype(out_ref.dtype)


def mlp_back_kernel(
    seqs, steps, g_ref, gain_ref, mid_ref, slope_ref, decay_ref, wo_ref, wu_ref, wd_ref,
    gr_ref, gpre_ref, gmid_ref, go_ref, ggain_ref, gh_ref, cp_ref, ca_ref, fin_ref,
    acc,
):
    at_step = pl.program_id(0)
    block = TURN * CHUNKS
    width = decay_ref.shape[1]
    places = [(seq, left) for seq in range(seqs) for left in range(0, width, WIDE)]

    @pl.when(at_step == 0)
    def _():
        gr_ref[...] = g_ref[...].astype(BF16)
        acc[...] = jnp.zeros_like(acc)

    @pl.when(at_step < STEPS)
    def _():
        gact = dot_nt(gr_ref[...], rows_of(wd_ref))
        gpre_ref[...] = (gact * slope_ref[...].astype(F32)).astype(BF16)
        acc[...] += dot_nt(gpre_ref[...], columns_of(wu_ref, 4))

    @pl.when(at_step == STEPS - 1)
    def _():
        back, ggain = rms_back(mid_ref[...], gain_ref[1:2, :], acc[...])
        ggain_ref[...] = ggain
        gmid = g_ref[...].astype(F32) + back
        gmid_ref[...] = gmid
        go_ref[...] = gmid.astype(BF16)

    @pl.when(at_step >= STEPS)
    def _():
        gh_ref[...] = dot_nt(go_ref[...], rows_of(wo_ref))

        def turn(turn_at, carry):
            at = steps // TURN - 1 - turn_at
            carry = list(carry)
            for k, (seq, left) in enumerate(places):
                span = pl.ds(pl.multiple_of(seq * steps * CHUNKS + at * block, block), block)
                cols = slice(left, left + WIDE)
                d, g = decay_ref[span, cols], gh_ref[span, cols]
                prod, state = carry[2 * k], carry[2 * k + 1]
                for t in reversed(range(TURN)):
                    dk = d[t * CHUNKS : (t + 1) * CHUNKS]
                    prod = prod * dk
                    state = dk * (g[t * CHUNKS : (t + 1) * CHUNKS] + state)
                carry[2 * k], carry[2 * k + 1] = prod, state
            return tuple(carry)

        one, zero = jnp.ones((CHUNKS, WIDE), F32), jnp.zeros((CHUNKS, WIDE), F32)
        carry = lax.fori_loop(0, steps // TURN, turn, (one, zero) * len(places))
        for k, (seq, left) in enumerate(places):
            prod, state = carry[2 * k], carry[2 * k + 1]
            cols = slice(left, left + WIDE)
            cp_ref[seq, :, cols], ca_ref[seq, :, cols] = prod, state
            whole, last = prod[CHUNKS - 1 :], state[CHUNKS - 1 :]
            for c in reversed(range(CHUNKS - 1)):
                whole, last = whole * prod[c : c + 1], last * prod[c : c + 1] + state[c : c + 1]
            fin_ref[seq : seq + 1, cols] = whole
            fin_ref[seqs + seq : seqs + seq + 1, cols] = last


def gate_back_kernel(
    seqs, steps, others, pos_ref, x_ref, gain_ref, gmid_ref, gh_ref, decay_ref, hidden_ref, e_ref, cand_ref,
    ff_ref, fi_ref, fc_ref, cp_ref, ca_ref, ent_ref, normed_ref, wf_ref, wi_ref, wc_ref, *refs,
):
    given = refs[: len(others)]
    keep_ref, send_ref, gbias_ref, gstream_ref, ggain_ref, acc, start, dz, rest = refs[len(others) :]
    at_step = pl.program_id(0)
    block = TURN * CHUNKS
    width = decay_ref.shape[1]
    places = [(seq, left) for seq in range(seqs) for left in range(0, width, WIDE)]

    @pl.when(at_step == 0)
    def _():
        acc[...] = jnp.zeros_like(acc)

    for seq in range(seqs):
        state = ent_ref[seq : seq + 1, :]
        for c in reversed(range(CHUNKS)):
            start[seq, c : c + 1, :] = state
            state = state * cp_ref[seq, c : c + 1, :] + ca_ref[seq, c : c + 1, :]

    def turn(of, at, carry):
        carry = list(carry)
        for k, (seq, left) in enumerate(places):
            if seq != of:
                continue
            cols = slice(left, left + WIDE)
            state, sum_f, sum_i = carry[3 * k : 3 * k + 3]
            base = seq * steps * CHUNKS + at * block
            span = slice(base, base + block)
            before = hidden_ref[base - CHUNKS : base, cols] if at else e_ref[seq, :, cols]
            d, g = decay_ref[span, cols], gh_ref[span, cols]
            previous = jnp.concatenate([before, hidden_ref[span, cols][: block - CHUNKS]], axis=0)
            found = []
            for t in reversed(range(TURN)):
                now = g[t * CHUNKS : (t + 1) * CHUNKS] + state
                found.append(now)
                state = d[t * CHUNKS : (t + 1) * CHUNKS] * now
            gstate = jnp.concatenate(found[::-1], axis=0)
            both = gstate * (cand_ref[span, cols] - previous)
            dzf = (-ff_ref[span, cols].astype(F32) * both).astype(BF16)
            dzi = (fi_ref[span, cols].astype(F32) * both).astype(BF16)
            dz[span, left : left + WIDE] = dzf
            dz[span, width + left : width + left + WIDE] = dzi
            dz[span, 2 * width + left : 2 * width + left + WIDE] = (fc_ref[span, cols].astype(F32) * gstate).astype(BF16)
            wide_f, wide_i = dzf.astype(F32), dzi.astype(F32)
            for t in range(TURN):
                sum_f = sum_f + wide_f[t * CHUNKS : (t + 1) * CHUNKS]
                sum_i = sum_i + wide_i[t * CHUNKS : (t + 1) * CHUNKS]
            carry[3 * k : 3 * k + 3] = state, sum_f, sum_i
        return tuple(carry)

    zero = jnp.zeros((CHUNKS, WIDE), F32)
    first_carry = [v for seq, left in places for v in (start[seq, :, left : left + WIDE], zero, zero)]
    carry = tuple(first_carry)
    weights = jnp.concatenate([columns_of(ref) for ref in (wf_ref, wi_ref, wc_ref)], axis=1)
    grad = None
    for seq in range(seqs):
        rows = slice(seq * steps * CHUNKS, (seq + 1) * steps * CHUNKS)
        for at in reversed(range(steps // TURN)):
            carry = turn(seq, at, carry)
        acc[rows, :] += dot_nt(dz[rows, :], weights)
        part = dot_tn(normed_ref[rows, :], dz[rows, :])
        grad = part if grad is None else grad + part
    for row in range(2):
        for left in range(0, width, WIDE):
            total = sum(carry[3 * k + 1 + row] for k, place in enumerate(places) if place[1] == left)
            gbias_ref[row : row + 1, left : left + WIDE] = jnp.sum(total, axis=0, keepdims=True)
    rows = wf_ref.shape[2]
    for m in range(3):
        put_columns(pos_ref, keep_ref, send_ref, m * rows, grad[:, m * width : (m + 1) * width])

    @pl.when(at_step == STEPS - 1)
    def _():
        back, ggain = rms_back(x_ref[...].astype(F32), gain_ref[0:1, :], acc[...])
        ggain_ref[...] = ggain
        gstream_ref[...] = (gmid_ref[...] + back).astype(gstream_ref.dtype)

    if others:

        def rows_to(ref, first_row):
            wide = ref.shape[1] // NS
            for r in range(ref.shape[0]):
                for s in range(NS):
                    rest[s, first_row + r : first_row + r + 1, :wide] = ref[r : r + 1, s * wide : (s + 1) * wide]

        @pl.when(at_step == 0)
        def _():
            rest[...] = jnp.zeros_like(rest)
            for ref, first_row in zip(given, others):
                rows_to(ref, first_row)

        wide = width * STEPS // NS
        for row in range(2):
            for s in range(width // wide):
                rest[at_step * (width // wide) + s, 1 + row : 2 + row, :wide] = gbias_ref[row : row + 1, s * wide : (s + 1) * wide]

        @pl.when(at_step == STEPS - 1)
        def _():
            rows_to(ggain_ref, 0)
            found = rest[...].astype(BF16)
            for x in range(2):
                keep_ref[:, x, 3 * rows :, :] = found
                send_ref[:, x, 3 * rows :, :] = found


def send_or_keep(mine, keep_ref, send_ref, put):
    @pl.when(mine)
    def _():
        put(keep_ref)

    @pl.when(jnp.logical_not(mine))
    def _():
        put(send_ref)


def put_columns(pos_ref, keep_ref, send_ref, start, value):
    rows, width = value.shape[0] // NS, value.shape[1] // 2
    x = pl.program_id(0)
    for core in range(2):
        parts = [
            value[:, left : left + LANE].astype(BF16).reshape(NS, rows, LANE)
            for left in range(core * width, (core + 1) * width, LANE)
        ]

        def put(ref):
            for j, part in enumerate(parts):
                ref[:, x, start + j * rows : start + (j + 1) * rows, :] = part

        send_or_keep(pos_ref[0] == core, keep_ref, send_ref, put)


def put_rows(pos_ref, keep_ref, send_ref, value):
    count = NS // STEPS
    for j in range(NB):
        part = value[:, j * LANE : (j + 1) * LANE].astype(BF16).reshape(count, -1, LANE)

        def put(ref):
            ref[pl.ds(pl.program_id(0) * count, count), j // 2] = part

        send_or_keep(pos_ref[0] == j % 2, keep_ref, send_ref, put)


def up_weight_kernel(pos_ref, n2_ref, gpre_ref, keep_ref, send_ref):
    put_columns(pos_ref, keep_ref, send_ref, 0, dot_tn(n2_ref[...], gpre_ref[...]))


def row_weight_kernel(pos_ref, left_ref, right_ref, keep_ref, send_ref):
    put_rows(pos_ref, keep_ref, send_ref, dot_tn(left_ref[...], right_ref[...]))


def add(*parts):
    total = parts[0].astype(F32)
    for part in parts[1:]:
        total = total + part.astype(F32)
    return total


def pair_sum_kernel(rows, pos_ref, *refs):
    count = len(rows)
    send, stay = refs[2 * count :]
    core, x, y, step = pos_ref[0], pos_ref[1], pos_ref[2], pos_ref[4]
    at = 0
    for keep, got, r in zip(refs[:count], refs[count : 2 * count], rows):
        for v in range(2):
            for out, first in ((send, 1 - step), (stay, step)):
                iy, ix = jnp.where(core == 0, v, first), jnp.where(core == 0, first, v)
                out[0, v, at : at + r] = add(keep[0, iy, ix], got[0, iy, ix]).astype(BF16)
        at += r


def plane_sum_kernel(pos_ref, *refs):
    second = pos_ref[5]
    *pairs, send, stay = refs
    at = 0
    for keep, got in zip(pairs[::2], pairs[1::2]):
        rows = slice(at, at + keep.shape[2])
        send[0, rows, :] = add(keep[0, 1 - second], got[0, 1 - second]).astype(BF16)
        stay[0, rows, :] = add(keep[0, second], got[0, second]).astype(BF16)
        at += keep.shape[2]


def line_sum_kernel(pos_ref, *refs):
    core, first = pos_ref[0], pos_ref[6]
    *pairs, send, stay = refs
    at = 0
    for keep, got in zip(pairs[::2], pairs[1::2]):
        rows = slice(at, at + keep.shape[1])
        for v in range(2):
            for out, f in ((send, 1 - first), (stay, first)):
                z = jnp.where(core == 0, f + 2 * v, 2 * f + v)
                out[v, rows, :] = add(keep[z], got[z]).astype(BF16)
        at += keep.shape[1]


def last_sum_kernel(pos_ref, keep, got, send, stay):
    second = pos_ref[7]
    send[...] = add(keep[1 - second], got[1 - second]).astype(BF16)
    stay[...] = add(keep[second], got[second]).astype(BF16)


def total_kernel(keep, got, out):
    out[...] = add(keep[...], got[...])


def finish_kernel(layout, *refs):
    at = 0
    ins = sum(parts for parts, _ in layout)
    outs = refs[ins:]
    for parts, pieces in layout:
        got = refs[at : at + parts]
        at += parts
        row = 0
        for out, layer, vectors in pieces:
            ref = outs[out]
            if vectors:
                ref[layer : layer + 1, :] = add(*[g[...] for g in got])[row : row + 1, : ref.shape[1]]
                row += 1
                continue
            r = ref.shape[1]
            for j in range(ref.shape[2] // LANE):
                ref[layer, :, j * LANE : (j + 1) * LANE] = add(*[g[row : row + r] for g in got])
                row += r


def pack_kernel(groups, *refs):
    ins = refs[: len(refs) - len(groups) - 1]
    outs, scratch = refs[len(ins) : -1], refs[-1]
    for out, group in zip(outs, groups):
        row = 0
        vec = 0
        for which, layer, vector in group:
            ref = ins[which]
            if vector:
                if vec == 0:
                    scratch[...] = jnp.zeros_like(scratch)
                scratch[vec : vec + 1, : ref.shape[1]] = ref[...].astype(F32)[layer : layer + 1]
                vec += 1
                continue
            r = ref.shape[1]
            for j in range(ref.shape[2] // LANE):
                out[row : row + r, :] = ref[layer, :, j * LANE : (j + 1) * LANE]
                row += r
        if vec:
            out[row:, :] = scratch[...].astype(BF16)


def line_gather_kernel(pos_ref, *refs):
    row = 0
    for out in refs[4:]:
        rows = out.shape[1]
        for k, part in enumerate(refs[:4]):
            out[pos_ref[3] ^ k] = part[row : row + rows, :]
        row += rows


def plane_gather_kernel(pos_ref, *refs):
    out = refs[-1]
    at, half = pl.program_id(0), pl.num_programs(0) // 2
    core, x, y = pos_ref[0], pos_ref[1], pos_ref[2]
    count = len(refs) // 2
    for c in range(2):
        own, first, second, *diagonal = refs[count * c : count * (c + 1)]
        other = core ^ c
        turn = other if count == 4 else 0
        out[0, y, x, other] = own[0]
        out[0, y ^ turn, x ^ (1 - turn), other] = first[0]
        out[0, y ^ (1 - turn), x ^ turn, other] = second[0]
        if count == 4:
            out[0, y ^ 1, x ^ 1, other] = diagonal[0][0]
            continue

        @pl.when(at < half)
        def _():
            out[0, y ^ 1, x ^ 1, other] = diagonal[0][0]

        @pl.when(at >= half)
        def _():
            out[0, y ^ 1, x ^ 1, other] = diagonal[1][0]


def vector_kernel(gained, w_ref, *refs):
    outs, scratch = refs[:-1], refs[-1]
    scratch[...] = w_ref[:, 0].astype(F32)
    for l in range(LAYERS):
        for which in range(4):
            out, row = ((outs[2 * l], which // 3) if which in (0, 3) else (outs[2 * l + 1], which - 1))
            wide = out.shape[1] // NS
            for s in range(NS):
                out[row : row + 1, s * wide : (s + 1) * wide] = scratch[s, 4 * l + which : 4 * l + which + 1, :wide]


def shape(dims, dtype=F32):
    return jax.ShapeDtypeStruct(dims, dtype)


def call(kernel, grid, ins, outs, scratch, us, name):
    def spec(a, block, index):
        if a.dtype == jnp.int32:
            return pl.BlockSpec(memory_space=pltpu.SMEM)
        return pl.BlockSpec(block, index)

    found = pl.pallas_call(
        kernel,
        grid=(grid,),
        in_specs=[spec(*one) for one in ins],
        out_specs=[pl.BlockSpec(block, index) for _, block, index, *_ in outs],
        out_shape=[pltpu.HBM(one[0].shape, one[0].dtype) if one[3:] else one[0] for one in outs],
        scratch_shapes=scratch,
        compiler_params=pltpu.CompilerParams(vmem_limit_bytes=VMEM),
        cost_estimate=pl.CostEstimate(flops=int(us * 1.1e9) + 1, bytes_accessed=1024, transcendentals=0),
        name=name,
    )(*[a for a, _, _ in ins])
    return found if len(found) > 1 else found[0]


def far(array):
    return pltpu.with_memory_space_constraint(array, pltpu.HBM)


def anywhere(array):
    return array


def whole(array):
    dims = array.shape
    return (array, dims, lambda i: (0,) * len(dims))


def whole_out(dims, dtype=F32):
    return (shape(dims, dtype), dims, lambda i: (0,) * len(dims))


def first(i):
    return jnp.minimum(i, STEPS - 1)


def second(i):
    return jnp.maximum(i - STEPS, 0)


class Sizes:
    def __init__(self, seqs, length, d, h, ff):
        self.seqs, self.steps, self.n = seqs, length // CHUNKS, seqs * length
        self.d, self.h, self.ff = d, h, ff
        self.hb, self.fb = h // STEPS, ff // STEPS


def column_weight(view, at, late=False, steps=STEPS):
    array, rows, place = view
    return (far(array) if late else array, (NS, NB // steps, rows, LANE), lambda i: (0, at(i), place, 0))


def row_weight(view, at):
    array, rows, place = view
    return (array, (NS // STEPS, NB, rows, LANE), lambda i: (at(i), 0, place, 0))


def same(i):
    return i


def gate_forward(sz, x, gain, bias, w, save):
    n, d, h, wide, s = sz.n, sz.d, sz.h, sz.h // GATE_STEPS, sz.seqs
    col = lambda i: (0, i)
    return call(
        functools.partial(gate_kernel, s, sz.steps), GATE_STEPS,
        [whole(x), whole(gain), (bias, (2, wide), col)] + [column_weight(w[m], same, False, GATE_STEPS) for m in "fic"],
        [whole_out((n, d), BF16) + save]
        + [(shape((n, h)), (n, wide), col) + save, (shape((n, h)), (n, wide), col), (shape((n, h)), (n, wide), col) + save]
        + [(shape((n, h), BF16), (n, wide), col) + save] * 3
        + [(shape((s, CHUNKS, h)), (s, CHUNKS, wide), lambda i: (0, 0, i))] * 2
        + [(shape((2 * s, h)), (2 * s, wide), col)],
        [pltpu.VMEM((n, 3 * wide), F32)], 9, "gates",
    )


def mix_forward(sz, x, gain, decay, inflow, cp, ch, ent, wt, last, save):
    n, d, h, ff, w, f, s = sz.n, sz.d, sz.h, sz.ff, sz.hb, sz.fb, sz.seqs
    col = lambda i: (0, first(i))
    late = lambda i: (0, second(i))
    deep = lambda i: (0, 0, first(i))
    return call(
        functools.partial(mix_kernel, s, sz.steps), 2 * STEPS,
        [
            whole(x), whole(gain), (decay, (n, w), col), (inflow, (n, w), col),
            (cp, (s, CHUNKS, w), deep), (ch, (s, CHUNKS, w), deep), (ent, (s, w), col),
            row_weight(wt["o"], first), column_weight(wt["u"], second), row_weight(wt["d"], second),
        ],
        [
            (shape((n, h)), (n, w), col, True), (shape((n, h), BF16), (n, w), col) + save,
            (shape((s, CHUNKS, h)), (s, CHUNKS, w), deep) + save,
            whole_out((n, d)) + save, whole_out((n, d), BF16) + save,
            (shape((n, ff), BF16), (n, f), late) + save, (shape((n, ff), BF16), (n, f), late) + save,
            whole_out((n, d), BF16 if last else F32),
        ],
        [pltpu.VMEM((n, d), F32)], 14, "mix",
    )


def mlp_backward(sz, g, gain, mid, slope, decay, wt):
    n, d, h, ff, w, f, s = sz.n, sz.d, sz.h, sz.ff, sz.hb, sz.fb, sz.seqs
    col = lambda i: (0, second(i))
    early = lambda i: (0, first(i))
    deep = lambda i: (0, 0, second(i))
    return call(
        functools.partial(mlp_back_kernel, s, sz.steps), 2 * STEPS,
        [
            whole(g), whole(gain), whole(mid), (slope, (n, f), early), (decay, (n, w), col),
            row_weight(wt["o"], second), column_weight(wt["u"], first), row_weight(wt["d"], first),
        ],
        [
            whole_out((n, d), BF16), (shape((n, ff), BF16), (n, f), early), whole_out((n, d)), whole_out((n, d), BF16),
            whole_out((1, d)), (shape((n, h)), (n, w), col),
            (shape((s, CHUNKS, h)), (s, CHUNKS, w), deep), (shape((s, CHUNKS, h)), (s, CHUNKS, w), deep),
            (shape((2 * s, h)), (2 * s, w), col),
        ],
        [pltpu.VMEM((n, d), F32)], 12, "mlp_back",
    )


def gate_backward(sz, pos, x, gain, gmid, gh, decay, hidden, e, cand, ff_, fi_, fc_, cp, ca, ent, normed, wt, last, vectors):
    n, d, h, w, s = sz.n, sz.d, sz.h, sz.hb, sz.seqs
    col = lambda i: (0, i)
    deep = lambda i: (0, 0, i)
    wide = lambda a: (a, (n, w), col)
    rows = 3 * d * h // (32 * LANE) + (16 if vectors else 0)
    return call(
        functools.partial(gate_back_kernel, s, sz.steps, tuple(row for _, row in vectors)), STEPS,
        [
            whole(pos), whole(x), whole(gain), whole(gmid), wide(gh), wide(decay), wide(hidden), (e, (s, CHUNKS, w), deep),
            wide(cand), wide(ff_), wide(fi_), wide(fc_), (cp, (s, CHUNKS, w), deep), (ca, (s, CHUNKS, w), deep),
            (ent, (s, w), col), whole(normed),
        ] + [column_weight(wt[m], same, True) for m in "fic"] + [whole(v) for v, _ in vectors],
        [whole_out((NS, 2, rows, LANE), BF16)] * 2
        + [(shape((2, h)), (2, w), col), whole_out((n, d), BF16 if last else F32), whole_out((1, d))],
        [
            pltpu.VMEM((n, d), F32), pltpu.VMEM((s, CHUNKS, w), F32), pltpu.VMEM((n, 3 * w), BF16),
            pltpu.VMEM((NS, 16, LANE), F32),
        ], 16, "gate_back",
    )


def up_weights(sz, pos, n2, gpre):
    n, d, ff, f = sz.n, sz.d, sz.ff, sz.fb
    dims = (NS, 2, d * ff // (32 * LANE), LANE)
    return call(
        up_weight_kernel, STEPS, [whole(pos), whole(n2), (gpre, (n, f), lambda i: (0, i))],
        [whole_out(dims, BF16)] * 2, [], 5, "up_weights",
    )


def row_weights(sz, pos, left, right, name):
    n, k, d = sz.n, left.shape[1], sz.d
    dims = (NS, 2, k // NS, LANE)
    return call(
        row_weight_kernel, STEPS, [whole(pos), (left, (n, k // STEPS), lambda i: (0, i)), whole(right)],
        [whole_out(dims, BF16)] * 2, [], 5, name,
    )


def swap(array, axes, bits):
    count = lax.axis_size(axes)
    return lax.ppermute(array, axes, [(i, i ^ bits) for i in range(count)])


BOTH = ("seq", "batch")


def after(array, *others):
    return lax.optimization_barrier((array,) + others)[0]


def by_line(a):
    return (a, (1,) + a.shape[1:], lambda i: (i,) + (0,) * (len(a.shape) - 1))


def by_line_out(*dims):
    return (shape(dims, BF16), (1,) + dims[1:], lambda i: (i,) + (0,) * (len(dims) - 1))


def core_exchange(pairs):
    return [(keep, swap(send, "batch", 1)) for keep, send in pairs]


FIRST, SECOND, FIRST_Z, SECOND_Z = (2, 4), (4, 2), (8, 16), (16, 8)


def cross(array, bits):
    count = lax.axis_size(BOTH)
    return lax.ppermute(array, BOTH, [(i, i ^ bits[i % 2]) for i in range(count)])


def pair_sum(pos, pairs):
    rows, lines = tuple(keep.shape[2] for keep, _ in pairs), pairs[0][0].shape[0] // 2
    view = lambda a: by_line(a.reshape((lines, 2, 2) + a.shape[2:]))
    return call(
        functools.partial(pair_sum_kernel, rows), lines,
        [whole(pos)] + [view(keep) for keep, _ in pairs] + [view(got) for _, got in pairs],
        [by_line_out(lines, 2, sum(rows), LANE)] * 2, [], 3, "pair_sum",
    )


def onward(parts, bits):
    return [parts[1], cross(parts[0], bits)]


def plane_sum(pos, parts):
    rows, lines = sum(part.shape[2] for part in parts[::2]), parts[0].shape[0]
    return call(
        plane_sum_kernel, lines, [whole(pos)] + [by_line(a) for a in parts], [by_line_out(lines, rows, LANE)] * 2, [], 0,
        "plane_sum",
    )


def line_sum(pos, parts):
    rows = sum(part.shape[1] for part in parts[::2])
    return call(
        line_sum_kernel, 1, [whole(pos)] + [whole(a) for a in parts], [whole_out((2, rows, LANE), BF16)] * 2, [], 0, "line_sum",
    )


def last_sum(pos, parts):
    rows = parts[0].shape[1]
    return call(
        last_sum_kernel, 1, [whole(pos)] + [whole(a) for a in parts], [whole_out((rows, LANE), BF16)] * 2, [], 0, "last_sum",
    )


SUMS = ((plane_sum, SECOND), (line_sum, FIRST_Z), (last_sum, SECOND_Z))


class Reduction:
    def __init__(self, pos, names, pairs):
        self.pos, self.names, self.stage = pos, names, 0
        self.parts = pair_sum(pos, pairs)
        self.seen = self.parts[0]
        self.parts = onward(self.parts, FIRST)

    def join(self, other):
        self.names, self.parts = self.names + other.names, self.parts + other.parts

    def step(self, *others):
        work, bits = SUMS[self.stage]
        if others:
            self.parts[0] = after(self.parts[0], *others)
        parts = work(self.pos, self.parts)
        self.stage, self.seen, self.parts = self.stage + 1, parts[0], onward(parts, bits)
        return self.seen

    def one_more(self, others, work, bits):
        if others:
            self.parts[0] = after(self.parts[0], *others)
        parts = work(self.pos, self.parts)
        self.seen, self.parts = parts[0], onward(parts, bits)
        return self.seen

    def total(self, *others):
        keep, got = self.parts
        keep = after(keep, *others)
        total = call(total_kernel, 1, [whole(keep), whole(got)], [whole_out(keep.shape)], [], 0, "total")
        self.parts = [total]
        return total


class UprightReduction(Reduction):
    def __init__(self, pos, names, pair):
        self.pos, self.names, self.stage = pos, names, 0
        self.rows = pair[0].shape[2]
        self.parts = [part.reshape(4, 4 * self.rows, LANE) for part in pair]
        self.one_more((), line_sum, FIRST_Z)

    def step(self, *others):
        self.stage += 1
        if self.stage == 1:
            return self.one_more(others, last_sum, SECOND_Z)
        if self.stage == 2:
            pairs = lambda pos, parts: pair_sum(pos, [tuple(part.reshape(2, 2, self.rows, LANE) for part in parts)])
            return self.one_more(others, pairs, FIRST)
        self.one_more(others, plane_sum, SECOND)
        self.parts = [part[0] for part in self.parts]
        return self.seen


def line_parts(own):
    return [own] + [swap(own, "seq", 2 * k) for k in range(1, 4)]


def line_gather(pos, parts, rows, place=anywhere):
    return call(
        line_gather_kernel, 1, [whole(pos)] + [whole(place(p)) for p in parts],
        [whole_out((4, r, LANE), BF16) for r in rows], [], 2, "line_gather",
    )


X_AXIS, Y_AXIS = ("batch", 2), ("seq", 1)


def plane_gather(pos, line, parts, behind=(), place=anywhere):
    rows = line.shape[1]
    parts = [line, *parts]
    parts += [swap(after(p, *behind) if behind else p, "batch", 1) for p in parts]
    each, low, high = (lambda i: (i, 0, 0)), (lambda i: (jnp.minimum(i, 1), 0, 0)), (lambda i: (jnp.maximum(i - 2, 0), 0, 0))
    maps = [each] * 4 if len(parts) == 8 else [each, each, each, low, high]
    got = call(
        plane_gather_kernel, 4, [whole(pos)] + [(place(p), (1, rows, LANE), m) for p, m in zip(parts, maps * 2)],
        [(shape((4, 2, 2, 2, rows, LANE), BF16), (1, 2, 2, 2, rows, LANE), lambda i: (i, 0, 0, 0, 0, 0))], [], 5, "plane_gather",
    )
    return got.reshape(NS, NB, rows, LANE)


def enter(fin, seqs, backward, fill=(), hold=None):
    count, mine = lax.axis_size("seq"), lax.axis_index("seq")
    prod, state = fin[:seqs], fin[seqs:]
    pre_p, pre_s = jnp.ones_like(prod), jnp.zeros_like(state)
    bit, message, done, other = 1, fin, [], fin
    for step in range(int(count).bit_length() - 1):
        before = hold(step, other) if hold else ()
        if before:
            message = after(message, *before)
        other = lax.ppermute(message, "seq", [(i, i ^ bit) for i in range(count)])
        if step < len(fill):
            done.append(fill[step](message))
        if done and bit * 2 == count:
            other = after(other, *done[-1])
        o_p, o_s = other[:seqs], other[seqs:]
        upper = ((mine // bit) % 2 == 1) ^ backward
        pre_p, pre_s = jnp.where(upper, o_p * pre_p, pre_p), jnp.where(upper, pre_p * o_s + pre_s, pre_s)
        state = jnp.where(upper, prod * o_s + state, o_p * state + o_s)
        prod = prod * o_p
        message = jnp.concatenate([prod, state])
        if step < len(fill):
            message = after(message, *done[-1])
        bit *= 2
    return pre_s, done


def slabs(matrix, seq_count, batch_count):
    rows, cols = matrix.shape[0] // NS, matrix.shape[1] // NB
    cut = matrix.reshape(NS, rows, NB, cols // LANE, LANE).transpose(0, 2, 3, 1, 4)
    return cut.reshape(NS, NB, rows * cols // LANE, LANE)


def unslab(blocks, rows, cols):
    r, c = rows // NS, cols // NB
    cut = blocks.reshape(NS, NB, c // LANE, r, LANE).transpose(0, 3, 1, 2, 4)
    return cut.reshape(rows, cols)


def body(
    tokens, norm_gain, w_forget, w_input, w_cand, forget_bias, input_bias, w_out, mlp_gain, w_up, w_down, cotangent
):
    seqs, length, d = tokens.shape
    seq_count, batch_count = lax.axis_size("seq"), lax.axis_size("batch")
    h, ff = w_forget.shape[2] * batch_count, w_up.shape[2] * batch_count
    sz = Sizes(seqs, length, d, h, ff)
    standard = (seq_count, batch_count) == (NS, NB)
    matrices = {"u": w_up, "d": w_down, "o": w_out, "f": w_forget, "i": w_input, "c": w_cand}
    vectors = (norm_gain, forget_bias, input_bias, mlp_gain)
    slab_rows = {"u": d * ff // (32 * LANE), "d": ff // NS, "o": h // NS}
    slab_rows.update({m: d * h // (32 * LANE) for m in "fic"})
    order = {name: k for k, name in enumerate(matrices)}

    if standard:
        s_at, b_at = lax.axis_index("seq"), lax.axis_index("batch")
        core, x, y, z = b_at % 2, b_at // 2, s_at % 2, s_at // 2
        turned = [jnp.where(core == 0, a, b) for a, b in ((x, y), (y, x), (z % 2, z // 2), (z // 2, z % 2))]
        pos = jnp.stack([core, x, y, z, *turned]).astype(jnp.int32)
        vecs = [(6 + k, at, True) for at in range(LAYERS) for k in range(4)]
        groups = []
        for l in range(LAYERS):
            groups += [[(order[m], l, False) for m in "fic"] + vecs * (l == 0), [(order[m], l, False) for m in "udo"]]
        gate_rows, rest_rows = sum(slab_rows[m] for m in "fic"), sum(slab_rows[m] for m in "udo")
        rows = [gate_rows + 16, rest_rows] + [gate_rows, rest_rows] * (LAYERS - 1)
        packs = call(
            functools.partial(pack_kernel, groups), 1,
            [whole(far(m)) for m in matrices.values()] + [whole(far(v)) for v in vectors],
            [whole_out((r, LANE), BF16) for r in rows], [pltpu.VMEM((16, LANE), F32)], 2, "pack",
        )
        line_g0 = line_gather(pos, line_parts(packs[0]), rows[:1], anywhere)
        parts_g0 = [swap(line_g0, *X_AXIS), swap(line_g0, *Y_AXIS)]
        parts_g0 += [swap(parts_g0[0][:2], *Y_AXIS), swap(parts_g0[1][2:], *X_AXIS)]
        line_r0 = line_gather(pos, line_parts(after(packs[1], line_g0)), rows[1:2])
        sent_r0 = after(line_r0, *parts_g0[:2])
        parts_r0 = [cross(sent_r0, FIRST), cross(sent_r0, SECOND)]
        parts_g1 = line_parts(after(packs[2], line_r0, *parts_g0[2:]))
        got = [plane_gather(pos, line_g0, parts_g0, (), anywhere), None]
        places = {"f": 0, "i": 1, "c": 2, "u": 0, "d": 1, "o": 4}
        view = lambda got: {m: (got[m in "udo"], slab_rows[m], places[m]) for m in "udofic"}
        weights, lines_at, parts_at = [view(got)], [line_r0], [parts_r0]
        vecs = call(
            functools.partial(vector_kernel, None), 1,
            [(got[0], (NS, 1, 16, LANE), lambda i: (0, 0, 3 * slab_rows["f"] // 16, 0))],
            [whole_out((2, size)) for l in range(LAYERS) for size in (d, h)],
            [pltpu.VMEM((NS, 16, LANE), F32)], 1, "vectors",
        )
        gains, biases = vecs[0::2], vecs[1::2]
    else:
        pos = jnp.zeros((8,), jnp.int32)

        def full(m):
            m = lax.all_gather(m, "batch", axis=1, tiled=True)
            return lax.all_gather(m, "seq", axis=0, tiled=True)

        weights = [
            {m: (slabs(full(matrices[m][l]), NS, NB), slab_rows[m], 0) for m in "udofic"} for l in range(LAYERS)
        ]
        whole_vectors = [lax.all_gather(v, "seq", axis=1, tiled=True).astype(F32) for v in vectors]
        gains = [jnp.stack([whole_vectors[0][l], whole_vectors[3][l]]) for l in range(LAYERS)]
        biases = [jnp.stack([whole_vectors[1][l], whole_vectors[2][l]]) for l in range(LAYERS)]

    def to_rows(v):
        return v.reshape(seqs, CHUNKS, sz.steps, d).transpose(0, 2, 1, 3).reshape(sz.n, d)

    def from_rows(v):
        return v.reshape(seqs, sz.steps, CHUNKS, d).transpose(0, 2, 1, 3).reshape(seqs, length, d)

    stream, grad = to_rows(tokens), to_rows(cotangent)
    kept, diagonals = [], []
    for l in range(LAYERS):
        save = (True,) if l + 1 < LAYERS else ()
        normed, decay, inflow, cand, f_f, f_i, f_c, cp, ch, fin = gate_forward(
            sz, stream, gains[l], biases[l], weights[l], (True,)
        )
        if standard:
            near, beside = parts_at[l]
            if l + 1 < LAYERS:
                line_g1 = line_gather(pos, [after(parts_g1[0], fin), *parts_g1[1:]], rows[2:3])

            def hold(step, other):
                if step == 0:
                    return [line_g1] if l + 1 < LAYERS else []
                if step == 1:
                    diagonals.append(cross(after(near, other, beside), SECOND))
                return []

            ent, _ = enter(fin, seqs, False, (), hold)
            diagonal = diagonals[l] = after(diagonals[l], ent)
            rest = plane_gather(pos, lines_at[l], [near, beside, diagonal])
            weights[l] = view([weights[l]["f"][0], rest])
        else:
            ent, _ = enter(fin, seqs, False)
        hidden, hb, e, mid, n2, act, slope, result = mix_forward(
            sz, stream, gains[l], decay, inflow, cp, ch, ent, weights[l], l == LAYERS - 1, save
        )
        if standard and l + 1 < LAYERS:
            own, *others = line_parts(after(packs[2 * l + 3], ent))
            line_r = line_gather(pos, [after(own, result), *others], rows[2 * l + 3 : 2 * l + 4])
            sent_g = after(line_g1, diagonal)
            parts_g = [cross(sent_g, FIRST), cross(sent_g, SECOND)]
            parts_g.append(cross(after(parts_g[0], line_r), SECOND))
            sent_r = after(line_r, *parts_g[:2])
            weights.append(view([plane_gather(pos, line_g1, parts_g, (result,)), None]))
            lines_at.append(line_r)
            parts_at.append([cross(sent_r, FIRST), cross(sent_r, SECOND)])
        kept.append((stream, normed, decay, cand, f_f, f_i, f_c, hidden, hb, e, mid, n2, act, slope))
        stream = result
    output = from_rows(stream)

    vector_grads, sums, pending = [None] * LAYERS, [], []
    above = None
    for l in reversed(range(LAYERS)):
        x, normed, decay, cand, f_f, f_i, f_c, hidden, hb, e, mid, n2, act, slope = kept[l]
        place = far if l + 1 < LAYERS else lambda a: a
        decay, cand, f_f, f_i, f_c, hidden = map(far, (decay, cand, f_f, f_i, f_c, hidden))
        mid, slope = place(mid), place(slope)
        gr, gpre, gmid, go, ggain_two, gh, cp, ca, fin = mlp_backward(sz, grad, gains[l], mid, slope, decay, weights[l])

        def up(message):
            if above:
                message = above_up.step(message)
            return up_weights(sz, pos, place(after(n2, message)), gpre)

        def down(message):
            if above:
                message = above.step(message)
            return row_weights(sz, pos, place(after(act, message)), gr, "down_weights")

        def out(message):
            return row_weights(sz, pos, place(after(hb, message)), go, "out_weights")

        def both(message):
            return [*down(message), *out(message)]

        def begin(message):
            if above:
                message = above_up.step(message)
            exchanged = core_exchange([made[0], made[1][:2], made[1][2:]])
            upright = None
            if not above:
                upright = UprightReduction(pos, [(l, "u")], (after(exchanged[0][0], message), exchanged[0][1]))
                message = upright.seen
            (keep, got), *others = exchanged[1:]
            begun.extend([exchanged, upright, Reduction(pos, [(l, "d"), (l, "o")], [(after(keep, message), got), *others])])
            return [begun[2].seen]

        made, begun = [], []

        def keep_made(work):
            def run(message):
                made.append(work(message))
                return made[-1]

            return run

        if standard:
            ent, _ = enter(fin, seqs, True, (keep_made(up), keep_made(both), begin))
            exchanged, upright, mlp = begun
            gmid = after(gmid, mlp.seen)
        else:
            ent, pairs = enter(fin, seqs, True, (up, down, out))
        final = []
        if l == 0 and standard:
            final = [(ggain_two, 3)]
            for at in range(1, LAYERS):
                final += [(v, 4 * at + row) for v, row in zip(vector_grads[at], (0, 1, 3))]
        *gate_pair, gbias, grad, ggain_one = gate_backward(
            sz, pos, x, gains[l], gmid, gh, decay, hidden, e, cand, f_f, f_i, f_c, cp, ca, ent, far(normed), weights[l],
            l == 0, final,
        )
        vector_grads[l] = (ggain_one, gbias, ggain_two)
        if not standard:
            pending.append((l, pairs + [gate_pair]))
            continue
        names = [(l, m) for m in "fic"]
        if l == 0:
            names += [(at, k) for at in range(LAYERS) for k in range(4)]
        if above:
            gate_pair[1] = after(gate_pair[1], above.step(gate_pair[0]))
        ((keep, got),) = core_exchange([gate_pair])
        gates = Reduction(pos, names, [(keep, got)])
        if l == 0:
            upright = UprightReduction(pos, [(l, "u")], (after(exchanged[0][0], gates.seen), exchanged[0][1]))
        if l > 0:
            grad, above, above_up = after(grad, gates.seen), mlp, upright
            above.join(gates)
            continue
        mlp.step(above.step(upright.seen))
        gates.step(mlp.seen)
        above_up.step(upright.step(above.total(gates.seen)))
        mlp.join(gates)
        mlp.step(above_up.seen)
        upright.step(mlp.seen)
        mlp.step(above_up.total(upright.step()))
        sums = [(one.names, one.parts) for one in (above, above_up, mlp, upright)]
    grad_tokens = from_rows(grad)

    if standard:
        layout, ins = [], []
        for names, parts in sums:
            pieces = [(order[m], l, False) if m in order else (6 + m, l, True) for l, m in names]
            layout.append((len(parts), pieces))
            ins += [whole(p) for p in parts]
        found = call(
            functools.partial(finish_kernel, layout), 1, ins,
            [whole_out(m.shape) for m in matrices.values()] + [whole_out(v.shape) for v in vectors], [], 3, "finish",
        )
        g_up, g_down, g_out, g_f, g_i, g_c, g_norm, g_fb, g_ib, g_mlp = found
    else:
        per_layer = {}
        for l, pairs in pending:
            blocks = [jnp.stack([keep, send], axis=2).reshape(NS, NB, -1, LANE) for keep, send in pairs]
            gates = jnp.split(blocks[3], 3, axis=2)
            for m, g in zip("udofic", blocks[:3] + gates):
                v = unslab(g, matrices[m].shape[1] * seq_count, matrices[m].shape[2] * batch_count)
                v = lax.psum_scatter(v, "seq", scatter_dimension=0, tiled=True)
                per_layer[m, l] = lax.psum_scatter(v, "batch", scatter_dimension=1, tiled=True).astype(F32)
        g_up, g_down, g_out, g_f, g_i, g_c = [
            jnp.stack([per_layer[m, l] for l in range(LAYERS)]) for m in matrices
        ]
        rows = [
            (ggain_one[0], gbias[0], gbias[1], ggain_two[0]) for ggain_one, gbias, ggain_two in vector_grads
        ]
        g_norm, g_fb, g_ib, g_mlp = [
            lax.psum(lax.psum_scatter(jnp.stack([r[k] for r in rows]), "seq", scatter_dimension=1, tiled=True), "batch")
            for k in range(4)
        ]
    return output, grad_tokens, g_norm, g_f, g_i, g_c, g_fb, g_ib, g_out, g_mlp, g_up, g_down


def solution(mesh):
    split, vector, matrix = P("batch", "seq", None), P(None, "seq"), P(None, "seq", "batch")
    order = (vector, matrix, matrix, matrix, vector, vector, matrix, vector, matrix, matrix)
    return jax.shard_map(
        body,
        mesh=mesh,
        in_specs=(split,) + order + (split,),
        out_specs=(split, split) + order,
        check_vma=False,
    )
```

```python
import functools

import jax
import jax.numpy as jnp
from jax import lax
from jax.experimental import pallas as pl
from jax.experimental.pallas import tpu as pltpu
from jax.sharding import PartitionSpec as P

LAYERS = 2
EPS = 1e-05
NS, NB, LANE = 8, 4, 128
CHUNKS = 8
STEPS = 2
GATE_STEPS = 4
TURN, WIDE = 2, 256
VMEM = 28 * 1024 * 1024
F32, BF16 = jnp.float32, jnp.bfloat16


def dot(left, right):
    return lax.dot_general(left, right, (((1,), (0,)), ((), ())), preferred_element_type=F32)


def dot_nt(left, right):
    return lax.dot_general(left, right, (((1,), (1,)), ((), ())), preferred_element_type=F32)


def dot_tn(left, right):
    return lax.dot_general(left, right, (((0,), (0,)), ((), ())), preferred_element_type=F32)


def columns_of(ref, slabs=2):
    rows = ref.shape[2] // slabs
    parts = [
        ref[:, b, j * rows : (j + 1) * rows, :].reshape(NS * rows, LANE) for b in range(ref.shape[1]) for j in range(slabs)
    ]
    return jnp.concatenate(parts, axis=1)


def rows_of(ref):
    parts = [ref[:, j].reshape(-1, LANE) for j in range(NB)]
    return jnp.concatenate(parts, axis=1)


def rms_scale(values):
    return lax.rsqrt(jnp.mean(values * values, axis=-1, keepdims=True) + EPS)


def rms_back(values, gain, grad):
    scale = rms_scale(values)
    unit = values * scale
    inner = grad * gain
    back = scale * (inner - unit * jnp.mean(inner * unit, axis=-1, keepdims=True))
    return back, jnp.sum(grad * unit, axis=0, keepdims=True)


def gate_kernel(
    seqs, steps, x_ref, gain_ref, bias_ref, wf_ref, wi_ref, wc_ref,
    normed_ref, decay_ref, inflow_ref, cand_ref, ff_ref, fi_ref, fc_ref, cp_ref, ch_ref, fin_ref,
    z,
):
    width = decay_ref.shape[1]

    @pl.when(pl.program_id(0) == 0)
    def _():
        x = x_ref[...].astype(F32)
        normed_ref[...] = (x * rms_scale(x) * gain_ref[0:1, :]).astype(BF16)

    weights = jnp.concatenate([columns_of(ref) for ref in (wf_ref, wi_ref, wc_ref)], axis=1)
    block = TURN * CHUNKS
    places = [(seq, left) for seq in range(seqs) for left in range(0, width, WIDE)]

    def turn(of, at, carry):
        carry = list(carry)
        for k, (seq, left) in enumerate(places):
            if seq != of:
                continue
            span = slice(seq * steps * CHUNKS + at * block, seq * steps * CHUNKS + (at + 1) * block)
            cols = slice(left, left + WIDE)
            f = z[span, cols] + bias_ref[0:1, cols]
            i = z[span, width + left : width + left + WIDE] + bias_ref[1:2, cols]
            c = z[span, 2 * width + left : 2 * width + left + WIDE]
            low = jnp.minimum(jnp.minimum(f, i), 0.0)
            e0, ef, ei = jnp.exp(low), jnp.exp(low - f), jnp.exp(low - i)
            a, b = e0 + ef, e0 + ei
            inv = 1.0 / (a + b)
            decay, other = b * inv, a * inv
            ec = jnp.exp(-jnp.abs(c))
            cand = jnp.maximum(c, 0.0) + jnp.log1p(ec)
            slope = jnp.where(c >= 0.0, 1.0, ec) / (1.0 + ec)
            inflow = other * cand
            decay_ref[span, cols] = decay
            inflow_ref[span, cols] = inflow
            cand_ref[span, cols] = cand
            ff_ref[span, cols] = (ef * inv * decay).astype(BF16)
            fi_ref[span, cols] = (ei * inv * other).astype(BF16)
            fc_ref[span, cols] = (other * slope).astype(BF16)
            prod, state = carry[2 * k], carry[2 * k + 1]
            for t in range(TURN):
                d = decay[t * CHUNKS : (t + 1) * CHUNKS]
                prod = prod * d
                state = state * d + inflow[t * CHUNKS : (t + 1) * CHUNKS]
            carry[2 * k], carry[2 * k + 1] = prod, state
        return tuple(carry)

    one, zero = jnp.ones((CHUNKS, WIDE), F32), jnp.zeros((CHUNKS, WIDE), F32)
    carry = (one, zero) * len(places)
    for seq in range(seqs):
        rows = slice(seq * steps * CHUNKS, (seq + 1) * steps * CHUNKS)
        z[rows, :] = dot(normed_ref[rows, :], weights)
        for at in range(steps // TURN):
            carry = turn(seq, at, carry)
    for k, (seq, left) in enumerate(places):
        prod, state = carry[2 * k], carry[2 * k + 1]
        cols = slice(left, left + WIDE)
        cp_ref[seq, :, cols], ch_ref[seq, :, cols] = prod, state
        whole, last = prod[0:1], state[0:1]
        for c in range(1, CHUNKS):
            whole, last = whole * prod[c : c + 1], last * prod[c : c + 1] + state[c : c + 1]
        fin_ref[seq : seq + 1, cols] = whole
        fin_ref[seqs + seq : seqs + seq + 1, cols] = last


def mix_kernel(
    seqs, steps, x_ref, gain_ref, decay_ref, inflow_ref, cp_ref, ch_ref, ent_ref, wo_ref, wu_ref, wd_ref,
    hidden_ref, hb_ref, e_ref, mid_ref, n2_ref, act_ref, slope_ref, out_ref,
    acc,
):
    at_step = pl.program_id(0)
    block = TURN * CHUNKS
    width = decay_ref.shape[1]
    places = [(seq, left) for seq in range(seqs) for left in range(0, width, WIDE)]

    @pl.when(at_step == 0)
    def _():
        acc[...] = x_ref[...].astype(F32)

    @pl.when(at_step < STEPS)
    def _():
        for seq in range(seqs):
            state = ent_ref[seq : seq + 1, :]
            for c in range(CHUNKS):
                e_ref[seq, c : c + 1, :] = state
                state = state * cp_ref[seq, c : c + 1, :] + ch_ref[seq, c : c + 1, :]

        def turn(at, carry):
            carry = list(carry)
            for k, (seq, left) in enumerate(places):
                span = pl.ds(pl.multiple_of(seq * steps * CHUNKS + at * block, block), block)
                cols = slice(left, left + WIDE)
                d, u = decay_ref[span, cols], inflow_ref[span, cols]
                state, found = carry[k], []
                for t in range(TURN):
                    state = state * d[t * CHUNKS : (t + 1) * CHUNKS] + u[t * CHUNKS : (t + 1) * CHUNKS]
                    found.append(state)
                carry[k] = state
                hidden = jnp.concatenate(found, axis=0)
                hidden_ref[span, cols] = hidden
                hb_ref[span, cols] = hidden.astype(BF16)
            return tuple(carry)

        lax.fori_loop(0, steps // TURN, turn, tuple(e_ref[seq, :, left : left + WIDE] for seq, left in places))
        acc[...] += dot(hb_ref[...], rows_of(wo_ref))

    @pl.when(at_step == STEPS - 1)
    def _():
        middle = acc[...]
        mid_ref[...] = middle
        n2_ref[...] = (middle * rms_scale(middle) * gain_ref[1:2, :]).astype(BF16)

    @pl.when(at_step >= STEPS)
    def _():
        w_up, w_down = columns_of(wu_ref, 4), rows_of(wd_ref)
        size = acc.shape[0] // 2
        for k in range(2):
            span = slice(k * size, (k + 1) * size)
            v = dot(n2_ref[span, :], w_up)
            phi = 0.5 + 0.5 * lax.erf(v * 0.7071067811865476)
            act = (v * phi).astype(BF16)
            act_ref[span, :] = act
            slope_ref[span, :] = (phi + v * (0.3989422804014327 * jnp.exp(v * v * -0.5))).astype(BF16)
            acc[span, :] += dot(act, w_down)

    @pl.when(at_step == 2 * STEPS - 1)
    def _():
        out_ref[...] = acc[...].astype(out_ref.dtype)


def mlp_back_kernel(
    seqs, steps, g_ref, gain_ref, mid_ref, slope_ref, decay_ref, wo_ref, wu_ref, wd_ref,
    gr_ref, gpre_ref, gmid_ref, go_ref, ggain_ref, gh_ref, cp_ref, ca_ref, fin_ref,
    acc,
):
    at_step = pl.program_id(0)
    block = TURN * CHUNKS
    width = decay_ref.shape[1]
    places = [(seq, left) for seq in range(seqs) for left in range(0, width, WIDE)]

    @pl.when(at_step == 0)
    def _():
        gr_ref[...] = g_ref[...].astype(BF16)
        acc[...] = jnp.zeros_like(acc)

    @pl.when(at_step < STEPS)
    def _():
        gact = dot_nt(gr_ref[...], rows_of(wd_ref))
        gpre_ref[...] = (gact * slope_ref[...].astype(F32)).astype(BF16)
        acc[...] += dot_nt(gpre_ref[...], columns_of(wu_ref, 4))

    @pl.when(at_step == STEPS - 1)
    def _():
        back, ggain = rms_back(mid_ref[...], gain_ref[1:2, :], acc[...])
        ggain_ref[...] = ggain
        gmid = g_ref[...].astype(F32) + back
        gmid_ref[...] = gmid
        go_ref[...] = gmid.astype(BF16)

    @pl.when(at_step >= STEPS)
    def _():
        gh_ref[...] = dot_nt(go_ref[...], rows_of(wo_ref))

        def turn(turn_at, carry):
            at = steps // TURN - 1 - turn_at
            carry = list(carry)
            for k, (seq, left) in enumerate(places):
                span = pl.ds(pl.multiple_of(seq * steps * CHUNKS + at * block, block), block)
                cols = slice(left, left + WIDE)
                d, g = decay_ref[span, cols], gh_ref[span, cols]
                prod, state = carry[2 * k], carry[2 * k + 1]
                for t in reversed(range(TURN)):
                    dk = d[t * CHUNKS : (t + 1) * CHUNKS]
                    prod = prod * dk
                    state = dk * (g[t * CHUNKS : (t + 1) * CHUNKS] + state)
                carry[2 * k], carry[2 * k + 1] = prod, state
            return tuple(carry)

        one, zero = jnp.ones((CHUNKS, WIDE), F32), jnp.zeros((CHUNKS, WIDE), F32)
        carry = lax.fori_loop(0, steps // TURN, turn, (one, zero) * len(places))
        for k, (seq, left) in enumerate(places):
            prod, state = carry[2 * k], carry[2 * k + 1]
            cols = slice(left, left + WIDE)
            cp_ref[seq, :, cols], ca_ref[seq, :, cols] = prod, state
            whole, last = prod[CHUNKS - 1 :], state[CHUNKS - 1 :]
            for c in reversed(range(CHUNKS - 1)):
                whole, last = whole * prod[c : c + 1], last * prod[c : c + 1] + state[c : c + 1]
            fin_ref[seq : seq + 1, cols] = whole
            fin_ref[seqs + seq : seqs + seq + 1, cols] = last


def gate_back_kernel(
    seqs, steps, others, pos_ref, x_ref, gain_ref, gmid_ref, gh_ref, decay_ref, hidden_ref, e_ref, cand_ref,
    ff_ref, fi_ref, fc_ref, cp_ref, ca_ref, ent_ref, normed_ref, wf_ref, wi_ref, wc_ref, *refs,
):
    given = refs[: len(others)]
    keep_ref, send_ref, gbias_ref, gstream_ref, ggain_ref, acc, start, dz, rest = refs[len(others) :]
    at_step = pl.program_id(0)
    block = TURN * CHUNKS
    width = decay_ref.shape[1]
    places = [(seq, left) for seq in range(seqs) for left in range(0, width, WIDE)]

    @pl.when(at_step == 0)
    def _():
        acc[...] = jnp.zeros_like(acc)

    for seq in range(seqs):
        state = ent_ref[seq : seq + 1, :]
        for c in reversed(range(CHUNKS)):
            start[seq, c : c + 1, :] = state
            state = state * cp_ref[seq, c : c + 1, :] + ca_ref[seq, c : c + 1, :]

    def turn(of, at, carry):
        carry = list(carry)
        for k, (seq, left) in enumerate(places):
            if seq != of:
                continue
            cols = slice(left, left + WIDE)
            state, sum_f, sum_i = carry[3 * k : 3 * k + 3]
            base = seq * steps * CHUNKS + at * block
            span = slice(base, base + block)
            before = hidden_ref[base - CHUNKS : base, cols] if at else e_ref[seq, :, cols]
            d, g = decay_ref[span, cols], gh_ref[span, cols]
            previous = jnp.concatenate([before, hidden_ref[span, cols][: block - CHUNKS]], axis=0)
            found = []
            for t in reversed(range(TURN)):
                now = g[t * CHUNKS : (t + 1) * CHUNKS] + state
                found.append(now)
                state = d[t * CHUNKS : (t + 1) * CHUNKS] * now
            gstate = jnp.concatenate(found[::-1], axis=0)
            both = gstate * (cand_ref[span, cols] - previous)
            dzf = (-ff_ref[span, cols].astype(F32) * both).astype(BF16)
            dzi = (fi_ref[span, cols].astype(F32) * both).astype(BF16)
            dz[span, left : left + WIDE] = dzf
            dz[span, width + left : width + left + WIDE] = dzi
            dz[span, 2 * width + left : 2 * width + left + WIDE] = (fc_ref[span, cols].astype(F32) * gstate).astype(BF16)
            wide_f, wide_i = dzf.astype(F32), dzi.astype(F32)
            for t in range(TURN):
                sum_f = sum_f + wide_f[t * CHUNKS : (t + 1) * CHUNKS]
                sum_i = sum_i + wide_i[t * CHUNKS : (t + 1) * CHUNKS]
            carry[3 * k : 3 * k + 3] = state, sum_f, sum_i
        return tuple(carry)

    zero = jnp.zeros((CHUNKS, WIDE), F32)
    first_carry = [v for seq, left in places for v in (start[seq, :, left : left + WIDE], zero, zero)]
    carry = tuple(first_carry)
    weights = jnp.concatenate([columns_of(ref) for ref in (wf_ref, wi_ref, wc_ref)], axis=1)
    grad = None
    for seq in range(seqs):
        rows = slice(seq * steps * CHUNKS, (seq + 1) * steps * CHUNKS)
        for at in reversed(range(steps // TURN)):
            carry = turn(seq, at, carry)
        acc[rows, :] += dot_nt(dz[rows, :], weights)
        part = dot_tn(normed_ref[rows, :], dz[rows, :])
        grad = part if grad is None else grad + part
    for row in range(2):
        for left in range(0, width, WIDE):
            total = sum(carry[3 * k + 1 + row] for k, place in enumerate(places) if place[1] == left)
            gbias_ref[row : row + 1, left : left + WIDE] = jnp.sum(total, axis=0, keepdims=True)
    rows = wf_ref.shape[2]
    for m in range(3):
        put_columns(pos_ref, keep_ref, send_ref, m * rows, grad[:, m * width : (m + 1) * width])

    @pl.when(at_step == STEPS - 1)
    def _():
        back, ggain = rms_back(x_ref[...].astype(F32), gain_ref[0:1, :], acc[...])
        ggain_ref[...] = ggain
        gstream_ref[...] = (gmid_ref[...] + back).astype(gstream_ref.dtype)

    if others:

        def rows_to(ref, first_row):
            wide = ref.shape[1] // NS
            for r in range(ref.shape[0]):
                for s in range(NS):
                    rest[s, first_row + r : first_row + r + 1, :wide] = ref[r : r + 1, s * wide : (s + 1) * wide]

        @pl.when(at_step == 0)
        def _():
            rest[...] = jnp.zeros_like(rest)
            for ref, first_row in zip(given, others):
                rows_to(ref, first_row)

        wide = width * STEPS // NS
        for row in range(2):
            for s in range(width // wide):
                rest[at_step * (width // wide) + s, 1 + row : 2 + row, :wide] = gbias_ref[row : row + 1, s * wide : (s + 1) * wide]

        @pl.when(at_step == STEPS - 1)
        def _():
            rows_to(ggain_ref, 0)
            found = rest[...].astype(BF16)
            for x in range(2):
                keep_ref[:, x, 3 * rows :, :] = found
                send_ref[:, x, 3 * rows :, :] = found


def send_or_keep(mine, keep_ref, send_ref, put):
    @pl.when(mine)
    def _():
        put(keep_ref)

    @pl.when(jnp.logical_not(mine))
    def _():
        put(send_ref)


def put_columns(pos_ref, keep_ref, send_ref, start, value):
    count = NB // pl.num_programs(0)
    rows, width = value.shape[0] // NS, value.shape[1] // count
    for block in range(count):
        x, core = pl.program_id(0) * (count // 2) + block // 2, block % 2
        parts = [
            value[:, left : left + LANE].astype(BF16).reshape(NS, rows, LANE)
            for left in range(block * width, (block + 1) * width, LANE)
        ]

        def put(ref):
            for j, part in enumerate(parts):
                ref[:, x, start + j * rows : start + (j + 1) * rows, :] = part

        send_or_keep(pos_ref[0] == core, keep_ref, send_ref, put)


def put_rows(pos_ref, keep_ref, send_ref, value):
    count = NS // pl.num_programs(0)
    for j in range(NB):
        part = value[:, j * LANE : (j + 1) * LANE].astype(BF16).reshape(count, -1, LANE)

        def put(ref):
            ref[pl.ds(pl.program_id(0) * count, count), j // 2] = part

        send_or_keep(pos_ref[0] == j % 2, keep_ref, send_ref, put)


def up_weight_kernel(pos_ref, n2_ref, gpre_ref, keep_ref, send_ref):
    put_columns(pos_ref, keep_ref, send_ref, 0, dot_tn(n2_ref[...], gpre_ref[...]))


def row_weight_kernel(pos_ref, left_ref, right_ref, keep_ref, send_ref):
    put_rows(pos_ref, keep_ref, send_ref, dot_tn(left_ref[...], right_ref[...]))


def add(*parts):
    total = parts[0].astype(F32)
    for part in parts[1:]:
        total = total + part.astype(F32)
    return total


def pair_sum_kernel(rows, pos_ref, *refs):
    count = len(rows)
    send, stay = refs[2 * count :]
    core, x, y, step = pos_ref[0], pos_ref[1], pos_ref[2], pos_ref[4]
    at = 0
    for keep, got, r in zip(refs[:count], refs[count : 2 * count], rows):
        for v in range(2):
            for out, first in ((send, 1 - step), (stay, step)):
                iy, ix = jnp.where(core == 0, v, first), jnp.where(core == 0, first, v)
                out[0, v, at : at + r] = add(keep[0, iy, ix], got[0, iy, ix]).astype(BF16)
        at += r


def plane_sum_kernel(pos_ref, *refs):
    second = pos_ref[5]
    *pairs, send, stay = refs
    at = 0
    for keep, got in zip(pairs[::2], pairs[1::2]):
        rows = slice(at, at + keep.shape[2])
        send[0, rows, :] = add(keep[0, 1 - second], got[0, 1 - second]).astype(BF16)
        stay[0, rows, :] = add(keep[0, second], got[0, second]).astype(BF16)
        at += keep.shape[2]


def line_sum_kernel(pos_ref, *refs):
    core, first = pos_ref[0], pos_ref[6]
    *pairs, send, stay = refs
    at = 0
    for keep, got in zip(pairs[::2], pairs[1::2]):
        rows = slice(at, at + keep.shape[1])
        for v in range(2):
            for out, f in ((send, 1 - first), (stay, first)):
                z = jnp.where(core == 0, f + 2 * v, 2 * f + v)
                out[v, rows, :] = add(keep[z], got[z]).astype(BF16)
        at += keep.shape[1]


def last_sum_kernel(pos_ref, keep, got, send, stay):
    second = pos_ref[7]
    send[...] = add(keep[1 - second], got[1 - second]).astype(BF16)
    stay[...] = add(keep[second], got[second]).astype(BF16)


def total_kernel(keep, got, out):
    out[...] = add(keep[...], got[...])


def finish_kernel(layout, *refs):
    at = 0
    ins = sum(parts for parts, _ in layout)
    outs = refs[ins:]
    for parts, pieces in layout:
        got = refs[at : at + parts]
        at += parts
        row = 0
        for out, layer, vectors in pieces:
            ref = outs[out]
            if vectors:
                ref[layer : layer + 1, :] = add(*[g[...] for g in got])[row : row + 1, : ref.shape[1]]
                row += 1
                continue
            r = ref.shape[1]
            for j in range(ref.shape[2] // LANE):
                ref[layer, :, j * LANE : (j + 1) * LANE] = add(*[g[row : row + r] for g in got])
                row += r


def pack_kernel(groups, *refs):
    ins = refs[: len(refs) - len(groups) - 1]
    outs, scratch = refs[len(ins) : -1], refs[-1]
    for out, group in zip(outs, groups):
        row = 0
        vec = 0
        for which, layer, vector in group:
            ref = ins[which]
            if vector:
                if vec == 0:
                    scratch[...] = jnp.zeros_like(scratch)
                scratch[vec : vec + 1, : ref.shape[1]] = ref[...].astype(F32)[layer : layer + 1]
                vec += 1
                continue
            r = ref.shape[1]
            for j in range(ref.shape[2] // LANE):
                out[row : row + r, :] = ref[layer, :, j * LANE : (j + 1) * LANE]
                row += r
        if vec:
            out[row:, :] = scratch[...].astype(BF16)


def line_gather_kernel(pos_ref, *refs):
    row = 0
    for out in refs[4:]:
        rows = out.shape[1]
        for k, part in enumerate(refs[:4]):
            out[pos_ref[3] ^ k] = part[row : row + rows, :]
        row += rows


def plane_gather_kernel(pos_ref, *refs):
    out = refs[-1]
    at, half = pl.program_id(0), pl.num_programs(0) // 2
    core, x, y = pos_ref[0], pos_ref[1], pos_ref[2]
    count = len(refs) // 2
    for c in range(2):
        own, first, second, *diagonal = refs[count * c : count * (c + 1)]
        other = core ^ c
        turn = other if count == 4 else 0
        out[0, y, x, other] = own[0]
        out[0, y ^ turn, x ^ (1 - turn), other] = first[0]
        out[0, y ^ (1 - turn), x ^ turn, other] = second[0]
        if count == 4:
            out[0, y ^ 1, x ^ 1, other] = diagonal[0][0]
            continue

        @pl.when(at < half)
        def _():
            out[0, y ^ 1, x ^ 1, other] = diagonal[0][0]

        @pl.when(at >= half)
        def _():
            out[0, y ^ 1, x ^ 1, other] = diagonal[1][0]


def vector_kernel(gained, w_ref, *refs):
    outs, scratch = refs[:-1], refs[-1]
    scratch[...] = w_ref[:, 0].astype(F32)
    for l in range(LAYERS):
        for which in range(4):
            out, row = ((outs[2 * l], which // 3) if which in (0, 3) else (outs[2 * l + 1], which - 1))
            wide = out.shape[1] // NS
            for s in range(NS):
                out[row : row + 1, s * wide : (s + 1) * wide] = scratch[s, 4 * l + which : 4 * l + which + 1, :wide]


def shape(dims, dtype=F32):
    return jax.ShapeDtypeStruct(dims, dtype)


def call(kernel, grid, ins, outs, scratch, us, name):
    def spec(a, block, index):
        if a.dtype == jnp.int32:
            return pl.BlockSpec(memory_space=pltpu.SMEM)
        return pl.BlockSpec(block, index)

    found = pl.pallas_call(
        kernel,
        grid=(grid,),
        in_specs=[spec(*one) for one in ins],
        out_specs=[pl.BlockSpec(block, index) for _, block, index, *_ in outs],
        out_shape=[pltpu.HBM(one[0].shape, one[0].dtype) if one[3:] else one[0] for one in outs],
        scratch_shapes=scratch,
        compiler_params=pltpu.CompilerParams(vmem_limit_bytes=VMEM),
        cost_estimate=pl.CostEstimate(flops=int(us * 1.1e9) + 1, bytes_accessed=1024, transcendentals=0),
        name=name,
    )(*[a for a, _, _ in ins])
    return found if len(found) > 1 else found[0]


def far(array):
    return pltpu.with_memory_space_constraint(array, pltpu.HBM)


def anywhere(array):
    return array


def whole(array):
    dims = array.shape
    return (array, dims, lambda i: (0,) * len(dims))


def whole_out(dims, dtype=F32):
    return (shape(dims, dtype), dims, lambda i: (0,) * len(dims))


def first(i):
    return jnp.minimum(i, STEPS - 1)


def second(i):
    return jnp.maximum(i - STEPS, 0)


class Sizes:
    def __init__(self, seqs, length, d, h, ff):
        self.seqs, self.steps, self.n = seqs, length // CHUNKS, seqs * length
        self.d, self.h, self.ff = d, h, ff
        self.hb, self.fb = h // STEPS, ff // STEPS


def column_weight(view, at, late=False, steps=STEPS):
    array, rows, place = view
    return (far(array) if late else array, (NS, NB // steps, rows, LANE), lambda i: (0, at(i), place, 0))


def row_weight(view, at):
    array, rows, place = view
    return (array, (NS // STEPS, NB, rows, LANE), lambda i: (at(i), 0, place, 0))


def same(i):
    return i


def gate_forward(sz, x, gain, bias, w, save):
    n, d, h, wide, s = sz.n, sz.d, sz.h, sz.h // GATE_STEPS, sz.seqs
    col = lambda i: (0, i)
    return call(
        functools.partial(gate_kernel, s, sz.steps), GATE_STEPS,
        [whole(x), whole(gain), (bias, (2, wide), col)] + [column_weight(w[m], same, False, GATE_STEPS) for m in "fic"],
        [whole_out((n, d), BF16) + save]
        + [(shape((n, h)), (n, wide), col) + save, (shape((n, h)), (n, wide), col), (shape((n, h)), (n, wide), col) + save]
        + [(shape((n, h), BF16), (n, wide), col) + save] * 3
        + [(shape((s, CHUNKS, h)), (s, CHUNKS, wide), lambda i: (0, 0, i))] * 2
        + [(shape((2 * s, h)), (2 * s, wide), col)],
        [pltpu.VMEM((n, 3 * wide), F32)], 9, "gates",
    )


def mix_forward(sz, x, gain, decay, inflow, cp, ch, ent, wt, last, save):
    n, d, h, ff, w, f, s = sz.n, sz.d, sz.h, sz.ff, sz.hb, sz.fb, sz.seqs
    col = lambda i: (0, first(i))
    late = lambda i: (0, second(i))
    deep = lambda i: (0, 0, first(i))
    return call(
        functools.partial(mix_kernel, s, sz.steps), 2 * STEPS,
        [
            whole(x), whole(gain), (decay, (n, w), col), (inflow, (n, w), col),
            (cp, (s, CHUNKS, w), deep), (ch, (s, CHUNKS, w), deep), (ent, (s, w), col),
            row_weight(wt["o"], first), column_weight(wt["u"], second), row_weight(wt["d"], second),
        ],
        [
            (shape((n, h)), (n, w), col, True), (shape((n, h), BF16), (n, w), col) + save,
            (shape((s, CHUNKS, h)), (s, CHUNKS, w), deep) + save,
            whole_out((n, d)) + save, whole_out((n, d), BF16) + save,
            (shape((n, ff), BF16), (n, f), late) + save, (shape((n, ff), BF16), (n, f), late) + save,
            whole_out((n, d), BF16 if last else F32),
        ],
        [pltpu.VMEM((n, d), F32)], 14, "mix",
    )


def mlp_backward(sz, g, gain, mid, slope, decay, wt):
    n, d, h, ff, w, f, s = sz.n, sz.d, sz.h, sz.ff, sz.hb, sz.fb, sz.seqs
    col = lambda i: (0, second(i))
    early = lambda i: (0, first(i))
    deep = lambda i: (0, 0, second(i))
    return call(
        functools.partial(mlp_back_kernel, s, sz.steps), 2 * STEPS,
        [
            whole(g), whole(gain), whole(mid), (slope, (n, f), early), (decay, (n, w), col),
            row_weight(wt["o"], second), column_weight(wt["u"], first), row_weight(wt["d"], first),
        ],
        [
            whole_out((n, d), BF16), (shape((n, ff), BF16), (n, f), early), whole_out((n, d)), whole_out((n, d), BF16),
            whole_out((1, d)), (shape((n, h)), (n, w), col),
            (shape((s, CHUNKS, h)), (s, CHUNKS, w), deep), (shape((s, CHUNKS, h)), (s, CHUNKS, w), deep),
            (shape((2 * s, h)), (2 * s, w), col),
        ],
        [pltpu.VMEM((n, d), F32)], 12, "mlp_back",
    )


def gate_backward(sz, pos, x, gain, gmid, gh, decay, hidden, e, cand, ff_, fi_, fc_, cp, ca, ent, normed, wt, last, vectors):
    n, d, h, w, s = sz.n, sz.d, sz.h, sz.hb, sz.seqs
    col = lambda i: (0, i)
    deep = lambda i: (0, 0, i)
    wide = lambda a: (a, (n, w), col)
    rows = 3 * d * h // (32 * LANE) + (16 if vectors else 0)
    return call(
        functools.partial(gate_back_kernel, s, sz.steps, tuple(row for _, row in vectors)), STEPS,
        [
            whole(pos), whole(x), whole(gain), whole(gmid), wide(gh), wide(decay), wide(hidden), (e, (s, CHUNKS, w), deep),
            wide(cand), wide(ff_), wide(fi_), wide(fc_), (cp, (s, CHUNKS, w), deep), (ca, (s, CHUNKS, w), deep),
            (ent, (s, w), col), whole(normed),
        ] + [column_weight(wt[m], same, True) for m in "fic"] + [whole(v) for v, _ in vectors],
        [whole_out((NS, 2, rows, LANE), BF16)] * 2
        + [(shape((2, h)), (2, w), col), whole_out((n, d), BF16 if last else F32), whole_out((1, d))],
        [
            pltpu.VMEM((n, d), F32), pltpu.VMEM((s, CHUNKS, w), F32), pltpu.VMEM((n, 3 * w), BF16),
            pltpu.VMEM((NS, 16, LANE), F32),
        ], 16, "gate_back",
    )


def up_weights(sz, pos, n2, gpre):
    n, d, ff = sz.n, sz.d, sz.ff
    dims = (NS, 2, d * ff // (32 * LANE), LANE)
    return call(
        up_weight_kernel, 1, [whole(pos), whole(n2), whole(gpre)],
        [whole_out(dims, BF16)] * 2, [], 5, "up_weights",
    )


def row_weights(sz, pos, left, right, name):
    n, k, d = sz.n, left.shape[1], sz.d
    dims = (NS, 2, k // NS, LANE)
    return call(
        row_weight_kernel, 1, [whole(pos), whole(left), whole(right)],
        [whole_out(dims, BF16)] * 2, [], 5, name,
    )


def swap(array, axes, bits):
    count = lax.axis_size(axes)
    return lax.ppermute(array, axes, [(i, i ^ bits) for i in range(count)])


BOTH = ("seq", "batch")


def after(array, *others):
    return lax.optimization_barrier((array,) + others)[0]


def by_line(a):
    return (a, (1,) + a.shape[1:], lambda i: (i,) + (0,) * (len(a.shape) - 1))


def by_line_out(*dims):
    return (shape(dims, BF16), (1,) + dims[1:], lambda i: (i,) + (0,) * (len(dims) - 1))


def core_exchange(pairs):
    return [(keep, swap(send, "batch", 1)) for keep, send in pairs]


FIRST, SECOND, FIRST_Z, SECOND_Z = (2, 4), (4, 2), (8, 16), (16, 8)


def cross(array, bits):
    count = lax.axis_size(BOTH)
    return lax.ppermute(array, BOTH, [(i, i ^ bits[i % 2]) for i in range(count)])


def pair_sum(pos, pairs):
    rows, lines = tuple(keep.shape[2] for keep, _ in pairs), pairs[0][0].shape[0] // 2
    view = lambda a: by_line(a.reshape((lines, 2, 2) + a.shape[2:]))
    return call(
        functools.partial(pair_sum_kernel, rows), lines,
        [whole(pos)] + [view(keep) for keep, _ in pairs] + [view(got) for _, got in pairs],
        [by_line_out(lines, 2, sum(rows), LANE)] * 2, [], 3, "pair_sum",
    )


def onward(parts, bits):
    return [parts[1], cross(parts[0], bits)]


def plane_sum(pos, parts):
    rows, lines = sum(part.shape[2] for part in parts[::2]), parts[0].shape[0]
    return call(
        plane_sum_kernel, lines, [whole(pos)] + [by_line(a) for a in parts], [by_line_out(lines, rows, LANE)] * 2, [], 0,
        "plane_sum",
    )


def line_sum(pos, parts):
    rows = sum(part.shape[1] for part in parts[::2])
    return call(
        line_sum_kernel, 1, [whole(pos)] + [whole(a) for a in parts], [whole_out((2, rows, LANE), BF16)] * 2, [], 0, "line_sum",
    )


def last_sum(pos, parts):
    rows = parts[0].shape[1]
    return call(
        last_sum_kernel, 1, [whole(pos)] + [whole(a) for a in parts], [whole_out((rows, LANE), BF16)] * 2, [], 0, "last_sum",
    )


SUMS = ((plane_sum, SECOND), (line_sum, FIRST_Z), (last_sum, SECOND_Z))


class Reduction:
    def __init__(self, pos, names, pairs):
        self.pos, self.names, self.stage = pos, names, 0
        self.parts = pair_sum(pos, pairs)
        self.seen = self.parts[0]
        self.parts = onward(self.parts, FIRST)

    def join(self, other):
        self.names, self.parts = self.names + other.names, self.parts + other.parts

    def step(self, *others):
        work, bits = SUMS[self.stage]
        if others:
            self.parts[0] = after(self.parts[0], *others)
        parts = work(self.pos, self.parts)
        self.stage, self.seen, self.parts = self.stage + 1, parts[0], onward(parts, bits)
        return self.seen

    def one_more(self, others, work, bits):
        if others:
            self.parts[0] = after(self.parts[0], *others)
        parts = work(self.pos, self.parts)
        self.seen, self.parts = parts[0], onward(parts, bits)
        return self.seen

    def total(self, *others):
        keep, got = self.parts
        keep = after(keep, *others)
        total = call(total_kernel, 1, [whole(keep), whole(got)], [whole_out(keep.shape)], [], 0, "total")
        self.parts = [total]
        return total


class UprightReduction(Reduction):
    def __init__(self, pos, names, pair):
        self.pos, self.names, self.stage = pos, names, 0
        self.rows = pair[0].shape[2]
        self.parts = [part.reshape(4, 4 * self.rows, LANE) for part in pair]
        self.one_more((), line_sum, FIRST_Z)

    def step(self, *others):
        self.stage += 1
        if self.stage == 1:
            return self.one_more(others, last_sum, SECOND_Z)
        if self.stage == 2:
            pairs = lambda pos, parts: pair_sum(pos, [tuple(part.reshape(2, 2, self.rows, LANE) for part in parts)])
            return self.one_more(others, pairs, FIRST)
        self.one_more(others, plane_sum, SECOND)
        self.parts = [part[0] for part in self.parts]
        return self.seen


def line_parts(own):
    return [own] + [swap(own, "seq", 2 * k) for k in range(1, 4)]


def line_gather(pos, parts, rows, place=anywhere):
    return call(
        line_gather_kernel, 1, [whole(pos)] + [whole(place(p)) for p in parts],
        [whole_out((4, r, LANE), BF16) for r in rows], [], 2, "line_gather",
    )


X_AXIS, Y_AXIS = ("batch", 2), ("seq", 1)


def plane_gather(pos, line, parts, behind=(), place=anywhere):
    rows = line.shape[1]
    parts = [line, *parts]
    parts += [swap(after(p, *behind) if behind else p, "batch", 1) for p in parts]
    each, low, high = (lambda i: (i, 0, 0)), (lambda i: (jnp.minimum(i, 1), 0, 0)), (lambda i: (jnp.maximum(i - 2, 0), 0, 0))
    maps = [each] * 4 if len(parts) == 8 else [each, each, each, low, high]
    got = call(
        plane_gather_kernel, 4, [whole(pos)] + [(place(p), (1, rows, LANE), m) for p, m in zip(parts, maps * 2)],
        [(shape((4, 2, 2, 2, rows, LANE), BF16), (1, 2, 2, 2, rows, LANE), lambda i: (i, 0, 0, 0, 0, 0))], [], 5, "plane_gather",
    )
    return got.reshape(NS, NB, rows, LANE)


def enter(fin, seqs, backward, fill=(), hold=None):
    count, mine = lax.axis_size("seq"), lax.axis_index("seq")
    prod, state = fin[:seqs], fin[seqs:]
    pre_p, pre_s = jnp.ones_like(prod), jnp.zeros_like(state)
    bit, message, done, other = 1, fin, [], fin
    for step in range(int(count).bit_length() - 1):
        before = hold(step, other) if hold else ()
        if before:
            message = after(message, *before)
        other = lax.ppermute(message, "seq", [(i, i ^ bit) for i in range(count)])
        if step < len(fill):
            done.append(fill[step](message))
        if done and bit * 2 == count:
            other = after(other, *done[-1])
        o_p, o_s = other[:seqs], other[seqs:]
        upper = ((mine // bit) % 2 == 1) ^ backward
        pre_p, pre_s = jnp.where(upper, o_p * pre_p, pre_p), jnp.where(upper, pre_p * o_s + pre_s, pre_s)
        state = jnp.where(upper, prod * o_s + state, o_p * state + o_s)
        prod = prod * o_p
        message = jnp.concatenate([prod, state])
        if step < len(fill):
            message = after(message, *done[-1])
        bit *= 2
    return pre_s, done


def slabs(matrix, seq_count, batch_count):
    rows, cols = matrix.shape[0] // NS, matrix.shape[1] // NB
    cut = matrix.reshape(NS, rows, NB, cols // LANE, LANE).transpose(0, 2, 3, 1, 4)
    return cut.reshape(NS, NB, rows * cols // LANE, LANE)


def unslab(blocks, rows, cols):
    r, c = rows // NS, cols // NB
    cut = blocks.reshape(NS, NB, c // LANE, r, LANE).transpose(0, 3, 1, 2, 4)
    return cut.reshape(rows, cols)


def body(
    tokens, norm_gain, w_forget, w_input, w_cand, forget_bias, input_bias, w_out, mlp_gain, w_up, w_down, cotangent
):
    seqs, length, d = tokens.shape
    seq_count, batch_count = lax.axis_size("seq"), lax.axis_size("batch")
    h, ff = w_forget.shape[2] * batch_count, w_up.shape[2] * batch_count
    sz = Sizes(seqs, length, d, h, ff)
    standard = (seq_count, batch_count) == (NS, NB)
    matrices = {"u": w_up, "d": w_down, "o": w_out, "f": w_forget, "i": w_input, "c": w_cand}
    vectors = (norm_gain, forget_bias, input_bias, mlp_gain)
    slab_rows = {"u": d * ff // (32 * LANE), "d": ff // NS, "o": h // NS}
    slab_rows.update({m: d * h // (32 * LANE) for m in "fic"})
    order = {name: k for k, name in enumerate(matrices)}

    if standard:
        s_at, b_at = lax.axis_index("seq"), lax.axis_index("batch")
        core, x, y, z = b_at % 2, b_at // 2, s_at % 2, s_at // 2
        turned = [jnp.where(core == 0, a, b) for a, b in ((x, y), (y, x), (z % 2, z // 2), (z // 2, z % 2))]
        pos = jnp.stack([core, x, y, z, *turned]).astype(jnp.int32)
        vecs = [(6 + k, at, True) for at in range(LAYERS) for k in range(4)]
        groups = []
        for l in range(LAYERS):
            groups += [[(order[m], l, False) for m in "fic"] + vecs * (l == 0), [(order[m], l, False) for m in "udo"]]
        gate_rows, rest_rows = sum(slab_rows[m] for m in "fic"), sum(slab_rows[m] for m in "udo")
        rows = [gate_rows + 16, rest_rows] + [gate_rows, rest_rows] * (LAYERS - 1)
        packs = call(
            functools.partial(pack_kernel, groups), 1,
            [whole(far(m)) for m in matrices.values()] + [whole(far(v)) for v in vectors],
            [whole_out((r, LANE), BF16) for r in rows], [pltpu.VMEM((16, LANE), F32)], 2, "pack",
        )
        line_g0 = line_gather(pos, line_parts(packs[0]), rows[:1], anywhere)
        parts_g0 = [swap(line_g0, *X_AXIS), swap(line_g0, *Y_AXIS)]
        parts_g0 += [swap(parts_g0[0][:2], *Y_AXIS), swap(parts_g0[1][2:], *X_AXIS)]
        line_r0 = line_gather(pos, line_parts(after(packs[1], line_g0)), rows[1:2])
        sent_r0 = after(line_r0, *parts_g0[:2])
        parts_r0 = [cross(sent_r0, FIRST), cross(sent_r0, SECOND)]
        parts_g1 = line_parts(after(packs[2], line_r0, *parts_g0[2:]))
        got = [plane_gather(pos, line_g0, parts_g0, (), anywhere), None]
        places = {"f": 0, "i": 1, "c": 2, "u": 0, "d": 1, "o": 4}
        view = lambda got: {m: (got[m in "udo"], slab_rows[m], places[m]) for m in "udofic"}
        weights, lines_at, parts_at = [view(got)], [line_r0], [parts_r0]
        vecs = call(
            functools.partial(vector_kernel, None), 1,
            [(got[0], (NS, 1, 16, LANE), lambda i: (0, 0, 3 * slab_rows["f"] // 16, 0))],
            [whole_out((2, size)) for l in range(LAYERS) for size in (d, h)],
            [pltpu.VMEM((NS, 16, LANE), F32)], 1, "vectors",
        )
        gains, biases = vecs[0::2], vecs[1::2]
    else:
        pos = jnp.zeros((8,), jnp.int32)

        def full(m):
            m = lax.all_gather(m, "batch", axis=1, tiled=True)
            return lax.all_gather(m, "seq", axis=0, tiled=True)

        weights = [
            {m: (slabs(full(matrices[m][l]), NS, NB), slab_rows[m], 0) for m in "udofic"} for l in range(LAYERS)
        ]
        whole_vectors = [lax.all_gather(v, "seq", axis=1, tiled=True).astype(F32) for v in vectors]
        gains = [jnp.stack([whole_vectors[0][l], whole_vectors[3][l]]) for l in range(LAYERS)]
        biases = [jnp.stack([whole_vectors[1][l], whole_vectors[2][l]]) for l in range(LAYERS)]

    def to_rows(v):
        return v.reshape(seqs, CHUNKS, sz.steps, d).transpose(0, 2, 1, 3).reshape(sz.n, d)

    def from_rows(v):
        return v.reshape(seqs, sz.steps, CHUNKS, d).transpose(0, 2, 1, 3).reshape(seqs, length, d)

    stream, grad = to_rows(tokens), to_rows(cotangent)
    kept, diagonals = [], []
    for l in range(LAYERS):
        save = (True,) if l + 1 < LAYERS else ()
        normed, decay, inflow, cand, f_f, f_i, f_c, cp, ch, fin = gate_forward(
            sz, stream, gains[l], biases[l], weights[l], (True,)
        )
        if standard:
            near, beside = parts_at[l]
            if l + 1 < LAYERS:
                line_g1 = line_gather(pos, [after(parts_g1[0], fin), *parts_g1[1:]], rows[2:3])

            def hold(step, other):
                if step == 0:
                    return [line_g1] if l + 1 < LAYERS else []
                if step == 1:
                    diagonals.append(cross(after(near, other, *([beside] if l == 0 else [])), SECOND))
                return [beside] if step == 2 and l else []

            ent, _ = enter(fin, seqs, False, (), hold)
            diagonal = diagonals[l] = after(diagonals[l], ent)
            rest = plane_gather(pos, lines_at[l], [near, beside, diagonal])
            weights[l] = view([weights[l]["f"][0], rest])
        else:
            ent, _ = enter(fin, seqs, False)
        hidden, hb, e, mid, n2, act, slope, result = mix_forward(
            sz, stream, gains[l], decay, inflow, cp, ch, ent, weights[l], l == LAYERS - 1, save
        )
        if standard and l + 1 < LAYERS:
            own, *others = line_parts(after(packs[2 * l + 3], ent))
            line_r = line_gather(pos, [after(own, result), *others], rows[2 * l + 3 : 2 * l + 4])
            sent_g = after(line_g1, diagonal)
            parts_g = [cross(sent_g, FIRST), cross(sent_g, SECOND)]
            parts_g.append(cross(after(parts_g[0], line_r), SECOND))
            sent_r = after(line_r, *parts_g[:2])
            weights.append(view([plane_gather(pos, line_g1, parts_g, (result,)), None]))
            lines_at.append(line_r)
            parts_at.append([cross(sent_r, FIRST), cross(sent_r, SECOND)])
        kept.append((stream, normed, decay, cand, f_f, f_i, f_c, hidden, hb, e, mid, n2, act, slope))
        stream = result
    output = from_rows(stream)

    vector_grads, sums, pending = [None] * LAYERS, [], []
    above = None
    for l in reversed(range(LAYERS)):
        x, normed, decay, cand, f_f, f_i, f_c, hidden, hb, e, mid, n2, act, slope = kept[l]
        place = far if l + 1 < LAYERS else lambda a: a
        decay, cand, f_f, f_i, f_c, hidden = map(far, (decay, cand, f_f, f_i, f_c, hidden))
        mid, slope = place(mid), place(slope)
        gr, gpre, gmid, go, ggain_two, gh, cp, ca, fin = mlp_backward(sz, grad, gains[l], mid, slope, decay, weights[l])

        def up(message):
            if above:
                message = above_up.step(message)
            return up_weights(sz, pos, place(after(n2, message)), gpre)

        def down(message):
            if above:
                message = above.step(message)
            return row_weights(sz, pos, place(after(act, message)), gr, "down_weights")

        def out(message):
            return row_weights(sz, pos, place(after(hb, message)), go, "out_weights")

        def both(message):
            return [*down(message), *out(message)]

        def begin(message):
            if above:
                message = above_up.step(message)
            exchanged = core_exchange([made[0], made[1][:2], made[1][2:]])
            upright = None
            if not above:
                upright = UprightReduction(pos, [(l, "u")], (after(exchanged[0][0], message), exchanged[0][1]))
                message = upright.seen
            (keep, got), *others = exchanged[1:]
            begun.extend([exchanged, upright, Reduction(pos, [(l, "d"), (l, "o")], [(after(keep, message), got), *others])])
            return [begun[2].seen]

        made, begun = [], []

        def keep_made(work):
            def run(message):
                made.append(work(message))
                return made[-1]

            return run

        if standard:
            ent, _ = enter(fin, seqs, True, (keep_made(up), keep_made(both), begin))
            exchanged, upright, mlp = begun
            gmid = after(gmid, mlp.seen)
        else:
            ent, pairs = enter(fin, seqs, True, (up, down, out))
        final = []
        if l == 0 and standard:
            final = [(ggain_two, 3)]
            for at in range(1, LAYERS):
                final += [(v, 4 * at + row) for v, row in zip(vector_grads[at], (0, 1, 3))]
        *gate_pair, gbias, grad, ggain_one = gate_backward(
            sz, pos, x, gains[l], gmid, gh, decay, hidden, e, cand, f_f, f_i, f_c, cp, ca, ent, far(normed), weights[l],
            l == 0, final,
        )
        vector_grads[l] = (ggain_one, gbias, ggain_two)
        if not standard:
            pending.append((l, pairs + [gate_pair]))
            continue
        names = [(l, m) for m in "fic"]
        if l == 0:
            names += [(at, k) for at in range(LAYERS) for k in range(4)]
        if above:
            gate_pair[1] = after(gate_pair[1], above.step(gate_pair[0]))
        ((keep, got),) = core_exchange([gate_pair])
        gates = Reduction(pos, names, [(keep, got)])
        if l == 0:
            upright = UprightReduction(pos, [(l, "u")], (after(exchanged[0][0], gates.seen), exchanged[0][1]))
        if l > 0:
            grad, above, above_up = after(grad, gates.seen), mlp, upright
            above.join(gates)
            continue
        mlp.step(above.step(upright.seen))
        gates.step(mlp.seen)
        above_up.step(upright.step(above.total(gates.seen)))
        mlp.join(gates)
        mlp.step(above_up.seen)
        upright.step(mlp.seen)
        mlp.step(above_up.total(upright.step()))
        sums = [(one.names, one.parts) for one in (above, above_up, mlp, upright)]
    grad_tokens = from_rows(grad)

    if standard:
        layout, ins = [], []
        for names, parts in sums:
            pieces = [(order[m], l, False) if m in order else (6 + m, l, True) for l, m in names]
            layout.append((len(parts), pieces))
            ins += [whole(p) for p in parts]
        found = call(
            functools.partial(finish_kernel, layout), 1, ins,
            [whole_out(m.shape) for m in matrices.values()] + [whole_out(v.shape) for v in vectors], [], 3, "finish",
        )
        g_up, g_down, g_out, g_f, g_i, g_c, g_norm, g_fb, g_ib, g_mlp = found
    else:
        per_layer = {}
        for l, pairs in pending:
            blocks = [jnp.stack([keep, send], axis=2).reshape(NS, NB, -1, LANE) for keep, send in pairs]
            gates = jnp.split(blocks[3], 3, axis=2)
            for m, g in zip("udofic", blocks[:3] + gates):
                v = unslab(g, matrices[m].shape[1] * seq_count, matrices[m].shape[2] * batch_count)
                v = lax.psum_scatter(v, "seq", scatter_dimension=0, tiled=True)
                per_layer[m, l] = lax.psum_scatter(v, "batch", scatter_dimension=1, tiled=True).astype(F32)
        g_up, g_down, g_out, g_f, g_i, g_c = [
            jnp.stack([per_layer[m, l] for l in range(LAYERS)]) for m in matrices
        ]
        rows = [
            (ggain_one[0], gbias[0], gbias[1], ggain_two[0]) for ggain_one, gbias, ggain_two in vector_grads
        ]
        g_norm, g_fb, g_ib, g_mlp = [
            lax.psum(lax.psum_scatter(jnp.stack([r[k] for r in rows]), "seq", scatter_dimension=1, tiled=True), "batch")
            for k in range(4)
        ]
    return output, grad_tokens, g_norm, g_f, g_i, g_c, g_fb, g_ib, g_out, g_mlp, g_up, g_down


def solution(mesh):
    split, vector, matrix = P("batch", "seq", None), P(None, "seq"), P(None, "seq", "batch")
    order = (vector, matrix, matrix, matrix, vector, vector, matrix, vector, matrix, matrix)
    return jax.shard_map(
        body,
        mesh=mesh,
        in_specs=(split,) + order + (split,),
        out_specs=(split, split) + order,
        check_vma=False,
    )
```
